32 devices in a mesh: batch: 16 (over z, y, x), rows: 2 (over core).
Axes of the slice: x: 2, y: 2, z: 4, core: 2. Of those that a mesh axis runs over, the one named last changes fastest.
Arguments:
- images: bfloat16 [2, 16, 64, 16, 1024], P(None, 'rows', 'batch'), may hold values from -6 to 6
- crop_sizes: int32 [2, 64], replicated, may hold values from 8 to 16, as said below
- reduce_a: bfloat16 [1024, 512], replicated, may hold values from -0.1875 to 0.1875
- reduce_gain_a: float32 [512], replicated, may hold values from 0.25 to 1.75
- reduce_bias_a: float32 [512], replicated, may hold values from -2 to 2
- spatial_a: bfloat16 [4608, 512], replicated, may hold values from -0.09375 to 0.09375
- spatial_gain_a: float32 [512], replicated, may hold values from 0.25 to 1.75
- spatial_bias_a: float32 [512], replicated, may hold values from -2 to 2
- expand_a: bfloat16 [512, 2048], replicated, may hold values from -0.25 to 0.25
- expand_gain_a: float32 [2048], P('rows'), may hold values from 0.25 to 1.75
- expand_bias_a: float32 [2048], P('rows'), may hold values from -2 to 2
- project_a: bfloat16 [1024, 2048], replicated, may hold values from -0.1875 to 0.1875
- project_gain_a: float32 [2048], P('rows'), may hold values from 0.25 to 1.75
- project_bias_a: float32 [2048], P('rows'), may hold values from -2 to 2
- squeeze_a: bfloat16 [2048, 128], P('rows'), may hold values from -0.25 to 0.25
- squeeze_bias_a: float32 [128], replicated, may hold values from -2.5 to 2.5
- excite_a: bfloat16 [128, 2048], P(None, 'rows'), may hold values from -1 to 1
- excite_bias_a: float32 [2048], P('rows'), may hold values from -4 to 4
- reduce_b: bfloat16 [2048, 512], P('rows'), may hold values from -0.125 to 0.125
- reduce_gain_b: float32 [512], replicated, may hold values from 0.25 to 1.75
- reduce_bias_b: float32 [512], replicated, may hold values from -2 to 2
- spatial_b: bfloat16 [4608, 512], replicated, may hold values from -0.09375 to 0.09375
- spatial_gain_b: float32 [512], replicated, may hold values from 0.25 to 1.75
- spatial_bias_b: float32 [512], replicated, may hold values from -2 to 2
- expand_b: bfloat16 [512, 2048], replicated, may hold values from -0.25 to 0.25
- expand_gain_b: float32 [2048], P('rows'), may hold values from 0.25 to 1.75
- expand_bias_b: float32 [2048], P('rows'), may hold values from -2 to 2
- squeeze_b: bfloat16 [2048, 128], P('rows'), may hold values from -0.25 to 0.25
- squeeze_bias_b: float32 [128], replicated, may hold values from -2.5 to 2.5
- excite_b: bfloat16 [128, 2048], P(None, 'rows'), may hold values from -1 to 1
- excite_bias_b: float32 [2048], P('rows'), may hold values from -4 to 4
- cotangent: bfloat16 [2, 8, 64, 8, 2048], P(None, None, 'batch', None, 'rows'), may hold values from -6 to 6
Outputs:
- block_out: bfloat16 [2, 8, 64, 8, 2048], P(None, None, 'batch', None, 'rows')
- images_grad: float32 [2, 16, 64, 16, 1024], P(None, 'rows', 'batch')
- grad_reduce_a: float32 [524288], P(('batch', 'rows'))
- grad_reduce_gain_a: float32 [512], replicated
- grad_reduce_bias_a: float32 [512], replicated
- grad_spatial_a: float32 [2359296], P(('batch', 'rows'))
- grad_spatial_gain_a: float32 [512], replicated
- grad_spatial_bias_a: float32 [512], replicated
- grad_expand_a: float32 [1048576], P(('batch', 'rows'))
- grad_expand_gain_a: float32 [2048], P('rows')
- grad_expand_bias_a: float32 [2048], P('rows')
- grad_project_a: float32 [2097152], P(('batch', 'rows'))
- grad_project_gain_a: float32 [2048], P('rows')
- grad_project_bias_a: float32 [2048], P('rows')
- grad_squeeze_a: float32 [2048, 128], P('rows')
- grad_squeeze_bias_a: float32 [128], replicated
- grad_excite_a: float32 [128, 2048], P(None, 'rows')
- grad_excite_bias_a: float32 [2048], P('rows')
- grad_reduce_b: float32 [2048, 512], P('rows')
- grad_reduce_gain_b: float32 [512], replicated
- grad_reduce_bias_b: float32 [512], replicated
- grad_spatial_b: float32 [2359296], P(('batch', 'rows'))
- grad_spatial_gain_b: float32 [512], replicated
- grad_spatial_bias_b: float32 [512], replicated
- grad_expand_b: float32 [1048576], P(('batch', 'rows'))
- grad_expand_gain_b: float32 [2048], P('rows')
- grad_expand_bias_b: float32 [2048], P('rows')
- grad_squeeze_b: float32 [2048, 128], P('rows')
- grad_squeeze_bias_b: float32 [128], replicated
- grad_excite_b: float32 [128, 2048], P(None, 'rows')
- grad_excite_bias_b: float32 [2048], P('rows')
The draws below stay inside these ranges and needn't reach their ends.
Inputs may be any that keep to these rules, and one draw needn't show every extreme that they name: crop_sizes[m, b] is the live side of image b's map in micro-batch m, either 16 or 8; both occur in every micro-batch.
All inputs are finite; a program needn't handle non-finite values.
Results may differ from the reference program's by a relative error of at most 0.025.
Values may be sent and summed in bfloat16 or wider, within the bound.
No kernel may reach another device: no remote copies, remote signals or barrier semaphores. Data moves between devices by JAX's collectives and lax.ppermute only.
A program may use at most 256 MiB of HBM per device.

```python
import jax
import jax.numpy as jnp
from jax import lax

C_IN = 1024
C_MID = 512
C_OUT = 2048
C_SE = 128
H = 16
MICRO = 2
H2 = 8
IMAGES = 64


def draw_crop_sizes(key, part):
    key = jax.random.fold_in(key, 11)
    coins = jax.random.randint(key, (MICRO, IMAGES), 0, 2)
    places = jnp.arange(IMAGES, dtype=jnp.int32)
    coins = jnp.where(places[None, :] == 0, 1, coins)
    coins = jnp.where(places[None, :] == 1, 0, coins)
    return (H // 2 * (1 + coins)).astype(jnp.int32)


def block_levels(stream_key, shape, pieces, smallest, high):
    level = 1.0
    for axis_at, blocks in pieces:
        steps = jax.random.uniform(jax.random.fold_in(jax.random.fold_in(stream_key, 6), axis_at), (blocks,), jnp.float32, smallest / len(pieces), high / len(pieces))
        level = level * jnp.repeat(jnp.exp(steps), shape[axis_at] // blocks).reshape((-1,) + (1,) * (len(shape) - 1 - axis_at))
    return level


def centred(own_key, extent, scale, reach, shards=(), kind=jnp.bfloat16):
    drawn = scale * jax.random.normal(own_key, extent, jnp.float32)
    if shards:
        drawn = drawn * block_levels(own_key, extent, shards, -0.22, 0.18)
    return jnp.clip(drawn, -reach, reach).astype(kind)


def setup_inputs(seed: int = 0) -> dict:
    key_of = jax.random.split(jax.random.key(seed), 33)
    images = centred(key_of[0], (MICRO, H, IMAGES, H, C_IN), 1.0, 6.0, ((1, 2), (2, 16)))
    crop_sizes = draw_crop_sizes(jax.random.fold_in(key_of[32], 71), 0)
    reduce_a = centred(key_of[2], (C_IN, C_MID), C_IN ** -0.5, 0.1875)
    reduce_gain_a = jnp.clip(1.0 + 0.15 * jax.random.normal(key_of[3], (C_MID,), jnp.float32), 0.25, 1.75)
    reduce_bias_a = centred(key_of[4], (C_MID,), 0.4, 2.0, (), jnp.float32)
    spatial_a = centred(key_of[5], (9 * C_MID, C_MID), (9 * C_MID) ** -0.5, 0.09375)
    spatial_gain_a = jnp.clip(1.0 + 0.15 * jax.random.normal(key_of[6], (C_MID,), jnp.float32), 0.25, 1.75)
    spatial_bias_a = centred(key_of[7], (C_MID,), 0.4, 2.0, (), jnp.float32)
    expand_a = centred(key_of[8], (C_MID, C_OUT), C_MID ** -0.5, 0.25)
    expand_gain_a = jnp.clip(1.0 + 0.15 * jax.random.normal(key_of[9], (C_OUT,), jnp.float32), 0.25, 1.75)
    expand_bias_a = centred(key_of[10], (C_OUT,), 0.4, 2.0, ((0, 2),), jnp.float32)
    project_a = centred(key_of[11], (C_IN, C_OUT), C_IN ** -0.5, 0.1875)
    project_gain_a = jnp.clip(1.0 + 0.15 * jax.random.normal(key_of[12], (C_OUT,), jnp.float32), 0.25, 1.75)
    project_bias_a = centred(key_of[13], (C_OUT,), 0.4, 2.0, ((0, 2),), jnp.float32)
    squeeze_a = centred(key_of[14], (C_OUT, C_SE), (C_OUT // 4) ** -0.5, 0.25, ((0, 2),))
    squeeze_bias_a = centred(key_of[15], (C_SE,), 0.5, 2.5, (), jnp.float32)
    excite_a = centred(key_of[16], (C_SE, C_OUT), (C_SE // 4) ** -0.5, 1.0, ((1, 2),))
    excite_bias_a = centred(key_of[17], (C_OUT,), 1.0, 4.0, ((0, 2),), jnp.float32)
    reduce_b = centred(key_of[18], (C_OUT, C_MID), C_OUT ** -0.5, 0.125, ((0, 2),))
    reduce_gain_b = jnp.clip(1.0 + 0.15 * jax.random.normal(key_of[19], (C_MID,), jnp.float32), 0.25, 1.75)
    reduce_bias_b = centred(key_of[20], (C_MID,), 0.4, 2.0, (), jnp.float32)
    spatial_b = centred(key_of[21], (9 * C_MID, C_MID), (9 * C_MID) ** -0.5, 0.09375)
    spatial_gain_b = jnp.clip(1.0 + 0.15 * jax.random.normal(key_of[22], (C_MID,), jnp.float32), 0.25, 1.75)
    spatial_bias_b = centred(key_of[23], (C_MID,), 0.4, 2.0, (), jnp.float32)
    expand_b = centred(key_of[24], (C_MID, C_OUT), C_MID ** -0.5, 0.25)
    expand_gain_b = jnp.clip(1.0 + 0.15 * jax.random.normal(key_of[25], (C_OUT,), jnp.float32), 0.25, 1.75)
    expand_bias_b = centred(key_of[26], (C_OUT,), 0.4, 2.0, ((0, 2),), jnp.float32)
    squeeze_b = centred(key_of[27], (C_OUT, C_SE), (C_OUT // 4) ** -0.5, 0.25, ((0, 2),))
    squeeze_bias_b = centred(key_of[28], (C_SE,), 0.5, 2.5, (), jnp.float32)
    excite_b = centred(key_of[29], (C_SE, C_OUT), (C_SE // 4) ** -0.5, 1.0, ((1, 2),))
    excite_bias_b = centred(key_of[30], (C_OUT,), 1.0, 4.0, ((0, 2),), jnp.float32)
    cotangent = centred(key_of[31], (MICRO, H2, IMAGES, H2, C_OUT), 1.0, 6.0, ((2, 16), (4, 2)))
    return {"images": images, "crop_sizes": crop_sizes, "reduce_a": reduce_a, "reduce_gain_a": reduce_gain_a, "reduce_bias_a": reduce_bias_a, "spatial_a": spatial_a, "spatial_gain_a": spatial_gain_a, "spatial_bias_a": spatial_bias_a, "expand_a": expand_a, "expand_gain_a": expand_gain_a, "expand_bias_a": expand_bias_a, "project_a": project_a, "project_gain_a": project_gain_a, "project_bias_a": project_bias_a, "squeeze_a": squeeze_a, "squeeze_bias_a": squeeze_bias_a, "excite_a": excite_a, "excite_bias_a": excite_bias_a, "reduce_b": reduce_b, "reduce_gain_b": reduce_gain_b, "reduce_bias_b": reduce_bias_b, "spatial_b": spatial_b, "spatial_gain_b": spatial_gain_b, "spatial_bias_b": spatial_bias_b, "expand_b": expand_b, "expand_gain_b": expand_gain_b, "expand_bias_b": expand_bias_b, "squeeze_b": squeeze_b, "squeeze_bias_b": squeeze_bias_b, "excite_b": excite_b, "excite_bias_b": excite_bias_b, "cotangent": cotangent}


@jax.custom_vjp
def low(v):
    return lax.optimization_barrier(v.astype(jnp.bfloat16)).astype(jnp.float32)

@jax.custom_vjp
def low_back(v):
    return v

def low_keep(v):
    return (low(v), None)

def low_pass(kept, grad):
    return (grad,)

def back_keep(v):
    return (v, None)

def back_low(kept, grad):
    return (low(grad),)
low.defvjp(low_keep, low_pass)
low_back.defvjp(back_keep, back_low)
epsilon = 1e-05

def live_mask(limits, side_length):
    places = jnp.arange(side_length, dtype=jnp.int32)
    inside = (places[:, None, None] < limits[None, :, None]) & (places[None, None, :] < limits[None, :, None])
    return inside.astype(jnp.float32)[..., None]

def product(inputs, weight):
    return jnp.dot(inputs, weight, precision=lax.Precision.HIGHEST)

def patches(fields, stride):
    padded = jnp.pad(fields, ((1, 1), (0, 0), (1, 1), (0, 0)))
    out_rows = fields.shape[0] // stride
    out_cols = fields.shape[2] // stride
    return jnp.concatenate([padded[row_tap:row_tap + stride * out_rows:stride, :, col_tap:col_tap + stride * out_cols:stride, :] for row_tap in range(3) for col_tap in range(3)], axis=3)

def batch_norm(values, inside, counted, gain_term, bias_term):
    centre = lax.optimization_barrier(jnp.sum(values * inside, axis=(0, 1, 2))) / counted
    squares = lax.optimization_barrier(jnp.sum(values * values * inside, axis=(0, 1, 2)))
    inverse = lax.rsqrt(squares / counted - centre * centre + epsilon)
    return ((values - centre) * inverse * gain_term + bias_term) * inside

def excitation(normed, pixel_count, squeeze, squeeze_bias, excite, excite_bias):
    pooled = lax.optimization_barrier(jnp.sum(normed, axis=(0, 2))) / pixel_count[:, None]
    hidden = jax.nn.silu(product(pooled, squeeze) + squeeze_bias)
    gating = jax.nn.sigmoid(product(hidden, excite) + excite_bias)
    return gating[None, :, None, :]

def two_blocks(source, crop_size, weights):
    reduce_a, reduce_gain_a, reduce_bias_a, spatial_a, spatial_gain_a, spatial_bias_a, expand_a, expand_gain_a, expand_bias_a, project_a, project_gain_a, project_bias_a, squeeze_a, squeeze_bias_a, excite_a, excite_bias_a, reduce_b, reduce_gain_b, reduce_bias_b, spatial_b, spatial_gain_b, spatial_bias_b, expand_b, expand_gain_b, expand_bias_b, squeeze_b, squeeze_bias_b, excite_b, excite_bias_b = weights
    half_size = crop_size // 2
    inside_fine = live_mask(crop_size, source.shape[0])
    inside_coarse = live_mask(half_size, source.shape[0] // 2)
    count_fine = jnp.sum(crop_size * crop_size).astype(jnp.float32)
    count_coarse = jnp.sum(half_size * half_size).astype(jnp.float32)
    pixel_count = (half_size * half_size).astype(jnp.float32)
    conv_one = low_back(product(source, reduce_a))
    active_one = low(jax.nn.silu(batch_norm(conv_one, inside_fine, count_fine, reduce_gain_a, reduce_bias_a)))
    conv_two = low_back(product(patches(active_one, 2), spatial_a))
    active_two = low(jax.nn.silu(batch_norm(conv_two, inside_coarse, count_coarse, spatial_gain_a, spatial_bias_a)))
    expanded = low_back(low(product(active_two, expand_a)))
    projected = low_back(low(product(source[::2, :, ::2, :], project_a)))
    normed_three = batch_norm(expanded, inside_coarse, count_coarse, expand_gain_a, expand_bias_a)
    normed_side = batch_norm(projected, inside_coarse, count_coarse, project_gain_a, project_bias_a)
    gate_one = excitation(normed_three, pixel_count, squeeze_a, squeeze_bias_a, excite_a, excite_bias_a)
    middle = low(jax.nn.silu(normed_three * gate_one + normed_side))
    conv_four = low_back(product(middle, reduce_b))
    active_four = low(jax.nn.silu(batch_norm(conv_four, inside_coarse, count_coarse, reduce_gain_b, reduce_bias_b)))
    conv_five = low_back(product(patches(active_four, 1), spatial_b))
    active_five = low(jax.nn.silu(batch_norm(conv_five, inside_coarse, count_coarse, spatial_gain_b, spatial_bias_b)))
    expanded_b = low_back(low(product(active_five, expand_b)))
    normed_six = batch_norm(expanded_b, inside_coarse, count_coarse, expand_gain_b, expand_bias_b)
    gate_two = excitation(normed_six, pixel_count, squeeze_b, squeeze_bias_b, excite_b, excite_bias_b)
    return jax.nn.silu(normed_six * gate_two + middle)

def reference(images, crop_sizes, reduce_a, reduce_gain_a, reduce_bias_a, spatial_a, spatial_gain_a, spatial_bias_a, expand_a, expand_gain_a, expand_bias_a, project_a, project_gain_a, project_bias_a, squeeze_a, squeeze_bias_a, excite_a, excite_bias_a, reduce_b, reduce_gain_b, reduce_bias_b, spatial_b, spatial_gain_b, spatial_bias_b, expand_b, expand_gain_b, expand_bias_b, squeeze_b, squeeze_bias_b, excite_b, excite_bias_b, cotangent):
    weights = tuple((weight.astype(jnp.float32) for weight in (reduce_a, reduce_gain_a, reduce_bias_a, spatial_a, spatial_gain_a, spatial_bias_a, expand_a, expand_gain_a, expand_bias_a, project_a, project_gain_a, project_bias_a, squeeze_a, squeeze_bias_a, excite_a, excite_bias_a, reduce_b, reduce_gain_b, reduce_bias_b, spatial_b, spatial_gain_b, spatial_bias_b, expand_b, expand_gain_b, expand_bias_b, squeeze_b, squeeze_bias_b, excite_b, excite_bias_b)))

    def forward(fields, params):
        stepper = jax.checkpoint(two_blocks)

        def one_micro(inputs_pair):
            return stepper(inputs_pair[0], inputs_pair[1], params)
        return lax.map(one_micro, (fields, crop_sizes))
    outputs, pullback = jax.vjp(forward, images.astype(jnp.float32), weights)
    images_grad, weight_grads = pullback(cotangent.astype(jnp.float32))
    grad_reduce_a, grad_reduce_gain_a, grad_reduce_bias_a, grad_spatial_a, grad_spatial_gain_a, grad_spatial_bias_a, grad_expand_a, grad_expand_gain_a, grad_expand_bias_a, grad_project_a, grad_project_gain_a, grad_project_bias_a, grad_squeeze_a, grad_squeeze_bias_a, grad_excite_a, grad_excite_bias_a, grad_reduce_b, grad_reduce_gain_b, grad_reduce_bias_b, grad_spatial_b, grad_spatial_gain_b, grad_spatial_bias_b, grad_expand_b, grad_expand_gain_b, grad_expand_bias_b, grad_squeeze_b, grad_squeeze_bias_b, grad_excite_b, grad_excite_bias_b = weight_grads
    return (outputs.astype(jnp.bfloat16), images_grad, grad_reduce_a.reshape(-1), grad_reduce_gain_a, grad_reduce_bias_a, grad_spatial_a.reshape(-1), grad_spatial_gain_a, grad_spatial_bias_a, grad_expand_a.reshape(-1), grad_expand_gain_a, grad_expand_bias_a, grad_project_a.reshape(-1), grad_project_gain_a, grad_project_bias_a, grad_squeeze_a, grad_squeeze_bias_a, grad_excite_a, grad_excite_bias_a, grad_reduce_b, grad_reduce_gain_b, grad_reduce_bias_b, grad_spatial_b.reshape(-1), grad_spatial_gain_b, grad_spatial_bias_b, grad_expand_b.reshape(-1), grad_expand_gain_b, grad_expand_bias_b, grad_squeeze_b, grad_squeeze_bias_b, grad_excite_b, grad_excite_bias_b)
```

```python
import jax
import jax.numpy as jnp
from jax import lax
from jax.sharding import PartitionSpec as P

epsilon = 1e-05
HIGHEST = lax.Precision.HIGHEST
BF16 = jnp.bfloat16
F32 = jnp.float32

PLANE_TAPS = (((1, 0),), ((2, 0), (0, 1)))


def swapped(block, axis, mask):
    route = [(i, i ^ mask) for i in range(lax.axis_size(axis))]
    return lax.ppermute(block, axis, route)


def bits_of(size):
    return [1 << k for k in range(size.bit_length() - 1)]


def all_sum(parts):
    parts = parts + swapped(parts, "rows", 1)
    size = lax.axis_size("batch")
    spread = jnp.broadcast_to(parts[None], (size,) + parts.shape)
    return jnp.sum(lax.all_to_all(spread, "batch", 0, 0, tiled=True), axis=0)


def halved(block, orders):
    size = lax.axis_size("batch")
    place = lax.axis_index("batch")
    bits = bits_of(size)
    count = block.shape[1]
    cut = count // 2 // 16 * 16
    parts = []
    for part, order in zip((block[:, :cut], block[:, cut:]), orders(bits)):
        shape = part.shape[1:]
        left = list(reversed(bits))
        part = part.reshape((2,) * len(bits) + shape)
        for bit in order:
            axis = left.index(bit)
            mine = (place // bit) % 2
            gone = lax.dynamic_index_in_dim(part, 1 - mine, axis, keepdims=False)
            kept = lax.dynamic_index_in_dim(part, mine, axis, keepdims=False)
            total = kept.astype(F32) + swapped(gone, "batch", bit).astype(F32)
            left.pop(axis)
            part = total.astype(BF16) if left else total
        parts.append(part)
    return jnp.concatenate(parts, axis=0)


def two_orders(bits):
    return (bits, bits[1::-1] + bits[2:])


def collected(block):
    place = lax.axis_index("batch")
    block = block[None]
    for bit in bits_of(lax.axis_size("batch")):
        other = swapped(block, "batch", bit)
        upper = (place // bit) % 2 == 1
        block = jnp.concatenate([jnp.where(upper, other, block), jnp.where(upper, block, other)], axis=0)
    return block


def core_sum(block, axis):
    core = lax.axis_index("rows")
    gone = lax.dynamic_index_in_dim(block, 1 - core, axis, keepdims=False)
    kept = lax.dynamic_index_in_dim(block, core, axis, keepdims=False)
    return (kept.astype(F32) + swapped(gone, "rows", 1).astype(F32)).astype(BF16)


def both_cores(block, axis):
    core = lax.axis_index("rows")
    other = swapped(block, "rows", 1)
    first = jnp.where(core == 0, block, other)
    second = jnp.where(core == 0, other, block)
    return jnp.concatenate([first, second], axis=axis)


def silu_slope(values):
    sigma = jax.nn.sigmoid(values)
    return sigma * (1.0 + values * (1.0 - sigma))


def forward_dot(inputs, weight):
    return jnp.dot(inputs, weight, preferred_element_type=F32)


def input_dot(grads, weight):
    return lax.dot_general(
        grads, weight, (((grads.ndim - 1,), (1,)), ((), ())), preferred_element_type=F32
    )


def weight_dot(inputs, grads):
    leading = tuple(range(inputs.ndim - 1))
    return lax.dot_general(
        inputs, grads, ((leading, leading), ((), ())), preferred_element_type=F32
    )


def shifted(values, rows, cols):
    zero = jnp.zeros((), values.dtype)
    pads = [(0, 0, 0)] * values.ndim
    pads[1] = (-rows, rows, 0)
    pads[3] = (-cols, cols, 0)
    if rows == 0 and cols == 0:
        return values
    return lax.pad(values, zero, pads)


PIX = (1, 2, 3)
FPIX = (0, 1, 3, 4, 5)


def moments(first, second, axes):
    return jnp.stack([jnp.sum(first, axis=axes), jnp.sum(first * second, axis=axes)], axis=1)


def wide(vector):
    return vector[:, None, None, None, :]


def norm_of(sums, counted):
    centre = sums[:, 0] / counted
    inverse = lax.rsqrt(sums[:, 1] / counted - centre * centre + epsilon)
    return wide(centre), wide(inverse)


def norm_back(live_grad, scaled, inverse, gain, sums, counted, inside):
    mean = wide(sums[:, 0] / counted)
    slope = wide(sums[:, 1] / counted)
    return ((live_grad - (mean + scaled * slope)) * (gain * inverse) * inside).astype(BF16)


def gate_forward(normed, pixel_count, squeeze, squeeze_bias, excite, excite_bias):
    pooled = jnp.sum(normed, axis=(1, 3)) / pixel_count[..., None]
    pooled = pooled.reshape(-1, pooled.shape[-1])
    inner = jnp.dot(pooled, squeeze.astype(F32), precision=HIGHEST) + squeeze_bias
    hidden = jax.nn.silu(inner)
    gating = jax.nn.sigmoid(jnp.dot(hidden, excite.astype(F32), precision=HIGHEST) + excite_bias)
    return gating, (pooled, inner, hidden)


def gate_backward(gate_grad, gating, cache, pixel_count, squeeze, excite):
    pooled, inner, hidden = cache
    logit_grad = gate_grad * gating * (1.0 - gating)
    excite_grad = jnp.dot(hidden.T, logit_grad, precision=HIGHEST)
    hidden_grad = jnp.dot(logit_grad, excite.astype(F32).T, precision=HIGHEST)
    inner_grad = hidden_grad * silu_slope(inner)
    squeeze_grad = jnp.dot(pooled.T, inner_grad, precision=HIGHEST)
    pooled_grad = jnp.dot(inner_grad, squeeze.astype(F32).T, precision=HIGHEST)
    biases = (jnp.sum(inner_grad, axis=0), jnp.sum(logit_grad, axis=0))
    return pooled_grad / pixel_count.reshape(-1, 1), squeeze_grad, excite_grad, biases


def per_map(values, micro, images):
    return values.reshape(micro, 1, images, 1, values.shape[-1])


def folded(grad):
    size = lax.axis_size("batch")
    rows, width = grad.shape
    grad = grad.astype(BF16).reshape(size, 2, rows // (2 * size), width // 512, 512)
    return jnp.swapaxes(grad, 2, 3).reshape(size, 2, -1, 512)


def unfolded(block, width):
    count = width // 512
    rows = block.shape[0] // count
    return jnp.swapaxes(block.reshape(count, rows, 512), 0, 1).reshape(-1)


def per_device(
    images,
    crop_sizes,
    reduce_a,
    reduce_gain_a,
    reduce_bias_a,
    spatial_a,
    spatial_gain_a,
    spatial_bias_a,
    expand_a,
    expand_gain_a,
    expand_bias_a,
    project_a,
    project_gain_a,
    project_bias_a,
    squeeze_a,
    squeeze_bias_a,
    excite_a,
    excite_bias_a,
    reduce_b,
    reduce_gain_b,
    reduce_bias_b,
    spatial_b,
    spatial_gain_b,
    spatial_bias_b,
    expand_b,
    expand_gain_b,
    expand_bias_b,
    squeeze_b,
    squeeze_bias_b,
    excite_b,
    excite_bias_b,
    cotangent,
):
    micro = images.shape[0]
    held = images.shape[2] // 2
    side = images.shape[3]
    half = side // 2
    core = lax.axis_index("rows")
    batch_index = lax.axis_index("batch")

    mine = lax.dynamic_slice_in_dim(images, core * held, held, axis=2)
    away = lax.dynamic_slice_in_dim(images, (1 - core) * held, held, axis=2)
    other = swapped(away, "rows", 1)
    source = jnp.concatenate(
        [jnp.where(core == 0, mine, other), jnp.where(core == 0, other, mine)], axis=1
    )
    mine = lax.dynamic_slice_in_dim(cotangent, core * held, held, axis=2)
    away = lax.dynamic_slice_in_dim(cotangent, (1 - core) * held, held, axis=2)
    other = swapped(away, "rows", 1)
    upstream = jnp.concatenate(
        [jnp.where(core == 0, mine, other), jnp.where(core == 0, other, mine)], axis=4
    )
    vectors = jnp.stack(
        [
            expand_gain_a,
            expand_bias_a,
            project_gain_a,
            project_bias_a,
            excite_bias_a,
            expand_gain_b,
            expand_bias_b,
            excite_bias_b,
        ]
    )
    vectors = both_cores(vectors, 1)
    tall = both_cores(jnp.concatenate([reduce_b, squeeze_a, squeeze_b], axis=1), 0)
    flat = both_cores(jnp.concatenate([excite_a, excite_b], axis=0), 1)
    expand_gain_a, expand_bias_a, project_gain_a, project_bias_a = (vectors[k] for k in range(4))
    excite_bias_a, expand_gain_b, expand_bias_b, excite_bias_b = (vectors[k] for k in range(4, 8))
    mid = reduce_b.shape[1]
    hid = squeeze_a.shape[1]
    reduce_b, squeeze_a, squeeze_b = tall[:, :mid], tall[:, mid : mid + hid], tall[:, mid + hid :]
    excite_a, excite_b = flat[:hid], flat[hid:]

    half_all = crop_sizes // 2
    count_fine = jnp.sum(crop_sizes * crop_sizes, axis=1).astype(F32)[:, None]
    count_coarse = jnp.sum(half_all * half_all, axis=1).astype(F32)[:, None]
    start = batch_index * 2 * held + core * held
    crops = lax.dynamic_slice_in_dim(crop_sizes, start, held, axis=1)
    halves = crops // 2
    pixel_count = (halves * halves).astype(F32)
    spots = jnp.arange(half, dtype=jnp.int32)

    def mask_of(limits, rows, cols):
        limits = limits[:, None, :, None]
        inside = (rows[None, :, None, None] < limits) & (cols[None, None, None, :] < limits)
        return inside.astype(F32)[..., None]

    mask_coarse = mask_of(halves, spots, spots)
    mask_fine = jnp.stack(
        [
            jnp.stack([mask_of(crops, 2 * spots + pr, 2 * spots + pc) for pc in range(2)])
            for pr in range(2)
        ]
    )

    planes = source.reshape(micro, half, 2, held, half, 2, source.shape[-1])
    planes = planes.transpose(2, 5, 0, 1, 3, 4, 6)

    conv_one = forward_dot(planes, reduce_a)
    strided = planes[0, 0]
    projected = forward_dot(strided, project_a).astype(BF16).astype(F32)
    sums_one = all_sum(moments(conv_one * mask_fine, conv_one, FPIX))
    centre_one, inverse_one = norm_of(sums_one, count_fine)
    scaled_one = (conv_one - centre_one) * inverse_one
    normed_one = (scaled_one * reduce_gain_a + reduce_bias_a) * mask_fine
    active_one = jax.nn.silu(normed_one).astype(BF16)
    taps = ((1, -1), (0, 0), (1, 0))
    patches_one = jnp.concatenate(
        [
            shifted(active_one[taps[i][0], taps[j][0]], taps[i][1], taps[j][1])
            for i in range(3)
            for j in range(3)
        ],
        axis=4,
    )
    conv_two = forward_dot(patches_one, spatial_a)
    sums_two = all_sum(moments(conv_two * mask_coarse, conv_two, PIX))
    centre_two, inverse_two = norm_of(sums_two, count_coarse)
    scaled_two = (conv_two - centre_two) * inverse_two
    normed_two = (scaled_two * spatial_gain_a + spatial_bias_a) * mask_coarse
    active_two = jax.nn.silu(normed_two).astype(BF16)
    expanded = forward_dot(active_two, expand_a).astype(BF16).astype(F32)
    sums_three = all_sum(
        jnp.stack(
            [
                moments(expanded * mask_coarse, expanded, PIX),
                moments(projected * mask_coarse, projected, PIX),
            ]
        )
    )
    centre_three, inverse_three = norm_of(sums_three[0], count_coarse)
    centre_side, inverse_side = norm_of(sums_three[1], count_coarse)
    scaled_three = (expanded - centre_three) * inverse_three
    scaled_side = (projected - centre_side) * inverse_side
    normed_three = (scaled_three * expand_gain_a + expand_bias_a) * mask_coarse
    normed_side = (scaled_side * project_gain_a + project_bias_a) * mask_coarse
    gate_one, cache_one = gate_forward(
        normed_three, pixel_count, squeeze_a, squeeze_bias_a, excite_a, excite_bias_a
    )
    wide_gate_one = per_map(gate_one, micro, held)
    summed_one = normed_three * wide_gate_one + normed_side
    middle = jax.nn.silu(summed_one).astype(BF16)

    conv_four = forward_dot(middle, reduce_b)
    sums_four = all_sum(moments(conv_four * mask_coarse, conv_four, PIX))
    centre_four, inverse_four = norm_of(sums_four, count_coarse)
    scaled_four = (conv_four - centre_four) * inverse_four
    normed_four = (scaled_four * reduce_gain_b + reduce_bias_b) * mask_coarse
    active_four = jax.nn.silu(normed_four).astype(BF16)
    patches_four = jnp.concatenate(
        [shifted(active_four, i - 1, j - 1) for i in range(3) for j in range(3)], axis=4
    )
    conv_five = forward_dot(patches_four, spatial_b)
    sums_five = all_sum(moments(conv_five * mask_coarse, conv_five, PIX))
    centre_five, inverse_five = norm_of(sums_five, count_coarse)
    scaled_five = (conv_five - centre_five) * inverse_five
    normed_five = (scaled_five * spatial_gain_b + spatial_bias_b) * mask_coarse
    active_five = jax.nn.silu(normed_five).astype(BF16)
    expanded_b = forward_dot(active_five, expand_b).astype(BF16).astype(F32)
    sums_six = all_sum(moments(expanded_b * mask_coarse, expanded_b, PIX))
    centre_six, inverse_six = norm_of(sums_six, count_coarse)
    scaled_six = (expanded_b - centre_six) * inverse_six
    normed_six = (scaled_six * expand_gain_b + expand_bias_b) * mask_coarse
    gate_two, cache_two = gate_forward(
        normed_six, pixel_count, squeeze_b, squeeze_bias_b, excite_b, excite_bias_b
    )
    wide_gate_two = per_map(gate_two, micro, held)
    summed_two = normed_six * wide_gate_two + middle.astype(F32)
    block_out = jax.nn.silu(summed_two).astype(BF16)

    grad_summed_two = upstream.astype(F32) * silu_slope(summed_two)
    gate_grad_two = jnp.sum(grad_summed_two * normed_six, axis=(1, 3)).reshape(gate_two.shape)
    pooled_two, grad_squeeze_b, grad_excite_b, small_two = gate_backward(
        gate_grad_two, gate_two, cache_two, pixel_count, squeeze_b, excite_b
    )
    live_six = (grad_summed_two * wide_gate_two + per_map(pooled_two, micro, held)) * mask_coarse
    back_sums_six = all_sum(moments(live_six, scaled_six, PIX))
    grad_six = norm_back(
        live_six, scaled_six, inverse_six, expand_gain_b, back_sums_six, count_coarse, mask_coarse
    )
    grad_expand_b = weight_dot(active_five, grad_six)
    live_five = input_dot(grad_six, expand_b) * silu_slope(normed_five) * mask_coarse
    back_sums_five = all_sum(moments(live_five, scaled_five, PIX))
    grad_five = norm_back(
        live_five, scaled_five, inverse_five, spatial_gain_b, back_sums_five, count_coarse, mask_coarse
    )
    grad_spatial_b = weight_dot(patches_four, grad_five)
    kernel = spatial_b.reshape(3, 3, mid, mid)
    grad_four = sum(
        input_dot(shifted(grad_five, 1 - i, 1 - j), kernel[i, j])
        for i in range(3)
        for j in range(3)
    )
    live_four = grad_four * silu_slope(normed_four) * mask_coarse
    back_sums_four = all_sum(moments(live_four, scaled_four, PIX))
    grad_four = norm_back(
        live_four, scaled_four, inverse_four, reduce_gain_b, back_sums_four, count_coarse, mask_coarse
    )
    grad_reduce_b = weight_dot(middle, grad_four)
    grad_middle = input_dot(grad_four, reduce_b) + grad_summed_two

    grad_summed_one = grad_middle * silu_slope(summed_one)
    gate_grad_one = jnp.sum(grad_summed_one * normed_three, axis=(1, 3)).reshape(gate_one.shape)
    pooled_one, grad_squeeze_a, grad_excite_a, small_one = gate_backward(
        gate_grad_one, gate_one, cache_one, pixel_count, squeeze_a, excite_a
    )
    live_three = (grad_summed_one * wide_gate_one + per_map(pooled_one, micro, held)) * mask_coarse
    live_side = grad_summed_one * mask_coarse
    back_sums_three = all_sum(
        jnp.stack([moments(live_three, scaled_three, PIX), moments(live_side, scaled_side, PIX)])
    )
    grad_three = norm_back(
        live_three,
        scaled_three,
        inverse_three,
        expand_gain_a,
        back_sums_three[0],
        count_coarse,
        mask_coarse,
    )
    grad_side = norm_back(
        live_side,
        scaled_side,
        inverse_side,
        project_gain_a,
        back_sums_three[1],
        count_coarse,
        mask_coarse,
    )
    grad_expand_a = weight_dot(active_two, grad_three)
    grad_project_a = weight_dot(strided, grad_side)
    live_two = input_dot(grad_three, expand_a) * silu_slope(normed_two) * mask_coarse
    back_sums_two = all_sum(moments(live_two, scaled_two, PIX))
    grad_two = norm_back(
        live_two, scaled_two, inverse_two, spatial_gain_a, back_sums_two, count_coarse, mask_coarse
    )
    grad_spatial_a = weight_dot(patches_one, grad_two)
    kernel = spatial_a.reshape(3, 3, mid, mid)
    grad_one = jnp.stack(
        [
            jnp.stack(
                [
                    sum(
                        input_dot(shifted(grad_two, rows, cols), kernel[i, j])
                        for i, rows in PLANE_TAPS[pr]
                        for j, cols in PLANE_TAPS[pc]
                    )
                    for pc in range(2)
                ]
            )
            for pr in range(2)
        ]
    )
    live_one = grad_one * silu_slope(normed_one) * mask_fine
    back_sums_one = all_sum(moments(live_one, scaled_one, FPIX))
    grad_one = norm_back(
        live_one, scaled_one, inverse_one, reduce_gain_a, back_sums_one, count_fine, mask_fine
    )
    grad_reduce_a = weight_dot(planes, grad_one)
    grad_one = grad_one.transpose(2, 3, 0, 4, 5, 1, 6).reshape(micro, side, held, side, mid)
    grad_source = input_dot(grad_one, reduce_a)
    grad_source = grad_source.at[:, ::2, :, ::2].add(input_dot(grad_side, project_a))

    rows_half = side // 2
    top = lax.dynamic_slice_in_dim(grad_source, core * rows_half, rows_half, axis=1)
    gone = lax.dynamic_slice_in_dim(grad_source, (1 - core) * rows_half, rows_half, axis=1)
    other = swapped(gone.astype(BF16), "rows", 1).astype(F32)
    images_grad = jnp.concatenate(
        [jnp.where(core == 0, top, other), jnp.where(core == 0, other, top)], axis=2
    )
    span = block_out.shape[4] // 2
    top = lax.dynamic_slice_in_dim(block_out, core * span, span, axis=4)
    gone = lax.dynamic_slice_in_dim(block_out, (1 - core) * span, span, axis=4)
    other = swapped(gone, "rows", 1)
    block_out = jnp.concatenate(
        [jnp.where(core == 0, top, other), jnp.where(core == 0, other, top)], axis=2
    )

    size = lax.axis_size("batch")

    def narrow(grad):
        return grad.astype(BF16).reshape(2, size, -1, 512)

    def by_core(grad):
        return jnp.swapaxes(grad.reshape(grad.shape[0], 2, -1), 0, 1)

    narrows = core_sum(
        jnp.concatenate(
            [
                narrow(grad_reduce_b),
                narrow(grad_squeeze_a),
                narrow(by_core(grad_excite_a)),
                narrow(grad_squeeze_b),
                narrow(by_core(grad_excite_b)),
            ],
            axis=2,
        ),
        0,
    )
    grads = (grad_expand_b, grad_spatial_b, grad_expand_a, grad_project_a, grad_spatial_a, grad_reduce_a)
    blocks = core_sum(jnp.concatenate([folded(grad) for grad in grads], axis=2), 1)
    summed = halved(jnp.concatenate([narrows, blocks], axis=1), two_orders)
    count = narrows.shape[1]
    gathered = collected(summed[:count].astype(BF16)).astype(F32)
    outs = []
    at = count
    for grad in grads:
        length = grad.size // (2 * size * 512)
        outs.append(unfolded(summed[at : at + length], grad.shape[1]))
        at += length
    out_expand_b, out_spatial_b, out_expand_a, out_project_a, out_spatial_a, out_reduce_a = outs
    unit = count // 8
    out_reduce_b = gathered[:, : 4 * unit].reshape(-1, mid)
    out_squeeze_a, out_excite_a, out_squeeze_b, out_excite_b = (
        gathered[:, k * unit : (k + 1) * unit] for k in range(4, 8)
    )
    small = all_sum(
        jnp.concatenate([small_one[0], small_one[1], small_two[0], small_two[1]]).reshape(-1, 128)
    ).reshape(-1)
    out = hid + vectors.shape[1]
    wide_out = vectors.shape[1]

    def own(vector):
        return lax.dynamic_slice_in_dim(vector, core * (wide_out // 2), wide_out // 2, axis=0)

    sums_all = [jnp.sum(s, axis=0) for s in (back_sums_one, back_sums_two, back_sums_four, back_sums_five)]
    three, side_sums, six = (
        jnp.sum(s, axis=0) for s in (back_sums_three[0], back_sums_three[1], back_sums_six)
    )
    return (
        block_out,
        images_grad,
        out_reduce_a,
        sums_all[0][1],
        sums_all[0][0],
        out_spatial_a,
        sums_all[1][1],
        sums_all[1][0],
        out_expand_a,
        own(three[1]),
        own(three[0]),
        out_project_a,
        own(side_sums[1]),
        own(side_sums[0]),
        out_squeeze_a.reshape(-1, hid),
        small[:hid],
        out_excite_a.reshape(hid, -1),
        own(small[hid:out]),
        out_reduce_b,
        sums_all[2][1],
        sums_all[2][0],
        out_spatial_b,
        sums_all[3][1],
        sums_all[3][0],
        out_expand_b,
        own(six[1]),
        own(six[0]),
        out_squeeze_b.reshape(-1, hid),
        small[out : out + hid],
        out_excite_b.reshape(hid, -1),
        own(small[out + hid :]),
    )


def solution(mesh):
    in_specs = (
        P(None, "rows", "batch", None, None),
        P(),
        P(),
        P(),
        P(),
        P(),
        P(),
        P(),
        P(),
        P("rows"),
        P("rows"),
        P(),
        P("rows"),
        P("rows"),
        P("rows", None),
        P(),
        P(None, "rows"),
        P("rows"),
        P("rows", None),
        P(),
        P(),
        P(),
        P(),
        P(),
        P(),
        P("rows"),
        P("rows"),
        P("rows", None),
        P(),
        P(None, "rows"),
        P("rows"),
        P(None, None, "batch", None, "rows"),
    )
    out_specs = (
        P(None, None, "batch", None, "rows"),
        P(None, "rows", "batch", None, None),
        P(("batch", "rows")),
        P(),
        P(),
        P(("batch", "rows")),
        P(),
        P(),
        P(("batch", "rows")),
        P("rows"),
        P("rows"),
        P(("batch", "rows")),
        P("rows"),
        P("rows"),
        P("rows", None),
        P(),
        P(None, "rows"),
        P("rows"),
        P("rows", None),
        P(),
        P(),
        P(("batch", "rows")),
        P(),
        P(),
        P(("batch", "rows")),
        P("rows"),
        P("rows"),
        P("rows", None),
        P(),
        P(None, "rows"),
        P("rows"),
    )
    return jax.shard_map(
        per_device, mesh=mesh, in_specs=in_specs, out_specs=out_specs, check_vma=False
    )
```

```python
import jax
import jax.numpy as jnp
from jax import lax
from jax.experimental import pallas as pl
from jax.experimental.pallas import tpu as pltpu
from jax.sharding import PartitionSpec as P

epsilon = 1e-05
HIGHEST = lax.Precision.HIGHEST
BF16 = jnp.bfloat16
F32 = jnp.float32

PLANE_TAPS = (((1, 0),), ((2, 0), (0, 1)))


def swapped(block, axis, mask):
    route = [(i, i ^ mask) for i in range(lax.axis_size(axis))]
    return lax.ppermute(block, axis, route)


def bits_of(size):
    return [1 << k for k in range(size.bit_length() - 1)]


def all_sum(parts):
    parts = parts + swapped(parts, "rows", 1)
    size = lax.axis_size("batch")
    spread = jnp.broadcast_to(parts[None], (size,) + parts.shape)
    return jnp.sum(lax.all_to_all(spread, "batch", 0, 0, tiled=True), axis=0)


def halved(block, orders):
    size = lax.axis_size("batch")
    place = lax.axis_index("batch")
    bits = bits_of(size)
    count = block.shape[1]
    cut = count // 2 // 16 * 16
    parts = []
    for part, order in zip((block[:, :cut], block[:, cut:]), orders(bits)):
        shape = part.shape[1:]
        left = list(reversed(bits))
        part = part.reshape((2,) * len(bits) + shape)
        for bit in order:
            axis = left.index(bit)
            mine = (place // bit) % 2
            gone = lax.dynamic_index_in_dim(part, 1 - mine, axis, keepdims=False)
            kept = lax.dynamic_index_in_dim(part, mine, axis, keepdims=False)
            total = kept.astype(F32) + swapped(gone, "batch", bit).astype(F32)
            left.pop(axis)
            part = total.astype(BF16) if left else total
        parts.append(part)
    return jnp.concatenate(parts, axis=0)


def two_orders(bits):
    return (bits, bits[1::-1] + bits[2:])


def collected(block):
    place = lax.axis_index("batch")
    block = block[None]
    for bit in bits_of(lax.axis_size("batch")):
        other = swapped(block, "batch", bit)
        upper = (place // bit) % 2 == 1
        block = jnp.concatenate([jnp.where(upper, other, block), jnp.where(upper, block, other)], axis=0)
    return block


def core_sum(block, axis):
    core = lax.axis_index("rows")
    gone = lax.dynamic_index_in_dim(block, 1 - core, axis, keepdims=False)
    kept = lax.dynamic_index_in_dim(block, core, axis, keepdims=False)
    return (kept.astype(F32) + swapped(gone, "rows", 1).astype(F32)).astype(BF16)


def both_cores(block, axis):
    core = lax.axis_index("rows")
    other = swapped(block, "rows", 1)
    first = jnp.where(core == 0, block, other)
    second = jnp.where(core == 0, other, block)
    return jnp.concatenate([first, second], axis=axis)


LANES = 128
VMEM_MIB = 64
ROOM = None
READS = (((1, 0),), ((2, 0), (0, -1)))
ALL_TAPS = ((0, -1), (1, 0), (2, 1))


class Near:
    def __init__(self, array):
        self.array = array
        self.shape = array[0] if isinstance(array, tuple) else array.shape


class Both:
    def __init__(self, array):
        self.array = array


class Late:
    def __init__(self, array):
        self.array = array
        self.shape = array.shape


class Pair:
    def __init__(self, own, other, axis):
        self.own, self.other, self.axis = own, other, axis
        shape = list(own.shape)
        shape[axis] *= 2
        self.shape, self.dtype = tuple(shape), own.dtype


class Part:
    def __init__(self, array, axis):
        self.array, self.axis = array, axis
        shape = list(array.shape)
        shape[axis] //= 2
        self.shape, self.dtype = tuple(shape), array.dtype


class Raw:
    def __init__(self, shape, dtype):
        self.shape, self.dtype = shape, dtype


def half_of(ref, axis, which, length):
    start = which * length
    if axis >= len(ref.shape) - 2:
        start = pl.multiple_of(start, length)
    return ref.at[(slice(None),) * axis + (pl.ds(start, length),)]


class Copies:
    def __init__(self, sems):
        self.sems, self.used = sems, 0
        self.waiting, self.open = {}, []

    def start(self, source, target):
        copy = pltpu.make_async_copy(source, target, self.sems.at[self.used])
        self.used += 1
        copy.start()
        return copy

    def need(self, *refs):
        for ref in refs:
            for copy in self.waiting.pop(id(ref), ()):
                copy.wait()

    def out(self, source, target):
        self.open.append(self.start(source, target))


def run(body, outs, args, scratch=(), flops=0, spare=0, ahead=(), room=None):
    operands, specs, plans, buffers = [], [], [], []
    far = pl.BlockSpec(memory_space=pltpu.HBM)
    vmem = pl.BlockSpec(memory_space=pltpu.VMEM)
    count, next_up = 0, []

    def plan(arg, late, keep):
        nonlocal count
        if isinstance(arg, Near) and keep is next_up:
            plans.append(("copy", len(operands), (len(keep), 0), late))
            operands.append(arg.array)
            specs.append(vmem)
            keep.append((tuple(arg.shape), arg.array.dtype))
            count += 1
            return
        if isinstance(arg, Near):
            plans.append(("near", len(operands), None, late))
            operands.append(arg.array)
            specs.append(vmem)
            return
        if isinstance(arg, Pair):
            kind, axis, parts = "pair", arg.axis, [arg.own, arg.other]
        elif isinstance(arg, Part):
            kind, axis, parts = "part", arg.axis, [arg.array]
        elif arg.ndim == 1:
            plans.append(("near", len(operands), None, late))
            operands.append(arg)
            specs.append(pl.BlockSpec(memory_space=pltpu.SMEM))
            return
        else:
            kind, axis, parts = "copy", 0, [arg]
        plans.append((kind, len(operands), (len(keep), axis), late))
        operands.extend(parts)
        specs.extend([far] * len(parts))
        keep.append((tuple(arg.shape), arg.dtype))
        count += len(parts)

    for arg in args:
        late = isinstance(arg, Late)
        plan(arg.array if late else arg, late, buffers)
    first_ahead = len(plans)
    for arg in ahead:
        plan(arg, True, next_up)
    shapes, out_specs, ways = [], [], []
    for item in outs:
        if isinstance(item, Raw):
            ways.append(("raw", len(shapes), None))
            shapes.append(jax.ShapeDtypeStruct(item.shape, item.dtype))
            out_specs.append(far)
        elif isinstance(item, Near):
            ways.append(("near", len(shapes), None))
            shapes.append(jax.ShapeDtypeStruct(*item.array))
            out_specs.append(vmem)
        elif isinstance(item, Both):
            ways.append(("both", len(shapes), None))
            shapes += [jax.ShapeDtypeStruct(*item.array)] * 2
            out_specs += [vmem, far]
            count += 1
        else:
            ways.append(("copy", len(shapes), len(buffers)))
            shapes.append(jax.ShapeDtypeStruct(*item))
            out_specs.append(far)
            buffers.append(item)
            count += 1
    first_next = len(shapes)
    for item in next_up:
        shapes.append(jax.ShapeDtypeStruct(*item))
        out_specs.append(vmem)
    sems = pltpu.SemaphoreType.DMA((max(count + spare, 1),))

    def kernel(*refs):
        ins = refs[: len(operands)]
        results = refs[len(operands) : len(operands) + len(shapes)]
        rest = refs[len(operands) + len(shapes) :]
        bufs, own = rest[: len(buffers)], rest[len(buffers) : -1]
        io = Copies(rest[-1])
        views, early = [], []
        for k, (kind, at, spot, late) in enumerate(plans):
            if kind == "near":
                views.append(ins[at])
                continue
            index, axis = spot
            buf = results[first_next + index] if k >= first_ahead else bufs[index]
            if kind == "copy":
                copies = [io.start(ins[at], buf)]
            elif kind == "pair":
                core = ins[0][0]
                length = ins[at].shape[axis]
                copies = [
                    io.start(ins[at], half_of(buf, axis, core, length)),
                    io.start(ins[at + 1], half_of(buf, axis, 1 - core, length)),
                ]
            else:
                core = ins[0][0]
                copies = [io.start(half_of(ins[at], axis, core, buf.shape[axis]), buf)]
            io.waiting[id(buf)] = copies
            if k < first_ahead:
                views.append(buf)
                if not late:
                    early.append(buf)
        io.need(*early)
        targets = {}
        for kind, at, index in ways:
            if kind == "copy":
                views.append(bufs[index])
                targets[id(bufs[index])] = (bufs[index], results[at])
            else:
                views.append(results[at])
                if kind == "both":
                    targets[id(results[at])] = (results[at], results[at + 1])

        def send(*sent):
            for ref in sent:
                io.out(*targets.pop(id(ref)))

        io.send = send
        body(io, *views, *own)
        for buf, ref in targets.values():
            io.out(buf, ref)
        for copies in io.waiting.values():
            for copy in copies:
                copy.wait()
        for copy in io.open:
            copy.wait()

    def bytes_of(shape, dtype):
        size = 1
        for n in shape:
            size *= n
        return size * jnp.dtype(dtype).itemsize

    moved = sum(a.size * a.dtype.itemsize for a in operands) + sum(
        bytes_of(s.shape, s.dtype) for s in shapes
    )
    held = sum(bytes_of(*item) for item in buffers) + sum(bytes_of(s.shape, s.dtype) for s in scratch)
    limit = held + (12 << 20)
    if room is not None:
        near = sum(a.size * a.dtype.itemsize for a, spec in zip(operands, specs) if spec is vmem)
        near += sum(bytes_of(s.shape, s.dtype) for s, spec in zip(shapes, out_specs) if spec is vmem)
        limit = max(limit, ((VMEM_MIB - room) << 20) - near)
    return pl.pallas_call(
        kernel,
        out_shape=shapes,
        in_specs=specs,
        out_specs=out_specs,
        scratch_shapes=[*(pltpu.VMEM(*item) for item in buffers), *scratch, sems],
        compiler_params=pltpu.CompilerParams(vmem_limit_bytes=limit),
        cost_estimate=pl.CostEstimate(flops=flops, bytes_accessed=0, transcendentals=0),
    )(*operands)


def dot(a, b):
    return lax.dot_general(a, b, (((1,), (0,)), ((), ())), preferred_element_type=F32)


def dot_nt(a, b):
    return lax.dot_general(a, b, (((1,), (1,)), ((), ())), preferred_element_type=F32)


def dot_tn(a, b):
    return lax.dot_general(a, b, (((0,), (0,)), ((), ())), preferred_element_type=F32)


def exact_dot(a, b, product):
    high = a.astype(BF16)
    low = (a - high.astype(F32)).astype(BF16)
    return product(high, b) + product(low, b)


def sigmoid(v):
    return 1.0 / (1.0 + jnp.exp(-v))


def slope_of(v):
    sigma = sigmoid(v)
    return sigma * (1.0 + v * (1.0 - sigma))


def counts_of(z, n_r, which):
    return [n_r[which * z.micro + m] for m in range(z.micro)]


def norm_rows(total, counted, micro):
    rows = []
    for m in range(micro):
        centre = total[2 * m : 2 * m + 1] / counted[m]
        square = total[2 * m + 1 : 2 * m + 2] / counted[m]
        rows.append((centre, lax.rsqrt(square - centre * centre + epsilon)))
    return rows


def fold_sums(first, second):
    return jnp.sum(first, axis=0, keepdims=True), jnp.sum(second, axis=0, keepdims=True)


def gain_rows(total, micro):
    gain = sum(total[2 * m + 1 : 2 * m + 2] for m in range(micro))
    bias = sum(total[2 * m : 2 * m + 1] for m in range(micro))
    return jnp.concatenate([gain, bias], axis=0)


def to_all(z, rows, s_r):
    for k, row in enumerate(rows):
        s_r[k : k + 1, :] = row


def place_patches(values, row_taps, col_taps, out_ref, base, lane, ch, group):
    size = values.shape[0]
    q = lax.broadcasted_iota(jnp.int32, values.shape, 0) % 8
    for col, cs in col_taps:
        if cs == -1:
            turned = jnp.where(q == 0, 0.0, pltpu.roll(values, 1, 0))
        elif cs == 1:
            turned = jnp.where(q == 7, 0.0, pltpu.roll(values, size - 1, 0))
        else:
            turned = values
        turned = turned.astype(BF16)
        gap = jnp.zeros((group, values.shape[1]), BF16)
        for row, rs in row_taps:
            at = (3 * row + col) * ch + lane
            lanes = slice(at, at + values.shape[1])
            if rs == 0:
                out_ref[base : base + size, lanes] = turned
            elif rs == -1:
                out_ref[base : base + group, lanes] = gap
                out_ref[base + group : base + size, lanes] = turned[: size - group]
            else:
                out_ref[base : base + size - group, lanes] = turned[group:]
                out_ref[base + size - group : base + size, lanes] = gap


class Sizes:
    def __init__(self, images, mid, out, hid, devices):
        self.micro = images.shape[0]
        self.held = images.shape[2] // 2
        self.side = images.shape[3]
        self.half = self.side // 2
        self.cin = images.shape[4]
        self.mid, self.out, self.hid, self.devices = mid, out, hid, devices
        self.group = self.held * self.half
        self.map = self.half * self.group
        self.coarse = self.micro * self.map
        self.fine = 4 * self.coarse
        self.maps = self.micro * self.held


def enter_kernel(z, place, images, other, perm, w_one, w_side, mask, ahead):
    def body(io, place_r, mine_r, other_r, perm_r, w1_r, ws_r, mask_r, planes_r, c1_r, p1_r, s1_r, ss_r):
        core = place_r[0]
        rows = z.map // 2
        for k, ref in ((0, mine_r), (1, other_r)):
            half = core if k == 0 else 1 - core
            io.need(ref)
            for m in range(z.micro):
                turned = dot(perm_r[...], ref[m].reshape(2 * z.map, z.cin)).astype(BF16)
                for p in range(4):
                    at = pl.multiple_of((p * z.micro + m) * z.map + half * rows, rows)
                    planes_r[pl.ds(at, rows), :] = turned[p * rows : (p + 1) * rows]
        io.send(planes_r)
        io.need(w1_r)
        for m in range(z.micro):
            one = [None, None]
            for p in range(4):
                at = (p * z.micro + m) * z.map
                c = dot(planes_r[at : at + z.map, :], w1_r[...])
                c1_r[at : at + z.map, :] = c
                live = c * mask_r[m * z.map : (m + 1) * z.map, :]
                a, b = fold_sums(live, live * c)
                one = [a, b] if p == 0 else [one[0] + a, one[1] + b]
            s1_r[2 * m : 2 * m + 1, :] = one[0]
            s1_r[2 * m + 1 : 2 * m + 2, :] = one[1]
        io.send(c1_r)
        io.need(ws_r)

        @pl.loop(0, z.out // 512)
        def _(j):
            lanes = pl.ds(pl.multiple_of(j * 512, 512), 512)
            p = dot(planes_r[: z.coarse, :], ws_r[:, lanes]).astype(BF16)
            p1_r[:, lanes] = p
            p = p.astype(F32)
            for m in range(z.micro):
                part = p[m * z.map : (m + 1) * z.map]
                live = part * mask_r[m * z.map : (m + 1) * z.map, :]
                a, b = fold_sums(live, live * part)
                ss_r[2 * m : 2 * m + 1, lanes] = a
                ss_r[2 * m + 1 : 2 * m + 2, lanes] = b

    return run(
        body,
        [
            ((z.fine, z.cin), BF16),
            Both(((z.fine, z.mid), F32)),
            ((z.coarse, z.out), BF16),
            Near(((2 * z.micro, z.mid), F32)),
            ((2 * z.micro, z.out), F32),
        ],
        (place, images, other, perm, w_one, w_side, mask),
        room=ROOM,
        ahead=ahead,
        flops=2 * z.fine * z.cin * z.mid,
    )


def taps_kernel(z, place, sums, counted, vec, conv, weight, mask, strided, ahead):
    planes = 4 if strided else 1
    nt = weight.shape[0]

    def body(io, place_r, sums_r, n_r, vec_r, c_r, w_r, mask_r, patch_r, out_r, t_r, s_r):
        total = sums_r[...]
        t_r[...] = total
        io.send(t_r)
        norms = norm_rows(total, counts_of(z, n_r, 0 if strided else 1), z.micro)
        for m in range(z.micro):
            centre, inverse = norms[m]
            scale = inverse * vec_r[0:1]
            offset = vec_r[1:2] - centre * scale
            live = mask_r[m * z.map : (m + 1) * z.map, :]
            for p in range(planes):
                at = (p * z.micro + m) * z.map
                for lane in range(0, z.mid, LANES):
                    lanes = slice(lane, lane + LANES)
                    v = (c_r[at : at + z.map, lanes] * scale[:, lanes] + offset[:, lanes]) * live
                    v = v * sigmoid(v)
                    rows = READS[p // 2] if strided else ALL_TAPS
                    cols = READS[p % 2] if strided else ALL_TAPS
                    place_patches(v, rows, cols, patch_r, m * z.map, lane, z.mid, z.group)
        io.send(patch_r)
        io.need(w_r)
        c = dot(patch_r[...], w_r[...])
        out_r[...] = c
        io.send(out_r)
        for m in range(z.micro):
            part = c[m * z.map : (m + 1) * z.map]
            live = part * mask_r[m * z.map : (m + 1) * z.map, :]
            a, b = fold_sums(live, live * part)
            s_r[2 * m : 2 * m + 1, :] = a
            s_r[2 * m + 1 : 2 * m + 2, :] = b

    return run(
        body,
        [
            ((z.coarse, nt), BF16),
            Both(((z.coarse, z.mid), F32)),
            ((2 * z.micro, z.mid), F32),
            Near(((2 * z.micro, z.mid), F32)),
        ],
        (place, Near(sums), counted, vec, conv, weight, mask),
        room=ROOM,
        ahead=ahead,
        flops=2 * z.coarse * nt * z.mid,
    )


def expand_kernel(z, place, sums, counted, vec, conv, weight, mask, side, ahead):
    height = 2 * z.micro

    def body(io, place_r, sums_r, n_r, vec_r, c_r, w_r, mask_r, *refs):
        if side is not None:
            refs[-1][height : 2 * height, :] = refs[0][...]
            refs = refs[1:]
        act_r, out_r, t_r, s_r = refs
        total = sums_r[...]
        t_r[...] = total
        io.send(t_r)
        norms = norm_rows(total, counts_of(z, n_r, 1), z.micro)
        for m in range(z.micro):
            rows = slice(m * z.map, (m + 1) * z.map)
            centre, inverse = norms[m]
            scale = inverse * vec_r[0:1]
            offset = vec_r[1:2] - centre * scale
            v = (c_r[rows, :] * scale + offset) * mask_r[rows, :]
            act_r[rows, :] = (v * sigmoid(v)).astype(BF16)
        io.send(act_r)
        io.need(w_r)

        @pl.loop(0, z.out // 512)
        def _(j):
            lanes = pl.ds(pl.multiple_of(j * 512, 512), 512)
            p = dot(act_r[...], w_r[:, lanes]).astype(BF16)
            out_r[:, lanes] = p
            p = p.astype(F32)
            for m in range(z.micro):
                part = p[m * z.map : (m + 1) * z.map]
                live = part * mask_r[m * z.map : (m + 1) * z.map, :]
                a, b = fold_sums(live, live * part)
                s_r[2 * m : 2 * m + 1, lanes] = a
                s_r[2 * m + 1 : 2 * m + 2, lanes] = b

    extra = () if side is None else (side,)
    return run(
        body,
        [
            ((z.coarse, z.mid), BF16),
            Both(((z.coarse, z.out), BF16)),
            ((2 * z.micro, z.mid), F32),
            Near(((height * (1 if side is None else 2), z.out), F32)),
        ],
        (place, Near(sums), counted, vec, conv, weight, mask, *extra),
        room=ROOM,
        ahead=ahead,
        flops=2 * z.coarse * z.out * z.mid,
    )


def by_map(z, v):
    return v.reshape(z.half, z.held, z.half, v.shape[-1])


def map_sums(z, v):
    return jnp.sum(jnp.sum(by_map(z, v), axis=0), axis=1)


def spread(z, rows):
    return jnp.broadcast_to(
        rows[None, :, None, :], (z.half, z.held, z.half, rows.shape[-1])
    ).reshape(z.map, rows.shape[-1])


def norms_at(z, total_r, n_r, m, lanes, first=0):
    counted = n_r[z.micro + m]
    at = first + 2 * m
    centre = total_r[at : at + 1, lanes] / counted
    square = total_r[at + 1 : at + 2, lanes] / counted
    return centre, lax.rsqrt(square - centre * centre + epsilon)


def gate_rows(pooled, squeeze_r, sq_bias, excite_r, ex_bias):
    inner = exact_dot(pooled, squeeze_r[...], dot) + sq_bias
    hidden = inner * sigmoid(inner)
    gate = sigmoid(exact_dot(hidden, excite_r[...], dot) + ex_bias)
    return inner, hidden, gate


def gate_back(dgate, gate, inner, squeeze_r, excite_r, pix):
    dl = dgate * gate * (1.0 - gate)
    dz = exact_dot(dl, excite_r[...], dot_nt) * slope_of(inner)
    du = exact_dot(dz, squeeze_r[...], dot_nt) / pix
    return dl, dz, du


def bias_sums(z, dl, dz, s_r, first):
    s_r[first : first + 1, :] = jnp.sum(dl, axis=0, keepdims=True)
    s_r[first + 1 : first + 2, :] = jnp.zeros((1, z.out), F32)
    s_r[first + 1 : first + 2, : z.hid] = jnp.sum(dz, axis=0, keepdims=True)


def middle_kernel(z, place, sums, counted, vectors, pix, e1, p1, squeeze, sq_bias, excite, w, mask, ahead):
    side = 2 * z.micro

    def body(
        io, place_r, t_r, n_r, vec_r, pix_r, e_r, p_r, sq_r, sqb_r, ex_r, w_r, mask_r,
        mid_r, c_r, gate_r, pool_r, inner_r, hid_r, total_r, s_r,
    ):
        io.out(t_r, total_r)

        @pl.loop(0, z.out // LANES)
        def _(j):
            lanes = pl.ds(pl.multiple_of(j * LANES, LANES), LANES)
            for m in range(z.micro):
                rows = slice(m * z.map, (m + 1) * z.map)
                centre, inverse = norms_at(z, t_r, n_r, m, lanes)
                scale = inverse * vec_r[0:1, lanes]
                offset = vec_r[1:2, lanes] - centre * scale
                v = (e_r[rows, lanes].astype(F32) * scale + offset) * mask_r[rows, :]
                at = slice(m * z.held, (m + 1) * z.held)
                pool_r[at, lanes] = map_sums(z, v) / pix_r[at, :]

        io.need(sq_r, ex_r)
        inner, hidden, gate = gate_rows(pool_r[...], sq_r, sqb_r[0:1], ex_r, vec_r[6:7])
        gate_r[...] = gate
        inner_r[...] = inner
        hid_r[...] = hidden
        io.send(gate_r, inner_r, hid_r, pool_r)
        io.need(p_r)

        @pl.loop(0, z.out // LANES)
        def _(j):
            lanes = pl.ds(pl.multiple_of(j * LANES, LANES), LANES)
            for m in range(z.micro):
                rows = slice(m * z.map, (m + 1) * z.map)
                centre, inverse = norms_at(z, t_r, n_r, m, lanes)
                scale = inverse * vec_r[0:1, lanes]
                offset = vec_r[1:2, lanes] - centre * scale
                v = e_r[rows, lanes].astype(F32) * scale + offset
                centre, inverse = norms_at(z, t_r, n_r, m, lanes, side)
                scale = inverse * vec_r[2:3, lanes]
                offset = vec_r[3:4, lanes] - centre * scale
                o = v * spread(z, gate_r[m * z.held : (m + 1) * z.held, lanes])
                o = (o + (p_r[rows, lanes].astype(F32) * scale + offset)) * mask_r[rows, :]
                mid_r[rows, lanes] = (o * sigmoid(o)).astype(BF16)

        io.send(mid_r)
        io.need(w_r)
        c = dot(mid_r[...], w_r[...])
        c_r[...] = c
        io.send(c_r)
        for m in range(z.micro):
            part = c[m * z.map : (m + 1) * z.map]
            live = part * mask_r[m * z.map : (m + 1) * z.map, :]
            a, b = fold_sums(live, live * part)
            s_r[2 * m : 2 * m + 1, :] = a
            s_r[2 * m + 1 : 2 * m + 2, :] = b

    return run(
        body,
        [
            ((z.coarse, z.out), BF16),
            Both(((z.coarse, z.mid), F32)),
            ((z.maps, z.out), F32),
            ((z.maps, z.out), F32),
            ((z.maps, z.hid), F32),
            ((z.maps, z.hid), F32),
            Raw((2 * side, z.out), F32),
            Near(((2 * z.micro, z.mid), F32)),
        ],
        (place, Near(sums), counted, vectors, pix, e1, p1, squeeze, sq_bias, excite, w, mask),
        room=ROOM,
        ahead=ahead,
        spare=1,
        flops=2 * z.coarse * z.out * z.mid,
    )


def output_kernel(z, place, sums, counted, vectors, pix, e2, middle, up, squeeze, sq_bias, excite, mask, final, ahead):
    span = z.out // 2

    def body(
        io, place_r, t_r, n_r, vec_r, pix_r, e_r, mid_r, up_r, sq_r, sqb_r, ex_r, mask_r,
        final_r, away_r, do_r, h_r, pool_r, hid_r, dl_r, dz_r, s_r, out_r, gate_r, du_r,
    ):
        core = place_r[0]

        @pl.loop(0, z.out // LANES)
        def _(j):
            lanes = pl.ds(pl.multiple_of(j * LANES, LANES), LANES)
            for m in range(z.micro):
                rows = slice(m * z.map, (m + 1) * z.map)
                centre, inverse = norms_at(z, t_r, n_r, m, lanes)
                scale = inverse * vec_r[4:5, lanes]
                offset = vec_r[5:6, lanes] - centre * scale
                v = (e_r[rows, lanes].astype(F32) * scale + offset) * mask_r[rows, :]
                at = slice(m * z.held, (m + 1) * z.held)
                pool_r[at, lanes] = map_sums(z, v) / pix_r[at, :]

        io.need(sq_r, ex_r)
        inner, hidden, gate = gate_rows(pool_r[...], sq_r, sqb_r[1:2], ex_r, vec_r[7:8])
        gate_r[...] = gate
        hid_r[...] = hidden
        io.send(pool_r, hid_r)
        io.need(mid_r, up_r)

        @pl.loop(0, z.out // LANES)
        def _(j):
            lanes = pl.ds(pl.multiple_of(j * LANES, LANES), LANES)
            for m in range(z.micro):
                rows = slice(m * z.map, (m + 1) * z.map)
                at = slice(m * z.held, (m + 1) * z.held)
                centre, inverse = norms_at(z, t_r, n_r, m, lanes)
                scale = inverse * vec_r[4:5, lanes]
                offset = vec_r[5:6, lanes] - centre * scale
                v = (e_r[rows, lanes].astype(F32) * scale + offset) * mask_r[rows, :]
                o = v * spread(z, gate_r[at, lanes]) + mid_r[rows, lanes].astype(F32)
                sigma = sigmoid(o)
                out_r[m, :, :, :, lanes] = by_map(z, o * sigma).astype(BF16)
                up = up_r[m, :, :, :, lanes].astype(F32).reshape(z.map, LANES)
                do = up * (sigma * (1.0 + o * (1.0 - sigma)))
                do_r[rows, lanes] = do
                dl_r[at, lanes] = map_sums(z, do * v)

        io.out(
            half_of(out_r, 4, core, span), final_r.at[:, :, pl.ds(core * z.held, z.held)]
        )
        io.out(half_of(out_r, 4, 1 - core, span), away_r)
        io.send(do_r)
        dl, dz, du = gate_back(dl_r[...], gate_r[...], inner, sq_r, ex_r, pix_r[...])
        dl_r[...] = dl
        dz_r[...] = dz
        du_r[...] = du
        io.send(dl_r, dz_r)
        bias_sums(z, dl, dz, s_r, 2 * z.micro)

        @pl.loop(0, z.out // LANES)
        def _(j):
            lanes = pl.ds(pl.multiple_of(j * LANES, LANES), LANES)
            for m in range(z.micro):
                rows = slice(m * z.map, (m + 1) * z.map)
                at = slice(m * z.held, (m + 1) * z.held)
                centre, inverse = norms_at(z, t_r, n_r, m, lanes)
                k = (e_r[rows, lanes].astype(F32) - centre) * inverse
                h = do_r[rows, lanes] * spread(z, gate_r[at, lanes]) + spread(z, du_r[at, lanes])
                h = h * mask_r[rows, :]
                h_r[rows, lanes] = h
                a, b = fold_sums(h, h * k)
                s_r[2 * m : 2 * m + 1, lanes] = a
                s_r[2 * m + 1 : 2 * m + 2, lanes] = b

    maps = (z.micro, z.half, z.held, z.half)
    return run(
        body,
        [
            Raw(final, BF16),
            Raw(maps + (span,), BF16),
            ((z.coarse, z.out), F32),
            Near(((z.coarse, z.out), F32)),
            ((z.maps, z.out), F32),
            ((z.maps, z.hid), F32),
            ((z.maps, z.out), F32),
            ((z.maps, z.hid), F32),
            Near(((2 * z.micro + 2, z.out), F32)),
        ],
        (place, Near(sums), counted, vectors, pix, e2, middle, up, squeeze, sq_bias, excite, mask),
        room=ROOM,
        ahead=ahead,
        scratch=[
            pltpu.VMEM(maps + (z.out,), BF16),
            pltpu.VMEM((z.maps, z.out), F32),
            pltpu.VMEM((z.maps, z.out), F32),
        ],
        spare=2,
    )


def wide_back(z, n_r, m, lanes, total_r, back_r, first, gain, e, h):
    centre, inverse = norms_at(z, total_r, n_r, m, lanes, first)
    k = (e - centre) * inverse
    at = first + 2 * m
    mean = back_r[at : at + 1, lanes] / n_r[z.micro + m]
    slope = back_r[at + 1 : at + 2, lanes] / n_r[z.micro + m]
    return (h - (mean + k * slope)) * (gain * inverse)


def unexpand_kernel(z, place, back, total, counted, vectors, row, e, h, w, total_n, vec_n, conv, mask, ahead):
    def body(
        io, place_r, b_r, t_r, n_r, vec_r, e_r, h_r, w_r, tn_r, vn_r, c_r, mask_r,
        de_r, live_r, s_r,
    ):
        @pl.loop(0, z.out // LANES)
        def _(j):
            lanes = pl.ds(pl.multiple_of(j * LANES, LANES), LANES)
            for m in range(z.micro):
                rows = slice(m * z.map, (m + 1) * z.map)
                h = h_r[rows, lanes]
                e = e_r[rows, lanes].astype(F32)
                d = wide_back(z, n_r, m, lanes, t_r, b_r, 0, vec_r[row : row + 1, lanes], e, h)
                de_r[rows, lanes] = (d * mask_r[rows, :]).astype(BF16)

        io.send(de_r)
        io.need(w_r)
        da = dot_nt(de_r[...], w_r[...])
        norms = norm_rows(tn_r[...], counts_of(z, n_r, 1), z.micro)
        sums = []
        for m in range(z.micro):
            rows = slice(m * z.map, (m + 1) * z.map)
            centre, inverse = norms[m]
            k = (c_r[rows, :] - centre) * inverse
            v = (k * vn_r[0:1] + vn_r[1:2]) * mask_r[rows, :]
            h = da[rows] * slope_of(v) * mask_r[rows, :]
            live_r[rows, :] = h
            sums += fold_sums(h, h * k)
        to_all(z, sums, s_r)

    return run(
        body,
        [
            ((z.coarse, z.out), BF16),
            Near(((z.coarse, z.mid), F32)),
            Near(((2 * z.micro, z.mid), F32)),
        ],
        (place, Near(back), total, counted, vectors, e, h, w, total_n, vec_n, conv, mask),
        ahead=ahead,
        flops=2 * z.coarse * z.out * z.mid,
    )


def narrow_back(m, norms, back, counted, gain, conv, live, mask):
    centre, inverse = norms[m]
    k = (conv - centre) * inverse
    mean = back[2 * m : 2 * m + 1] / counted[m]
    slope = back[2 * m + 1 : 2 * m + 2] / counted[m]
    return (live - (mean + k * slope)) * (gain * inverse) * mask


def untap_kernel(z, place, back, total, counted, vec, conv, live, w, total_n, vec_n, conv_n, mask, strided, ahead):
    planes = 4 if strided else 1

    def body(io, place_r, b_r, t_r, n_r, vec_r, c_r, h_r, w_r, tn_r, vn_r, cn_r, mask_r, dc_r, live_r, g_r, s_r, tap_r):
        counted = counts_of(z, n_r, 1)
        back = b_r[...]
        g_r[...] = gain_rows(back, z.micro)
        io.send(g_r)
        norms = norm_rows(t_r[...], counted, z.micro)
        taps = ((0, 0), (1, 1)) if strided else ((0, 1), (1, 0), (2, -1))
        for m in range(z.micro):
            rows = slice(m * z.map, (m + 1) * z.map)
            d = narrow_back(
                m, norms, back, counted, vec_r[0:1], c_r[rows, :], h_r[rows, :], mask_r[rows, :]
            )
            dc_r[rows, :] = d.astype(BF16)
            for lane in range(0, z.mid, LANES):
                place_patches(
                    d[:, lane : lane + LANES], taps, taps, tap_r, m * z.map, lane, z.mid, z.group
                )
        io.send(dc_r)
        norms = norm_rows(tn_r[...], counts_of(z, n_r, 0 if strided else 1), z.micro)
        acc = [[None, None] for _ in range(z.micro)]
        io.need(w_r, cn_r)
        for p in range(planes):
            da = None
            if strided:
                terms = [
                    (3 * i + j, 3 * rs + cs)
                    for i, rs in PLANE_TAPS[p // 2]
                    for j, cs in PLANE_TAPS[p % 2]
                ]
            else:
                terms = [(t, t) for t in range(9)]
            for t, slot in terms:
                part = dot_nt(
                    tap_r[:, slot * z.mid : (slot + 1) * z.mid], w_r[t * z.mid : (t + 1) * z.mid, :]
                )
                da = part if da is None else da + part
            for m in range(z.micro):
                rows = slice(m * z.map, (m + 1) * z.map)
                at = (p * z.micro + m) * z.map
                centre, inverse = norms[m]
                k = (cn_r[at : at + z.map, :] - centre) * inverse
                v = (k * vn_r[0:1] + vn_r[1:2]) * mask_r[rows, :]
                h = da[rows] * slope_of(v) * mask_r[rows, :]
                live_r[at : at + z.map, :] = h
                a, b = fold_sums(h, h * k)
                acc[m] = [a, b] if p == 0 else [acc[m][0] + a, acc[m][1] + b]
        to_all(z, [row for pair in acc for row in pair], s_r)

    return run(
        body,
        [
            ((z.coarse, z.mid), BF16),
            Near(((planes * z.coarse, z.mid), F32)),
            ((2, z.mid), F32),
            Near(((2 * z.micro, z.mid), F32)),
        ],
        (place, Near(back), total, counted, vec, conv, live, w, total_n, vec_n, conv_n, mask),
        ahead=ahead,
        scratch=[pltpu.VMEM((z.coarse, 9 * z.mid), BF16)],
        flops=2 * z.coarse * 9 * z.mid * z.mid,
    )


def unreduce_kernel(
    z, place, back, total, counted, vec, conv, live, w, do2, total_w, vectors, gate, inner, e1, p1, squeeze, excite, pix, mask, ahead
):
    side = 2 * z.micro

    def body(
        io, place_r, b_r, t_r, n_r, vec_r, c_r, h_r, w_r, do2_r, tw_r, vw_r, gate_r, in_r, e_r, p_r, sq_r, ex_r, pix_r, mask_r,
        dc_r, do_r, wide_r, g_r, dl_r, dz_r, s_r, du_r,
    ):
        counted = counts_of(z, n_r, 1)
        back = b_r[...]
        g_r[...] = gain_rows(back, z.micro)
        norms = norm_rows(t_r[...], counted, z.micro)
        for m in range(z.micro):
            rows = slice(m * z.map, (m + 1) * z.map)
            d = narrow_back(
                m, norms, back, counted, vec_r[0:1], c_r[rows, :], h_r[rows, :], mask_r[rows, :]
            )
            dc_r[rows, :] = d.astype(BF16)
        io.send(g_r, dc_r)
        io.need(w_r, do2_r, e_r, p_r)

        @pl.loop(0, z.out // 256)
        def _(j):
            wide_lanes = pl.ds(pl.multiple_of(j * 256, 256), 256)
            dm = dot_nt(dc_r[...], w_r[wide_lanes, :])
            for i in range(2):
                lanes = pl.ds(pl.multiple_of(j * 256 + i * LANES, LANES), LANES)
                for m in range(z.micro):
                    rows = slice(m * z.map, (m + 1) * z.map)
                    at = slice(m * z.held, (m + 1) * z.held)
                    live = mask_r[rows, :]
                    centre, inverse = norms_at(z, tw_r, n_r, m, lanes)
                    k = (e_r[rows, lanes].astype(F32) - centre) * inverse
                    q = (k * vw_r[0:1, lanes] + vw_r[1:2, lanes]) * live
                    centre, inverse = norms_at(z, tw_r, n_r, m, lanes, side)
                    kp = (p_r[rows, lanes].astype(F32) - centre) * inverse
                    t = (kp * vw_r[2:3, lanes] + vw_r[3:4, lanes]) * live
                    o = q * spread(z, gate_r[at, lanes]) + t
                    d = (dm[rows, i * LANES : (i + 1) * LANES] + do2_r[rows, lanes]) * slope_of(o)
                    do_r[rows, lanes] = d
                    dl_r[at, lanes] = map_sums(z, d * q)
                    d = d * live
                    a, b = fold_sums(d, d * kp)
                    s_r[side + 2 * m : side + 2 * m + 1, lanes] = a
                    s_r[side + 2 * m + 1 : side + 2 * m + 2, lanes] = b

        io.send(do_r)
        io.need(sq_r, ex_r)
        dl, dz, du = gate_back(dl_r[...], gate_r[...], in_r[...], sq_r, ex_r, pix_r[...])
        dl_r[...] = dl
        dz_r[...] = dz
        du_r[...] = du
        io.send(dl_r, dz_r)
        bias_sums(z, dl, dz, s_r, 2 * side)

        @pl.loop(0, z.out // LANES)
        def _(j):
            lanes = pl.ds(pl.multiple_of(j * LANES, LANES), LANES)
            for m in range(z.micro):
                rows = slice(m * z.map, (m + 1) * z.map)
                at = slice(m * z.held, (m + 1) * z.held)
                centre, inverse = norms_at(z, tw_r, n_r, m, lanes)
                k = (e_r[rows, lanes].astype(F32) - centre) * inverse
                h = do_r[rows, lanes] * spread(z, gate_r[at, lanes]) + spread(z, du_r[at, lanes])
                h = h * mask_r[rows, :]
                wide_r[rows, lanes] = h
                a, b = fold_sums(h, h * k)
                s_r[2 * m : 2 * m + 1, lanes] = a
                s_r[2 * m + 1 : 2 * m + 2, lanes] = b

    return run(
        body,
        [
            ((z.coarse, z.mid), BF16),
            ((z.coarse, z.out), F32),
            Near(((z.coarse, z.out), F32)),
            ((2, z.mid), F32),
            ((z.maps, z.out), F32),
            ((z.maps, z.hid), F32),
            Near(((2 * side + 2, z.out), F32)),
        ],
        (
            place, Near(back), total, counted, vec, conv, live, w, do2, total_w, vectors, gate, inner,
            e1, p1, squeeze, excite, pix, mask,
        ),
        scratch=[pltpu.VMEM((z.maps, z.out), F32)],
        ahead=ahead,
        flops=2 * z.coarse * z.out * z.mid,
    )


def side_kernel(z, place, back, total, counted, vectors, p1, do, mask):
    def body(io, place_r, b_r, t_r, n_r, vec_r, p_r, do_r, mask_r, dp_r):
        @pl.loop(0, z.out // LANES)
        def _(j):
            lanes = pl.ds(pl.multiple_of(j * LANES, LANES), LANES)
            for m in range(z.micro):
                rows = slice(m * z.map, (m + 1) * z.map)
                p = p_r[rows, lanes].astype(F32)
                h = do_r[rows, lanes]
                d = wide_back(z, n_r, m, lanes, t_r, b_r, 2 * z.micro, vec_r[2:3, lanes], p, h)
                dp_r[rows, lanes] = (d * mask_r[rows, :]).astype(BF16)

    return run(
        body,
        [((z.coarse, z.out), BF16)],
        (place, back, total, counted, vectors, p1, do, mask),
    )[0]


def leave_kernel(z, place, back, total, counted, vec, conv, live, w_one, dp, w_side, perm, mask, final):
    block = 2 * z.map
    maps = (z.half, z.held, z.side)

    def body(
        io, place_r, b_r, t_r, n_r, vec_r, c_r, h_r, w_r, dp_r, ws_r, perm_r, mask_r,
        dc_r, final_r, away_r, g_r, keep_r, grad_r,
    ):
        core = place_r[0]
        counted = counts_of(z, n_r, 0)
        back = b_r[...]
        g_r[...] = gain_rows(back, z.micro)
        norms = norm_rows(t_r[...], counted, z.micro)
        for m in range(z.micro):
            for p in range(4):
                at = (p * z.micro + m) * z.map
                rows = slice(at, at + z.map)
                d = narrow_back(
                    m, norms, back, counted, vec_r[0:1], c_r[rows, :], h_r[rows, :],
                    mask_r[m * z.map : (m + 1) * z.map, :],
                )
                dc_r[rows, :] = d.astype(BF16)
        io.send(dc_r)
        io.need(w_r, dp_r, ws_r)
        rows = z.map // 2
        for m in range(z.micro):
            side = dot_nt(dp_r[m * z.map : (m + 1) * z.map, :], ws_r[...])
            for half in range(2):
                stacked = jnp.concatenate(
                    [
                        dc_r[(p * z.micro + m) * z.map + half * rows : (p * z.micro + m) * z.map + (half + 1) * rows, :]
                        for p in range(4)
                    ],
                    axis=0,
                )
                ordered = dot_tn(perm_r[...], stacked).astype(BF16)
                grad = dot_nt(ordered, w_r[...])
                for n in range(z.cin // LANES):
                    lanes = slice(n * LANES, (n + 1) * LANES)
                    grad_r[n] = grad[:, lanes]
                    for o in range(z.half // 2):
                        for b in range(z.held):
                            at = 2 * o * z.held * z.side + b * z.side
                            src = half * rows + (o * z.held + b) * z.half
                            spots = pl.ds(at, z.half, stride=2)
                            grad_r[n, spots, :] = grad_r[n, spots, :] + side[src : src + z.half, lanes]

                @pl.when(core == half)
                def _():
                    for n in range(z.cin // LANES):
                        keep_r[m, :, :, :, n * LANES : (n + 1) * LANES] = grad_r[n].reshape(maps + (LANES,))

                @pl.when(core != half)
                def _():
                    for n in range(z.cin // LANES):
                        away_r[m, :, n * LANES : (n + 1) * LANES] = grad_r[n].astype(BF16)

            io.out(keep_r.at[m], final_r.at[m, :, pl.ds(core * z.held, z.held)])

    return run(
        body,
        [
            ((z.fine, z.mid), BF16),
            Raw(final, F32),
            ((z.micro, block, z.cin), BF16),
            ((2, z.mid), F32),
        ],
        (place, Near(back), total, counted, vec, conv, live, w_one, dp, w_side, perm, mask),
        scratch=[
            pltpu.VMEM((z.micro,) + maps + (z.cin,), F32),
            pltpu.VMEM((z.cin // LANES, block, LANES), F32),
        ],
        spare=z.micro,
        flops=2 * z.fine * z.cin * z.mid,
    )


def finish_images(z, place, got, final):
    maps = (z.half, z.held, z.side)

    def body(place_r, got_r, _, final_r, in_r, out_r, sems):
        other = 1 - place_r[0]
        loads = [pltpu.make_async_copy(got_r.at[m], in_r.at[m], sems.at[m]) for m in range(z.micro)]
        stores = [
            pltpu.make_async_copy(
                out_r.at[m], final_r.at[m, :, pl.ds(other * z.held, z.held)], sems.at[z.micro + m]
            )
            for m in range(z.micro)
        ]
        for copy in loads:
            copy.start()
        for m in range(z.micro):
            loads[m].wait()
            out_r[m] = in_r[m].astype(F32).reshape(maps + (z.cin,))
            stores[m].start()
        for copy in stores:
            copy.wait()

    any_spec = pl.BlockSpec(memory_space=pl.ANY)
    return pl.pallas_call(
        body,
        out_shape=jax.ShapeDtypeStruct(final.shape, final.dtype),
        in_specs=[pl.BlockSpec(memory_space=pltpu.SMEM), any_spec, any_spec],
        out_specs=any_spec,
        input_output_aliases={2: 0},
        scratch_shapes=[
            pltpu.VMEM(got.shape, got.dtype),
            pltpu.VMEM((z.micro,) + maps + (z.cin,), F32),
            pltpu.SemaphoreType.DMA((2 * z.micro,)),
        ],
        compiler_params=pltpu.CompilerParams(vmem_limit_bytes=16 << 20),
    )(place, got, final)


def finish_output(z, place, got, final):
    def body(place_r, got_r, _, final_r, buf_r, sems):
        other = 1 - place_r[0]
        copy = pltpu.make_async_copy(got_r, buf_r, sems.at[0])
        copy.start()
        copy.wait()
        copy = pltpu.make_async_copy(buf_r, final_r.at[:, :, pl.ds(other * z.held, z.held)], sems.at[1])
        copy.start()
        copy.wait()

    any_spec = pl.BlockSpec(memory_space=pl.ANY)
    return pl.pallas_call(
        body,
        out_shape=jax.ShapeDtypeStruct(final.shape, final.dtype),
        in_specs=[pl.BlockSpec(memory_space=pltpu.SMEM), any_spec, any_spec],
        out_specs=any_spec,
        input_output_aliases={2: 0},
        scratch_shapes=[pltpu.VMEM(got.shape, got.dtype), pltpu.SemaphoreType.DMA((2,))],
    )(place, got, final)


def gradient_kernel(z, place, size, jobs, args):
    starts, at = [], 0
    for kind, i, j in jobs:
        starts.append(at)
        at += args[i].shape[1] * args[j].shape[1] // (2 * size * 512)
    height = at

    def body(io, place_r, *refs):
        out_r = refs[-1]
        refs = refs[:-1]
        core, me = place_r[0], place_r[1]

        def put(c, b, first, length, values):
            p = b ^ me
            p = p // 4 * 4 + p % 2 * 2 + p // 2 % 2 if c else p
            out_r[c ^ core, p, first : first + length, :] = values

        for (kind, i, j), start in zip(jobs, starts):
            lhs, rhs = refs[i], refs[j]
            io.need(lhs, rhs)
            k, n = lhs.shape[1], rhs.shape[1]
            if kind == "flat":
                per = k // (2 * size)
                for r in range(0, k, 512):
                    for c in range(0, n, 512):
                        d = dot_tn(lhs[: rhs.shape[0], r : r + 512], rhs[:, c : c + 512]).astype(BF16)
                        at = r
                        while at < r + 512:
                            chunk, inside = divmod(at, per)
                            length = min(per - inside, r + 512 - at)
                            first = start + (c // 512) * per + inside
                            put(chunk % 2, chunk // 2, first, length, d[at - r : at - r + length])
                            at += length
            elif kind == "rows" and n == 512:
                per = k // (2 * size)
                for r in range(0, k, 512):
                    d = dot_tn(lhs[:, r : r + 512], rhs[...]).astype(BF16)
                    for at in range(r, r + 512, per):
                        c, b = divmod(at // per, size)
                        put(c, b, start, per, d[at - r : at - r + per])
            elif kind == "rows":
                per = k // (2 * size)
                d = dot_tn(lhs[...].astype(BF16), rhs[...].astype(BF16)).astype(BF16)
                parts = 512 // n
                unit = per // parts
                for at in range(0, k, per):
                    c, b = divmod(at // per, size)
                    rows = [d[at + q * unit : at + (q + 1) * unit] for q in range(parts)]
                    put(c, b, start, unit, jnp.concatenate(rows, axis=1))
            else:
                d = dot_tn(lhs[...].astype(BF16), rhs[...].astype(BF16)).astype(BF16)
                across = n // 1024
                per = k * across // size
                for c in range(2):
                    for b in range(size):
                        r, lane = divmod(b, across)
                        first = c * (n // 2) + lane * 512
                        put(c, b, start, per, d[r * per : (r + 1) * per, first : first + 512])
    return body, height, starts


def gradients(z, place, size, jobs, args):
    body, height, starts = gradient_kernel(z, place, size, jobs, args)

    def outer(io, place_r, *refs):
        ins, (keep_r, send_r, both_r) = refs[:-3], refs[-3:]
        body(io, place_r, *ins, both_r)
        io.out(both_r.at[1], send_r)
        io.out(both_r.at[0], keep_r)

    shape = (size, height, 512)
    keep, send = run(
        outer,
        [Near((shape, BF16))] * 2,
        (place, *(Late(a) for a in args)),
        scratch=[pltpu.VMEM((2,) + shape, BF16)],
        spare=2,
    )
    return keep, send, starts


def part_kernel(sources, spans):
    count = sources[0][0].shape[0]
    outs = []
    for _, length, bit in spans:
        if bit:
            outs += [Near(((count // 2, length, 512), BF16))] * 2
        else:
            outs += [Near(((length, 512), BF16))] * count

    def body(io, *refs):
        ins, results = refs[: 2 * len(sources)], list(refs[2 * len(sources) :])
        pairs, at = [], 0
        for k in range(len(sources)):
            kept, come = ins[2 * k], ins[2 * k + 1]
            io.need(kept, come)
            pairs.append((at, at + kept.shape[1], kept, come))
            at += kept.shape[1]

        def pieces(first, length):
            for low, high, kept, come in pairs:
                start, stop = max(first, low), min(first + length, high)
                if start < stop:
                    yield start - first, slice(start - low, stop - low), kept, come

        for first, length, bit in spans:
            if not bit:
                for p in range(count):
                    ref = results.pop(0)
                    for to, rows, kept, come in pieces(first, length):
                        total = kept[p, rows].astype(F32) + come[p, rows].astype(F32)
                        ref[to : to + rows.stop - rows.start, :] = total.astype(BF16)
                continue
            kept_r, sent_r = results.pop(0), results.pop(0)
            for which, ref in ((1, sent_r), (0, kept_r)):
                for p in range(count):
                    if (p // bit) % 2 == which:
                        at = p // (2 * bit) * bit + p % bit
                        for to, rows, kept, come in pieces(first, length):
                            size = rows.stop - rows.start
                            total = kept[p, rows].astype(F32) + come[p, rows].astype(F32)
                            ref[at, to : to + size, :] = total.astype(BF16)

    return run(body, outs, [Near(a) for pair in sources for a in pair])


def total_kernel(blocks):
    def body(io, *refs):
        refs[-1][...] = tree_sum([ref[...].astype(F32) for ref in refs[:-1]])

    return run(body, [(blocks[0].shape, F32)], [Near(b) for b in blocks])[0]


def crossed(block, first, second):
    count = 2 * lax.axis_size("batch")
    route = [(i, (i // 2 ^ (second if i % 2 else first)) * 2 + i % 2) for i in range(count)]
    return lax.ppermute(block, ("batch", "rows"), route)


class Halving:
    def __init__(self, blocks):
        self.height = sum(keep.shape[1] for keep, _ in blocks)
        self.sources = blocks
        self.step = 0

    def prepare(self, *after):
        (kept, came), *others = self.sources
        bit = 1 if self.step < 2 else 0
        self.kept, *self.sent = part_kernel(
            [(tied(kept, *after), came), *others], ((0, self.height, bit),)
        )
        return self.sent[0]

    def send(self, *after):
        sent = [tied(s, *after) for s in self.sent]
        if self.step == 2:
            came = [swapped(s, "batch", 4 * (k + 1)) for k, s in enumerate(sent)]
            self.blocks = [self.kept] + came
        else:
            came = [crossed(sent[0], self.step + 1, 2 - self.step)]
            self.sources = [(self.kept, came[0])]
        self.step += 1
        return came

    def finish(self, *after):
        while self.step < 3:
            self.prepare(*after)
            self.send()
        return total_kernel(self.blocks)


def N(array):
    return Near(array)


def tied(value, *others):
    return lax.optimization_barrier((value, *others))[0] if others else value


def gathered_kernel(z, place, size, blocks, starts):
    across = z.out // 1024
    unit = z.out // 2 // size
    parts = 512 // z.hid
    tall = unit // parts
    wide = z.hid * across // size
    height = blocks[0].shape[1]

    def body(io, place_r, near_r, far_r, red_r, sqb_r, exb_r, sqa_r, exa_r, all_r):
        core, me = place_r[0], place_r[1]
        for high, ref in ((0, near_r), (1, far_r)):
            for low in range(2):
                for k in range(size // 4):
                    p = 4 * k + 2 * low + high + core * (high - low)
                    all_r[p] = ref[low * (size // 4) + k]

        def rows(p, first, length):
            return all_r[p, first : first + length].astype(F32)

        for b in range(size):
            p = b ^ me
            red_r[b * unit : (b + 1) * unit, :] = rows(p, starts[0], unit)
            for at, ref in ((starts[1], sqb_r), (starts[3], sqa_r)):
                block = rows(p, at, tall)
                for q in range(parts):
                    ref[b * unit + q * tall : b * unit + (q + 1) * tall, :] = block[:, q * z.hid : (q + 1) * z.hid]
            r, lane = divmod(b, across)
            for at, ref in ((starts[2], exb_r), (starts[4], exa_r)):
                ref[r * wide : (r + 1) * wide, lane * 512 : (lane + 1) * 512] = rows(p, at, wide)

    half = z.out // 2
    return run(
        body,
        [
            ((half, z.mid), F32),
            ((half, z.hid), F32),
            ((z.hid, half), F32),
            ((half, z.hid), F32),
            ((z.hid, half), F32),
        ],
        (place, *(Near(b) for b in blocks)),
        scratch=[pltpu.VMEM((size, height, 512), BF16)],
    )


def gathered(block):
    size = lax.axis_size("batch")
    part = jnp.stack([block] + [swapped(block, "batch", 4 * k) for k in range(1, size // 4)])
    part = jnp.concatenate([part, crossed(part, 2, 1)], axis=0)
    return part, crossed(part, 1, 2)


def weight_dot(inputs, grads):
    return lax.dot_general(inputs, grads, (((0,), (0,)), ((), ())), preferred_element_type=F32)


def folded(grad):
    size = lax.axis_size("batch")
    rows, width = grad.shape
    grad = grad.astype(BF16).reshape(size, 2, rows // (2 * size), width // 512, 512)
    return jnp.swapaxes(grad, 2, 3).reshape(size, 2, -1, 512)


def unfolded(block, width):
    count = width // 512
    rows = block.shape[0] // count
    return jnp.swapaxes(block.reshape(count, rows, 512), 0, 1).reshape(-1)


def tree_sum(terms):
    while len(terms) > 1:
        terms = [a + b for a, b in zip(terms[::2], terms[1::2])] + terms[len(terms) // 2 * 2 :]
    return terms[0]


def wide_sum(parts, first=(), second=()):
    parts = parts + swapped(parts, "rows", 1)
    bits = bits_of(lax.axis_size("batch"))
    partial = parts
    for at in range(0, len(bits), 2):
        parts = tied(parts, *(first if at == 0 else second if at == 2 else ()))
        pair = bits[at : at + 2]
        masks = [pair[0], pair[1], pair[0] + pair[1]] if len(pair) == 2 else pair
        parts = tree_sum([parts] + [swapped(parts, "batch", mask) for mask in masks])
        partial = parts if at == 0 else partial
    return parts, partial


def plain_gradients(jobs, size):
    blocks, starts, at = [], [], 0
    for kind, lhs, rhs in jobs:
        grad = weight_dot(lhs[: rhs.shape[0]].astype(BF16), rhs.astype(BF16))
        k, n = grad.shape
        if kind == "flat":
            block = core_sum(folded(grad), 1)
        elif kind == "rows" and n == 512:
            block = core_sum(grad.astype(BF16).reshape(2, size, -1, 512), 0)
        elif kind == "rows":
            parts = 512 // n
            block = grad.astype(BF16).reshape(2, size, parts, -1, n)
            block = core_sum(jnp.swapaxes(block, 2, 3).reshape(2, size, -1, 512), 0)
        else:
            across = n // 1024
            block = grad.astype(BF16).reshape(size // across, -1, 2, across, 512)
            block = core_sum(block.transpose(2, 0, 3, 1, 4).reshape(2, size, -1, 512), 0)
        starts.append(at)
        at += block.shape[1]
        blocks.append(block)
    return halved(jnp.concatenate(blocks, axis=1), two_orders), starts


def per_device(
    images,
    crop_sizes,
    reduce_a,
    reduce_gain_a,
    reduce_bias_a,
    spatial_a,
    spatial_gain_a,
    spatial_bias_a,
    expand_a,
    expand_gain_a,
    expand_bias_a,
    project_a,
    project_gain_a,
    project_bias_a,
    squeeze_a,
    squeeze_bias_a,
    excite_a,
    excite_bias_a,
    reduce_b,
    reduce_gain_b,
    reduce_bias_b,
    spatial_b,
    spatial_gain_b,
    spatial_bias_b,
    expand_b,
    expand_gain_b,
    expand_bias_b,
    squeeze_b,
    squeeze_bias_b,
    excite_b,
    excite_bias_b,
    cotangent,
):
    mid = reduce_a.shape[1]
    out = expand_a.shape[1]
    hid = squeeze_a.shape[1]
    size = lax.axis_size("batch")
    z = Sizes(images, mid, out, hid, size * lax.axis_size("rows"))
    micro, held, side, half = z.micro, z.held, z.side, z.half
    core = lax.axis_index("rows")
    me = lax.axis_index("batch")
    place = jnp.stack([core, me]).astype(jnp.int32)

    away = lax.dynamic_slice_in_dim(images, (1 - core) * held, held, axis=2)
    other = swapped(away, "rows", 1)
    up_away = lax.dynamic_slice_in_dim(cotangent, (1 - core) * held, held, axis=2)
    up_mine = lax.dynamic_slice_in_dim(cotangent, core * held, held, axis=2)
    vectors = jnp.stack(
        [
            expand_gain_a,
            expand_bias_a,
            project_gain_a,
            project_bias_a,
            expand_gain_b,
            expand_bias_b,
            excite_bias_a,
            excite_bias_b,
        ]
    )

    def pair(own, axis):
        return Pair(own, swapped(own, "rows", 1), axis)

    vectors = pair(vectors, 1)
    pair_sq_a, pair_sq_b = pair(squeeze_a, 0), pair(squeeze_b, 0)
    pair_ex_a, pair_ex_b = pair(excite_a, 1), pair(excite_b, 1)
    pair_red = pair(reduce_b, 0)
    sq_biases = jnp.stack([squeeze_bias_a, squeeze_bias_b])
    vec_one = jnp.stack([reduce_gain_a, reduce_bias_a])
    vec_two = jnp.stack([spatial_gain_a, spatial_bias_a])
    vec_four = jnp.stack([reduce_gain_b, reduce_bias_b])
    vec_five = jnp.stack([spatial_gain_b, spatial_bias_b])

    half_all = crop_sizes // 2
    counted = jnp.stack(
        [jnp.sum(crop_sizes * crop_sizes, axis=1), jnp.sum(half_all * half_all, axis=1)]
    ).astype(F32).reshape(-1)
    halves = lax.dynamic_slice_in_dim(half_all, (me * 2 + core) * held, held, axis=1)
    pix = (halves * halves).astype(F32).reshape(-1, 1)
    spots = jnp.arange(half, dtype=jnp.int32)
    limits = halves[:, None, :, None]
    inside = (spots[None, :, None, None] < limits) & (spots[None, None, None, :] < limits)
    mask = inside.astype(F32).reshape(z.coarse, 1)

    block = 2 * z.map
    spot = jnp.arange(block, dtype=jnp.int32)
    row_pair, rest = spot // (2 * z.group), spot % (2 * z.group)
    row_odd, spot_b, column = spot // (held * side) % 2, spot % (held * side) // side, spot % side
    row_pair = spot // (2 * held * side)
    target = ((row_odd * 2 + column % 2) * (half // 2) + row_pair) * z.group
    target = target + spot_b * half + column // 2
    perm = (target[None, :] == jnp.arange(block, dtype=jnp.int32)[:, None]).astype(BF16)

    other, perm, mask, pix, counted, sq_biases, vec_one, vec_two, vec_four, vec_five, up_mine, up_away, vectors.own = (
        lax.optimization_barrier(
            (other, perm, mask, pix, counted, sq_biases, vec_one, vec_two, vec_four, vec_five, up_mine, up_away, vectors.own)
        )
    )
    up_other = swapped(up_away, "rows", 1)
    vectors.other = swapped(vectors.own, "rows", 1)

    first_one, first_side, first_perm, first_mask, first_images = run(
        lambda io, place_r: None, [], (place,), ahead=(reduce_a, project_a, perm, mask, Part(images, 2)), room=ROOM
    )
    planes, c1_near, c1, p1, s1, s_side, *got = enter_kernel(
        z, place, N(first_images), N(other), N(first_perm), N(first_one), N(first_side), N(first_mask),
        (vec_one, spatial_a, mask),
    )
    vec_near, w_near, mask_near = map(N, got)
    patches_one, c2_near, c2, t1, s2, *got = taps_kernel(
        z, place, wide_sum(s1)[0], counted, vec_near, N(c1_near), w_near, mask_near, True,
        (vec_two, expand_a, mask, s_side),
    )
    vec_near, w_near, mask_near, side_near = map(N, got)
    active_two, e1_near, e1, t2, s3, *got = expand_kernel(
        z, place, wide_sum(s2)[0], counted, vec_near, N(c2_near), w_near, mask_near, side_near,
        (vectors, pix, p1, pair_sq_a, sq_biases, pair_ex_a, pair_red, mask),
    )
    vectors_near, pix_near, p1_near, sq_near, sqb_near, ex_near, w_near, mask_near = map(N, got)
    sums_three, _ = wide_sum(s3)
    middle, c4_near, c4, gate_one, pool_one, inner_one, hidden_one, total_three, s4, *got = middle_kernel(
        z, place, sums_three, counted, vectors_near, pix_near, N(e1_near), p1_near, sq_near, sqb_near, ex_near,
        w_near, mask_near, (vec_four, spatial_b, mask),
    )
    vec_near, w_near, mask_near = map(N, got)
    patches_four, c5_near, c5, t4, s5, *got = taps_kernel(
        z, place, wide_sum(s4)[0], counted, vec_near, N(c4_near), w_near, mask_near, False,
        (vec_five, expand_b, mask),
    )
    vec_near, w_near, mask_near = map(N, got)
    active_five, e2_near, e2, t5, s6, *got = expand_kernel(
        z, place, wide_sum(s5)[0], counted, vec_near, N(c5_near), w_near, mask_near, None,
        (vectors, pix, middle, Pair(up_mine, up_other, 4), pair_sq_b, sq_biases, pair_ex_b, mask),
    )
    vectors_near, pix_near, mid_near, up_near, sq_near, sqb_near, ex_near, mask_near = map(N, got)
    sums_six, _ = wide_sum(s6)
    final = (micro, half, 2 * held, half, out // 2)
    block_out, block_away, do2, h_near, pool_two, hidden_two, dl_two, dz_two, b6, *got = output_kernel(
        z, place, sums_six, counted, vectors_near, pix_near, N(e2_near), mid_near, up_near,
        sq_near, sqb_near, ex_near, mask_near, final,
        (N(sums_six), vectors, e2, expand_b, t5, vec_five, c5, mask),
    )
    total_near, vectors_near, e_near, w_near, tn_near, vn_near, cn_near, mask_near = map(N, got)

    whole_tiles = mid * 9 // (2 * size) % 16 == 0

    def made(jobs):
        if not whole_tiles:
            return None
        args, spec = [], []
        for kind, lhs, rhs in jobs:
            spec.append((kind, len(args), len(args) + 1))
            args += [lhs, rhs]
        keep, send, _ = gradients(z, place, size, spec, args)
        return keep, send

    def steps(make):
        return list(make()) if whole_tiles else []

    def exchanged(blocks):
        keep, send = blocks
        return keep, swapped(send, "rows", 1)

    back_six, _ = wide_sum(b6)
    de2, live_near, b5, *got = unexpand_kernel(
        z, place, back_six, total_near, counted, vectors_near, 4, e_near, N(h_near), w_near,
        tn_near, vn_near, cn_near, mask_near, (t5, vec_five, c5, spatial_b, t4, vec_four, c4, mask),
    )
    t_near, v_near, c_near, w_near, tn_near, vn_near, cn_near, mask_near = map(N, got)
    jobs_e = (("flat", active_five, de2),)
    made_e = made(jobs_e)
    back_five, _ = wide_sum(b5, (), steps(lambda: [made_e[0]]))
    dc5, live_near, g5, b4, *got = untap_kernel(
        z, place, back_five, t_near, counted, v_near, c_near, N(live_near), w_near,
        tn_near, vn_near, cn_near, mask_near, False,
        (t4, vec_four, c4, pair_red, do2, total_three, vectors, gate_one, inner_one, e1, p1, pair_sq_a, pair_ex_a, pix, mask),
    )
    t_near, v_near, c_near, w_near, *rest_near = map(N, got)
    jobs_s = (("flat", patches_four, dc5),)
    made_s = made(jobs_s)
    if whole_tiles:
        sum_e = Halving([exchanged(made_e)])
    back_four, _ = wide_sum(b4, (), steps(lambda: [made_s[0], sum_e.prepare()]))
    came = steps(lambda: sum_e.send(back_four))
    dc4, do1, h_near, g4, dl_one, dz_one, b3, *got = unreduce_kernel(
        z, place, back_four, t_near, counted, v_near, c_near, N(live_near), w_near, *rest_near,
        (total_three, vectors, e1, expand_a, t2, vec_two, c2, mask),
    )
    total_near, vectors_near, e_near, w_near, tn_near, vn_near, cn_near, mask_near = map(N, got)
    jobs_n = (
        ("rows", middle, dc4),
        ("rows", pool_two, dz_two),
        ("lanes", hidden_two, dl_two),
        ("rows", pool_one, dz_one),
        ("lanes", hidden_one, dl_one),
    )
    made_n = made(jobs_n)
    if whole_tiles:
        sum_s = Halving([exchanged(made_s)])
        came += [sum_s.sources[0][1]]
    back_three, _ = wide_sum(
        tied(b3, *came), (), steps(lambda: [made_n[0], sum_s.prepare(), sum_e.prepare()])
    )
    came = steps(lambda: sum_s.send(back_three) + sum_e.send(back_three))
    de1, live_near, b2, *got = unexpand_kernel(
        z, place, back_three, total_near, counted, vectors_near, 0, e_near, N(h_near), w_near,
        tn_near, vn_near, cn_near, mask_near, (t2, vec_two, c2, spatial_a, t1, vec_one, c1, mask),
    )
    t_near, v_near, c_near, w_near, tn_near, vn_near, cn_near, mask_near = map(N, got)
    dp1 = side_kernel(z, place, N(back_three), total_three, counted, vectors, p1, do1, mask)
    jobs_w = (("flat", active_two, de1), ("flat", planes, dp1))
    made_w = made(jobs_w)
    if whole_tiles:
        sum_n = Halving([exchanged(made_n)])
        came += [made_w[0], sum_n.sources[0][1]]
    back_two, _ = wide_sum(
        tied(b2, dp1, *came), (), steps(lambda: [sum_n.prepare(), sum_s.prepare(), sum_e.prepare()])
    )
    came = steps(lambda: sum_n.send(back_two) + sum_e.send(back_two))
    dc2, live_near, g2, b1, *got = untap_kernel(
        z, place, back_two, t_near, counted, v_near, c_near, N(live_near), w_near,
        tn_near, vn_near, cn_near, mask_near, True,
        (t1, vec_one, c1, reduce_a, dp1, project_a, perm, mask),
    )
    t_near, v_near, c_near, *rest_near = map(N, got)
    jobs_t = (("flat", patches_one, dc2),)
    made_t = made(jobs_t)
    if whole_tiles:
        sum_w = Halving([exchanged(made_w)])
        came += [made_t[0], sum_w.sources[0][1]]
    back_one, _ = wide_sum(tied(b1, *came), (), steps(lambda: [sum_n.prepare(), sum_w.prepare()]))
    came = steps(lambda: sum_n.send(back_one) + sum_s.send(back_one) + sum_w.send(back_one))
    dc1, images_grad, grad_away, g1 = leave_kernel(
        z, place, back_one, t_near, counted, v_near, c_near, N(live_near), *rest_near,
        (micro, side // 2, 2 * held, side, z.cin),
    )
    jobs_r = (("flat", planes, dc1),)
    made_r = made(jobs_r)

    images_grad = finish_images(z, place, swapped(grad_away, "rows", 1), images_grad)
    block_out = finish_output(z, place, swapped(block_away, "rows", 1), block_out)

    if whole_tiles:
        sum_t = Halving([exchanged(made_t), exchanged(made_r)])
        sum_n.prepare(made_r[0])
        sum_n.send()
        sum_t.prepare(sum_n.sent[0])
        sum_t.send()
        sum_s.prepare(sum_t.sent[0])
        sum_s.send()
        second = sum_n.finish()
        sum_w.prepare(second)
        sum_w.send()
        third = sum_t.finish()
        rest = sum_w.finish()
        first = jnp.concatenate([sum_e.finish(), sum_s.finish()], axis=0)
        heights = [a.shape[1] * b.shape[1] // (2 * size * 512) for _, a, b in jobs_n]
        at_second = [sum(heights[:k]) for k in range(len(heights) + 1)]
    else:
        second, at_second = plain_gradients(jobs_n, size)
        at_second = at_second + [second.shape[0]]
        first = plain_gradients(jobs_e + jobs_s, size)[0]
        rest = plain_gradients(jobs_w, size)[0]
        third = plain_gradients(jobs_t + jobs_r, size)[0]
    edge_first = expand_b.size // (2 * size * 512)
    edge_rest = expand_a.size // (2 * size * 512)
    edge_third = spatial_a.size // (2 * size * 512)

    narrows = second.astype(BF16)
    if whole_tiles:
        out_reduce, out_sq_b, out_ex_b, out_sq_a, out_ex_a = gathered_kernel(
            z, place, size, gathered(narrows), at_second
        )
    else:
        every = collected(narrows).astype(F32)

        def tall_of(k):
            block = every[:, at_second[k] : at_second[k + 1]]
            block = block.reshape(size, block.shape[1], 512 // hid, hid)
            return jnp.swapaxes(block, 1, 2).reshape(-1, hid)

        def flat_of(k):
            block = every[:, at_second[k] : at_second[k + 1]]
            across = (out // 2) // 512
            block = block.reshape(size // across, across, -1, 512)
            return jnp.swapaxes(block, 1, 2).reshape(hid, out // 2)

        out_reduce = every[:, : at_second[1]].reshape(-1, mid)
        out_sq_b, out_ex_b, out_sq_a, out_ex_a = tall_of(1), flat_of(2), tall_of(3), flat_of(4)
    span = out // 2

    def own(rows):
        return lax.dynamic_slice_in_dim(rows, core * span, span, axis=rows.ndim - 1)

    def wide_gains(total, first):
        rows = own(total)
        gain = sum(rows[first + 2 * m + 1] for m in range(micro))
        return gain, sum(rows[first + 2 * m] for m in range(micro))

    gain_six, bias_six = wide_gains(back_six, 0)
    gain_three, bias_three = wide_gains(back_three, 0)
    gain_side, bias_side = wide_gains(back_three, 2 * micro)
    return (
        block_out,
        images_grad,
        unfolded(third[edge_third:], mid),
        g1[0],
        g1[1],
        unfolded(third[:edge_third], mid),
        g2[0],
        g2[1],
        unfolded(rest[:edge_rest], out),
        gain_three,
        bias_three,
        unfolded(rest[edge_rest:], out),
        gain_side,
        bias_side,
        out_sq_a,
        back_three[4 * micro + 1, :hid],
        out_ex_a,
        own(back_three[4 * micro]),
        out_reduce,
        g4[0],
        g4[1],
        unfolded(first[edge_first:], mid),
        g5[0],
        g5[1],
        unfolded(first[:edge_first], out),
        gain_six,
        bias_six,
        out_sq_b,
        back_six[2 * micro + 1, :hid],
        out_ex_b,
        own(back_six[2 * micro]),
    )


def solution(mesh):
    in_specs = (
        P(None, "rows", "batch", None, None),
        P(),
        P(),
        P(),
        P(),
        P(),
        P(),
        P(),
        P(),
        P("rows"),
        P("rows"),
        P(),
        P("rows"),
        P("rows"),
        P("rows", None),
        P(),
        P(None, "rows"),
        P("rows"),
        P("rows", None),
        P(),
        P(),
        P(),
        P(),
        P(),
        P(),
        P("rows"),
        P("rows"),
        P("rows", None),
        P(),
        P(None, "rows"),
        P("rows"),
        P(None, None, "batch", None, "rows"),
    )
    out_specs = (
        P(None, None, "batch", None, "rows"),
        P(None, "rows", "batch", None, None),
        P(("batch", "rows")),
        P(),
        P(),
        P(("batch", "rows")),
        P(),
        P(),
        P(("batch", "rows")),
        P("rows"),
        P("rows"),
        P(("batch", "rows")),
        P("rows"),
        P("rows"),
        P("rows", None),
        P(),
        P(None, "rows"),
        P("rows"),
        P("rows", None),
        P(),
        P(),
        P(("batch", "rows")),
        P(),
        P(),
        P(("batch", "rows")),
        P("rows"),
        P("rows"),
        P("rows", None),
        P(),
        P(None, "rows"),
        P("rows"),
    )
    return jax.shard_map(
        per_device, mesh=mesh, in_specs=in_specs, out_specs=out_specs, check_vma=False
    )
```

```python
import jax
import jax.numpy as jnp
from jax import lax
from jax.experimental import pallas as pl
from jax.experimental.pallas import tpu as pltpu
from jax.sharding import PartitionSpec as P

epsilon = 1e-05
HIGHEST = lax.Precision.HIGHEST
BF16 = jnp.bfloat16
F32 = jnp.float32

PLANE_TAPS = (((1, 0),), ((2, 0), (0, 1)))


def swapped(block, axis, mask):
    route = [(i, i ^ mask) for i in range(lax.axis_size(axis))]
    return lax.ppermute(block, axis, route)


def bits_of(size):
    return [1 << k for k in range(size.bit_length() - 1)]


def all_sum(parts):
    parts = parts + swapped(parts, "rows", 1)
    size = lax.axis_size("batch")
    spread = jnp.broadcast_to(parts[None], (size,) + parts.shape)
    return jnp.sum(lax.all_to_all(spread, "batch", 0, 0, tiled=True), axis=0)


def halved(block, orders):
    size = lax.axis_size("batch")
    place = lax.axis_index("batch")
    bits = bits_of(size)
    count = block.shape[1]
    cut = count // 2 // 16 * 16
    parts = []
    for part, order in zip((block[:, :cut], block[:, cut:]), orders(bits)):
        shape = part.shape[1:]
        left = list(reversed(bits))
        part = part.reshape((2,) * len(bits) + shape)
        for bit in order:
            axis = left.index(bit)
            mine = (place // bit) % 2
            gone = lax.dynamic_index_in_dim(part, 1 - mine, axis, keepdims=False)
            kept = lax.dynamic_index_in_dim(part, mine, axis, keepdims=False)
            total = kept.astype(F32) + swapped(gone, "batch", bit).astype(F32)
            left.pop(axis)
            part = total.astype(BF16) if left else total
        parts.append(part)
    return jnp.concatenate(parts, axis=0)


def two_orders(bits):
    return (bits, bits[1::-1] + bits[2:])


def collected(block):
    place = lax.axis_index("batch")
    block = block[None]
    for bit in bits_of(lax.axis_size("batch")):
        other = swapped(block, "batch", bit)
        upper = (place // bit) % 2 == 1
        block = jnp.concatenate([jnp.where(upper, other, block), jnp.where(upper, block, other)], axis=0)
    return block


def core_sum(block, axis):
    core = lax.axis_index("rows")
    gone = lax.dynamic_index_in_dim(block, 1 - core, axis, keepdims=False)
    kept = lax.dynamic_index_in_dim(block, core, axis, keepdims=False)
    return (kept.astype(F32) + swapped(gone, "rows", 1).astype(F32)).astype(BF16)


def both_cores(block, axis):
    core = lax.axis_index("rows")
    other = swapped(block, "rows", 1)
    first = jnp.where(core == 0, block, other)
    second = jnp.where(core == 0, other, block)
    return jnp.concatenate([first, second], axis=axis)


LANES = 128
VMEM_MIB = 64
ROOM = None
READS = (((1, 0),), ((2, 0), (0, -1)))
ALL_TAPS = ((0, -1), (1, 0), (2, 1))


class Near:
    def __init__(self, array):
        self.array = array
        self.shape = array[0] if isinstance(array, tuple) else array.shape


class Both:
    def __init__(self, array):
        self.array = array


class Late:
    def __init__(self, array):
        self.array = array
        self.shape = array.shape


class Pair:
    def __init__(self, own, other, axis):
        self.own, self.other, self.axis = own, other, axis
        shape = list(own.shape)
        shape[axis] *= 2
        self.shape, self.dtype = tuple(shape), own.dtype


class Part:
    def __init__(self, array, axis):
        self.array, self.axis = array, axis
        shape = list(array.shape)
        shape[axis] //= 2
        self.shape, self.dtype = tuple(shape), array.dtype


class Away:
    def __init__(self, array, axis):
        self.array, self.axis = array, axis
        shape = list(array.shape)
        shape[axis] //= 2
        self.shape, self.dtype = tuple(shape), array.dtype


class Join:
    def __init__(self, array, cut, other, axis):
        self.array, self.cut, self.other, self.axis = array, cut, other, axis
        shape = list(other.shape)
        shape[axis] *= 2
        self.shape, self.dtype = tuple(shape), array.dtype


class Raw:
    def __init__(self, shape, dtype):
        self.shape, self.dtype = shape, dtype


def half_of(ref, axis, which, length):
    start = which * length
    if axis >= len(ref.shape) - 2:
        start = pl.multiple_of(start, length)
    return ref.at[(slice(None),) * axis + (pl.ds(start, length),)]


class Copies:
    def __init__(self, sems):
        self.sems, self.used = sems, 0
        self.waiting, self.open = {}, []

    def start(self, source, target):
        copy = pltpu.make_async_copy(source, target, self.sems.at[self.used])
        self.used += 1
        copy.start()
        return copy

    def need(self, *refs):
        for ref in refs:
            for copy in self.waiting.pop(id(ref), ()):
                copy.wait()

    def out(self, source, target):
        self.open.append(self.start(source, target))


def run(body, outs, args, scratch=(), flops=0, spare=0, ahead=(), room=None):
    operands, specs, plans, buffers = [], [], [], []
    far = pl.BlockSpec(memory_space=pltpu.HBM)
    vmem = pl.BlockSpec(memory_space=pltpu.VMEM)
    count, next_up = 0, []

    def plan(arg, late, keep):
        nonlocal count
        if isinstance(arg, Near) and keep is next_up:
            plans.append(("copy", len(operands), (len(keep), 0), late))
            operands.append(arg.array)
            specs.append(vmem)
            keep.append((tuple(arg.shape), arg.array.dtype))
            count += 1
            return
        if isinstance(arg, Near):
            plans.append(("near", len(operands), None, late))
            operands.append(arg.array)
            specs.append(vmem)
            return
        if isinstance(arg, Pair):
            kind, axis, parts = "pair", arg.axis, [arg.own, arg.other]
        elif isinstance(arg, Part):
            kind, axis, parts = "part", arg.axis, [arg.array]
        elif isinstance(arg, Away):
            kind, axis, parts = "away", arg.axis, [arg.array]
        elif isinstance(arg, Join):
            kind, axis, parts = "join", (arg.cut, arg.axis), [arg.array, arg.other]
        elif arg.ndim == 1:
            plans.append(("near", len(operands), None, late))
            operands.append(arg)
            specs.append(pl.BlockSpec(memory_space=pltpu.SMEM))
            return
        else:
            kind, axis, parts = "copy", 0, [arg]
        plans.append((kind, len(operands), (len(keep), axis), late))
        operands.extend(parts)
        specs.extend([far] * len(parts))
        keep.append((tuple(arg.shape), arg.dtype))
        count += len(parts)

    for arg in args:
        late = isinstance(arg, Late)
        plan(arg.array if late else arg, late, buffers)
    first_ahead = len(plans)
    for arg in ahead:
        plan(arg, True, next_up)
    shapes, out_specs, ways = [], [], []
    for item in outs:
        if isinstance(item, Raw):
            ways.append(("raw", len(shapes), None))
            shapes.append(jax.ShapeDtypeStruct(item.shape, item.dtype))
            out_specs.append(far)
        elif isinstance(item, Near):
            ways.append(("near", len(shapes), None))
            shapes.append(jax.ShapeDtypeStruct(*item.array))
            out_specs.append(vmem)
        elif isinstance(item, Both):
            ways.append(("both", len(shapes), None))
            shapes += [jax.ShapeDtypeStruct(*item.array)] * 2
            out_specs += [vmem, far]
            count += 1
        else:
            ways.append(("copy", len(shapes), len(buffers)))
            shapes.append(jax.ShapeDtypeStruct(*item))
            out_specs.append(far)
            buffers.append(item)
            count += 1
    first_next = len(shapes)
    for item in next_up:
        shapes.append(jax.ShapeDtypeStruct(*item))
        out_specs.append(vmem)
    sems = pltpu.SemaphoreType.DMA((max(count + spare, 1),))

    def kernel(*refs):
        ins = refs[: len(operands)]
        results = refs[len(operands) : len(operands) + len(shapes)]
        rest = refs[len(operands) + len(shapes) :]
        bufs, own = rest[: len(buffers)], rest[len(buffers) : -1]
        io = Copies(rest[-1])
        views, early = [], []
        for k, (kind, at, spot, late) in enumerate(plans):
            if kind == "near":
                views.append(ins[at])
                continue
            index, axis = spot
            buf = results[first_next + index] if k >= first_ahead else bufs[index]
            if kind == "copy":
                copies = [io.start(ins[at], buf)]
            elif kind == "pair":
                core = ins[0][0]
                length = ins[at].shape[axis]
                copies = [
                    io.start(ins[at], half_of(buf, axis, core, length)),
                    io.start(ins[at + 1], half_of(buf, axis, 1 - core, length)),
                ]
            elif kind == "join":
                core, (cut, axis) = ins[0][0], axis
                mine = half_of(ins[at], cut, core, ins[at + 1].shape[cut])
                length = ins[at + 1].shape[axis]
                copies = [
                    io.start(mine, half_of(buf, axis, core, length)),
                    io.start(ins[at + 1], half_of(buf, axis, 1 - core, length)),
                ]
            else:
                core = ins[0][0] if kind == "part" else 1 - ins[0][0]
                copies = [io.start(half_of(ins[at], axis, core, buf.shape[axis]), buf)]
            io.waiting[id(buf)] = copies
            if k < first_ahead:
                views.append(buf)
                if not late:
                    early.append(buf)
        io.need(*early)
        targets = {}
        for kind, at, index in ways:
            if kind == "copy":
                views.append(bufs[index])
                targets[id(bufs[index])] = (bufs[index], results[at])
            else:
                views.append(results[at])
                if kind == "both":
                    targets[id(results[at])] = (results[at], results[at + 1])

        def send(*sent):
            for ref in sent:
                io.out(*targets.pop(id(ref)))

        io.send = send
        body(io, *views, *own)
        for buf, ref in targets.values():
            io.out(buf, ref)
        for copies in io.waiting.values():
            for copy in copies:
                copy.wait()
        for copy in io.open:
            copy.wait()

    def bytes_of(shape, dtype):
        size = 1
        for n in shape:
            size *= n
        return size * jnp.dtype(dtype).itemsize

    moved = sum(a.size * a.dtype.itemsize for a in operands) + sum(
        bytes_of(s.shape, s.dtype) for s in shapes
    )
    held = sum(bytes_of(*item) for item in buffers) + sum(bytes_of(s.shape, s.dtype) for s in scratch)
    limit = held + (12 << 20)
    if room is not None:
        near = sum(a.size * a.dtype.itemsize for a, spec in zip(operands, specs) if spec is vmem)
        near += sum(bytes_of(s.shape, s.dtype) for s, spec in zip(shapes, out_specs) if spec is vmem)
        limit = max(limit, ((VMEM_MIB - room) << 20) - near)
    return pl.pallas_call(
        kernel,
        out_shape=shapes,
        in_specs=specs,
        out_specs=out_specs,
        scratch_shapes=[*(pltpu.VMEM(*item) for item in buffers), *scratch, sems],
        compiler_params=pltpu.CompilerParams(vmem_limit_bytes=limit),
        cost_estimate=pl.CostEstimate(flops=flops, bytes_accessed=0, transcendentals=0),
    )(*operands)


def dot(a, b):
    return lax.dot_general(a, b, (((1,), (0,)), ((), ())), preferred_element_type=F32)


def dot_nt(a, b):
    return lax.dot_general(a, b, (((1,), (1,)), ((), ())), preferred_element_type=F32)


def dot_tn(a, b):
    return lax.dot_general(a, b, (((0,), (0,)), ((), ())), preferred_element_type=F32)


def exact_dot(a, b, product):
    high = a.astype(BF16)
    low = (a - high.astype(F32)).astype(BF16)
    return product(high, b) + product(low, b)


def sigmoid(v):
    return 0.5 + 0.5 * jnp.tanh(0.5 * v)


def slope_of(v):
    sigma = sigmoid(v)
    return sigma * (1.0 + v * (1.0 - sigma))


def counts_of(z, n_r, which):
    return [n_r[which * z.micro + m] for m in range(z.micro)]


def norm_rows(total, counted, micro):
    rows = []
    for m in range(micro):
        centre = total[2 * m : 2 * m + 1] / counted[m]
        square = total[2 * m + 1 : 2 * m + 2] / counted[m]
        rows.append((centre, lax.rsqrt(square - centre * centre + epsilon)))
    return rows


def fold_sums(first, second):
    return jnp.sum(first, axis=0, keepdims=True), jnp.sum(second, axis=0, keepdims=True)


def gain_rows(total, micro):
    gain = sum(total[2 * m + 1 : 2 * m + 2] for m in range(micro))
    bias = sum(total[2 * m : 2 * m + 1] for m in range(micro))
    return jnp.concatenate([gain, bias], axis=0)


def to_all(z, rows, s_r):
    for k, row in enumerate(rows):
        s_r[k : k + 1, :] = row


def place_patches(values, row_taps, col_taps, out_ref, base, lane, ch, group):
    size = values.shape[0]
    q = lax.broadcasted_iota(jnp.int32, values.shape, 0) % 8
    for col, cs in col_taps:
        if cs == -1:
            turned = jnp.where(q == 0, 0.0, pltpu.roll(values, 1, 0))
        elif cs == 1:
            turned = jnp.where(q == 7, 0.0, pltpu.roll(values, size - 1, 0))
        else:
            turned = values
        turned = turned.astype(BF16)
        gap = jnp.zeros((group, values.shape[1]), BF16)
        for row, rs in row_taps:
            at = (3 * row + col) * ch + lane
            lanes = slice(at, at + values.shape[1])
            if rs == 0:
                out_ref[base : base + size, lanes] = turned
            elif rs == -1:
                out_ref[base : base + group, lanes] = gap
                out_ref[base + group : base + size, lanes] = turned[: size - group]
            else:
                out_ref[base : base + size - group, lanes] = turned[group:]
                out_ref[base + size - group : base + size, lanes] = gap


class Sizes:
    def __init__(self, images, mid, out, hid, devices):
        self.micro = images.shape[0]
        self.held = images.shape[2] // 2
        self.side = images.shape[3]
        self.half = self.side // 2
        self.cin = images.shape[4]
        self.mid, self.out, self.hid, self.devices = mid, out, hid, devices
        self.group = self.held * self.half
        self.map = self.half * self.group
        self.coarse = self.micro * self.map
        self.fine = 4 * self.coarse
        self.maps = self.micro * self.held


def enter_kernel(z, place, images, other, perm, w_one, w_side, mask, ahead):
    def body(io, place_r, mine_r, other_r, perm_r, w1_r, ws_r, mask_r, planes_r, c1_r, p1_r, s1_r, ss_r):
        core = place_r[0]
        rows = z.map // 2
        for k, ref in ((0, mine_r), (1, other_r)):
            half = core if k == 0 else 1 - core
            io.need(ref)
            for m in range(z.micro):
                turned = dot(perm_r[...], ref[m].reshape(2 * z.map, z.cin)).astype(BF16)
                for p in range(4):
                    at = pl.multiple_of((p * z.micro + m) * z.map + half * rows, rows)
                    planes_r[pl.ds(at, rows), :] = turned[p * rows : (p + 1) * rows]
        io.send(planes_r)
        io.need(w1_r)
        for m in range(z.micro):
            one = [None, None]
            for p in range(4):
                at = (p * z.micro + m) * z.map
                c = dot(planes_r[at : at + z.map, :], w1_r[...])
                c1_r[at : at + z.map, :] = c
                live = c * mask_r[m * z.map : (m + 1) * z.map, 0:1]
                a, b = fold_sums(live, live * c)
                one = [a, b] if p == 0 else [one[0] + a, one[1] + b]
            s1_r[2 * m : 2 * m + 1, :] = one[0]
            s1_r[2 * m + 1 : 2 * m + 2, :] = one[1]
        io.send(c1_r)
        io.need(ws_r)

        @pl.loop(0, z.out // 512)
        def _(j):
            lanes = pl.ds(pl.multiple_of(j * 512, 512), 512)
            p = dot(planes_r[: z.coarse, :], ws_r[:, lanes]).astype(BF16)
            p1_r[:, lanes] = p
            p = p.astype(F32)
            for m in range(z.micro):
                part = p[m * z.map : (m + 1) * z.map]
                live = part * mask_r[m * z.map : (m + 1) * z.map, 0:1]
                a, b = fold_sums(live, live * part)
                ss_r[2 * m : 2 * m + 1, lanes] = a
                ss_r[2 * m + 1 : 2 * m + 2, lanes] = b

    return run(
        body,
        [
            ((z.fine, z.cin), BF16),
            Both(((z.fine, z.mid), F32)),
            ((z.coarse, z.out), BF16),
            Near(((2 * z.micro, z.mid), F32)),
            ((2 * z.micro, z.out), F32),
        ],
        (place, images, other, perm, w_one, w_side, mask),
        room=ROOM,
        ahead=ahead,
        flops=2 * z.fine * z.cin * z.mid,
    )


def taps_kernel(z, place, sums, counted, vec, conv, weight, mask, strided, ahead):
    planes = 4 if strided else 1
    nt = weight.shape[0]

    def body(io, place_r, sums_r, n_r, vec_r, c_r, w_r, mask_r, patch_r, out_r, t_r, s_r):
        total = sums_r[...]
        t_r[...] = total
        io.send(t_r)
        norms = norm_rows(total, counts_of(z, n_r, 0 if strided else 1), z.micro)
        for m in range(z.micro):
            centre, inverse = norms[m]
            scale = inverse * vec_r[0:1]
            offset = vec_r[1:2] - centre * scale
            live = mask_r[m * z.map : (m + 1) * z.map, 0:1]
            for p in range(planes):
                at = (p * z.micro + m) * z.map
                for lane in range(0, z.mid, LANES):
                    lanes = slice(lane, lane + LANES)
                    v = (c_r[at : at + z.map, lanes] * scale[:, lanes] + offset[:, lanes]) * live
                    v = v * sigmoid(v)
                    rows = READS[p // 2] if strided else ALL_TAPS
                    cols = READS[p % 2] if strided else ALL_TAPS
                    place_patches(v, rows, cols, patch_r, m * z.map, lane, z.mid, z.group)
        io.send(patch_r)
        io.need(w_r)
        c = dot(patch_r[...], w_r[...])
        out_r[...] = c
        io.send(out_r)
        for m in range(z.micro):
            part = c[m * z.map : (m + 1) * z.map]
            live = part * mask_r[m * z.map : (m + 1) * z.map, 0:1]
            a, b = fold_sums(live, live * part)
            s_r[2 * m : 2 * m + 1, :] = a
            s_r[2 * m + 1 : 2 * m + 2, :] = b

    return run(
        body,
        [
            ((z.coarse, nt), BF16),
            Both(((z.coarse, z.mid), F32)),
            ((2 * z.micro, z.mid), F32),
            Near(((2 * z.micro, z.mid), F32)),
        ],
        (place, Near(sums), counted, vec, conv, weight, mask),
        room=ROOM,
        ahead=ahead,
        flops=2 * z.coarse * nt * z.mid,
    )


def expand_kernel(z, place, sums, counted, vec, conv, weight, mask, side, ahead):
    height = 2 * z.micro

    def body(io, place_r, sums_r, n_r, vec_r, c_r, w_r, mask_r, *refs):
        if side is not None:
            refs[-1][height : 2 * height, :] = refs[0][...]
            refs = refs[1:]
        act_r, out_r, t_r, s_r = refs
        total = sums_r[...]
        t_r[...] = total
        io.send(t_r)
        norms = norm_rows(total, counts_of(z, n_r, 1), z.micro)
        for m in range(z.micro):
            rows = slice(m * z.map, (m + 1) * z.map)
            centre, inverse = norms[m]
            scale = inverse * vec_r[0:1]
            offset = vec_r[1:2] - centre * scale
            v = (c_r[rows, :] * scale + offset) * mask_r[rows, 0:1]
            act_r[rows, :] = (v * sigmoid(v)).astype(BF16)
        io.send(act_r)
        io.need(w_r)

        @pl.loop(0, z.out // 512)
        def _(j):
            lanes = pl.ds(pl.multiple_of(j * 512, 512), 512)
            p = dot(act_r[...], w_r[:, lanes]).astype(BF16)
            out_r[:, lanes] = p
            p = p.astype(F32)
            for m in range(z.micro):
                part = p[m * z.map : (m + 1) * z.map]
                live = part * mask_r[m * z.map : (m + 1) * z.map, 0:1]
                a, b = fold_sums(live, live * part)
                s_r[2 * m : 2 * m + 1, lanes] = a
                s_r[2 * m + 1 : 2 * m + 2, lanes] = b

    extra = () if side is None else (side,)
    return run(
        body,
        [
            ((z.coarse, z.mid), BF16),
            Both(((z.coarse, z.out), BF16)),
            ((2 * z.micro, z.mid), F32),
            Near(((height * (1 if side is None else 2), z.out), F32)),
        ],
        (place, Near(sums), counted, vec, conv, weight, mask, *extra),
        room=ROOM,
        ahead=ahead,
        flops=2 * z.coarse * z.out * z.mid,
    )


def by_map(z, v):
    return v.reshape(z.half, z.held, z.half, v.shape[-1])


def map_sums(z, v):
    return jnp.sum(jnp.sum(by_map(z, v), axis=0), axis=1)


def spread(z, rows):
    return jnp.broadcast_to(
        rows[None, :, None, :], (z.half, z.held, z.half, rows.shape[-1])
    ).reshape(z.map, rows.shape[-1])


def norms_at(z, total_r, n_r, m, lanes, first=0):
    counted = n_r[z.micro + m]
    at = first + 2 * m
    centre = total_r[at : at + 1, lanes] / counted
    square = total_r[at + 1 : at + 2, lanes] / counted
    return centre, lax.rsqrt(square - centre * centre + epsilon)


def gate_rows(pooled, squeeze_r, sq_bias, excite_r, ex_bias):
    inner = exact_dot(pooled, squeeze_r[...], dot) + sq_bias
    hidden = inner * sigmoid(inner)
    gate = sigmoid(exact_dot(hidden, excite_r[...], dot) + ex_bias)
    return inner, hidden, gate


def gate_back(dgate, gate, inner, squeeze_r, excite_r, pix):
    dl = dgate * gate * (1.0 - gate)
    dz = exact_dot(dl, excite_r[...], dot_nt) * slope_of(inner)
    du = exact_dot(dz, squeeze_r[...], dot_nt) / pix
    return dl, dz, du


def bias_sums(z, dl, dz, s_r, first):
    s_r[first : first + 1, :] = jnp.sum(dl, axis=0, keepdims=True)
    s_r[first + 1 : first + 2, :] = jnp.zeros((1, z.out), F32)
    s_r[first + 1 : first + 2, : z.hid] = jnp.sum(dz, axis=0, keepdims=True)


def middle_kernel(z, place, sums, counted, vectors, pix, e1, p1, squeeze, sq_bias, excite, w, mask, ahead):
    side = 2 * z.micro

    def body(
        io, place_r, t_r, n_r, vec_r, pix_r, e_r, p_r, sq_r, sqb_r, ex_r, w_r, mask_r,
        mid_r, c_r, gate_r, pool_r, inner_r, hid_r, total_r, s_r,
    ):
        io.out(t_r, total_r)

        @pl.loop(0, z.out // LANES, unroll=4)
        def _(j):
            lanes = pl.ds(pl.multiple_of(j * LANES, LANES), LANES)
            for m in range(z.micro):
                rows = slice(m * z.map, (m + 1) * z.map)
                centre, inverse = norms_at(z, t_r, n_r, m, lanes)
                scale = inverse * vec_r[0:1, lanes]
                offset = vec_r[1:2, lanes] - centre * scale
                v = (e_r[rows, lanes].astype(F32) * scale + offset) * mask_r[rows, 0:1]
                at = slice(m * z.held, (m + 1) * z.held)
                pool_r[at, lanes] = map_sums(z, v) / pix_r[at, 0:1]

        io.need(sq_r, ex_r)
        inner, hidden, gate = gate_rows(pool_r[...], sq_r, sqb_r[0:1], ex_r, vec_r[6:7])
        gate_r[...] = gate
        inner_r[...] = inner
        hid_r[...] = hidden
        io.send(gate_r, inner_r, hid_r, pool_r)
        io.need(p_r)

        @pl.loop(0, z.out // LANES, unroll=4)
        def _(j):
            lanes = pl.ds(pl.multiple_of(j * LANES, LANES), LANES)
            for m in range(z.micro):
                rows = slice(m * z.map, (m + 1) * z.map)
                centre, inverse = norms_at(z, t_r, n_r, m, lanes)
                scale = inverse * vec_r[0:1, lanes]
                offset = vec_r[1:2, lanes] - centre * scale
                v = e_r[rows, lanes].astype(F32) * scale + offset
                centre, inverse = norms_at(z, t_r, n_r, m, lanes, side)
                scale = inverse * vec_r[2:3, lanes]
                offset = vec_r[3:4, lanes] - centre * scale
                o = v * spread(z, gate_r[m * z.held : (m + 1) * z.held, lanes])
                o = (o + (p_r[rows, lanes].astype(F32) * scale + offset)) * mask_r[rows, 0:1]
                mid_r[rows, lanes] = (o * sigmoid(o)).astype(BF16)

        io.send(mid_r)
        io.need(w_r)
        c = dot(mid_r[...], w_r[...])
        c_r[...] = c
        io.send(c_r)
        for m in range(z.micro):
            part = c[m * z.map : (m + 1) * z.map]
            live = part * mask_r[m * z.map : (m + 1) * z.map, 0:1]
            a, b = fold_sums(live, live * part)
            s_r[2 * m : 2 * m + 1, :] = a
            s_r[2 * m + 1 : 2 * m + 2, :] = b

    return run(
        body,
        [
            ((z.coarse, z.out), BF16),
            Both(((z.coarse, z.mid), F32)),
            ((z.maps, z.out), F32),
            ((z.maps, z.out), F32),
            ((z.maps, z.hid), F32),
            ((z.maps, z.hid), F32),
            Raw((2 * side, z.out), F32),
            Near(((2 * z.micro, z.mid), F32)),
        ],
        (place, Near(sums), counted, vectors, pix, e1, p1, squeeze, sq_bias, excite, w, mask),
        room=ROOM,
        ahead=ahead,
        spare=1,
        flops=2 * z.coarse * z.out * z.mid,
    )


def output_kernel(z, place, sums, counted, vectors, pix, e2, middle, up, squeeze, sq_bias, excite, mask, final, ahead):
    span = z.out // 2

    def body(
        io, place_r, t_r, n_r, vec_r, pix_r, e_r, mid_r, up_r, sq_r, sqb_r, ex_r, mask_r,
        final_r, away_r, do_r, h_r, pool_r, hid_r, dl_r, dz_r, s_r, out_r, gate_r, du_r,
    ):
        core = place_r[0]

        @pl.loop(0, z.out // LANES, unroll=4)
        def _(j):
            lanes = pl.ds(pl.multiple_of(j * LANES, LANES), LANES)
            for m in range(z.micro):
                rows = slice(m * z.map, (m + 1) * z.map)
                centre, inverse = norms_at(z, t_r, n_r, m, lanes)
                scale = inverse * vec_r[4:5, lanes]
                offset = vec_r[5:6, lanes] - centre * scale
                v = (e_r[rows, lanes].astype(F32) * scale + offset) * mask_r[rows, 0:1]
                at = slice(m * z.held, (m + 1) * z.held)
                pool_r[at, lanes] = map_sums(z, v) / pix_r[at, 0:1]

        io.need(sq_r, ex_r)
        inner, hidden, gate = gate_rows(pool_r[...], sq_r, sqb_r[1:2], ex_r, vec_r[7:8])
        gate_r[...] = gate
        hid_r[...] = hidden
        io.send(pool_r, hid_r)
        io.need(mid_r, up_r)

        @pl.loop(0, z.out // LANES, unroll=4)
        def _(j):
            lanes = pl.ds(pl.multiple_of(j * LANES, LANES), LANES)
            for m in range(z.micro):
                rows = slice(m * z.map, (m + 1) * z.map)
                at = slice(m * z.held, (m + 1) * z.held)
                centre, inverse = norms_at(z, t_r, n_r, m, lanes)
                scale = inverse * vec_r[4:5, lanes]
                offset = vec_r[5:6, lanes] - centre * scale
                v = (e_r[rows, lanes].astype(F32) * scale + offset) * mask_r[rows, 0:1]
                o = v * spread(z, gate_r[at, lanes]) + mid_r[rows, lanes].astype(F32)
                sigma = sigmoid(o)
                out_r[m, :, :, :, lanes] = by_map(z, o * sigma).astype(BF16)
                up = up_r[m, :, :, :, lanes].astype(F32).reshape(z.map, LANES)
                do = up * (sigma * (1.0 + o * (1.0 - sigma)))
                do_r[rows, lanes] = do
                dl_r[at, lanes] = map_sums(z, do * v)

        io.out(
            half_of(out_r, 4, core, span), final_r.at[:, :, pl.ds(core * z.held, z.held)]
        )
        io.out(half_of(out_r, 4, 1 - core, span), away_r)
        io.send(do_r)
        dl, dz, du = gate_back(dl_r[...], gate_r[...], inner, sq_r, ex_r, pix_r[:, 0:1])
        dl_r[...] = dl
        dz_r[...] = dz
        du_r[...] = du
        io.send(dl_r, dz_r)
        bias_sums(z, dl, dz, s_r, 2 * z.micro)

        @pl.loop(0, z.out // LANES, unroll=4)
        def _(j):
            lanes = pl.ds(pl.multiple_of(j * LANES, LANES), LANES)
            for m in range(z.micro):
                rows = slice(m * z.map, (m + 1) * z.map)
                at = slice(m * z.held, (m + 1) * z.held)
                centre, inverse = norms_at(z, t_r, n_r, m, lanes)
                k = (e_r[rows, lanes].astype(F32) - centre) * inverse
                h = do_r[rows, lanes] * spread(z, gate_r[at, lanes]) + spread(z, du_r[at, lanes])
                h = h * mask_r[rows, 0:1]
                h_r[rows, lanes] = h
                a, b = fold_sums(h, h * k)
                s_r[2 * m : 2 * m + 1, lanes] = a
                s_r[2 * m + 1 : 2 * m + 2, lanes] = b

    maps = (z.micro, z.half, z.held, z.half)
    return run(
        body,
        [
            Raw(final, BF16),
            Raw(maps + (span,), BF16),
            ((z.coarse, z.out), F32),
            Near(((z.coarse, z.out), F32)),
            ((z.maps, z.out), F32),
            ((z.maps, z.hid), F32),
            ((z.maps, z.out), F32),
            ((z.maps, z.hid), F32),
            Near(((2 * z.micro + 2, z.out), F32)),
        ],
        (place, Near(sums), counted, vectors, pix, e2, middle, up, squeeze, sq_bias, excite, mask),
        room=ROOM,
        ahead=ahead,
        scratch=[
            pltpu.VMEM(maps + (z.out,), BF16),
            pltpu.VMEM((z.maps, z.out), F32),
            pltpu.VMEM((z.maps, z.out), F32),
        ],
        spare=2,
    )


def wide_back(z, n_r, m, lanes, total_r, back_r, first, gain, e, h):
    centre, inverse = norms_at(z, total_r, n_r, m, lanes, first)
    k = (e - centre) * inverse
    at = first + 2 * m
    mean = back_r[at : at + 1, lanes] / n_r[z.micro + m]
    slope = back_r[at + 1 : at + 2, lanes] / n_r[z.micro + m]
    return (h - (mean + k * slope)) * (gain * inverse)


def unexpand_kernel(z, place, back, total, counted, vectors, row, e, h, w, total_n, vec_n, conv, mask, ahead):
    def body(
        io, place_r, b_r, t_r, n_r, vec_r, e_r, h_r, w_r, tn_r, vn_r, c_r, mask_r,
        de_r, live_r, s_r,
    ):
        @pl.loop(0, z.out // LANES, unroll=4)
        def _(j):
            lanes = pl.ds(pl.multiple_of(j * LANES, LANES), LANES)
            for m in range(z.micro):
                rows = slice(m * z.map, (m + 1) * z.map)
                h = h_r[rows, lanes]
                e = e_r[rows, lanes].astype(F32)
                d = wide_back(z, n_r, m, lanes, t_r, b_r, 0, vec_r[row : row + 1, lanes], e, h)
                de_r[rows, lanes] = (d * mask_r[rows, 0:1]).astype(BF16)

        io.send(de_r)
        io.need(w_r)
        da = dot_nt(de_r[...], w_r[...])
        norms = norm_rows(tn_r[...], counts_of(z, n_r, 1), z.micro)
        sums = []
        for m in range(z.micro):
            rows = slice(m * z.map, (m + 1) * z.map)
            centre, inverse = norms[m]
            k = (c_r[rows, :] - centre) * inverse
            v = (k * vn_r[0:1] + vn_r[1:2]) * mask_r[rows, 0:1]
            h = da[rows] * slope_of(v) * mask_r[rows, 0:1]
            live_r[rows, :] = h
            sums += fold_sums(h, h * k)
        to_all(z, sums, s_r)

    return run(
        body,
        [
            ((z.coarse, z.out), BF16),
            Near(((z.coarse, z.mid), F32)),
            Near(((2 * z.micro, z.mid), F32)),
        ],
        (place, Near(back), total, counted, vectors, e, h, w, total_n, vec_n, conv, mask),
        ahead=ahead,
        flops=2 * z.coarse * z.out * z.mid,
    )


def narrow_back(m, norms, back, counted, gain, conv, live, mask):
    centre, inverse = norms[m]
    k = (conv - centre) * inverse
    mean = back[2 * m : 2 * m + 1] / counted[m]
    slope = back[2 * m + 1 : 2 * m + 2] / counted[m]
    return (live - (mean + k * slope)) * (gain * inverse) * mask


def untap_kernel(z, place, back, total, counted, vec, conv, live, w, total_n, vec_n, conv_n, mask, strided, ahead):
    planes = 4 if strided else 1

    def body(io, place_r, b_r, t_r, n_r, vec_r, c_r, h_r, w_r, tn_r, vn_r, cn_r, mask_r, dc_r, live_r, g_r, s_r, tap_r):
        counted = counts_of(z, n_r, 1)
        back = b_r[...]
        g_r[...] = gain_rows(back, z.micro)
        io.send(g_r)
        norms = norm_rows(t_r[...], counted, z.micro)
        taps = ((0, 0), (1, 1)) if strided else ((0, 1), (1, 0), (2, -1))
        for m in range(z.micro):
            rows = slice(m * z.map, (m + 1) * z.map)
            d = narrow_back(
                m, norms, back, counted, vec_r[0:1], c_r[rows, :], h_r[rows, :], mask_r[rows, 0:1]
            )
            dc_r[rows, :] = d.astype(BF16)
            for lane in range(0, z.mid, LANES):
                place_patches(
                    d[:, lane : lane + LANES], taps, taps, tap_r, m * z.map, lane, z.mid, z.group
                )
        io.send(dc_r)
        norms = norm_rows(tn_r[...], counts_of(z, n_r, 0 if strided else 1), z.micro)
        acc = [[None, None] for _ in range(z.micro)]
        io.need(w_r, cn_r)
        for p in range(planes):
            da = None
            if strided:
                terms = [
                    (3 * i + j, 3 * rs + cs)
                    for i, rs in PLANE_TAPS[p // 2]
                    for j, cs in PLANE_TAPS[p % 2]
                ]
            else:
                terms = [(t, t) for t in range(9)]
            for t, slot in terms:
                part = dot_nt(
                    tap_r[:, slot * z.mid : (slot + 1) * z.mid], w_r[t * z.mid : (t + 1) * z.mid, :]
                )
                da = part if da is None else da + part
            for m in range(z.micro):
                rows = slice(m * z.map, (m + 1) * z.map)
                at = (p * z.micro + m) * z.map
                centre, inverse = norms[m]
                k = (cn_r[at : at + z.map, :] - centre) * inverse
                v = (k * vn_r[0:1] + vn_r[1:2]) * mask_r[rows, 0:1]
                h = da[rows] * slope_of(v) * mask_r[rows, 0:1]
                live_r[at : at + z.map, :] = h
                a, b = fold_sums(h, h * k)
                acc[m] = [a, b] if p == 0 else [acc[m][0] + a, acc[m][1] + b]
        to_all(z, [row for pair in acc for row in pair], s_r)

    return run(
        body,
        [
            ((z.coarse, z.mid), BF16),
            Near(((planes * z.coarse, z.mid), F32)),
            ((2, z.mid), F32),
            Near(((2 * z.micro, z.mid), F32)),
        ],
        (place, Near(back), total, counted, vec, conv, live, w, total_n, vec_n, conv_n, mask),
        ahead=ahead,
        scratch=[pltpu.VMEM((z.coarse, 9 * z.mid), BF16)],
        flops=2 * z.coarse * 9 * z.mid * z.mid,
    )


def unreduce_kernel(
    z, place, back, total, counted, vec, conv, live, w, do2, total_w, vectors, gate, inner, e1, p1, squeeze, excite, pix, mask, ahead
):
    side = 2 * z.micro

    def body(
        io, place_r, b_r, t_r, n_r, vec_r, c_r, h_r, w_r, do2_r, tw_r, vw_r, gate_r, in_r, e_r, p_r, sq_r, ex_r, pix_r, mask_r,
        dc_r, do_r, wide_r, g_r, dl_r, dz_r, s_r, du_r,
    ):
        counted = counts_of(z, n_r, 1)
        back = b_r[...]
        g_r[...] = gain_rows(back, z.micro)
        norms = norm_rows(t_r[...], counted, z.micro)
        for m in range(z.micro):
            rows = slice(m * z.map, (m + 1) * z.map)
            d = narrow_back(
                m, norms, back, counted, vec_r[0:1], c_r[rows, :], h_r[rows, :], mask_r[rows, 0:1]
            )
            dc_r[rows, :] = d.astype(BF16)
        io.send(g_r, dc_r)
        io.need(w_r, do2_r, e_r, p_r)

        @pl.loop(0, z.out // 256)
        def _(j):
            wide_lanes = pl.ds(pl.multiple_of(j * 256, 256), 256)
            dm = dot_nt(dc_r[...], w_r[wide_lanes, :])
            for i in range(2):
                lanes = pl.ds(pl.multiple_of(j * 256 + i * LANES, LANES), LANES)
                for m in range(z.micro):
                    rows = slice(m * z.map, (m + 1) * z.map)
                    at = slice(m * z.held, (m + 1) * z.held)
                    live = mask_r[rows, 0:1]
                    centre, inverse = norms_at(z, tw_r, n_r, m, lanes)
                    k = (e_r[rows, lanes].astype(F32) - centre) * inverse
                    q = (k * vw_r[0:1, lanes] + vw_r[1:2, lanes]) * live
                    centre, inverse = norms_at(z, tw_r, n_r, m, lanes, side)
                    kp = (p_r[rows, lanes].astype(F32) - centre) * inverse
                    t = (kp * vw_r[2:3, lanes] + vw_r[3:4, lanes]) * live
                    o = q * spread(z, gate_r[at, lanes]) + t
                    d = (dm[rows, i * LANES : (i + 1) * LANES] + do2_r[rows, lanes]) * slope_of(o)
                    do_r[rows, lanes] = d
                    dl_r[at, lanes] = map_sums(z, d * q)
                    d = d * live
                    a, b = fold_sums(d, d * kp)
                    s_r[side + 2 * m : side + 2 * m + 1, lanes] = a
                    s_r[side + 2 * m + 1 : side + 2 * m + 2, lanes] = b

        io.send(do_r)
        io.need(sq_r, ex_r)
        dl, dz, du = gate_back(dl_r[...], gate_r[...], in_r[...], sq_r, ex_r, pix_r[:, 0:1])
        dl_r[...] = dl
        dz_r[...] = dz
        du_r[...] = du
        io.send(dl_r, dz_r)
        bias_sums(z, dl, dz, s_r, 2 * side)

        @pl.loop(0, z.out // LANES, unroll=4)
        def _(j):
            lanes = pl.ds(pl.multiple_of(j * LANES, LANES), LANES)
            for m in range(z.micro):
                rows = slice(m * z.map, (m + 1) * z.map)
                at = slice(m * z.held, (m + 1) * z.held)
                centre, inverse = norms_at(z, tw_r, n_r, m, lanes)
                k = (e_r[rows, lanes].astype(F32) - centre) * inverse
                h = do_r[rows, lanes] * spread(z, gate_r[at, lanes]) + spread(z, du_r[at, lanes])
                h = h * mask_r[rows, 0:1]
                wide_r[rows, lanes] = h
                a, b = fold_sums(h, h * k)
                s_r[2 * m : 2 * m + 1, lanes] = a
                s_r[2 * m + 1 : 2 * m + 2, lanes] = b

    return run(
        body,
        [
            ((z.coarse, z.mid), BF16),
            ((z.coarse, z.out), F32),
            Near(((z.coarse, z.out), F32)),
            ((2, z.mid), F32),
            ((z.maps, z.out), F32),
            ((z.maps, z.hid), F32),
            Near(((2 * side + 2, z.out), F32)),
        ],
        (
            place, Near(back), total, counted, vec, conv, live, w, do2, total_w, vectors, gate, inner,
            e1, p1, squeeze, excite, pix, mask,
        ),
        scratch=[pltpu.VMEM((z.maps, z.out), F32)],
        ahead=ahead,
        flops=2 * z.coarse * z.out * z.mid,
    )


def side_kernel(z, place, back, total, counted, vectors, p1, do, mask):
    def body(io, place_r, b_r, t_r, n_r, vec_r, p_r, do_r, mask_r, dp_r):
        @pl.loop(0, z.out // LANES, unroll=4)
        def _(j):
            lanes = pl.ds(pl.multiple_of(j * LANES, LANES), LANES)
            for m in range(z.micro):
                rows = slice(m * z.map, (m + 1) * z.map)
                p = p_r[rows, lanes].astype(F32)
                h = do_r[rows, lanes]
                d = wide_back(z, n_r, m, lanes, t_r, b_r, 2 * z.micro, vec_r[2:3, lanes], p, h)
                dp_r[rows, lanes] = (d * mask_r[rows, 0:1]).astype(BF16)

    return run(
        body,
        [((z.coarse, z.out), BF16)],
        (place, back, total, counted, vectors, p1, do, mask),
    )[0]


def leave_kernel(z, place, back, total, counted, vec, conv, live, w_one, dp, w_side, perm, mask, final):
    block = 2 * z.map
    maps = (z.half, z.held, z.side)

    def body(
        io, place_r, b_r, t_r, n_r, vec_r, c_r, h_r, w_r, dp_r, ws_r, perm_r, mask_r,
        dc_r, final_r, away_r, g_r, keep_r, grad_r,
    ):
        core = place_r[0]
        counted = counts_of(z, n_r, 0)
        back = b_r[...]
        g_r[...] = gain_rows(back, z.micro)
        norms = norm_rows(t_r[...], counted, z.micro)
        for m in range(z.micro):
            for p in range(4):
                at = (p * z.micro + m) * z.map
                rows = slice(at, at + z.map)
                d = narrow_back(
                    m, norms, back, counted, vec_r[0:1], c_r[rows, :], h_r[rows, :],
                    mask_r[m * z.map : (m + 1) * z.map, 0:1],
                )
                dc_r[rows, :] = d.astype(BF16)
        io.send(dc_r)
        io.need(w_r, dp_r, ws_r)
        rows = z.map // 2
        for m in range(z.micro):
            side = dot_nt(dp_r[m * z.map : (m + 1) * z.map, :], ws_r[...])
            for half in range(2):
                stacked = jnp.concatenate(
                    [
                        dc_r[(p * z.micro + m) * z.map + half * rows : (p * z.micro + m) * z.map + (half + 1) * rows, :]
                        for p in range(4)
                    ],
                    axis=0,
                )
                ordered = dot_tn(perm_r[...], stacked).astype(BF16)
                grad = dot_nt(ordered, w_r[...])
                for n in range(z.cin // LANES):
                    lanes = slice(n * LANES, (n + 1) * LANES)
                    grad_r[n] = grad[:, lanes]
                    for o in range(z.half // 2):
                        for b in range(z.held):
                            at = 2 * o * z.held * z.side + b * z.side
                            src = half * rows + (o * z.held + b) * z.half
                            spots = pl.ds(at, z.half, stride=2)
                            grad_r[n, spots, :] = grad_r[n, spots, :] + side[src : src + z.half, lanes]

                @pl.when(core == half)
                def _():
                    for n in range(z.cin // LANES):
                        keep_r[m, :, :, :, n * LANES : (n + 1) * LANES] = grad_r[n].reshape(maps + (LANES,))

                @pl.when(core != half)
                def _():
                    for n in range(z.cin // LANES):
                        away_r[m, :, n * LANES : (n + 1) * LANES] = grad_r[n].astype(BF16)

            io.out(keep_r.at[m], final_r.at[m, :, pl.ds(core * z.held, z.held)])

    return run(
        body,
        [
            ((z.fine, z.mid), BF16),
            Raw(final, F32),
            ((z.micro, block, z.cin), BF16),
            ((2, z.mid), F32),
        ],
        (place, Near(back), total, counted, vec, conv, live, w_one, dp, w_side, perm, mask),
        scratch=[
            pltpu.VMEM((z.micro,) + maps + (z.cin,), F32),
            pltpu.VMEM((z.cin // LANES, block, LANES), F32),
        ],
        spare=z.micro,
        flops=2 * z.fine * z.cin * z.mid,
    )


def finish_images(z, place, got, final):
    maps = (z.half, z.held, z.side)

    def body(place_r, got_r, _, final_r, in_r, out_r, sems):
        other = 1 - place_r[0]
        loads = [pltpu.make_async_copy(got_r.at[m], in_r.at[m], sems.at[m]) for m in range(z.micro)]
        stores = [
            pltpu.make_async_copy(
                out_r.at[m], final_r.at[m, :, pl.ds(other * z.held, z.held)], sems.at[z.micro + m]
            )
            for m in range(z.micro)
        ]
        for copy in loads:
            copy.start()
        for m in range(z.micro):
            loads[m].wait()
            out_r[m] = in_r[m].astype(F32).reshape(maps + (z.cin,))
            stores[m].start()
        for copy in stores:
            copy.wait()

    any_spec = pl.BlockSpec(memory_space=pl.ANY)
    return pl.pallas_call(
        body,
        out_shape=jax.ShapeDtypeStruct(final.shape, final.dtype),
        in_specs=[pl.BlockSpec(memory_space=pltpu.SMEM), any_spec, any_spec],
        out_specs=any_spec,
        input_output_aliases={2: 0},
        scratch_shapes=[
            pltpu.VMEM(got.shape, got.dtype),
            pltpu.VMEM((z.micro,) + maps + (z.cin,), F32),
            pltpu.SemaphoreType.DMA((2 * z.micro,)),
        ],
        compiler_params=pltpu.CompilerParams(vmem_limit_bytes=10 << 20),
    )(place, got, final)


def finish_output(z, place, got, final):
    def body(place_r, got_r, _, final_r, buf_r, sems):
        other = 1 - place_r[0]
        copy = pltpu.make_async_copy(got_r, buf_r, sems.at[0])
        copy.start()
        copy.wait()
        copy = pltpu.make_async_copy(buf_r, final_r.at[:, :, pl.ds(other * z.held, z.held)], sems.at[1])
        copy.start()
        copy.wait()

    any_spec = pl.BlockSpec(memory_space=pl.ANY)
    return pl.pallas_call(
        body,
        out_shape=jax.ShapeDtypeStruct(final.shape, final.dtype),
        in_specs=[pl.BlockSpec(memory_space=pltpu.SMEM), any_spec, any_spec],
        out_specs=any_spec,
        input_output_aliases={2: 0},
        scratch_shapes=[pltpu.VMEM(got.shape, got.dtype), pltpu.SemaphoreType.DMA((2,))],
        compiler_params=pltpu.CompilerParams(vmem_limit_bytes=6 << 20),
    )(place, got, final)


def gradient_kernel(z, place, size, jobs, args):
    starts, at = [], 0
    for kind, i, j in jobs:
        starts.append(at)
        at += args[i].shape[1] * args[j].shape[1] // (2 * size * 512)
    height = at

    def body(io, place_r, *refs):
        out_r = refs[-1]
        refs = refs[:-1]
        core, me = place_r[0], place_r[1]

        def put(c, b, first, length, values):
            p = b ^ me
            p = p // 4 * 4 + p % 2 * 2 + p // 2 % 2 if c else p
            out_r[c ^ core, p, first : first + length, :] = values

        for (kind, i, j), start in zip(jobs, starts):
            lhs, rhs = refs[i], refs[j]
            io.need(lhs, rhs)
            k, n = lhs.shape[1], rhs.shape[1]
            if kind == "flat":
                per = k // (2 * size)
                for r in range(0, k, 512):
                    for c in range(0, n, 512):
                        d = dot_tn(lhs[: rhs.shape[0], r : r + 512], rhs[:, c : c + 512]).astype(BF16)
                        at = r
                        while at < r + 512:
                            chunk, inside = divmod(at, per)
                            length = min(per - inside, r + 512 - at)
                            first = start + (c // 512) * per + inside
                            put(chunk % 2, chunk // 2, first, length, d[at - r : at - r + length])
                            at += length
            elif kind == "rows" and n == 512:
                per = k // (2 * size)
                for r in range(0, k, 512):
                    d = dot_tn(lhs[:, r : r + 512], rhs[...]).astype(BF16)
                    for at in range(r, r + 512, per):
                        c, b = divmod(at // per, size)
                        put(c, b, start, per, d[at - r : at - r + per])
            elif kind == "rows":
                per = k // (2 * size)
                d = dot_tn(lhs[...].astype(BF16), rhs[...].astype(BF16)).astype(BF16)
                parts = 512 // n
                unit = per // parts
                for at in range(0, k, per):
                    c, b = divmod(at // per, size)
                    rows = [d[at + q * unit : at + (q + 1) * unit] for q in range(parts)]
                    put(c, b, start, unit, jnp.concatenate(rows, axis=1))
            else:
                d = dot_tn(lhs[...].astype(BF16), rhs[...].astype(BF16)).astype(BF16)
                across = n // 1024
                per = k * across // size
                for c in range(2):
                    for b in range(size):
                        r, lane = divmod(b, across)
                        first = c * (n // 2) + lane * 512
                        put(c, b, start, per, d[r * per : (r + 1) * per, first : first + 512])
    return body, height, starts


def gradients(z, place, size, jobs, args):
    body, height, starts = gradient_kernel(z, place, size, jobs, args)

    def outer(io, place_r, *refs):
        ins, (keep_r, send_r, both_r) = refs[:-3], refs[-3:]
        body(io, place_r, *ins, both_r)
        io.out(both_r.at[1], send_r)
        io.out(both_r.at[0], keep_r)

    shape = (size, height, 512)
    keep, send = run(
        outer,
        [Near((shape, BF16))] * 2,
        (place, *(Late(a) for a in args)),
        scratch=[pltpu.VMEM((2,) + shape, BF16)],
        spare=2,
    )
    return keep, send, starts


def part_kernel(sources, spans):
    count = sources[0][0].shape[0]
    outs = []
    for _, length, bit in spans:
        if bit:
            outs += [Near(((count // 2, length, 512), BF16))] * 2
        else:
            outs += [Near(((length, 512), BF16))] * count

    def body(io, *refs):
        ins, results = refs[: 2 * len(sources)], list(refs[2 * len(sources) :])
        pairs, at = [], 0
        for k in range(len(sources)):
            kept, come = ins[2 * k], ins[2 * k + 1]
            io.need(kept, come)
            pairs.append((at, at + kept.shape[1], kept, come))
            at += kept.shape[1]

        def pieces(first, length):
            for low, high, kept, come in pairs:
                start, stop = max(first, low), min(first + length, high)
                if start < stop:
                    yield start - first, slice(start - low, stop - low), kept, come

        for first, length, bit in spans:
            if not bit:
                for p in range(count):
                    ref = results.pop(0)
                    for to, rows, kept, come in pieces(first, length):
                        total = kept[p, rows].astype(F32) + come[p, rows].astype(F32)
                        ref[to : to + rows.stop - rows.start, :] = total.astype(BF16)
                continue
            kept_r, sent_r = results.pop(0), results.pop(0)
            for which, ref in ((1, sent_r), (0, kept_r)):
                for p in range(count):
                    if (p // bit) % 2 == which:
                        at = p // (2 * bit) * bit + p % bit
                        for to, rows, kept, come in pieces(first, length):
                            size = rows.stop - rows.start
                            total = kept[p, rows].astype(F32) + come[p, rows].astype(F32)
                            ref[at, to : to + size, :] = total.astype(BF16)

    return run(body, outs, [Near(a) for pair in sources for a in pair])


def second_step(kept, come, narrow):
    count, height = kept.shape[0] // 2, kept.shape[1]
    rows = narrow[0].shape[0]

    def body(io, a, b, *refs):
        *blocks, kept_r, sent_r = refs
        for p in range(count):
            total = a[2 * p + 1].astype(F32) + b[2 * p + 1].astype(F32)
            sent_r[p, :height, :] = total.astype(BF16)
            sent_r[p, height:, :] = blocks[p][...]
        for p in range(count):
            kept_r[p] = (a[2 * p].astype(F32) + b[2 * p].astype(F32)).astype(BF16)

    outs = [Near(((count, height, 512), BF16)), Near(((count, height + rows, 512), BF16))]
    return run(body, outs, [Near(a) for a in (kept, come, *narrow)])


def third_step(kept, come, narrow):
    count, height = kept.shape[0], kept.shape[1]
    rows = narrow[0].shape[0]

    def body(io, a, b, *refs):
        blocks, outs, part_r = refs[:count], refs[count : 2 * count], refs[2 * count]
        for p in reversed(range(count)):
            total = a[p].astype(F32) + b[p, :height].astype(F32)
            outs[p][...] = total.astype(BF16)
        for p in range(count):
            part_r[p] = blocks[p][...]
            part_r[count + p] = b[p, height:]

    outs = [Near(((height, 512), BF16))] * count + [Near(((2 * count, rows, 512), BF16))]
    return run(body, outs, [Near(a) for a in (kept, come, *narrow)])


def total_kernel(blocks, grads=None):
    shape = blocks[0].shape

    def body(io, *refs):
        ins, outs = refs[: len(blocks)], refs[len(blocks) :]
        if grads is None:
            outs[0][...] = tree_sum([ref[...].astype(F32) for ref in ins])
            return
        first = 0
        for out_r, (rows, width) in zip(outs, grads):
            height = rows * 512 // width
            for part in range(width // 512):
                at = first + part * height
                total = tree_sum([ref[at : at + height, :].astype(F32) for ref in ins])
                for k in range(512 // LANES):
                    spots = pl.ds(part * (512 // LANES) + k, height, stride=width // LANES)
                    out_r[spots, :] = total[:, k * LANES : (k + 1) * LANES]
            first += rows

    if grads is None:
        return run(body, [(shape, F32)], [Near(b) for b in blocks])[0]
    outs = [((rows * 512 // LANES, LANES), F32) for rows, _ in grads]
    return [flat.reshape(-1) for flat in run(body, outs, [Near(b) for b in blocks])]


def crossed(block, first, second):
    count = 2 * lax.axis_size("batch")
    route = [(i, (i // 2 ^ (second if i % 2 else first)) * 2 + i % 2) for i in range(count)]
    return lax.ppermute(block, ("batch", "rows"), route)


class Halving:
    def __init__(self, blocks):
        self.height = sum(keep.shape[1] for keep, _ in blocks)
        self.sources = blocks
        self.step = 0

    def prepare(self, *after):
        (kept, came), *others = self.sources
        bit = 1 if self.step < 2 else 0
        self.kept, *self.sent = part_kernel(
            [(tied(kept, *after), came), *others], ((0, self.height, bit),)
        )
        return self.sent[0]

    def send(self, *after):
        sent = [tied(s, *after) for s in self.sent]
        if self.step == 2:
            came = [swapped(s, "batch", 4 * (k + 1)) for k, s in enumerate(sent)]
            self.blocks = [self.kept] + came
        else:
            came = [crossed(sent[0], self.step + 1, 2 - self.step)]
            self.sources = [(self.kept, came[0])]
        self.step += 1
        return came

    def finish(self, grads):
        return total_kernel(self.blocks, grads)


def N(array):
    return Near(array)


def tied(value, *others):
    return lax.optimization_barrier((value, *others))[0] if others else value


def gathered_kernel(z, place, size, blocks, starts):
    across = z.out // 1024
    unit = z.out // 2 // size
    parts = 512 // z.hid
    tall = unit // parts
    wide = z.hid * across // size
    height = blocks[0].shape[1]

    def body(io, place_r, near_r, far_r, red_r, sqb_r, exb_r, sqa_r, exa_r, all_r):
        core, me = place_r[0], place_r[1]
        for high, ref in ((0, near_r), (1, far_r)):
            for low in range(2):
                for k in range(size // 4):
                    p = 4 * k + 2 * low + high + core * (high - low)
                    all_r[p] = ref[low * (size // 4) + k]

        def rows(p, first, length):
            return all_r[p, first : first + length].astype(F32)

        for b in range(size):
            p = b ^ me
            red_r[b * unit : (b + 1) * unit, :] = rows(p, starts[0], unit)
            for at, ref in ((starts[1], sqb_r), (starts[3], sqa_r)):
                block = rows(p, at, tall)
                for q in range(parts):
                    ref[b * unit + q * tall : b * unit + (q + 1) * tall, :] = block[:, q * z.hid : (q + 1) * z.hid]
            r, lane = divmod(b, across)
            for at, ref in ((starts[2], exb_r), (starts[4], exa_r)):
                ref[r * wide : (r + 1) * wide, lane * 512 : (lane + 1) * 512] = rows(p, at, wide)

    half = z.out // 2
    return run(
        body,
        [
            ((half, z.mid), F32),
            ((half, z.hid), F32),
            ((z.hid, half), F32),
            ((half, z.hid), F32),
            ((z.hid, half), F32),
        ],
        (place, *(Near(b) for b in blocks)),
        scratch=[pltpu.VMEM((size, height, 512), BF16)],
    )


def weight_dot(inputs, grads):
    return lax.dot_general(inputs, grads, (((0,), (0,)), ((), ())), preferred_element_type=F32)


def folded(grad):
    size = lax.axis_size("batch")
    rows, width = grad.shape
    grad = grad.astype(BF16).reshape(size, 2, rows // (2 * size), width // 512, 512)
    return jnp.swapaxes(grad, 2, 3).reshape(size, 2, -1, 512)


def unfolded(block, width):
    count = width // 512
    rows = block.shape[0] // count
    return jnp.swapaxes(block.reshape(count, rows, 512), 0, 1).reshape(-1)


def tree_sum(terms):
    while len(terms) > 1:
        terms = [a + b for a, b in zip(terms[::2], terms[1::2])] + terms[len(terms) // 2 * 2 :]
    return terms[0]


def wide_sum(parts, first=(), second=()):
    parts = parts + swapped(parts, "rows", 1)
    bits = bits_of(lax.axis_size("batch"))
    partial = parts
    for at in range(0, len(bits), 2):
        parts = tied(parts, *(first if at == 0 else second if at == 2 else ()))
        pair = bits[at : at + 2]
        masks = [pair[0], pair[1], pair[0] + pair[1]] if len(pair) == 2 else pair
        parts = tree_sum([parts] + [swapped(parts, "batch", mask) for mask in masks])
        partial = parts if at == 0 else partial
    return parts, partial


def plain_gradients(jobs, size):
    blocks, starts, at = [], [], 0
    for kind, lhs, rhs in jobs:
        grad = weight_dot(lhs[: rhs.shape[0]].astype(BF16), rhs.astype(BF16))
        k, n = grad.shape
        if kind == "flat":
            block = core_sum(folded(grad), 1)
        elif kind == "rows" and n == 512:
            block = core_sum(grad.astype(BF16).reshape(2, size, -1, 512), 0)
        elif kind == "rows":
            parts = 512 // n
            block = grad.astype(BF16).reshape(2, size, parts, -1, n)
            block = core_sum(jnp.swapaxes(block, 2, 3).reshape(2, size, -1, 512), 0)
        else:
            across = n // 1024
            block = grad.astype(BF16).reshape(size // across, -1, 2, across, 512)
            block = core_sum(block.transpose(2, 0, 3, 1, 4).reshape(2, size, -1, 512), 0)
        starts.append(at)
        at += block.shape[1]
        blocks.append(block)
    return halved(jnp.concatenate(blocks, axis=1), two_orders), starts


def per_device(
    images,
    crop_sizes,
    reduce_a,
    reduce_gain_a,
    reduce_bias_a,
    spatial_a,
    spatial_gain_a,
    spatial_bias_a,
    expand_a,
    expand_gain_a,
    expand_bias_a,
    project_a,
    project_gain_a,
    project_bias_a,
    squeeze_a,
    squeeze_bias_a,
    excite_a,
    excite_bias_a,
    reduce_b,
    reduce_gain_b,
    reduce_bias_b,
    spatial_b,
    spatial_gain_b,
    spatial_bias_b,
    expand_b,
    expand_gain_b,
    expand_bias_b,
    squeeze_b,
    squeeze_bias_b,
    excite_b,
    excite_bias_b,
    cotangent,
):
    mid = reduce_a.shape[1]
    out = expand_a.shape[1]
    hid = squeeze_a.shape[1]
    size = lax.axis_size("batch")
    z = Sizes(images, mid, out, hid, size * lax.axis_size("rows"))
    micro, held, side, half = z.micro, z.held, z.side, z.half
    core = lax.axis_index("rows")
    me = lax.axis_index("batch")
    place = jnp.stack([core, me]).astype(jnp.int32)

    away = lax.dynamic_slice_in_dim(images, (1 - core) * held, held, axis=2)
    other = swapped(away, "rows", 1)
    vectors = jnp.stack(
        [
            expand_gain_a,
            expand_bias_a,
            project_gain_a,
            project_bias_a,
            expand_gain_b,
            expand_bias_b,
            excite_bias_a,
            excite_bias_b,
        ]
    )

    def pair(own, axis):
        return Pair(own, swapped(own, "rows", 1), axis)

    vectors = pair(vectors, 1)
    pair_sq_a, pair_sq_b = pair(squeeze_a, 0), pair(squeeze_b, 0)
    pair_ex_a, pair_ex_b = pair(excite_a, 1), pair(excite_b, 1)
    pair_red = pair(reduce_b, 0)
    sq_biases = jnp.stack([squeeze_bias_a, squeeze_bias_b])
    vec_one = jnp.stack([reduce_gain_a, reduce_bias_a])
    vec_two = jnp.stack([spatial_gain_a, spatial_bias_a])
    vec_four = jnp.stack([reduce_gain_b, reduce_bias_b])
    vec_five = jnp.stack([spatial_gain_b, spatial_bias_b])

    half_all = crop_sizes // 2
    counted = jnp.stack(
        [jnp.sum(crop_sizes * crop_sizes, axis=1), jnp.sum(half_all * half_all, axis=1)]
    ).astype(F32).reshape(-1)
    halves = lax.dynamic_slice_in_dim(half_all, (me * 2 + core) * held, held, axis=1)
    pix = jnp.broadcast_to((halves * halves).astype(F32).reshape(-1, 1), (z.maps, LANES))
    spots = jnp.arange(half, dtype=jnp.int32)
    limits = halves[:, None, :, None]
    inside = (spots[None, :, None, None] < limits) & (spots[None, None, None, :] < limits)
    mask = jnp.broadcast_to(inside.astype(F32).reshape(z.coarse, 1), (z.coarse, LANES))

    block = 2 * z.map
    spot = jnp.arange(block, dtype=jnp.int32)
    row_pair, rest = spot // (2 * z.group), spot % (2 * z.group)
    row_odd, spot_b, column = spot // (held * side) % 2, spot % (held * side) // side, spot % side
    row_pair = spot // (2 * held * side)
    target = ((row_odd * 2 + column % 2) * (half // 2) + row_pair) * z.group
    target = target + spot_b * half + column // 2
    perm = (target[None, :] == jnp.arange(block, dtype=jnp.int32)[:, None]).astype(BF16)

    other, perm, mask, pix, counted, sq_biases, vec_one, vec_two, vec_four, vec_five, vectors.own = (
        lax.optimization_barrier(
            (other, perm, mask, pix, counted, sq_biases, vec_one, vec_two, vec_four, vec_five, vectors.own)
        )
    )
    vectors.other = swapped(vectors.own, "rows", 1)

    first_one, first_side, first_perm, first_mask, first_images = run(
        lambda io, place_r: None, [], (place,), ahead=(reduce_a, project_a, perm, mask, Part(images, 2)), room=ROOM
    )
    planes, c1_near, c1, p1, s1, s_side, *got = enter_kernel(
        z, place, N(first_images), N(other), N(first_perm), N(first_one), N(first_side), N(first_mask),
        (vec_one, spatial_a, mask),
    )
    vec_near, w_near, mask_near = map(N, got)
    patches_one, c2_near, c2, t1, s2, *got = taps_kernel(
        z, place, wide_sum(s1)[0], counted, vec_near, N(c1_near), w_near, mask_near, True,
        (vec_two, expand_a, mask, s_side, Away(cotangent, 2)),
    )
    vec_near, w_near, mask_near, side_near = map(N, got[:4])
    up = Join(cotangent, 2, swapped(got[4], "rows", 1), 4)
    active_two, e1_near, e1, t2, s3, *got = expand_kernel(
        z, place, wide_sum(s2)[0], counted, vec_near, N(c2_near), w_near, mask_near, side_near,
        (vectors, pix, p1, pair_sq_a, sq_biases, pair_ex_a, pair_red, mask),
    )
    vectors_near, pix_near, p1_near, sq_near, sqb_near, ex_near, w_near, mask_near = map(N, got)
    sums_three, _ = wide_sum(s3)
    middle, c4_near, c4, gate_one, pool_one, inner_one, hidden_one, total_three, s4, *got = middle_kernel(
        z, place, sums_three, counted, vectors_near, pix_near, N(e1_near), p1_near, sq_near, sqb_near, ex_near,
        w_near, mask_near, (vec_four, spatial_b, mask),
    )
    vec_near, w_near, mask_near = map(N, got)
    patches_four, c5_near, c5, t4, s5, *got = taps_kernel(
        z, place, wide_sum(s4)[0], counted, vec_near, N(c4_near), w_near, mask_near, False,
        (vec_five, expand_b, mask),
    )
    vec_near, w_near, mask_near = map(N, got)
    active_five, e2_near, e2, t5, s6, *got = expand_kernel(
        z, place, wide_sum(s5)[0], counted, vec_near, N(c5_near), w_near, mask_near, None,
        (vectors, pix, middle, up, pair_sq_b, sq_biases, pair_ex_b, mask),
    )
    vectors_near, pix_near, mid_near, up_near, sq_near, sqb_near, ex_near, mask_near = map(N, got)
    sums_six, _ = wide_sum(s6)
    final = (micro, half, 2 * held, half, out // 2)
    block_out, block_away, do2, h_near, pool_two, hidden_two, dl_two, dz_two, b6, *got = output_kernel(
        z, place, sums_six, counted, vectors_near, pix_near, N(e2_near), mid_near, up_near,
        sq_near, sqb_near, ex_near, mask_near, final,
        (N(sums_six), vectors, e2, expand_b, t5, vec_five, c5, mask),
    )
    total_near, vectors_near, e_near, w_near, tn_near, vn_near, cn_near, mask_near = map(N, got)

    whole_tiles = mid * 9 // (2 * size) % 16 == 0

    def made(jobs):
        if not whole_tiles:
            return None
        args, spec = [], []
        for kind, lhs, rhs in jobs:
            spec.append((kind, len(args), len(args) + 1))
            args += [lhs, rhs]
        keep, send, _ = gradients(z, place, size, spec, args)
        return keep, send

    def steps(make):
        return list(make()) if whole_tiles else []

    def exchanged(blocks, *after):
        keep, send = blocks
        return keep, swapped(tied(send, *after), "rows", 1)

    back_six, _ = wide_sum(b6)
    de2, live_near, b5, *got = unexpand_kernel(
        z, place, back_six, total_near, counted, vectors_near, 4, e_near, N(h_near), w_near,
        tn_near, vn_near, cn_near, mask_near, (t5, vec_five, c5, spatial_b, t4, vec_four, c4, mask),
    )
    t_near, v_near, c_near, w_near, tn_near, vn_near, cn_near, mask_near = map(N, got)
    jobs_e = (("flat", active_five, de2),)
    made_e = made(jobs_e)
    block_out = finish_output(z, place, swapped(block_away, "rows", 1), block_out)
    back_five, _ = wide_sum(b5, (), [block_out, *steps(lambda: [made_e[0]])])
    dc5, live_near, g5, b4, *got = untap_kernel(
        z, place, back_five, t_near, counted, v_near, c_near, N(live_near), w_near,
        tn_near, vn_near, cn_near, mask_near, False,
        (t4, vec_four, c4, pair_red, do2, total_three, vectors, gate_one, inner_one, e1, p1, pair_sq_a, pair_ex_a, pix, mask),
    )
    t_near, v_near, c_near, w_near, *rest_near = map(N, got)
    jobs_s = (("flat", patches_four, dc5),)
    made_s = made(jobs_s)
    if whole_tiles:
        sum_e = Halving([exchanged(made_e, back_five)])
        b4 = tied(b4, sum_e.sources[0][1])
    back_four, _ = wide_sum(b4, (), steps(lambda: [made_s[0], sum_e.prepare()]))
    came = steps(lambda: sum_e.send(back_four))
    dc4, do1, h_near, g4, dl_one, dz_one, b3, *got = unreduce_kernel(
        z, place, back_four, t_near, counted, v_near, c_near, N(live_near), w_near, *rest_near,
        (total_three, vectors, e1, expand_a, t2, vec_two, c2, mask),
    )
    total_near, vectors_near, e_near, w_near, tn_near, vn_near, cn_near, mask_near = map(N, got)
    jobs_n = (
        ("rows", middle, dc4),
        ("rows", pool_two, dz_two),
        ("lanes", hidden_two, dl_two),
        ("rows", pool_one, dz_one),
        ("lanes", hidden_one, dl_one),
    )
    made_n = made(jobs_n)
    if whole_tiles:
        sum_s = Halving([exchanged(made_s, back_four)])
        came += [sum_s.sources[0][1]]
    back_three, _ = wide_sum(
        tied(b3, *came), (), steps(lambda: [made_n[0], sum_s.prepare(), sum_e.prepare()])
    )
    came = steps(lambda: sum_s.send(back_three) + sum_e.send(back_three))
    de1, live_near, b2, *got = unexpand_kernel(
        z, place, back_three, total_near, counted, vectors_near, 0, e_near, N(h_near), w_near,
        tn_near, vn_near, cn_near, mask_near, (t2, vec_two, c2, spatial_a, t1, vec_one, c1, mask),
    )
    t_near, v_near, c_near, w_near, tn_near, vn_near, cn_near, mask_near = map(N, got)
    dp1 = side_kernel(z, place, N(back_three), total_three, counted, vectors, p1, do1, mask)
    jobs_w = (("flat", active_two, de1), ("flat", planes, dp1))
    made_w = made(jobs_w)
    if whole_tiles:
        sum_n = Halving([exchanged(made_n, back_three)])
        came += [made_w[0], sum_n.sources[0][1]]
    back_two, _ = wide_sum(
        tied(b2, dp1, *came), (), steps(lambda: [sum_n.prepare(), sum_s.prepare(), sum_e.prepare()])
    )
    came = steps(lambda: sum_n.send(back_two) + sum_e.send(back_two))
    dc2, live_near, g2, b1, *got = untap_kernel(
        z, place, back_two, t_near, counted, v_near, c_near, N(live_near), w_near,
        tn_near, vn_near, cn_near, mask_near, True,
        (t1, vec_one, c1, reduce_a, dp1, project_a, perm, mask),
    )
    t_near, v_near, c_near, *rest_near = map(N, got)
    jobs_t = (("flat", patches_one, dc2),)
    made_t = made(jobs_t)
    came_w = exchanged(made_w, back_two) if whole_tiles else None
    came += steps(lambda: [made_t[0], came_w[1]])
    back_one, _ = wide_sum(tied(b1, *came), (), steps(lambda: [sum_n.prepare()]))
    came_t = exchanged(made_t, back_one) if whole_tiles else None
    came = steps(lambda: sum_n.send(back_one) + sum_s.send(back_one))
    dc1, images_grad, grad_away, g1 = leave_kernel(
        z, place, back_one, t_near, counted, v_near, c_near, N(live_near), *rest_near,
        (micro, side // 2, 2 * held, side, z.cin),
    )
    jobs_r = (("flat", planes, dc1),)
    made_r = made(jobs_r)

    images_grad = finish_images(z, place, swapped(grad_away, "rows", 1), images_grad)

    if whole_tiles:
        heights = [a.shape[1] * b.shape[1] // (2 * size * 512) for _, a, b in jobs_n]
        at_second = [sum(heights[:k]) for k in range(len(heights) + 1)]
        here = [made_r[0], *came, came_t[1]]
        came_r = exchanged(made_r, *here)
        sum_n.prepare(*here)
        came = sum_n.send()
        sum_w = Halving([came_w, came_t, came_r])
        sum_w.prepare(sum_n.sent[0])
        came += sum_w.send()
        second = total_kernel(sum_n.blocks)
        narrows = second.astype(BF16)
        around = [swapped(narrows, "batch", 4 * k) for k in range(1, size // 4)]
        here = [images_grad, *came, *around]
        narrow = [narrows, *around]
        sum_s.prepare(*here)
        came = sum_s.send()
        (kept, come), = sum_w.sources
        kept, sent = second_step(tied(kept, sum_s.sent[0]), come, narrow)
        come = crossed(sent, 2, 1)
        *blocks, part = third_step(tied(kept, *came), come, narrow)
        sum_w.blocks = blocks[:1] + [
            swapped(block, "batch", 4 * (k + 1)) for k, block in enumerate(blocks[1:])
        ]
        sum_w.step = 3
        every = part, crossed(part, 1, 2)
        narrow_outs = gathered_kernel(z, place, size, every, at_second)
        sum_w.blocks[0] = tied(sum_w.blocks[0], narrow_outs[0])
        def rows_of(grad):
            return grad.size // (2 * size * 512), grad.shape[1]

        out_expand_a, out_project_a, out_spatial_a, out_reduce_a = sum_w.finish(
            [rows_of(grad) for grad in (expand_a, project_a, spatial_a, reduce_a)]
        )
        sum_e.blocks[0] = tied(sum_e.blocks[0], every[1])
        sum_s.blocks[0] = tied(sum_s.blocks[0], every[1])
        (out_expand_b,) = sum_e.finish([rows_of(expand_b)])
        (out_spatial_b,) = sum_s.finish([rows_of(spatial_b)])
        back_six, back_three, g1, g2, g4, g5 = lax.optimization_barrier(
            (back_six, back_three, g1, g2, g4, g5, every[1])
        )[:6]
    else:
        second, at_second = plain_gradients(jobs_n, size)
        at_second = at_second + [second.shape[0]]
        edge_first = expand_b.size // (2 * size * 512)
        edge_rest = expand_a.size // (2 * size * 512)
        edge_third = spatial_a.size // (2 * size * 512)
        first = plain_gradients(jobs_e + jobs_s, size)[0]
        rest = plain_gradients(jobs_w, size)[0]
        third = plain_gradients(jobs_t + jobs_r, size)[0]
        out_expand_b, out_spatial_b = unfolded(first[:edge_first], out), unfolded(first[edge_first:], mid)
        out_expand_a, out_project_a = unfolded(rest[:edge_rest], out), unfolded(rest[edge_rest:], out)
        out_spatial_a, out_reduce_a = unfolded(third[:edge_third], mid), unfolded(third[edge_third:], mid)
    if whole_tiles:
        out_reduce, out_sq_b, out_ex_b, out_sq_a, out_ex_a = narrow_outs
    else:
        every = collected(second.astype(BF16)).astype(F32)

        def tall_of(k):
            block = every[:, at_second[k] : at_second[k + 1]]
            block = block.reshape(size, block.shape[1], 512 // hid, hid)
            return jnp.swapaxes(block, 1, 2).reshape(-1, hid)

        def flat_of(k):
            block = every[:, at_second[k] : at_second[k + 1]]
            across = (out // 2) // 512
            block = block.reshape(size // across, across, -1, 512)
            return jnp.swapaxes(block, 1, 2).reshape(hid, out // 2)

        out_reduce = every[:, : at_second[1]].reshape(-1, mid)
        out_sq_b, out_ex_b, out_sq_a, out_ex_a = tall_of(1), flat_of(2), tall_of(3), flat_of(4)
    span = out // 2

    def own(rows):
        return lax.dynamic_slice_in_dim(rows, core * span, span, axis=rows.ndim - 1)

    def wide_gains(total, first):
        rows = own(total)
        gain = sum(rows[first + 2 * m + 1] for m in range(micro))
        return gain, sum(rows[first + 2 * m] for m in range(micro))

    gain_six, bias_six = wide_gains(back_six, 0)
    gain_three, bias_three = wide_gains(back_three, 0)
    gain_side, bias_side = wide_gains(back_three, 2 * micro)
    return (
        block_out,
        images_grad,
        out_reduce_a,
        g1[0],
        g1[1],
        out_spatial_a,
        g2[0],
        g2[1],
        out_expand_a,
        gain_three,
        bias_three,
        out_project_a,
        gain_side,
        bias_side,
        out_sq_a,
        back_three[4 * micro + 1, :hid],
        out_ex_a,
        own(back_three[4 * micro]),
        out_reduce,
        g4[0],
        g4[1],
        out_spatial_b,
        g5[0],
        g5[1],
        out_expand_b,
        gain_six,
        bias_six,
        out_sq_b,
        back_six[2 * micro + 1, :hid],
        out_ex_b,
        own(back_six[2 * micro]),
    )


def solution(mesh):
    in_specs = (
        P(None, "rows", "batch", None, None),
        P(),
        P(),
        P(),
        P(),
        P(),
        P(),
        P(),
        P(),
        P("rows"),
        P("rows"),
        P(),
        P("rows"),
        P("rows"),
        P("rows", None),
        P(),
        P(None, "rows"),
        P("rows"),
        P("rows", None),
        P(),
        P(),
        P(),
        P(),
        P(),
        P(),
        P("rows"),
        P("rows"),
        P("rows", None),
        P(),
        P(None, "rows"),
        P("rows"),
        P(None, None, "batch", None, "rows"),
    )
    out_specs = (
        P(None, None, "batch", None, "rows"),
        P(None, "rows", "batch", None, None),
        P(("batch", "rows")),
        P(),
        P(),
        P(("batch", "rows")),
        P(),
        P(),
        P(("batch", "rows")),
        P("rows"),
        P("rows"),
        P(("batch", "rows")),
        P("rows"),
        P("rows"),
        P("rows", None),
        P(),
        P(None, "rows"),
        P("rows"),
        P("rows", None),
        P(),
        P(),
        P(("batch", "rows")),
        P(),
        P(),
        P(("batch", "rows")),
        P("rows"),
        P("rows"),
        P("rows", None),
        P(),
        P(None, "rows"),
        P("rows"),
    )
    return jax.shard_map(
        per_device, mesh=mesh, in_specs=in_specs, out_specs=out_specs, check_vma=False
    )
```

```python
import jax
import jax.numpy as jnp
from jax import lax
from jax.experimental import pallas as pl
from jax.experimental.pallas import tpu as pltpu
from jax.sharding import PartitionSpec as P

epsilon = 1e-05
HIGHEST = lax.Precision.HIGHEST
BF16 = jnp.bfloat16
F32 = jnp.float32

PLANE_TAPS = (((1, 0),), ((2, 0), (0, 1)))


def swapped(block, axis, mask):
    route = [(i, i ^ mask) for i in range(lax.axis_size(axis))]
    return lax.ppermute(block, axis, route)


def bits_of(size):
    return [1 << k for k in range(size.bit_length() - 1)]


def all_sum(parts):
    parts = parts + swapped(parts, "rows", 1)
    size = lax.axis_size("batch")
    spread = jnp.broadcast_to(parts[None], (size,) + parts.shape)
    return jnp.sum(lax.all_to_all(spread, "batch", 0, 0, tiled=True), axis=0)


def halved(block, orders):
    size = lax.axis_size("batch")
    place = lax.axis_index("batch")
    bits = bits_of(size)
    count = block.shape[1]
    cut = count // 2 // 16 * 16
    parts = []
    for part, order in zip((block[:, :cut], block[:, cut:]), orders(bits)):
        shape = part.shape[1:]
        left = list(reversed(bits))
        part = part.reshape((2,) * len(bits) + shape)
        for bit in order:
            axis = left.index(bit)
            mine = (place // bit) % 2
            gone = lax.dynamic_index_in_dim(part, 1 - mine, axis, keepdims=False)
            kept = lax.dynamic_index_in_dim(part, mine, axis, keepdims=False)
            total = kept.astype(F32) + swapped(gone, "batch", bit).astype(F32)
            left.pop(axis)
            part = total.astype(BF16) if left else total
        parts.append(part)
    return jnp.concatenate(parts, axis=0)


def two_orders(bits):
    return (bits, bits[1::-1] + bits[2:])


def collected(block):
    place = lax.axis_index("batch")
    block = block[None]
    for bit in bits_of(lax.axis_size("batch")):
        other = swapped(block, "batch", bit)
        upper = (place // bit) % 2 == 1
        block = jnp.concatenate([jnp.where(upper, other, block), jnp.where(upper, block, other)], axis=0)
    return block


def core_sum(block, axis):
    core = lax.axis_index("rows")
    gone = lax.dynamic_index_in_dim(block, 1 - core, axis, keepdims=False)
    kept = lax.dynamic_index_in_dim(block, core, axis, keepdims=False)
    return (kept.astype(F32) + swapped(gone, "rows", 1).astype(F32)).astype(BF16)


def both_cores(block, axis):
    core = lax.axis_index("rows")
    other = swapped(block, "rows", 1)
    first = jnp.where(core == 0, block, other)
    second = jnp.where(core == 0, other, block)
    return jnp.concatenate([first, second], axis=axis)


LANES = 128
VMEM_MIB = 64
ROOM = None
READS = (((1, 0),), ((2, 0), (0, -1)))
ALL_TAPS = ((0, -1), (1, 0), (2, 1))


class Near:
    def __init__(self, array):
        self.array = array
        self.shape = array[0] if isinstance(array, tuple) else array.shape


class Both:
    def __init__(self, array):
        self.array = array


class Late:
    def __init__(self, array):
        self.array = array
        self.shape = array.shape


class Pair:
    def __init__(self, own, other, axis):
        self.own, self.other, self.axis = own, other, axis
        shape = list(own.shape)
        shape[axis] *= 2
        self.shape, self.dtype = tuple(shape), own.dtype


class Part:
    def __init__(self, array, axis):
        self.array, self.axis = array, axis
        shape = list(array.shape)
        shape[axis] //= 2
        self.shape, self.dtype = tuple(shape), array.dtype


class Top:
    def __init__(self, array, rows):
        self.array, self.rows = array, rows
        self.shape, self.dtype = (rows,) + tuple(array.shape[1:]), array.dtype


class Away:
    def __init__(self, array, axis):
        self.array, self.axis = array, axis
        shape = list(array.shape)
        shape[axis] //= 2
        self.shape, self.dtype = tuple(shape), array.dtype


class Join:
    def __init__(self, array, cut, other, axis):
        self.array, self.cut, self.other, self.axis = array, cut, other, axis
        shape = list(other.shape)
        shape[axis] *= 2
        self.shape, self.dtype = tuple(shape), array.dtype


class Raw:
    def __init__(self, shape, dtype):
        self.shape, self.dtype = shape, dtype


def half_of(ref, axis, which, length):
    start = which * length
    if axis >= len(ref.shape) - 2:
        start = pl.multiple_of(start, length)
    return ref.at[(slice(None),) * axis + (pl.ds(start, length),)]


class Copies:
    def __init__(self, sems):
        self.sems, self.used = sems, 0
        self.waiting, self.open = {}, []

    def start(self, source, target):
        copy = pltpu.make_async_copy(source, target, self.sems.at[self.used])
        self.used += 1
        copy.start()
        return copy

    def need(self, *refs):
        for ref in refs:
            for copy in self.waiting.pop(id(ref), ()):
                copy.wait()

    def out(self, source, target):
        self.open.append(self.start(source, target))


def run(body, outs, args, scratch=(), flops=0, spare=0, ahead=(), room=None):
    operands, specs, plans, buffers = [], [], [], []
    far = pl.BlockSpec(memory_space=pltpu.HBM)
    vmem = pl.BlockSpec(memory_space=pltpu.VMEM)
    count, next_up = 0, []

    def plan(arg, late, keep):
        nonlocal count
        if isinstance(arg, Near) and keep is next_up:
            plans.append(("copy", len(operands), (len(keep), 0), late))
            operands.append(arg.array)
            specs.append(vmem)
            keep.append((tuple(arg.shape), arg.array.dtype))
            count += 1
            return
        if isinstance(arg, Near):
            plans.append(("near", len(operands), None, late))
            operands.append(arg.array)
            specs.append(vmem)
            return
        if isinstance(arg, Pair):
            kind, axis, parts = "pair", arg.axis, [arg.own, arg.other]
        elif isinstance(arg, Part):
            kind, axis, parts = "part", arg.axis, [arg.array]
        elif isinstance(arg, Away):
            kind, axis, parts = "away", arg.axis, [arg.array]
        elif isinstance(arg, Top):
            kind, axis, parts = "top", 0, [arg.array]
        elif isinstance(arg, Join):
            kind, axis, parts = "join", (arg.cut, arg.axis), [arg.array, arg.other]
        elif arg.ndim == 1:
            plans.append(("near", len(operands), None, late))
            operands.append(arg)
            specs.append(pl.BlockSpec(memory_space=pltpu.SMEM))
            return
        else:
            kind, axis, parts = "copy", 0, [arg]
        plans.append((kind, len(operands), (len(keep), axis), late))
        operands.extend(parts)
        specs.extend([far] * len(parts))
        keep.append((tuple(arg.shape), arg.dtype))
        count += len(parts)

    for arg in args:
        late = isinstance(arg, Late)
        plan(arg.array if late else arg, late, buffers)
    first_ahead = len(plans)
    for arg in ahead:
        plan(arg, True, next_up)
    shapes, out_specs, ways = [], [], []
    for item in outs:
        if isinstance(item, Raw):
            ways.append(("raw", len(shapes), None))
            shapes.append(jax.ShapeDtypeStruct(item.shape, item.dtype))
            out_specs.append(far)
        elif isinstance(item, Near):
            ways.append(("near", len(shapes), None))
            shapes.append(jax.ShapeDtypeStruct(*item.array))
            out_specs.append(vmem)
        elif isinstance(item, Both):
            ways.append(("both", len(shapes), None))
            shapes += [jax.ShapeDtypeStruct(*item.array)] * 2
            out_specs += [vmem, far]
            count += 1
        else:
            ways.append(("copy", len(shapes), len(buffers)))
            shapes.append(jax.ShapeDtypeStruct(*item))
            out_specs.append(far)
            buffers.append(item)
            count += 1
    first_next = len(shapes)
    for item in next_up:
        shapes.append(jax.ShapeDtypeStruct(*item))
        out_specs.append(vmem)
    sems = pltpu.SemaphoreType.DMA((max(count + spare, 1),))

    def kernel(*refs):
        ins = refs[: len(operands)]
        results = refs[len(operands) : len(operands) + len(shapes)]
        rest = refs[len(operands) + len(shapes) :]
        bufs, own = rest[: len(buffers)], rest[len(buffers) : -1]
        io = Copies(rest[-1])
        views, early = [], []
        for k, (kind, at, spot, late) in enumerate(plans):
            if kind == "near":
                views.append(ins[at])
                continue
            index, axis = spot
            buf = results[first_next + index] if k >= first_ahead else bufs[index]
            if kind == "copy":
                copies = [io.start(ins[at], buf)]
            elif kind == "pair":
                core = ins[0][0]
                length = ins[at].shape[axis]
                copies = [
                    io.start(ins[at], half_of(buf, axis, core, length)),
                    io.start(ins[at + 1], half_of(buf, axis, 1 - core, length)),
                ]
            elif kind == "top":
                copies = [io.start(ins[at].at[pl.ds(0, buf.shape[0])], buf)]
            elif kind == "join":
                core, (cut, axis) = ins[0][0], axis
                mine = half_of(ins[at], cut, core, ins[at + 1].shape[cut])
                length = ins[at + 1].shape[axis]
                copies = [
                    io.start(mine, half_of(buf, axis, core, length)),
                    io.start(ins[at + 1], half_of(buf, axis, 1 - core, length)),
                ]
            else:
                core = ins[0][0] if kind == "part" else 1 - ins[0][0]
                copies = [io.start(half_of(ins[at], axis, core, buf.shape[axis]), buf)]
            io.waiting[id(buf)] = copies
            if k < first_ahead:
                views.append(buf)
                if not late:
                    early.append(buf)
        io.need(*early)
        targets = {}
        for kind, at, index in ways:
            if kind == "copy":
                views.append(bufs[index])
                targets[id(bufs[index])] = (bufs[index], results[at])
            else:
                views.append(results[at])
                if kind == "both":
                    targets[id(results[at])] = (results[at], results[at + 1])

        def send(*sent):
            for ref in sent:
                io.out(*targets.pop(id(ref)))

        io.send = send
        body(io, *views, *own)
        for buf, ref in targets.values():
            io.out(buf, ref)
        for copies in io.waiting.values():
            for copy in copies:
                copy.wait()
        for copy in io.open:
            copy.wait()

    def bytes_of(shape, dtype):
        size = 1
        for n in shape:
            size *= n
        return size * jnp.dtype(dtype).itemsize

    moved = sum(a.size * a.dtype.itemsize for a in operands) + sum(
        bytes_of(s.shape, s.dtype) for s in shapes
    )
    held = sum(bytes_of(*item) for item in buffers) + sum(bytes_of(s.shape, s.dtype) for s in scratch)
    limit = held + (12 << 20)
    if room is not None:
        near = sum(a.size * a.dtype.itemsize for a, spec in zip(operands, specs) if spec is vmem)
        near += sum(bytes_of(s.shape, s.dtype) for s, spec in zip(shapes, out_specs) if spec is vmem)
        limit = max(limit, ((VMEM_MIB - room) << 20) - near)
    return pl.pallas_call(
        kernel,
        out_shape=shapes,
        in_specs=specs,
        out_specs=out_specs,
        scratch_shapes=[*(pltpu.VMEM(*item) for item in buffers), *scratch, sems],
        compiler_params=pltpu.CompilerParams(vmem_limit_bytes=limit),
        cost_estimate=pl.CostEstimate(flops=flops, bytes_accessed=0, transcendentals=0),
    )(*operands)


def dot(a, b):
    return lax.dot_general(a, b, (((1,), (0,)), ((), ())), preferred_element_type=F32)


def dot_nt(a, b):
    return lax.dot_general(a, b, (((1,), (1,)), ((), ())), preferred_element_type=F32)


def dot_tn(a, b):
    return lax.dot_general(a, b, (((0,), (0,)), ((), ())), preferred_element_type=F32)


def exact_dot(a, b, product):
    high = a.astype(BF16)
    low = (a - high.astype(F32)).astype(BF16)
    return product(high, b) + product(low, b)


def sigmoid(v):
    return 0.5 + 0.5 * jnp.tanh(0.5 * v)


def slope_of(v):
    sigma = sigmoid(v)
    return sigma * (1.0 + v * (1.0 - sigma))


def counts_of(z, n_r, which):
    return [n_r[which * z.micro + m] for m in range(z.micro)]


def norm_rows(total, counted, micro):
    rows = []
    for m in range(micro):
        centre = total[2 * m : 2 * m + 1] / counted[m]
        square = total[2 * m + 1 : 2 * m + 2] / counted[m]
        rows.append((centre, lax.rsqrt(square - centre * centre + epsilon)))
    return rows


def fold_sums(first, second):
    return jnp.sum(first, axis=0, keepdims=True), jnp.sum(second, axis=0, keepdims=True)


def flat_row(row, out_ref):
    for k in range(row.shape[1] // LANES):
        out_ref[k : k + 1, :] = row[:, k * LANES : (k + 1) * LANES]


def flat_of(n):
    return ((n // LANES, LANES), F32)


def gains_out(total, micro, gain_r, bias_r):
    flat_row(sum(total[2 * m + 1 : 2 * m + 2] for m in range(micro)), gain_r)
    flat_row(sum(total[2 * m : 2 * m + 1] for m in range(micro)), bias_r)


def to_all(z, rows, s_r):
    for k, row in enumerate(rows):
        s_r[k : k + 1, :] = row


def place_patches(values, row_taps, col_taps, out_ref, base, lane, ch, group):
    size = values.shape[0]
    q = lax.broadcasted_iota(jnp.int32, values.shape, 0) % 8
    for col, cs in col_taps:
        if cs == -1:
            turned = jnp.where(q == 0, 0.0, pltpu.roll(values, 1, 0))
        elif cs == 1:
            turned = jnp.where(q == 7, 0.0, pltpu.roll(values, size - 1, 0))
        else:
            turned = values
        turned = turned.astype(BF16)
        gap = jnp.zeros((group, values.shape[1]), BF16)
        for row, rs in row_taps:
            at = (3 * row + col) * ch + lane
            lanes = slice(at, at + values.shape[1])
            if rs == 0:
                out_ref[base : base + size, lanes] = turned
            elif rs == -1:
                out_ref[base : base + group, lanes] = gap
                out_ref[base + group : base + size, lanes] = turned[: size - group]
            else:
                out_ref[base : base + size - group, lanes] = turned[group:]
                out_ref[base + size - group : base + size, lanes] = gap


class Sizes:
    def __init__(self, images, mid, out, hid, devices):
        self.micro = images.shape[0]
        self.held = images.shape[2] // 2
        self.side = images.shape[3]
        self.half = self.side // 2
        self.cin = images.shape[4]
        self.mid, self.out, self.hid, self.devices = mid, out, hid, devices
        self.group = self.held * self.half
        self.map = self.half * self.group
        self.coarse = self.micro * self.map
        self.fine = 4 * self.coarse
        self.maps = self.micro * self.held


def enter_kernel(z, place, images, other, perm, w_one, mask, ahead):
    def body(io, place_r, mine_r, other_r, perm_r, w1_r, mask_r, planes_r, c1_r, s1_r):
        core = place_r[0]
        rows = z.map // 2
        for k, ref in ((0, mine_r), (1, other_r)):
            half = core if k == 0 else 1 - core
            io.need(ref)
            for m in range(z.micro):
                turned = dot(perm_r[...], ref[m].reshape(2 * z.map, z.cin)).astype(BF16)
                for p in range(4):
                    at = pl.multiple_of((p * z.micro + m) * z.map + half * rows, rows)
                    planes_r[pl.ds(at, rows), :] = turned[p * rows : (p + 1) * rows]
        io.send(planes_r)
        io.need(w1_r)
        c1_r[...] = dot(planes_r[...], w1_r[...])
        for m in range(z.micro):
            one = [None, None]
            for p in range(4):
                at = (p * z.micro + m) * z.map
                c = c1_r[at : at + z.map, :]
                live = c * mask_r[m * z.map : (m + 1) * z.map, 0:1]
                a, b = fold_sums(live, live * c)
                one = [a, b] if p == 0 else [one[0] + a, one[1] + b]
            s1_r[2 * m : 2 * m + 1, :] = one[0]
            s1_r[2 * m + 1 : 2 * m + 2, :] = one[1]
        io.send(c1_r)

    return run(
        body,
        [
            ((z.fine, z.cin), BF16),
            Both(((z.fine, z.mid), F32)),
            Near(((2 * z.micro, z.mid), F32)),
        ],
        (place, images, other, perm, w_one, mask),
        room=ROOM,
        ahead=ahead,
        flops=2 * z.fine * z.cin * z.mid,
    )


def taps_kernel(z, place, sums, counted, vec, conv, weight, mask, strided, ahead):
    planes = 4 if strided else 1
    nt = weight.shape[0]

    def body(io, place_r, sums_r, n_r, vec_r, c_r, w_r, mask_r, patch_r, out_r, t_r, s_r):
        total = sums_r[...]
        t_r[...] = total
        io.send(t_r)
        norms = norm_rows(total, counts_of(z, n_r, 0 if strided else 1), z.micro)
        for m in range(z.micro):
            centre, inverse = norms[m]
            scale = inverse * vec_r[0:1]
            offset = vec_r[1:2] - centre * scale
            live = mask_r[m * z.map : (m + 1) * z.map, 0:1]
            for p in range(planes):
                at = (p * z.micro + m) * z.map
                for lane in range(0, z.mid, LANES):
                    lanes = slice(lane, lane + LANES)
                    v = (c_r[at : at + z.map, lanes] * scale[:, lanes] + offset[:, lanes]) * live
                    v = v * sigmoid(v)
                    rows = READS[p // 2] if strided else ALL_TAPS
                    cols = READS[p % 2] if strided else ALL_TAPS
                    place_patches(v, rows, cols, patch_r, m * z.map, lane, z.mid, z.group)
        io.send(patch_r)
        io.need(w_r)
        c = dot(patch_r[...], w_r[...])
        out_r[...] = c
        io.send(out_r)
        for m in range(z.micro):
            part = c[m * z.map : (m + 1) * z.map]
            live = part * mask_r[m * z.map : (m + 1) * z.map, 0:1]
            a, b = fold_sums(live, live * part)
            s_r[2 * m : 2 * m + 1, :] = a
            s_r[2 * m + 1 : 2 * m + 2, :] = b

    return run(
        body,
        [
            ((z.coarse, nt), BF16),
            Both(((z.coarse, z.mid), F32)),
            ((2 * z.micro, z.mid), F32),
            Near(((2 * z.micro, z.mid), F32)),
        ],
        (place, Near(sums), counted, vec, conv, weight, mask),
        room=ROOM,
        ahead=ahead,
        flops=2 * z.coarse * nt * z.mid,
    )


def expand_kernel(z, place, sums, counted, vec, conv, weight, mask, side, ahead):
    height = 2 * z.micro

    def body(io, place_r, sums_r, n_r, vec_r, c_r, w_r, mask_r, *refs):
        if side is not None:
            plane_r, ws_r, act_r, out_r, t_r, p1_r, s_r = refs
        else:
            act_r, out_r, t_r, s_r = refs
        total = sums_r[...]
        t_r[...] = total
        io.send(t_r)
        norms = norm_rows(total, counts_of(z, n_r, 1), z.micro)
        for m in range(z.micro):
            rows = slice(m * z.map, (m + 1) * z.map)
            centre, inverse = norms[m]
            scale = inverse * vec_r[0:1]
            offset = vec_r[1:2] - centre * scale
            v = (c_r[rows, :] * scale + offset) * mask_r[rows, 0:1]
            act_r[rows, :] = (v * sigmoid(v)).astype(BF16)
        io.send(act_r)
        io.need(w_r)

        @pl.loop(0, z.out // 512)
        def _(j):
            lanes = pl.ds(pl.multiple_of(j * 512, 512), 512)
            products = [(dot(act_r[...], w_r[:, lanes]), out_r, 0)]
            if side is not None:
                products.append((dot(plane_r[...], ws_r[:, lanes]), p1_r, height))
            for p, ref, first in products:
                p = p.astype(BF16)
                ref[:, lanes] = p
                p = p.astype(F32)
                for m in range(z.micro):
                    part = p[m * z.map : (m + 1) * z.map]
                    live = part * mask_r[m * z.map : (m + 1) * z.map, 0:1]
                    a, b = fold_sums(live, live * part)
                    at = first + 2 * m
                    s_r[at : at + 1, lanes] = a
                    s_r[at + 1 : at + 2, lanes] = b

    extra = () if side is None else side
    wide = [] if side is None else [Both(((z.coarse, z.out), BF16))]
    return run(
        body,
        [
            ((z.coarse, z.mid), BF16),
            Both(((z.coarse, z.out), BF16)),
            ((2 * z.micro, z.mid), F32),
            *wide,
            Near(((height * (1 if side is None else 2), z.out), F32)),
        ],
        (place, Near(sums), counted, vec, conv, weight, mask, *extra),
        room=ROOM,
        ahead=ahead,
        flops=2 * z.coarse * z.out * z.mid,
    )


def by_map(z, v):
    return v.reshape(z.half, z.held, z.half, v.shape[-1])


def map_sums(z, v):
    return jnp.sum(jnp.sum(by_map(z, v), axis=0), axis=1)


def spread(z, rows):
    return jnp.broadcast_to(
        rows[None, :, None, :], (z.half, z.held, z.half, rows.shape[-1])
    ).reshape(z.map, rows.shape[-1])


def norms_at(z, total_r, n_r, m, lanes, first=0):
    counted = n_r[z.micro + m]
    at = first + 2 * m
    centre = total_r[at : at + 1, lanes] / counted
    square = total_r[at + 1 : at + 2, lanes] / counted
    return centre, lax.rsqrt(square - centre * centre + epsilon)


def gate_rows(pooled, squeeze_r, sq_bias, excite_r, ex_bias):
    inner = exact_dot(pooled, squeeze_r[...], dot) + sq_bias
    hidden = inner * sigmoid(inner)
    gate = sigmoid(exact_dot(hidden, excite_r[...], dot) + ex_bias)
    return inner, hidden, gate


def gate_back(dgate, gate, inner, squeeze_r, excite_r, pix):
    dl = dgate * gate * (1.0 - gate)
    dz = exact_dot(dl, excite_r[...], dot_nt) * slope_of(inner)
    du = exact_dot(dz, squeeze_r[...], dot_nt) / pix
    return dl, dz, du


def bias_sums(z, dl, dz, s_r, first):
    s_r[first : first + 1, :] = jnp.sum(dl, axis=0, keepdims=True)
    s_r[first + 1 : first + 2, :] = jnp.zeros((1, z.out), F32)
    s_r[first + 1 : first + 2, : z.hid] = jnp.sum(dz, axis=0, keepdims=True)


def middle_kernel(z, place, sums, counted, vectors, pix, e1, p1, squeeze, sq_bias, excite, w, mask, ahead):
    side = 2 * z.micro

    def body(
        io, place_r, t_r, n_r, vec_r, pix_r, e_r, p_r, sq_r, sqb_r, ex_r, w_r, mask_r,
        mid_r, c_r, gate_r, pool_r, inner_r, hid_r, total_r, s_r,
    ):
        io.out(t_r, total_r)

        @pl.loop(0, z.out // LANES, unroll=4)
        def _(j):
            lanes = pl.ds(pl.multiple_of(j * LANES, LANES), LANES)
            for m in range(z.micro):
                rows = slice(m * z.map, (m + 1) * z.map)
                centre, inverse = norms_at(z, t_r, n_r, m, lanes)
                scale = inverse * vec_r[0:1, lanes]
                offset = vec_r[1:2, lanes] - centre * scale
                v = (e_r[rows, lanes].astype(F32) * scale + offset) * mask_r[rows, 0:1]
                at = slice(m * z.held, (m + 1) * z.held)
                pool_r[at, lanes] = map_sums(z, v) / pix_r[at, 0:1]

        io.need(sq_r, ex_r)
        inner, hidden, gate = gate_rows(pool_r[...], sq_r, sqb_r[0:1], ex_r, vec_r[6:7])
        gate_r[...] = gate
        inner_r[...] = inner
        hid_r[...] = hidden
        io.send(gate_r, inner_r, hid_r, pool_r)
        io.need(p_r)

        @pl.loop(0, z.out // LANES, unroll=4)
        def _(j):
            lanes = pl.ds(pl.multiple_of(j * LANES, LANES), LANES)
            for m in range(z.micro):
                rows = slice(m * z.map, (m + 1) * z.map)
                centre, inverse = norms_at(z, t_r, n_r, m, lanes)
                scale = inverse * vec_r[0:1, lanes]
                offset = vec_r[1:2, lanes] - centre * scale
                v = e_r[rows, lanes].astype(F32) * scale + offset
                centre, inverse = norms_at(z, t_r, n_r, m, lanes, side)
                scale = inverse * vec_r[2:3, lanes]
                offset = vec_r[3:4, lanes] - centre * scale
                o = v * spread(z, gate_r[m * z.held : (m + 1) * z.held, lanes])
                o = (o + (p_r[rows, lanes].astype(F32) * scale + offset)) * mask_r[rows, 0:1]
                mid_r[rows, lanes] = (o * sigmoid(o)).astype(BF16)

        io.send(mid_r)
        io.need(w_r)
        c = dot(mid_r[...], w_r[...])
        c_r[...] = c
        io.send(c_r)
        for m in range(z.micro):
            part = c[m * z.map : (m + 1) * z.map]
            live = part * mask_r[m * z.map : (m + 1) * z.map, 0:1]
            a, b = fold_sums(live, live * part)
            s_r[2 * m : 2 * m + 1, :] = a
            s_r[2 * m + 1 : 2 * m + 2, :] = b

    return run(
        body,
        [
            ((z.coarse, z.out), BF16),
            Both(((z.coarse, z.mid), F32)),
            ((z.maps, z.out), F32),
            ((z.maps, z.out), F32),
            ((z.maps, z.hid), F32),
            ((z.maps, z.hid), F32),
            Raw((2 * side, z.out), F32),
            Near(((2 * z.micro, z.mid), F32)),
        ],
        (place, Near(sums), counted, vectors, pix, e1, p1, squeeze, sq_bias, excite, w, mask),
        room=ROOM,
        ahead=ahead,
        spare=1,
        flops=2 * z.coarse * z.out * z.mid,
    )


def output_kernel(z, place, sums, counted, vectors, pix, e2, middle, up, squeeze, sq_bias, excite, mask, final, ahead):
    span = z.out // 2

    def body(
        io, place_r, t_r, n_r, vec_r, pix_r, e_r, mid_r, up_r, sq_r, sqb_r, ex_r, mask_r,
        final_r, away_r, do_r, h_r, pool_r, hid_r, dl_r, dz_r, s_r, out_r, gate_r, du_r,
    ):
        core = place_r[0]

        @pl.loop(0, z.out // LANES, unroll=4)
        def _(j):
            lanes = pl.ds(pl.multiple_of(j * LANES, LANES), LANES)
            for m in range(z.micro):
                rows = slice(m * z.map, (m + 1) * z.map)
                centre, inverse = norms_at(z, t_r, n_r, m, lanes)
                scale = inverse * vec_r[4:5, lanes]
                offset = vec_r[5:6, lanes] - centre * scale
                v = (e_r[rows, lanes].astype(F32) * scale + offset) * mask_r[rows, 0:1]
                at = slice(m * z.held, (m + 1) * z.held)
                pool_r[at, lanes] = map_sums(z, v) / pix_r[at, 0:1]

        io.need(sq_r, ex_r)
        inner, hidden, gate = gate_rows(pool_r[...], sq_r, sqb_r[1:2], ex_r, vec_r[7:8])
        gate_r[...] = gate
        hid_r[...] = hidden
        io.send(pool_r, hid_r)
        io.need(mid_r, up_r)

        @pl.loop(0, z.out // LANES, unroll=4)
        def _(j):
            lanes = pl.ds(pl.multiple_of(j * LANES, LANES), LANES)
            for m in range(z.micro):
                rows = slice(m * z.map, (m + 1) * z.map)
                at = slice(m * z.held, (m + 1) * z.held)
                centre, inverse = norms_at(z, t_r, n_r, m, lanes)
                scale = inverse * vec_r[4:5, lanes]
                offset = vec_r[5:6, lanes] - centre * scale
                v = (e_r[rows, lanes].astype(F32) * scale + offset) * mask_r[rows, 0:1]
                o = v * spread(z, gate_r[at, lanes]) + mid_r[rows, lanes].astype(F32)
                sigma = sigmoid(o)
                out_r[m, :, :, :, lanes] = by_map(z, o * sigma).astype(BF16)
                up = up_r[m, :, :, :, lanes].astype(F32).reshape(z.map, LANES)
                do = up * (sigma * (1.0 + o * (1.0 - sigma)))
                do_r[rows, lanes] = do
                dl_r[at, lanes] = map_sums(z, do * v)

        io.out(
            half_of(out_r, 4, core, span), final_r.at[:, :, pl.ds(core * z.held, z.held)]
        )
        io.out(half_of(out_r, 4, 1 - core, span), away_r)
        io.send(do_r)
        dl, dz, du = gate_back(dl_r[...], gate_r[...], inner, sq_r, ex_r, pix_r[:, 0:1])
        dl_r[...] = dl
        dz_r[...] = dz
        du_r[...] = du
        io.send(dl_r, dz_r)
        bias_sums(z, dl, dz, s_r, 2 * z.micro)

        @pl.loop(0, z.out // LANES, unroll=4)
        def _(j):
            lanes = pl.ds(pl.multiple_of(j * LANES, LANES), LANES)
            for m in range(z.micro):
                rows = slice(m * z.map, (m + 1) * z.map)
                at = slice(m * z.held, (m + 1) * z.held)
                centre, inverse = norms_at(z, t_r, n_r, m, lanes)
                k = (e_r[rows, lanes].astype(F32) - centre) * inverse
                h = do_r[rows, lanes] * spread(z, gate_r[at, lanes]) + spread(z, du_r[at, lanes])
                h = h * mask_r[rows, 0:1]
                h_r[rows, lanes] = h
                a, b = fold_sums(h, h * k)
                s_r[2 * m : 2 * m + 1, lanes] = a
                s_r[2 * m + 1 : 2 * m + 2, lanes] = b

    maps = (z.micro, z.half, z.held, z.half)
    return run(
        body,
        [
            Raw(final, BF16),
            Raw(maps + (span,), BF16),
            ((z.coarse, z.out), F32),
            Near(((z.coarse, z.out), F32)),
            ((z.maps, z.out), F32),
            ((z.maps, z.hid), F32),
            ((z.maps, z.out), F32),
            ((z.maps, z.hid), F32),
            Near(((2 * z.micro + 2, z.out), F32)),
        ],
        (place, Near(sums), counted, vectors, pix, e2, middle, up, squeeze, sq_bias, excite, mask),
        room=ROOM,
        ahead=ahead,
        scratch=[
            pltpu.VMEM(maps + (z.out,), BF16),
            pltpu.VMEM((z.maps, z.out), F32),
            pltpu.VMEM((z.maps, z.out), F32),
        ],
        spare=2,
    )


def wide_back(z, n_r, m, lanes, total_r, back_r, first, gain, e, h):
    centre, inverse = norms_at(z, total_r, n_r, m, lanes, first)
    k = (e - centre) * inverse
    at = first + 2 * m
    mean = back_r[at : at + 1, lanes] / n_r[z.micro + m]
    slope = back_r[at + 1 : at + 2, lanes] / n_r[z.micro + m]
    return (h - (mean + k * slope)) * (gain * inverse)


def unexpand_kernel(z, place, back, total, counted, vectors, row, e, h, w, total_n, vec_n, conv, mask, ahead):
    span = z.out // 2
    groups = back.shape[0] // (2 * z.micro)

    def body(
        io, place_r, b_r, t_r, n_r, vec_r, e_r, h_r, w_r, tn_r, vn_r, c_r, mask_r,
        de_r, live_r, s_r, *small_r,
    ):
        lanes = pl.ds(pl.multiple_of(place_r[0] * span, span), span)
        own = b_r[:, lanes]
        for g in range(groups):
            gains_out(own[2 * z.micro * g :], z.micro, small_r[2 * g], small_r[2 * g + 1])
        flat_row(own[2 * z.micro * groups : 2 * z.micro * groups + 1], small_r[-2])
        small_r[-1][...] = b_r[2 * z.micro * groups + 1 : 2 * z.micro * groups + 2, : z.hid]
        io.send(*small_r)

        @pl.loop(0, z.out // LANES, unroll=4)
        def _(j):
            lanes = pl.ds(pl.multiple_of(j * LANES, LANES), LANES)
            for m in range(z.micro):
                rows = slice(m * z.map, (m + 1) * z.map)
                h = h_r[rows, lanes]
                e = e_r[rows, lanes].astype(F32)
                d = wide_back(z, n_r, m, lanes, t_r, b_r, 0, vec_r[row : row + 1, lanes], e, h)
                de_r[rows, lanes] = (d * mask_r[rows, 0:1]).astype(BF16)

        io.send(de_r)
        io.need(w_r)
        da = dot_nt(de_r[...], w_r[...])
        norms = norm_rows(tn_r[...], counts_of(z, n_r, 1), z.micro)
        sums = []
        for m in range(z.micro):
            rows = slice(m * z.map, (m + 1) * z.map)
            centre, inverse = norms[m]
            k = (c_r[rows, :] - centre) * inverse
            v = (k * vn_r[0:1] + vn_r[1:2]) * mask_r[rows, 0:1]
            h = da[rows] * slope_of(v) * mask_r[rows, 0:1]
            live_r[rows, :] = h
            sums += fold_sums(h, h * k)
        to_all(z, sums, s_r)

    return run(
        body,
        [
            ((z.coarse, z.out), BF16),
            Near(((z.coarse, z.mid), F32)),
            Near(((2 * z.micro, z.mid), F32)),
            *([flat_of(span)] * (2 * groups + 1)),
            ((1, z.hid), F32),
        ],
        (place, Near(back), total, counted, vectors, e, h, w, total_n, vec_n, conv, mask),
        ahead=ahead,
        flops=2 * z.coarse * z.out * z.mid,
    )


def narrow_back(m, norms, back, counted, gain, conv, live, mask):
    centre, inverse = norms[m]
    k = (conv - centre) * inverse
    mean = back[2 * m : 2 * m + 1] / counted[m]
    slope = back[2 * m + 1 : 2 * m + 2] / counted[m]
    return (live - (mean + k * slope)) * (gain * inverse) * mask


def untap_kernel(z, place, back, total, counted, vec, conv, live, w, total_n, vec_n, conv_n, mask, strided, ahead):
    planes = 4 if strided else 1

    def body(io, place_r, b_r, t_r, n_r, vec_r, c_r, h_r, w_r, tn_r, vn_r, cn_r, mask_r, dc_r, live_r, gain_r, bias_r, s_r, tap_r):
        counted = counts_of(z, n_r, 1)
        back = b_r[...]
        gains_out(back, z.micro, gain_r, bias_r)
        io.send(gain_r, bias_r)
        norms = norm_rows(t_r[...], counted, z.micro)
        taps = ((0, 0), (1, 1)) if strided else ((0, 1), (1, 0), (2, -1))
        for m in range(z.micro):
            rows = slice(m * z.map, (m + 1) * z.map)
            d = narrow_back(
                m, norms, back, counted, vec_r[0:1], c_r[rows, :], h_r[rows, :], mask_r[rows, 0:1]
            )
            dc_r[rows, :] = d.astype(BF16)
            for lane in range(0, z.mid, LANES):
                place_patches(
                    d[:, lane : lane + LANES], taps, taps, tap_r, m * z.map, lane, z.mid, z.group
                )
        io.send(dc_r)
        norms = norm_rows(tn_r[...], counts_of(z, n_r, 0 if strided else 1), z.micro)
        acc = [[None, None] for _ in range(z.micro)]
        io.need(w_r, cn_r)
        for p in range(planes):
            da = None
            if strided:
                terms = [
                    (3 * i + j, 3 * rs + cs)
                    for i, rs in PLANE_TAPS[p // 2]
                    for j, cs in PLANE_TAPS[p % 2]
                ]
            else:
                terms = [(t, t) for t in range(9)]
            for t, slot in terms:
                part = dot_nt(
                    tap_r[:, slot * z.mid : (slot + 1) * z.mid], w_r[t * z.mid : (t + 1) * z.mid, :]
                )
                da = part if da is None else da + part
            for m in range(z.micro):
                rows = slice(m * z.map, (m + 1) * z.map)
                at = (p * z.micro + m) * z.map
                centre, inverse = norms[m]
                k = (cn_r[at : at + z.map, :] - centre) * inverse
                v = (k * vn_r[0:1] + vn_r[1:2]) * mask_r[rows, 0:1]
                h = da[rows] * slope_of(v) * mask_r[rows, 0:1]
                live_r[at : at + z.map, :] = h
                a, b = fold_sums(h, h * k)
                acc[m] = [a, b] if p == 0 else [acc[m][0] + a, acc[m][1] + b]
        to_all(z, [row for pair in acc for row in pair], s_r)

    return run(
        body,
        [
            ((z.coarse, z.mid), BF16),
            Near(((planes * z.coarse, z.mid), F32)),
            flat_of(z.mid),
            flat_of(z.mid),
            Near(((2 * z.micro, z.mid), F32)),
        ],
        (place, Near(back), total, counted, vec, conv, live, w, total_n, vec_n, conv_n, mask),
        ahead=ahead,
        scratch=[pltpu.VMEM((z.coarse, 9 * z.mid), BF16)],
        flops=2 * z.coarse * 9 * z.mid * z.mid,
    )


def unreduce_kernel(
    z, place, back, total, counted, vec, conv, live, w, do2, total_w, vectors, gate, inner, e1, p1, squeeze, excite, pix, mask, ahead
):
    side = 2 * z.micro

    def body(
        io, place_r, b_r, t_r, n_r, vec_r, c_r, h_r, w_r, do2_r, tw_r, vw_r, gate_r, in_r, e_r, p_r, sq_r, ex_r, pix_r, mask_r,
        dc_r, do_r, wide_r, gain_r, bias_r, dl_r, dz_r, s_r, du_r,
    ):
        counted = counts_of(z, n_r, 1)
        back = b_r[...]
        gains_out(back, z.micro, gain_r, bias_r)
        norms = norm_rows(t_r[...], counted, z.micro)
        for m in range(z.micro):
            rows = slice(m * z.map, (m + 1) * z.map)
            d = narrow_back(
                m, norms, back, counted, vec_r[0:1], c_r[rows, :], h_r[rows, :], mask_r[rows, 0:1]
            )
            dc_r[rows, :] = d.astype(BF16)
        io.send(gain_r, bias_r, dc_r)
        io.need(w_r, do2_r, e_r, p_r)

        @pl.loop(0, z.out // 256)
        def _(j):
            wide_lanes = pl.ds(pl.multiple_of(j * 256, 256), 256)
            dm = dot_nt(dc_r[...], w_r[wide_lanes, :])
            for i in range(2):
                lanes = pl.ds(pl.multiple_of(j * 256 + i * LANES, LANES), LANES)
                for m in range(z.micro):
                    rows = slice(m * z.map, (m + 1) * z.map)
                    at = slice(m * z.held, (m + 1) * z.held)
                    live = mask_r[rows, 0:1]
                    centre, inverse = norms_at(z, tw_r, n_r, m, lanes)
                    k = (e_r[rows, lanes].astype(F32) - centre) * inverse
                    q = (k * vw_r[0:1, lanes] + vw_r[1:2, lanes]) * live
                    centre, inverse = norms_at(z, tw_r, n_r, m, lanes, side)
                    kp = (p_r[rows, lanes].astype(F32) - centre) * inverse
                    t = (kp * vw_r[2:3, lanes] + vw_r[3:4, lanes]) * live
                    o = q * spread(z, gate_r[at, lanes]) + t
                    d = (dm[rows, i * LANES : (i + 1) * LANES] + do2_r[rows, lanes]) * slope_of(o)
                    do_r[rows, lanes] = d
                    dl_r[at, lanes] = map_sums(z, d * q)
                    d = d * live
                    a, b = fold_sums(d, d * kp)
                    s_r[side + 2 * m : side + 2 * m + 1, lanes] = a
                    s_r[side + 2 * m + 1 : side + 2 * m + 2, lanes] = b

        io.send(do_r)
        io.need(sq_r, ex_r)
        dl, dz, du = gate_back(dl_r[...], gate_r[...], in_r[...], sq_r, ex_r, pix_r[:, 0:1])
        dl_r[...] = dl
        dz_r[...] = dz
        du_r[...] = du
        io.send(dl_r, dz_r)
        bias_sums(z, dl, dz, s_r, 2 * side)

        @pl.loop(0, z.out // LANES, unroll=4)
        def _(j):
            lanes = pl.ds(pl.multiple_of(j * LANES, LANES), LANES)
            for m in range(z.micro):
                rows = slice(m * z.map, (m + 1) * z.map)
                at = slice(m * z.held, (m + 1) * z.held)
                centre, inverse = norms_at(z, tw_r, n_r, m, lanes)
                k = (e_r[rows, lanes].astype(F32) - centre) * inverse
                h = do_r[rows, lanes] * spread(z, gate_r[at, lanes]) + spread(z, du_r[at, lanes])
                h = h * mask_r[rows, 0:1]
                wide_r[rows, lanes] = h
                a, b = fold_sums(h, h * k)
                s_r[2 * m : 2 * m + 1, lanes] = a
                s_r[2 * m + 1 : 2 * m + 2, lanes] = b

    return run(
        body,
        [
            ((z.coarse, z.mid), BF16),
            ((z.coarse, z.out), F32),
            Near(((z.coarse, z.out), F32)),
            flat_of(z.mid),
            flat_of(z.mid),
            ((z.maps, z.out), F32),
            ((z.maps, z.hid), F32),
            Near(((2 * side + 2, z.out), F32)),
        ],
        (
            place, Near(back), total, counted, vec, conv, live, w, do2, total_w, vectors, gate, inner,
            e1, p1, squeeze, excite, pix, mask,
        ),
        scratch=[pltpu.VMEM((z.maps, z.out), F32)],
        ahead=ahead,
        flops=2 * z.coarse * z.out * z.mid,
    )


def side_kernel(z, place, back, total, counted, vectors, p1, do, mask):
    def body(io, place_r, b_r, t_r, n_r, vec_r, p_r, do_r, mask_r, dp_r):
        @pl.loop(0, z.out // LANES, unroll=4)
        def _(j):
            lanes = pl.ds(pl.multiple_of(j * LANES, LANES), LANES)
            for m in range(z.micro):
                rows = slice(m * z.map, (m + 1) * z.map)
                p = p_r[rows, lanes].astype(F32)
                h = do_r[rows, lanes]
                d = wide_back(z, n_r, m, lanes, t_r, b_r, 2 * z.micro, vec_r[2:3, lanes], p, h)
                dp_r[rows, lanes] = (d * mask_r[rows, 0:1]).astype(BF16)

    return run(
        body,
        [((z.coarse, z.out), BF16)],
        (place, back, total, counted, vectors, p1, do, mask),
    )[0]


def leave_kernel(z, place, back, total, counted, vec, conv, live, w_one, dp, w_side, perm, mask, final):
    block = 2 * z.map
    maps = (z.half, z.held, z.side)

    def body(
        io, place_r, b_r, t_r, n_r, vec_r, c_r, h_r, w_r, dp_r, ws_r, perm_r, mask_r,
        dc_r, final_r, away_r, gain_r, bias_r, keep_r, grad_r,
    ):
        core = place_r[0]
        counted = counts_of(z, n_r, 0)
        back = b_r[...]
        gains_out(back, z.micro, gain_r, bias_r)
        norms = norm_rows(t_r[...], counted, z.micro)
        for m in range(z.micro):
            for p in range(4):
                at = (p * z.micro + m) * z.map
                rows = slice(at, at + z.map)
                d = narrow_back(
                    m, norms, back, counted, vec_r[0:1], c_r[rows, :], h_r[rows, :],
                    mask_r[m * z.map : (m + 1) * z.map, 0:1],
                )
                dc_r[rows, :] = d.astype(BF16)
        io.send(dc_r)
        io.need(w_r, dp_r, ws_r)
        rows = z.map // 2
        sides = dot_nt(dp_r[...], ws_r[...])
        for m in range(z.micro):
            side = sides[m * z.map : (m + 1) * z.map]
            for half in range(2):
                stacked = jnp.concatenate(
                    [
                        dc_r[(p * z.micro + m) * z.map + half * rows : (p * z.micro + m) * z.map + (half + 1) * rows, :]
                        for p in range(4)
                    ],
                    axis=0,
                )
                ordered = dot_tn(perm_r[...], stacked).astype(BF16)
                grad = dot_nt(ordered, w_r[...])
                for n in range(z.cin // LANES):
                    lanes = slice(n * LANES, (n + 1) * LANES)
                    grad_r[n] = grad[:, lanes]
                    for o in range(z.half // 2):
                        for b in range(z.held):
                            at = 2 * o * z.held * z.side + b * z.side
                            src = half * rows + (o * z.held + b) * z.half
                            spots = pl.ds(at, z.half, stride=2)
                            grad_r[n, spots, :] = grad_r[n, spots, :] + side[src : src + z.half, lanes]

                @pl.when(core == half)
                def _():
                    for n in range(z.cin // LANES):
                        keep_r[m, :, :, :, n * LANES : (n + 1) * LANES] = grad_r[n].reshape(maps + (LANES,))

                @pl.when(core != half)
                def _():
                    for n in range(z.cin // LANES):
                        away_r[m, :, n * LANES : (n + 1) * LANES] = grad_r[n].astype(BF16)

            io.out(keep_r.at[m], final_r.at[m, :, pl.ds(core * z.held, z.held)])

    return run(
        body,
        [
            ((z.fine, z.mid), BF16),
            Raw(final, F32),
            ((z.micro, block, z.cin), BF16),
            flat_of(z.mid),
            flat_of(z.mid),
        ],
        (place, Near(back), total, counted, vec, conv, live, w_one, dp, w_side, perm, mask),
        scratch=[
            pltpu.VMEM((z.micro,) + maps + (z.cin,), F32),
            pltpu.VMEM((z.cin // LANES, block, LANES), F32),
        ],
        spare=z.micro,
        flops=2 * z.fine * z.cin * z.mid,
    )


def finish_images(z, place, got, final):
    maps = (z.half, z.held, z.side)

    def body(place_r, got_r, _, final_r, in_r, out_r, sems):
        other = 1 - place_r[0]
        loads = [pltpu.make_async_copy(got_r.at[m], in_r.at[m], sems.at[m]) for m in range(z.micro)]
        stores = [
            pltpu.make_async_copy(
                out_r.at[m], final_r.at[m, :, pl.ds(other * z.held, z.held)], sems.at[z.micro + m]
            )
            for m in range(z.micro)
        ]
        for copy in loads:
            copy.start()
        for m in range(z.micro):
            loads[m].wait()
            out_r[m] = in_r[m].astype(F32).reshape(maps + (z.cin,))
            stores[m].start()
        for copy in stores:
            copy.wait()

    any_spec = pl.BlockSpec(memory_space=pl.ANY)
    return pl.pallas_call(
        body,
        out_shape=jax.ShapeDtypeStruct(final.shape, final.dtype),
        in_specs=[pl.BlockSpec(memory_space=pltpu.SMEM), any_spec, any_spec],
        out_specs=any_spec,
        input_output_aliases={2: 0},
        scratch_shapes=[
            pltpu.VMEM(got.shape, got.dtype),
            pltpu.VMEM((z.micro,) + maps + (z.cin,), F32),
            pltpu.SemaphoreType.DMA((2 * z.micro,)),
        ],
        compiler_params=pltpu.CompilerParams(vmem_limit_bytes=10 << 20),
    )(place, got, final)


def finish_output(z, place, got, final):
    def body(place_r, got_r, _, final_r, buf_r, sems):
        other = 1 - place_r[0]
        copy = pltpu.make_async_copy(got_r, buf_r, sems.at[0])
        copy.start()
        copy.wait()
        copy = pltpu.make_async_copy(buf_r, final_r.at[:, :, pl.ds(other * z.held, z.held)], sems.at[1])
        copy.start()
        copy.wait()

    any_spec = pl.BlockSpec(memory_space=pl.ANY)
    return pl.pallas_call(
        body,
        out_shape=jax.ShapeDtypeStruct(final.shape, final.dtype),
        in_specs=[pl.BlockSpec(memory_space=pltpu.SMEM), any_spec, any_spec],
        out_specs=any_spec,
        input_output_aliases={2: 0},
        scratch_shapes=[pltpu.VMEM(got.shape, got.dtype), pltpu.SemaphoreType.DMA((2,))],
        compiler_params=pltpu.CompilerParams(vmem_limit_bytes=6 << 20),
    )(place, got, final)


def gradient_kernel(z, place, size, jobs, args):
    starts, at = [], 0
    for kind, i, j in jobs:
        starts.append(at)
        at += args[i].shape[1] * args[j].shape[1] // (2 * size * 512)
    height = at

    def body(io, place_r, *refs):
        out_r = refs[-1]
        refs = refs[:-1]
        core, me = place_r[0], place_r[1]

        def put(c, b, first, length, values):
            p = b ^ me
            p = p // 4 * 4 + p % 2 * 2 + p // 2 % 2 if c else p
            out_r[c ^ core, p, first : first + length, :] = values

        for (kind, i, j), start in zip(jobs, starts):
            lhs, rhs = refs[i], refs[j]
            io.need(lhs, rhs)
            k, n = lhs.shape[1], rhs.shape[1]
            if kind == "flat":
                per = k // (2 * size)
                for r in range(0, k, 512):
                    for c in range(0, n, 512):
                        d = dot_tn(lhs[: rhs.shape[0], r : r + 512], rhs[:, c : c + 512]).astype(BF16)
                        at = r
                        while at < r + 512:
                            chunk, inside = divmod(at, per)
                            length = min(per - inside, r + 512 - at)
                            first = start + (c // 512) * per + inside
                            put(chunk % 2, chunk // 2, first, length, d[at - r : at - r + length])
                            at += length
            elif kind == "rows" and n == 512:
                per = k // (2 * size)
                for r in range(0, k, 512):
                    d = dot_tn(lhs[:, r : r + 512], rhs[...]).astype(BF16)
                    for at in range(r, r + 512, per):
                        c, b = divmod(at // per, size)
                        put(c, b, start, per, d[at - r : at - r + per])
            elif kind == "rows":
                per = k // (2 * size)
                d = dot_tn(lhs[...].astype(BF16), rhs[...].astype(BF16)).astype(BF16)
                parts = 512 // n
                unit = per // parts
                for at in range(0, k, per):
                    c, b = divmod(at // per, size)
                    rows = [d[at + q * unit : at + (q + 1) * unit] for q in range(parts)]
                    put(c, b, start, unit, jnp.concatenate(rows, axis=1))
            else:
                d = dot_tn(lhs[...].astype(BF16), rhs[...].astype(BF16)).astype(BF16)
                across = n // 1024
                per = k * across // size
                for c in range(2):
                    for b in range(size):
                        r, lane = divmod(b, across)
                        first = c * (n // 2) + lane * 512
                        put(c, b, start, per, d[r * per : (r + 1) * per, first : first + 512])
    return body, height, starts


def gradients(z, place, size, jobs, args):
    body, height, starts = gradient_kernel(z, place, size, jobs, args)

    def outer(io, place_r, *refs):
        ins, (keep_r, send_r, both_r) = refs[:-3], refs[-3:]
        body(io, place_r, *ins, both_r)
        io.out(both_r.at[1], send_r)
        io.out(both_r.at[0], keep_r)

    shape = (size, height, 512)
    keep, send = run(
        outer,
        [Near((shape, BF16))] * 2,
        (place, *(Late(a) for a in args)),
        scratch=[pltpu.VMEM((2,) + shape, BF16)],
        spare=2,
    )
    return keep, send, starts


def part_kernel(sources, spans):
    count = sources[0][0].shape[0]
    outs = []
    for _, length, bit in spans:
        if bit:
            outs += [Near(((count // 2, length, 512), BF16))] * 2
        else:
            outs += [Near(((length, 512), BF16))] * count

    def body(io, *refs):
        ins, results = refs[: 2 * len(sources)], list(refs[2 * len(sources) :])
        pairs, at = [], 0
        for k in range(len(sources)):
            kept, come = ins[2 * k], ins[2 * k + 1]
            io.need(kept, come)
            pairs.append((at, at + kept.shape[1], kept, come))
            at += kept.shape[1]

        def pieces(first, length):
            for low, high, kept, come in pairs:
                start, stop = max(first, low), min(first + length, high)
                if start < stop:
                    yield start - first, slice(start - low, stop - low), kept, come

        for first, length, bit in spans:
            if not bit:
                for p in range(count):
                    ref = results.pop(0)
                    for to, rows, kept, come in pieces(first, length):
                        total = kept[p, rows].astype(F32) + come[p, rows].astype(F32)
                        ref[to : to + rows.stop - rows.start, :] = total.astype(BF16)
                continue
            kept_r, sent_r = results.pop(0), results.pop(0)
            for which, ref in ((1, sent_r), (0, kept_r)):
                for p in range(count):
                    if (p // bit) % 2 == which:
                        at = p // (2 * bit) * bit + p % bit
                        for to, rows, kept, come in pieces(first, length):
                            size = rows.stop - rows.start
                            total = kept[p, rows].astype(F32) + come[p, rows].astype(F32)
                            ref[at, to : to + size, :] = total.astype(BF16)

    return run(body, outs, [Near(a) for pair in sources for a in pair])


def second_step(kept, come, narrow):
    count, height = kept.shape[0] // 2, kept.shape[1]
    rows = narrow[0].shape[0]

    def body(io, a, b, *refs):
        *blocks, kept_r, sent_r = refs
        for p in range(count):
            total = a[2 * p + 1].astype(F32) + b[2 * p + 1].astype(F32)
            sent_r[p, :height, :] = total.astype(BF16)
            sent_r[p, height:, :] = blocks[p][...]
        for p in range(count):
            kept_r[p] = (a[2 * p].astype(F32) + b[2 * p].astype(F32)).astype(BF16)

    outs = [Near(((count, height, 512), BF16)), Near(((count, height + rows, 512), BF16))]
    return run(body, outs, [Near(a) for a in (kept, come, *narrow)])


def third_step(kept, come, narrow):
    count, height = kept.shape[0], kept.shape[1]
    rows = narrow[0].shape[0]

    def body(io, a, b, *refs):
        blocks, outs, part_r = refs[:count], refs[count : 2 * count], refs[2 * count]
        for p in reversed(range(count)):
            total = a[p].astype(F32) + b[p, :height].astype(F32)
            outs[p][...] = total.astype(BF16)
        for p in range(count):
            part_r[p] = blocks[p][...]
            part_r[count + p] = b[p, height:]

    outs = [Near(((height, 512), BF16))] * count + [Near(((2 * count, rows, 512), BF16))]
    return run(body, outs, [Near(a) for a in (kept, come, *narrow)])


def total_kernel(blocks, grads=None):
    shape = blocks[0].shape

    def body(io, *refs):
        ins, outs = refs[: len(blocks)], refs[len(blocks) :]
        if grads is None:
            outs[0][...] = tree_sum([ref[...].astype(F32) for ref in ins])
            return
        first = 0
        for out_r, (rows, width) in zip(outs, grads):
            height = rows * 512 // width
            for part in range(width // 512):
                at = first + part * height
                total = tree_sum([ref[at : at + height, :].astype(F32) for ref in ins])
                for k in range(512 // LANES):
                    spots = pl.ds(part * (512 // LANES) + k, height, stride=width // LANES)
                    out_r[spots, :] = total[:, k * LANES : (k + 1) * LANES]
            first += rows

    if grads is None:
        return run(body, [(shape, F32)], [Near(b) for b in blocks])[0]
    outs = [((rows * 512 // LANES, LANES), F32) for rows, _ in grads]
    return [flat.reshape(-1) for flat in run(body, outs, [Near(b) for b in blocks])]


def crossed(block, first, second):
    count = 2 * lax.axis_size("batch")
    route = [(i, (i // 2 ^ (second if i % 2 else first)) * 2 + i % 2) for i in range(count)]
    return lax.ppermute(block, ("batch", "rows"), route)


class Halving:
    def __init__(self, blocks):
        self.height = sum(keep.shape[1] for keep, _ in blocks)
        self.sources = blocks
        self.step = 0

    def prepare(self, *after):
        (kept, came), *others = self.sources
        bit = 1 if self.step < 2 else 0
        self.kept, *self.sent = part_kernel(
            [(tied(kept, *after), came), *others], ((0, self.height, bit),)
        )
        return self.sent[0]

    def send(self, *after):
        sent = [tied(s, *after) for s in self.sent]
        if self.step == 2:
            came = [swapped(s, "batch", 4 * (k + 1)) for k, s in enumerate(sent)]
            self.blocks = [self.kept] + came
        else:
            came = [crossed(sent[0], self.step + 1, 2 - self.step)]
            self.sources = [(self.kept, came[0])]
        self.step += 1
        return came

    def finish(self, grads):
        return total_kernel(self.blocks, grads)


def N(array):
    return Near(array)


def tied(value, *others):
    return lax.optimization_barrier((value, *others))[0] if others else value


def gathered_kernel(z, place, size, blocks, starts):
    across = z.out // 1024
    unit = z.out // 2 // size
    parts = 512 // z.hid
    tall = unit // parts
    wide = z.hid * across // size
    height = blocks[0].shape[1]

    def body(io, place_r, near_r, far_r, red_r, sqb_r, exb_r, sqa_r, exa_r, all_r):
        core, me = place_r[0], place_r[1]
        for high, ref in ((0, near_r), (1, far_r)):
            for low in range(2):
                for k in range(size // 4):
                    p = 4 * k + 2 * low + high + core * (high - low)
                    all_r[p] = ref[low * (size // 4) + k]

        def rows(p, first, length):
            return all_r[p, first : first + length].astype(F32)

        for b in range(size):
            p = b ^ me
            red_r[b * unit : (b + 1) * unit, :] = rows(p, starts[0], unit)
            for at, ref in ((starts[1], sqb_r), (starts[3], sqa_r)):
                block = rows(p, at, tall)
                for q in range(parts):
                    ref[b * unit + q * tall : b * unit + (q + 1) * tall, :] = block[:, q * z.hid : (q + 1) * z.hid]
            r, lane = divmod(b, across)
            for at, ref in ((starts[2], exb_r), (starts[4], exa_r)):
                ref[r * wide : (r + 1) * wide, lane * 512 : (lane + 1) * 512] = rows(p, at, wide)

    half = z.out // 2
    return run(
        body,
        [
            ((half, z.mid), F32),
            ((half, z.hid), F32),
            ((z.hid, half), F32),
            ((half, z.hid), F32),
            ((z.hid, half), F32),
        ],
        (place, *(Near(b) for b in blocks)),
        scratch=[pltpu.VMEM((size, height, 512), BF16)],
    )


def weight_dot(inputs, grads):
    return lax.dot_general(inputs, grads, (((0,), (0,)), ((), ())), preferred_element_type=F32)


def folded(grad):
    size = lax.axis_size("batch")
    rows, width = grad.shape
    grad = grad.astype(BF16).reshape(size, 2, rows // (2 * size), width // 512, 512)
    return jnp.swapaxes(grad, 2, 3).reshape(size, 2, -1, 512)


def unfolded(block, width):
    count = width // 512
    rows = block.shape[0] // count
    return jnp.swapaxes(block.reshape(count, rows, 512), 0, 1).reshape(-1)


def tree_sum(terms):
    while len(terms) > 1:
        terms = [a + b for a, b in zip(terms[::2], terms[1::2])] + terms[len(terms) // 2 * 2 :]
    return terms[0]


def wide_sum(parts, first=(), second=(), kind=F32):
    parts = parts.astype(kind)
    parts = parts.astype(F32) + swapped(parts, "rows", 1).astype(F32)
    bits = bits_of(lax.axis_size("batch"))
    partial = parts
    for at in range(0, len(bits), 2):
        parts = tied(parts, *(first if at == 0 else second if at == 2 else ()))
        pair = bits[at : at + 2]
        masks = [pair[0], pair[1], pair[0] + pair[1]] if len(pair) == 2 else pair
        parts = parts.astype(kind)
        terms = [parts] + [swapped(parts, "batch", mask) for mask in masks]
        parts = tree_sum([term.astype(F32) for term in terms])
        partial = parts if at == 0 else partial
    return parts, partial


def plain_gradients(jobs, size):
    blocks, starts, at = [], [], 0
    for kind, lhs, rhs in jobs:
        grad = weight_dot(lhs[: rhs.shape[0]].astype(BF16), rhs.astype(BF16))
        k, n = grad.shape
        if kind == "flat":
            block = core_sum(folded(grad), 1)
        elif kind == "rows" and n == 512:
            block = core_sum(grad.astype(BF16).reshape(2, size, -1, 512), 0)
        elif kind == "rows":
            parts = 512 // n
            block = grad.astype(BF16).reshape(2, size, parts, -1, n)
            block = core_sum(jnp.swapaxes(block, 2, 3).reshape(2, size, -1, 512), 0)
        else:
            across = n // 1024
            block = grad.astype(BF16).reshape(size // across, -1, 2, across, 512)
            block = core_sum(block.transpose(2, 0, 3, 1, 4).reshape(2, size, -1, 512), 0)
        starts.append(at)
        at += block.shape[1]
        blocks.append(block)
    return halved(jnp.concatenate(blocks, axis=1), two_orders), starts


def per_device(
    images,
    crop_sizes,
    reduce_a,
    reduce_gain_a,
    reduce_bias_a,
    spatial_a,
    spatial_gain_a,
    spatial_bias_a,
    expand_a,
    expand_gain_a,
    expand_bias_a,
    project_a,
    project_gain_a,
    project_bias_a,
    squeeze_a,
    squeeze_bias_a,
    excite_a,
    excite_bias_a,
    reduce_b,
    reduce_gain_b,
    reduce_bias_b,
    spatial_b,
    spatial_gain_b,
    spatial_bias_b,
    expand_b,
    expand_gain_b,
    expand_bias_b,
    squeeze_b,
    squeeze_bias_b,
    excite_b,
    excite_bias_b,
    cotangent,
):
    mid = reduce_a.shape[1]
    out = expand_a.shape[1]
    hid = squeeze_a.shape[1]
    size = lax.axis_size("batch")
    z = Sizes(images, mid, out, hid, size * lax.axis_size("rows"))
    micro, held, side, half = z.micro, z.held, z.side, z.half
    core = lax.axis_index("rows")
    me = lax.axis_index("batch")
    place = jnp.stack([core, me]).astype(jnp.int32)

    away = lax.dynamic_slice_in_dim(images, (1 - core) * held, held, axis=2)
    other = swapped(away, "rows", 1)
    vectors = jnp.stack(
        [
            expand_gain_a,
            expand_bias_a,
            project_gain_a,
            project_bias_a,
            expand_gain_b,
            expand_bias_b,
            excite_bias_a,
            excite_bias_b,
        ]
    )

    def pair(own, axis):
        return Pair(own, swapped(own, "rows", 1), axis)

    vectors = pair(vectors, 1)
    pair_sq_a, pair_sq_b = pair(squeeze_a, 0), pair(squeeze_b, 0)
    pair_ex_a, pair_ex_b = pair(excite_a, 1), pair(excite_b, 1)
    pair_red = pair(reduce_b, 0)
    sq_biases = jnp.stack([squeeze_bias_a, squeeze_bias_b])
    vec_one = jnp.stack([reduce_gain_a, reduce_bias_a])
    vec_two = jnp.stack([spatial_gain_a, spatial_bias_a])
    vec_four = jnp.stack([reduce_gain_b, reduce_bias_b])
    vec_five = jnp.stack([spatial_gain_b, spatial_bias_b])

    half_all = crop_sizes // 2
    counted = jnp.stack(
        [jnp.sum(crop_sizes * crop_sizes, axis=1), jnp.sum(half_all * half_all, axis=1)]
    ).astype(F32).reshape(-1)
    halves = lax.dynamic_slice_in_dim(half_all, (me * 2 + core) * held, held, axis=1)
    pix = jnp.broadcast_to((halves * halves).astype(F32).reshape(-1, 1), (z.maps, LANES))
    spots = jnp.arange(half, dtype=jnp.int32)
    limits = halves[:, None, :, None]
    inside = (spots[None, :, None, None] < limits) & (spots[None, None, None, :] < limits)
    mask = jnp.broadcast_to(inside.astype(F32).reshape(z.coarse, 1), (z.coarse, LANES))

    block = 2 * z.map
    spot = jnp.arange(block, dtype=jnp.int32)
    row_pair, rest = spot // (2 * z.group), spot % (2 * z.group)
    row_odd, spot_b, column = spot // (held * side) % 2, spot % (held * side) // side, spot % side
    row_pair = spot // (2 * held * side)
    target = ((row_odd * 2 + column % 2) * (half // 2) + row_pair) * z.group
    target = target + spot_b * half + column // 2
    perm = (target[None, :] == jnp.arange(block, dtype=jnp.int32)[:, None]).astype(BF16)

    other, perm, mask, pix, counted, sq_biases, vec_one, vec_two, vec_four, vec_five, vectors.own = (
        lax.optimization_barrier(
            (other, perm, mask, pix, counted, sq_biases, vec_one, vec_two, vec_four, vec_five, vectors.own)
        )
    )
    vectors.other = swapped(vectors.own, "rows", 1)

    first_one, first_perm, first_mask, first_images = run(
        lambda io, place_r: None, [], (place,), ahead=(reduce_a, perm, mask, Part(images, 2)), room=ROOM
    )
    planes, c1_near, c1, s1, *got = enter_kernel(
        z, place, N(first_images), N(other), N(first_perm), N(first_one), N(first_mask),
        (vec_one, spatial_a, mask),
    )
    vec_near, w_near, mask_near = map(N, got)
    patches_one, c2_near, c2, t1, s2, *got = taps_kernel(
        z, place, wide_sum(s1)[0], counted, vec_near, N(c1_near), w_near, mask_near, True,
        (vec_two, expand_a, mask, Top(planes, z.coarse), project_a, Away(cotangent, 2)),
    )
    vec_near, w_near, mask_near, *side_near = map(N, got[:5])
    up = Join(cotangent, 2, swapped(got[5], "rows", 1), 4)
    active_two, e1_near, e1, t2, p1_near, p1, s3, *got = expand_kernel(
        z, place, wide_sum(s2)[0], counted, vec_near, N(c2_near), w_near, mask_near, side_near,
        (vectors, pix, pair_sq_a, sq_biases, pair_ex_a, pair_red, mask),
    )
    vectors_near, pix_near, sq_near, sqb_near, ex_near, w_near, mask_near = map(N, got)
    sums_three, _ = wide_sum(s3)
    middle, c4_near, c4, gate_one, pool_one, inner_one, hidden_one, total_three, s4, *got = middle_kernel(
        z, place, sums_three, counted, vectors_near, pix_near, N(e1_near), N(p1_near), sq_near, sqb_near, ex_near,
        w_near, mask_near, (vec_four, spatial_b, mask),
    )
    vec_near, w_near, mask_near = map(N, got)
    patches_four, c5_near, c5, t4, s5, *got = taps_kernel(
        z, place, wide_sum(s4)[0], counted, vec_near, N(c4_near), w_near, mask_near, False,
        (vec_five, expand_b, mask),
    )
    vec_near, w_near, mask_near = map(N, got)
    active_five, e2_near, e2, t5, s6, *got = expand_kernel(
        z, place, wide_sum(s5)[0], counted, vec_near, N(c5_near), w_near, mask_near, None,
        (vectors, pix, middle, up, pair_sq_b, sq_biases, pair_ex_b, mask),
    )
    vectors_near, pix_near, mid_near, up_near, sq_near, sqb_near, ex_near, mask_near = map(N, got)
    sums_six, _ = wide_sum(s6)
    final = (micro, half, 2 * held, half, out // 2)
    block_out, block_away, do2, h_near, pool_two, hidden_two, dl_two, dz_two, b6, *got = output_kernel(
        z, place, sums_six, counted, vectors_near, pix_near, N(e2_near), mid_near, up_near,
        sq_near, sqb_near, ex_near, mask_near, final,
        (N(sums_six), vectors, e2, expand_b, t5, vec_five, c5, mask),
    )
    total_near, vectors_near, e_near, w_near, tn_near, vn_near, cn_near, mask_near = map(N, got)

    whole_tiles = mid * 9 // (2 * size) % 16 == 0

    def made(jobs):
        if not whole_tiles:
            return None
        args, spec = [], []
        for kind, lhs, rhs in jobs:
            spec.append((kind, len(args), len(args) + 1))
            args += [lhs, rhs]
        keep, send, _ = gradients(z, place, size, spec, args)
        return keep, send

    def steps(make):
        return list(make()) if whole_tiles else []

    def exchanged(blocks, *after):
        keep, send = blocks
        return keep, swapped(tied(send, *after), "rows", 1)

    back_six, _ = wide_sum(b6, kind=BF16)
    de2, live_near, b5, gain_six, bias_six, ex_bias_two, sq_bias_two, *got = unexpand_kernel(
        z, place, back_six, total_near, counted, vectors_near, 4, e_near, N(h_near), w_near,
        tn_near, vn_near, cn_near, mask_near, (t5, vec_five, c5, spatial_b, t4, vec_four, c4, mask),
    )
    t_near, v_near, c_near, w_near, tn_near, vn_near, cn_near, mask_near = map(N, got)
    jobs_e = (("flat", active_five, de2),)
    made_e = made(jobs_e)
    block_out = finish_output(z, place, swapped(block_away, "rows", 1), block_out)
    back_five, _ = wide_sum(b5, (), [block_out, *steps(lambda: [made_e[0]])])
    dc5, live_near, g5, h5, b4, *got = untap_kernel(
        z, place, back_five, t_near, counted, v_near, c_near, N(live_near), w_near,
        tn_near, vn_near, cn_near, mask_near, False,
        (t4, vec_four, c4, pair_red, do2, total_three, vectors, gate_one, inner_one, e1, p1, pair_sq_a, pair_ex_a, pix, mask),
    )
    t_near, v_near, c_near, w_near, *rest_near = map(N, got)
    jobs_s = (("flat", patches_four, dc5),)
    made_s = made(jobs_s)
    if whole_tiles:
        sum_e = Halving([exchanged(made_e, back_five)])
        b4 = tied(b4, sum_e.sources[0][1])
    back_four, _ = wide_sum(b4, (), steps(lambda: [made_s[0], sum_e.prepare()]))
    came = steps(lambda: sum_e.send(back_four))
    dc4, do1, h_near, g4, h4, dl_one, dz_one, b3, *got = unreduce_kernel(
        z, place, back_four, t_near, counted, v_near, c_near, N(live_near), w_near, *rest_near,
        (total_three, vectors, e1, expand_a, t2, vec_two, c2, mask),
    )
    total_near, vectors_near, e_near, w_near, tn_near, vn_near, cn_near, mask_near = map(N, got)
    jobs_n = (
        ("rows", middle, dc4),
        ("rows", pool_two, dz_two),
        ("lanes", hidden_two, dl_two),
        ("rows", pool_one, dz_one),
        ("lanes", hidden_one, dl_one),
    )
    made_n = made(jobs_n)
    if whole_tiles:
        sum_s = Halving([exchanged(made_s, back_four)])
        came += [sum_s.sources[0][1]]
    back_three, _ = wide_sum(
        tied(b3, *came), (), steps(lambda: [made_n[0], sum_s.prepare(), sum_e.prepare()]), BF16
    )
    came = steps(lambda: sum_s.send(back_three) + sum_e.send(back_three))
    (
        de1, live_near, b2, gain_three, bias_three, gain_side, bias_side, ex_bias_one, sq_bias_one, *got
    ) = unexpand_kernel(
        z, place, back_three, total_near, counted, vectors_near, 0, e_near, N(h_near), w_near,
        tn_near, vn_near, cn_near, mask_near, (t2, vec_two, c2, spatial_a, t1, vec_one, c1, mask),
    )
    t_near, v_near, c_near, w_near, tn_near, vn_near, cn_near, mask_near = map(N, got)
    dp1 = side_kernel(z, place, N(back_three), total_three, counted, vectors, p1, do1, mask)
    jobs_w = (("flat", active_two, de1), ("flat", planes, dp1))
    made_w = made(jobs_w)
    if whole_tiles:
        sum_n = Halving([exchanged(made_n, back_three)])
        came += [made_w[0], sum_n.sources[0][1]]
    back_two, _ = wide_sum(
        tied(b2, dp1, *came), (), steps(lambda: [sum_n.prepare(), sum_s.prepare(), sum_e.prepare()])
    )
    came = steps(lambda: sum_n.send(back_two) + sum_e.send(back_two))
    dc2, live_near, g2, h2, b1, *got = untap_kernel(
        z, place, back_two, t_near, counted, v_near, c_near, N(live_near), w_near,
        tn_near, vn_near, cn_near, mask_near, True,
        (t1, vec_one, c1, reduce_a, dp1, project_a, perm, mask),
    )
    t_near, v_near, c_near, *rest_near = map(N, got)
    jobs_t = (("flat", patches_one, dc2),)
    made_t = made(jobs_t)
    if whole_tiles:
        sum_w = Halving([exchanged(made_w, back_two)])
        came += [made_t[0], sum_w.sources[0][1]]
    back_one, _ = wide_sum(tied(b1, *came), (), steps(lambda: [sum_n.prepare(), sum_w.prepare()]))
    came_t = exchanged(made_t, back_one) if whole_tiles else None
    came = steps(lambda: sum_n.send(back_one) + sum_s.send(back_one))
    dc1, images_grad, grad_away, g1, h1 = leave_kernel(
        z, place, back_one, t_near, counted, v_near, c_near, N(live_near), *rest_near,
        (micro, side // 2, 2 * held, side, z.cin),
    )
    jobs_r = (("flat", planes, dc1),)
    made_r = made(jobs_r)

    images_grad = finish_images(z, place, swapped(grad_away, "rows", 1), images_grad)

    if whole_tiles:
        heights = [a.shape[1] * b.shape[1] // (2 * size * 512) for _, a, b in jobs_n]
        at_second = [sum(heights[:k]) for k in range(len(heights) + 1)]
        def rows_of(grad):
            return grad.size // (2 * size * 512), grad.shape[1]

        here = [made_r[0], *came, came_t[1]]
        came = sum_w.send(*here)
        came_r = exchanged(made_r, *here)
        sum_n.prepare(*here)
        came += sum_n.send()
        sum_t = Halving([came_t, came_r])
        here = [images_grad, *came, sum_t.prepare()]
        came = sum_t.send(*here)
        second = total_kernel([tied(sum_n.blocks[0], *here), *sum_n.blocks[1:]])
        narrows = second.astype(BF16)
        around = [swapped(narrows, "batch", 4 * k) for k in range(1, size // 4)]
        sum_w.prepare(*here)
        came += sum_w.send()
        sum_s.prepare(sum_w.sent[0])
        here = [*came, *around, *sum_s.send()]
        narrow = [narrows, *around]
        sum_e.blocks[0] = tied(sum_e.blocks[0], around[0])
        (out_expand_b,) = sum_e.finish([rows_of(expand_b)])
        sum_w.prepare(out_expand_b, *here)
        came = sum_w.send()
        (kept, come), = sum_t.sources
        kept, sent = second_step(tied(kept, sum_w.sent[0]), come, narrow)
        come = crossed(sent, 2, 1)
        sum_s.blocks[0] = tied(sum_s.blocks[0], sent)
        (out_spatial_b,) = sum_s.finish([rows_of(spatial_b)])
        *blocks, part = third_step(tied(kept, out_spatial_b, *came), come, narrow)
        sum_t.blocks = blocks[:1] + [
            swapped(block, "batch", 4 * (k + 1)) for k, block in enumerate(blocks[1:])
        ]
        every = part, crossed(part, 1, 2)
        narrow_outs = gathered_kernel(z, place, size, every, at_second)
        sum_t.blocks[0] = tied(sum_t.blocks[0], narrow_outs[0])
        sum_w.blocks[0] = tied(sum_w.blocks[0], every[1])
        out_expand_a, out_project_a = sum_w.finish([rows_of(expand_a), rows_of(project_a)])
        out_spatial_a, out_reduce_a = sum_t.finish([rows_of(spatial_a), rows_of(reduce_a)])
    else:
        second, at_second = plain_gradients(jobs_n, size)
        at_second = at_second + [second.shape[0]]
        edge_first = expand_b.size // (2 * size * 512)
        edge_rest = expand_a.size // (2 * size * 512)
        edge_third = spatial_a.size // (2 * size * 512)
        first = plain_gradients(jobs_e + jobs_s, size)[0]
        rest = plain_gradients(jobs_w, size)[0]
        third = plain_gradients(jobs_t + jobs_r, size)[0]
        out_expand_b, out_spatial_b = unfolded(first[:edge_first], out), unfolded(first[edge_first:], mid)
        out_expand_a, out_project_a = unfolded(rest[:edge_rest], out), unfolded(rest[edge_rest:], out)
        out_spatial_a, out_reduce_a = unfolded(third[:edge_third], mid), unfolded(third[edge_third:], mid)
    if whole_tiles:
        out_reduce, out_sq_b, out_ex_b, out_sq_a, out_ex_a = narrow_outs
    else:
        every = collected(second.astype(BF16)).astype(F32)

        def tall_of(k):
            block = every[:, at_second[k] : at_second[k + 1]]
            block = block.reshape(size, block.shape[1], 512 // hid, hid)
            return jnp.swapaxes(block, 1, 2).reshape(-1, hid)

        def flat_of(k):
            block = every[:, at_second[k] : at_second[k + 1]]
            across = (out // 2) // 512
            block = block.reshape(size // across, across, -1, 512)
            return jnp.swapaxes(block, 1, 2).reshape(hid, out // 2)

        out_reduce = every[:, : at_second[1]].reshape(-1, mid)
        out_sq_b, out_ex_b, out_sq_a, out_ex_a = tall_of(1), flat_of(2), tall_of(3), flat_of(4)
    span = out // 2

    return (
        block_out,
        images_grad,
        out_reduce_a,
        g1.reshape(-1),
        h1.reshape(-1),
        out_spatial_a,
        g2.reshape(-1),
        h2.reshape(-1),
        out_expand_a,
        gain_three.reshape(-1),
        bias_three.reshape(-1),
        out_project_a,
        gain_side.reshape(-1),
        bias_side.reshape(-1),
        out_sq_a,
        sq_bias_one.reshape(-1),
        out_ex_a,
        ex_bias_one.reshape(-1),
        out_reduce,
        g4.reshape(-1),
        h4.reshape(-1),
        out_spatial_b,
        g5.reshape(-1),
        h5.reshape(-1),
        out_expand_b,
        gain_six.reshape(-1),
        bias_six.reshape(-1),
        out_sq_b,
        sq_bias_two.reshape(-1),
        out_ex_b,
        ex_bias_two.reshape(-1),
    )


def solution(mesh):
    in_specs = (
        P(None, "rows", "batch", None, None),
        P(),
        P(),
        P(),
        P(),
        P(),
        P(),
        P(),
        P(),
        P("rows"),
        P("rows"),
        P(),
        P("rows"),
        P("rows"),
        P("rows", None),
        P(),
        P(None, "rows"),
        P("rows"),
        P("rows", None),
        P(),
        P(),
        P(),
        P(),
        P(),
        P(),
        P("rows"),
        P("rows"),
        P("rows", None),
        P(),
        P(None, "rows"),
        P("rows"),
        P(None, None, "batch", None, "rows"),
    )
    out_specs = (
        P(None, None, "batch", None, "rows"),
        P(None, "rows", "batch", None, None),
        P(("batch", "rows")),
        P(),
        P(),
        P(("batch", "rows")),
        P(),
        P(),
        P(("batch", "rows")),
        P("rows"),
        P("rows"),
        P(("batch", "rows")),
        P("rows"),
        P("rows"),
        P("rows", None),
        P(),
        P(None, "rows"),
        P("rows"),
        P("rows", None),
        P(),
        P(),
        P(("batch", "rows")),
        P(),
        P(),
        P(("batch", "rows")),
        P("rows"),
        P("rows"),
        P("rows", None),
        P(),
        P(None, "rows"),
        P("rows"),
    )
    return jax.shard_map(
        per_device, mesh=mesh, in_specs=in_specs, out_specs=out_specs, check_vma=False
    )
```

```python
import jax
import jax.numpy as jnp
from jax import lax
from jax.experimental import pallas as pl
from jax.experimental.pallas import tpu as pltpu
from jax.sharding import PartitionSpec as P

epsilon = 1e-05
HIGHEST = lax.Precision.HIGHEST
BF16 = jnp.bfloat16
F32 = jnp.float32

PLANE_TAPS = (((1, 0),), ((2, 0), (0, 1)))


def swapped(block, axis, mask):
    route = [(i, i ^ mask) for i in range(lax.axis_size(axis))]
    return lax.ppermute(block, axis, route)


def bits_of(size):
    return [1 << k for k in range(size.bit_length() - 1)]


def all_sum(parts):
    parts = parts + swapped(parts, "rows", 1)
    size = lax.axis_size("batch")
    spread = jnp.broadcast_to(parts[None], (size,) + parts.shape)
    return jnp.sum(lax.all_to_all(spread, "batch", 0, 0, tiled=True), axis=0)


def halved(block, orders):
    size = lax.axis_size("batch")
    place = lax.axis_index("batch")
    bits = bits_of(size)
    count = block.shape[1]
    cut = count // 2 // 16 * 16
    parts = []
    for part, order in zip((block[:, :cut], block[:, cut:]), orders(bits)):
        shape = part.shape[1:]
        left = list(reversed(bits))
        part = part.reshape((2,) * len(bits) + shape)
        for bit in order:
            axis = left.index(bit)
            mine = (place // bit) % 2
            gone = lax.dynamic_index_in_dim(part, 1 - mine, axis, keepdims=False)
            kept = lax.dynamic_index_in_dim(part, mine, axis, keepdims=False)
            total = kept.astype(F32) + swapped(gone, "batch", bit).astype(F32)
            left.pop(axis)
            part = total.astype(BF16) if left else total
        parts.append(part)
    return jnp.concatenate(parts, axis=0)


def two_orders(bits):
    return (bits, bits[1::-1] + bits[2:])


def collected(block):
    place = lax.axis_index("batch")
    block = block[None]
    for bit in bits_of(lax.axis_size("batch")):
        other = swapped(block, "batch", bit)
        upper = (place // bit) % 2 == 1
        block = jnp.concatenate([jnp.where(upper, other, block), jnp.where(upper, block, other)], axis=0)
    return block


def core_sum(block, axis):
    core = lax.axis_index("rows")
    gone = lax.dynamic_index_in_dim(block, 1 - core, axis, keepdims=False)
    kept = lax.dynamic_index_in_dim(block, core, axis, keepdims=False)
    return (kept.astype(F32) + swapped(gone, "rows", 1).astype(F32)).astype(BF16)


def both_cores(block, axis):
    core = lax.axis_index("rows")
    other = swapped(block, "rows", 1)
    first = jnp.where(core == 0, block, other)
    second = jnp.where(core == 0, other, block)
    return jnp.concatenate([first, second], axis=axis)


LANES = 128
VMEM_MIB = 64
ROOM = None
MARGIN_MIB = 3
READS = (((1, 0),), ((2, 0), (0, -1)))
ALL_TAPS = ((0, -1), (1, 0), (2, 1))


class Near:
    def __init__(self, array):
        self.array = array
        self.shape = array[0] if isinstance(array, tuple) else array.shape


class Both:
    def __init__(self, array):
        self.array = array


class Late:
    def __init__(self, array):
        self.array = array
        self.shape = array.shape


class Pair:
    def __init__(self, own, other, axis):
        self.own, self.other, self.axis = own, other, axis
        shape = list(own.shape)
        shape[axis] *= 2
        self.shape, self.dtype = tuple(shape), own.dtype


class Part:
    def __init__(self, array, axis):
        self.array, self.axis = array, axis
        shape = list(array.shape)
        shape[axis] //= 2
        self.shape, self.dtype = tuple(shape), array.dtype


class Top:
    def __init__(self, array, rows):
        self.array, self.rows = array, rows
        self.shape, self.dtype = (rows,) + tuple(array.shape[1:]), array.dtype


class Away:
    def __init__(self, array, axis):
        self.array, self.axis = array, axis
        shape = list(array.shape)
        shape[axis] //= 2
        self.shape, self.dtype = tuple(shape), array.dtype


class Join:
    def __init__(self, array, cut, other, axis):
        self.array, self.cut, self.other, self.axis = array, cut, other, axis
        shape = list(other.shape)
        shape[axis] *= 2
        self.shape, self.dtype = tuple(shape), array.dtype


class Raw:
    def __init__(self, shape, dtype):
        self.shape, self.dtype = shape, dtype


def half_of(ref, axis, which, length):
    start = which * length
    if axis >= len(ref.shape) - 2:
        start = pl.multiple_of(start, length)
    return ref.at[(slice(None),) * axis + (pl.ds(start, length),)]


class Copies:
    def __init__(self, sems):
        self.sems, self.used = sems, 0
        self.waiting, self.open = {}, []

    def start(self, source, target):
        copy = pltpu.make_async_copy(source, target, self.sems.at[self.used])
        self.used += 1
        copy.start()
        return copy

    def need(self, *refs):
        for ref in refs:
            for copy in self.waiting.pop(id(ref), ()):
                copy.wait()

    def out(self, source, target):
        self.open.append(self.start(source, target))


def run(body, outs, args, scratch=(), flops=0, spare=0, ahead=(), room=None):
    operands, specs, plans, buffers = [], [], [], []
    far = pl.BlockSpec(memory_space=pltpu.HBM)
    vmem = pl.BlockSpec(memory_space=pltpu.VMEM)
    count, next_up = 0, []

    def plan(arg, late, keep):
        nonlocal count
        if isinstance(arg, Near) and keep is next_up:
            plans.append(("copy", len(operands), (len(keep), 0), late))
            operands.append(arg.array)
            specs.append(vmem)
            keep.append((tuple(arg.shape), arg.array.dtype))
            count += 1
            return
        if isinstance(arg, Near):
            plans.append(("near", len(operands), None, late))
            operands.append(arg.array)
            specs.append(vmem)
            return
        if isinstance(arg, Pair):
            kind, axis, parts = "pair", arg.axis, [arg.own, arg.other]
        elif isinstance(arg, Part):
            kind, axis, parts = "part", arg.axis, [arg.array]
        elif isinstance(arg, Away):
            kind, axis, parts = "away", arg.axis, [arg.array]
        elif isinstance(arg, Top):
            kind, axis, parts = "top", 0, [arg.array]
        elif isinstance(arg, Join):
            kind, axis, parts = "join", (arg.cut, arg.axis), [arg.array, arg.other]
        elif arg.ndim == 1:
            plans.append(("near", len(operands), None, late))
            operands.append(arg)
            specs.append(pl.BlockSpec(memory_space=pltpu.SMEM))
            return
        else:
            kind, axis, parts = "copy", 0, [arg]
        plans.append((kind, len(operands), (len(keep), axis), late))
        operands.extend(parts)
        specs.extend([far] * len(parts))
        keep.append((tuple(arg.shape), arg.dtype))
        count += len(parts)

    for arg in args:
        late = isinstance(arg, Late)
        plan(arg.array if late else arg, late, buffers)
    first_ahead = len(plans)
    for arg in ahead:
        plan(arg, True, next_up)
    shapes, out_specs, ways = [], [], []
    for item in outs:
        if isinstance(item, Raw):
            ways.append(("raw", len(shapes), None))
            shapes.append(jax.ShapeDtypeStruct(item.shape, item.dtype))
            out_specs.append(far)
        elif isinstance(item, Near):
            ways.append(("near", len(shapes), None))
            shapes.append(jax.ShapeDtypeStruct(*item.array))
            out_specs.append(vmem)
        elif isinstance(item, Both):
            ways.append(("both", len(shapes), None))
            shapes += [jax.ShapeDtypeStruct(*item.array)] * 2
            out_specs += [vmem, far]
            count += 1
        else:
            ways.append(("copy", len(shapes), len(buffers)))
            shapes.append(jax.ShapeDtypeStruct(*item))
            out_specs.append(far)
            buffers.append(item)
            count += 1
    first_next = len(shapes)
    for item in next_up:
        shapes.append(jax.ShapeDtypeStruct(*item))
        out_specs.append(vmem)
    sems = pltpu.SemaphoreType.DMA((max(count + spare, 1),))

    def kernel(*refs):
        ins = refs[: len(operands)]
        results = refs[len(operands) : len(operands) + len(shapes)]
        rest = refs[len(operands) + len(shapes) :]
        bufs, own = rest[: len(buffers)], rest[len(buffers) : -1]
        io = Copies(rest[-1])
        views, early = [], []
        for k, (kind, at, spot, late) in enumerate(plans):
            if kind == "near":
                views.append(ins[at])
                continue
            index, axis = spot
            buf = results[first_next + index] if k >= first_ahead else bufs[index]
            if kind == "copy":
                copies = [io.start(ins[at], buf)]
            elif kind == "pair":
                core = ins[0][0]
                length = ins[at].shape[axis]
                copies = [
                    io.start(ins[at], half_of(buf, axis, core, length)),
                    io.start(ins[at + 1], half_of(buf, axis, 1 - core, length)),
                ]
            elif kind == "top":
                copies = [io.start(ins[at].at[pl.ds(0, buf.shape[0])], buf)]
            elif kind == "join":
                core, (cut, axis) = ins[0][0], axis
                mine = half_of(ins[at], cut, core, ins[at + 1].shape[cut])
                length = ins[at + 1].shape[axis]
                copies = [
                    io.start(mine, half_of(buf, axis, core, length)),
                    io.start(ins[at + 1], half_of(buf, axis, 1 - core, length)),
                ]
            else:
                core = ins[0][0] if kind == "part" else 1 - ins[0][0]
                copies = [io.start(half_of(ins[at], axis, core, buf.shape[axis]), buf)]
            io.waiting[id(buf)] = copies
            if k < first_ahead:
                views.append(buf)
                if not late:
                    early.append(buf)
        io.need(*early)
        targets = {}
        for kind, at, index in ways:
            if kind == "copy":
                views.append(bufs[index])
                targets[id(bufs[index])] = (bufs[index], results[at])
            else:
                views.append(results[at])
                if kind == "both":
                    targets[id(results[at])] = (results[at], results[at + 1])

        def send(*sent):
            for ref in sent:
                io.out(*targets.pop(id(ref)))

        io.send = send
        body(io, *views, *own)
        for buf, ref in targets.values():
            io.out(buf, ref)
        for copies in io.waiting.values():
            for copy in copies:
                copy.wait()
        for copy in io.open:
            copy.wait()

    def bytes_of(shape, dtype):
        size = 1
        for n in shape:
            size *= n
        return size * jnp.dtype(dtype).itemsize

    moved = sum(a.size * a.dtype.itemsize for a in operands) + sum(
        bytes_of(s.shape, s.dtype) for s in shapes
    )
    held = sum(bytes_of(*item) for item in buffers) + sum(bytes_of(s.shape, s.dtype) for s in scratch)
    limit = held + (MARGIN_MIB << 20)
    if room is not None:
        near = sum(a.size * a.dtype.itemsize for a, spec in zip(operands, specs) if spec is vmem)
        near += sum(bytes_of(s.shape, s.dtype) for s, spec in zip(shapes, out_specs) if spec is vmem)
        limit = max(limit, ((VMEM_MIB - room) << 20) - near)
    return pl.pallas_call(
        kernel,
        out_shape=shapes,
        in_specs=specs,
        out_specs=out_specs,
        scratch_shapes=[*(pltpu.VMEM(*item) for item in buffers), *scratch, sems],
        compiler_params=pltpu.CompilerParams(vmem_limit_bytes=limit),
        cost_estimate=pl.CostEstimate(flops=flops, bytes_accessed=0, transcendentals=0),
    )(*operands)


def dot(a, b):
    return lax.dot_general(a, b, (((1,), (0,)), ((), ())), preferred_element_type=F32)


def dot_nt(a, b):
    return lax.dot_general(a, b, (((1,), (1,)), ((), ())), preferred_element_type=F32)


def dot_tn(a, b):
    return lax.dot_general(a, b, (((0,), (0,)), ((), ())), preferred_element_type=F32)


def exact_dot(a, b, product):
    high = a.astype(BF16)
    low = (a - high.astype(F32)).astype(BF16)
    return product(high, b) + product(low, b)


def sigmoid(v):
    return 0.5 + 0.5 * jnp.tanh(0.5 * v)


def slope_of(v):
    sigma = sigmoid(v)
    return sigma * (1.0 + v * (1.0 - sigma))


def counts_of(z, n_r, which):
    return [n_r[which * z.micro + m] for m in range(z.micro)]


def norm_rows(total, counted, micro):
    rows = []
    for m in range(micro):
        centre = total[2 * m : 2 * m + 1] / counted[m]
        square = total[2 * m + 1 : 2 * m + 2] / counted[m]
        rows.append((centre, lax.rsqrt(square - centre * centre + epsilon)))
    return rows


def fold_sums(first, second):
    return jnp.sum(first, axis=0, keepdims=True), jnp.sum(second, axis=0, keepdims=True)


def flat_row(row, out_ref):
    for k in range(row.shape[1] // LANES):
        out_ref[k : k + 1, :] = row[:, k * LANES : (k + 1) * LANES]


def flat_of(n):
    return ((n // LANES, LANES), F32)


def gains_out(total, micro, gain_r, bias_r):
    flat_row(sum(total[2 * m + 1 : 2 * m + 2] for m in range(micro)), gain_r)
    flat_row(sum(total[2 * m : 2 * m + 1] for m in range(micro)), bias_r)


def to_all(z, rows, s_r):
    for k, row in enumerate(rows):
        s_r[k : k + 1, :] = row


def place_patches(values, row_taps, col_taps, out_ref, base, lane, ch, group):
    size = values.shape[0]
    q = lax.broadcasted_iota(jnp.int32, values.shape, 0) % 8
    for col, cs in col_taps:
        if cs == -1:
            turned = jnp.where(q == 0, 0.0, pltpu.roll(values, 1, 0))
        elif cs == 1:
            turned = jnp.where(q == 7, 0.0, pltpu.roll(values, size - 1, 0))
        else:
            turned = values
        turned = turned.astype(BF16)
        gap = jnp.zeros((group, values.shape[1]), BF16)
        for row, rs in row_taps:
            at = (3 * row + col) * ch + lane
            lanes = slice(at, at + values.shape[1])
            if rs == 0:
                out_ref[base : base + size, lanes] = turned
            elif rs == -1:
                out_ref[base : base + group, lanes] = gap
                out_ref[base + group : base + size, lanes] = turned[: size - group]
            else:
                out_ref[base : base + size - group, lanes] = turned[group:]
                out_ref[base + size - group : base + size, lanes] = gap


class Sizes:
    def __init__(self, images, mid, out, hid, devices):
        self.micro = images.shape[0]
        self.held = images.shape[2] // 2
        self.side = images.shape[3]
        self.half = self.side // 2
        self.cin = images.shape[4]
        self.mid, self.out, self.hid, self.devices = mid, out, hid, devices
        self.group = self.held * self.half
        self.map = self.half * self.group
        self.coarse = self.micro * self.map
        self.fine = 4 * self.coarse
        self.maps = self.micro * self.held


def enter_kernel(z, place, images, other, perm, w_one, mask, ahead):
    def body(io, place_r, mine_r, other_r, perm_r, w1_r, mask_r, planes_r, c1_r, s1_r):
        core = place_r[0]
        rows = z.map // 2
        for k, ref in ((0, mine_r), (1, other_r)):
            half = core if k == 0 else 1 - core
            io.need(ref)
            for m in range(z.micro):
                turned = dot(perm_r[...], ref[m].reshape(2 * z.map, z.cin)).astype(BF16)
                for p in range(4):
                    at = pl.multiple_of((p * z.micro + m) * z.map + half * rows, rows)
                    planes_r[pl.ds(at, rows), :] = turned[p * rows : (p + 1) * rows]
        io.send(planes_r)
        io.need(w1_r)
        c1_r[...] = dot(planes_r[...], w1_r[...])
        for m in range(z.micro):
            one = [None, None]
            for p in range(4):
                at = (p * z.micro + m) * z.map
                c = c1_r[at : at + z.map, :]
                live = c * mask_r[m * z.map : (m + 1) * z.map, 0:1]
                a, b = fold_sums(live, live * c)
                one = [a, b] if p == 0 else [one[0] + a, one[1] + b]
            s1_r[2 * m : 2 * m + 1, :] = one[0]
            s1_r[2 * m + 1 : 2 * m + 2, :] = one[1]
        io.send(c1_r)

    return run(
        body,
        [
            ((z.fine, z.cin), BF16),
            Both(((z.fine, z.mid), F32)),
            Near(((2 * z.micro, z.mid), F32)),
        ],
        (place, images, other, perm, w_one, mask),
        room=ROOM,
        ahead=ahead,
        flops=2 * z.fine * z.cin * z.mid,
    )


def taps_kernel(z, place, sums, counted, vec, conv, weight, mask, strided, ahead):
    planes = 4 if strided else 1
    nt = weight.shape[0]

    def body(io, place_r, sums_r, n_r, vec_r, c_r, w_r, mask_r, patch_r, out_r, t_r, s_r):
        total = sums_r[...]
        t_r[...] = total
        io.send(t_r)
        norms = norm_rows(total, counts_of(z, n_r, 0 if strided else 1), z.micro)
        for m in range(z.micro):
            centre, inverse = norms[m]
            scale = inverse * vec_r[0:1]
            offset = vec_r[1:2] - centre * scale
            live = mask_r[m * z.map : (m + 1) * z.map, 0:1]
            for p in range(planes):
                at = (p * z.micro + m) * z.map
                for lane in range(0, z.mid, LANES):
                    lanes = slice(lane, lane + LANES)
                    v = (c_r[at : at + z.map, lanes] * scale[:, lanes] + offset[:, lanes]) * live
                    v = v * sigmoid(v)
                    rows = READS[p // 2] if strided else ALL_TAPS
                    cols = READS[p % 2] if strided else ALL_TAPS
                    place_patches(v, rows, cols, patch_r, m * z.map, lane, z.mid, z.group)
        io.send(patch_r)
        io.need(w_r)
        c = dot(patch_r[...], w_r[...])
        out_r[...] = c
        io.send(out_r)
        for m in range(z.micro):
            part = c[m * z.map : (m + 1) * z.map]
            live = part * mask_r[m * z.map : (m + 1) * z.map, 0:1]
            a, b = fold_sums(live, live * part)
            s_r[2 * m : 2 * m + 1, :] = a
            s_r[2 * m + 1 : 2 * m + 2, :] = b

    return run(
        body,
        [
            ((z.coarse, nt), BF16),
            Both(((z.coarse, z.mid), F32)),
            ((2 * z.micro, z.mid), F32),
            Near(((2 * z.micro, z.mid), F32)),
        ],
        (place, Near(sums), counted, vec, conv, weight, mask),
        room=ROOM,
        ahead=ahead,
        flops=2 * z.coarse * nt * z.mid,
    )


def expand_kernel(z, place, sums, counted, vec, conv, weight, mask, side, ahead):
    height = 2 * z.micro

    def body(io, place_r, sums_r, n_r, vec_r, c_r, w_r, mask_r, *refs):
        if side is not None:
            plane_r, ws_r, act_r, out_r, t_r, p1_r, s_r = refs
        else:
            act_r, out_r, t_r, s_r = refs
        total = sums_r[...]
        t_r[...] = total
        io.send(t_r)
        norms = norm_rows(total, counts_of(z, n_r, 1), z.micro)
        for m in range(z.micro):
            rows = slice(m * z.map, (m + 1) * z.map)
            centre, inverse = norms[m]
            scale = inverse * vec_r[0:1]
            offset = vec_r[1:2] - centre * scale
            v = (c_r[rows, :] * scale + offset) * mask_r[rows, 0:1]
            act_r[rows, :] = (v * sigmoid(v)).astype(BF16)
        io.send(act_r)
        io.need(w_r)

        @pl.loop(0, z.out // 512, unroll=4)
        def _(j):
            lanes = pl.ds(pl.multiple_of(j * 512, 512), 512)
            products = [(dot(act_r[...], w_r[:, lanes]), out_r, 0)]
            if side is not None:
                products.append((dot(plane_r[...], ws_r[:, lanes]), p1_r, height))
            for p, ref, first in products:
                p = p.astype(BF16)
                ref[:, lanes] = p
                p = p.astype(F32)
                for m in range(z.micro):
                    part = p[m * z.map : (m + 1) * z.map]
                    live = part * mask_r[m * z.map : (m + 1) * z.map, 0:1]
                    a, b = fold_sums(live, live * part)
                    at = first + 2 * m
                    s_r[at : at + 1, lanes] = a
                    s_r[at + 1 : at + 2, lanes] = b

    extra = () if side is None else side
    wide = [] if side is None else [Both(((z.coarse, z.out), BF16))]
    return run(
        body,
        [
            ((z.coarse, z.mid), BF16),
            Both(((z.coarse, z.out), BF16)),
            ((2 * z.micro, z.mid), F32),
            *wide,
            Near(((height * (1 if side is None else 2), z.out), F32)),
        ],
        (place, Near(sums), counted, vec, conv, weight, mask, *extra),
        room=ROOM,
        ahead=ahead,
        flops=2 * z.coarse * z.out * z.mid,
    )


def by_map(z, v):
    return v.reshape(z.half, z.held, z.half, v.shape[-1])


def map_sums(z, v):
    return jnp.sum(jnp.sum(by_map(z, v), axis=0), axis=1)


def spread(z, rows):
    return jnp.broadcast_to(
        rows[None, :, None, :], (z.half, z.held, z.half, rows.shape[-1])
    ).reshape(z.map, rows.shape[-1])


def norms_at(z, total_r, n_r, m, lanes, first=0):
    counted = n_r[z.micro + m]
    at = first + 2 * m
    centre = total_r[at : at + 1, lanes] / counted
    square = total_r[at + 1 : at + 2, lanes] / counted
    return centre, lax.rsqrt(square - centre * centre + epsilon)


def gate_rows(pooled, squeeze_r, sq_bias, excite_r, ex_bias):
    inner = exact_dot(pooled, squeeze_r[...], dot) + sq_bias
    hidden = inner * sigmoid(inner)
    gate = sigmoid(exact_dot(hidden, excite_r[...], dot) + ex_bias)
    return inner, hidden, gate


def gate_back(dgate, gate, inner, squeeze_r, excite_r, pix):
    dl = dgate * gate * (1.0 - gate)
    dz = exact_dot(dl, excite_r[...], dot_nt) * slope_of(inner)
    du = exact_dot(dz, squeeze_r[...], dot_nt) / pix
    return dl, dz, du


def bias_sums(z, dl, dz, s_r, first):
    s_r[first : first + 1, :] = jnp.sum(dl, axis=0, keepdims=True)
    s_r[first + 1 : first + 2, :] = jnp.zeros((1, z.out), F32)
    s_r[first + 1 : first + 2, : z.hid] = jnp.sum(dz, axis=0, keepdims=True)


def middle_kernel(z, place, sums, counted, vectors, pix, e1, p1, squeeze, sq_bias, excite, w, mask, ahead):
    side = 2 * z.micro

    def body(
        io, place_r, t_r, n_r, vec_r, pix_r, e_r, p_r, sq_r, sqb_r, ex_r, w_r, mask_r,
        mid_r, c_r, gate_r, pool_r, inner_r, hid_r, total_r, s_r,
    ):
        io.out(t_r, total_r)

        @pl.loop(0, z.out // LANES, unroll=8)
        def _(j):
            lanes = pl.ds(pl.multiple_of(j * LANES, LANES), LANES)
            for m in range(z.micro):
                rows = slice(m * z.map, (m + 1) * z.map)
                centre, inverse = norms_at(z, t_r, n_r, m, lanes)
                scale = inverse * vec_r[0:1, lanes]
                offset = vec_r[1:2, lanes] - centre * scale
                v = (e_r[rows, lanes].astype(F32) * scale + offset) * mask_r[rows, 0:1]
                at = slice(m * z.held, (m + 1) * z.held)
                pool_r[at, lanes] = map_sums(z, v) / pix_r[at, 0:1]

        io.need(sq_r, ex_r)
        inner, hidden, gate = gate_rows(pool_r[...], sq_r, sqb_r[0:1], ex_r, vec_r[6:7])
        gate_r[...] = gate
        inner_r[...] = inner
        hid_r[...] = hidden
        io.send(gate_r, inner_r, hid_r, pool_r)
        io.need(p_r)

        @pl.loop(0, z.out // LANES, unroll=8)
        def _(j):
            lanes = pl.ds(pl.multiple_of(j * LANES, LANES), LANES)
            for m in range(z.micro):
                rows = slice(m * z.map, (m + 1) * z.map)
                centre, inverse = norms_at(z, t_r, n_r, m, lanes)
                scale = inverse * vec_r[0:1, lanes]
                offset = vec_r[1:2, lanes] - centre * scale
                v = e_r[rows, lanes].astype(F32) * scale + offset
                centre, inverse = norms_at(z, t_r, n_r, m, lanes, side)
                scale = inverse * vec_r[2:3, lanes]
                offset = vec_r[3:4, lanes] - centre * scale
                o = v * spread(z, gate_r[m * z.held : (m + 1) * z.held, lanes])
                o = (o + (p_r[rows, lanes].astype(F32) * scale + offset)) * mask_r[rows, 0:1]
                mid_r[rows, lanes] = (o * sigmoid(o)).astype(BF16)

        io.send(mid_r)
        io.need(w_r)
        c = dot(mid_r[...], w_r[...])
        c_r[...] = c
        io.send(c_r)
        for m in range(z.micro):
            part = c[m * z.map : (m + 1) * z.map]
            live = part * mask_r[m * z.map : (m + 1) * z.map, 0:1]
            a, b = fold_sums(live, live * part)
            s_r[2 * m : 2 * m + 1, :] = a
            s_r[2 * m + 1 : 2 * m + 2, :] = b

    return run(
        body,
        [
            ((z.coarse, z.out), BF16),
            Both(((z.coarse, z.mid), F32)),
            ((z.maps, z.out), F32),
            ((z.maps, z.out), F32),
            ((z.maps, z.hid), F32),
            ((z.maps, z.hid), F32),
            Raw((2 * side, z.out), F32),
            Near(((2 * z.micro, z.mid), F32)),
        ],
        (place, Near(sums), counted, vectors, pix, e1, p1, squeeze, sq_bias, excite, w, mask),
        room=ROOM,
        ahead=ahead,
        spare=1,
        flops=2 * z.coarse * z.out * z.mid,
    )


def output_kernel(z, place, sums, counted, vectors, pix, e2, middle, up, squeeze, sq_bias, excite, mask, final, ahead):
    span = z.out // 2

    def body(
        io, place_r, t_r, n_r, vec_r, pix_r, e_r, mid_r, up_r, sq_r, sqb_r, ex_r, mask_r,
        final_r, away_r, do_r, h_r, pool_r, hid_r, dl_r, dz_r, s_r, out_r, gate_r, du_r,
    ):
        core = place_r[0]

        @pl.loop(0, z.out // LANES, unroll=8)
        def _(j):
            lanes = pl.ds(pl.multiple_of(j * LANES, LANES), LANES)
            for m in range(z.micro):
                rows = slice(m * z.map, (m + 1) * z.map)
                centre, inverse = norms_at(z, t_r, n_r, m, lanes)
                scale = inverse * vec_r[4:5, lanes]
                offset = vec_r[5:6, lanes] - centre * scale
                v = (e_r[rows, lanes].astype(F32) * scale + offset) * mask_r[rows, 0:1]
                at = slice(m * z.held, (m + 1) * z.held)
                pool_r[at, lanes] = map_sums(z, v) / pix_r[at, 0:1]

        io.need(sq_r, ex_r)
        inner, hidden, gate = gate_rows(pool_r[...], sq_r, sqb_r[1:2], ex_r, vec_r[7:8])
        gate_r[...] = gate
        hid_r[...] = hidden
        io.send(pool_r, hid_r)
        io.need(mid_r, up_r)

        @pl.loop(0, z.out // LANES, unroll=8)
        def _(j):
            lanes = pl.ds(pl.multiple_of(j * LANES, LANES), LANES)
            for m in range(z.micro):
                rows = slice(m * z.map, (m + 1) * z.map)
                at = slice(m * z.held, (m + 1) * z.held)
                centre, inverse = norms_at(z, t_r, n_r, m, lanes)
                scale = inverse * vec_r[4:5, lanes]
                offset = vec_r[5:6, lanes] - centre * scale
                v = (e_r[rows, lanes].astype(F32) * scale + offset) * mask_r[rows, 0:1]
                o = v * spread(z, gate_r[at, lanes]) + mid_r[rows, lanes].astype(F32)
                sigma = sigmoid(o)
                out_r[m, :, :, :, lanes] = by_map(z, o * sigma).astype(BF16)
                up = up_r[m, :, :, :, lanes].astype(F32).reshape(z.map, LANES)
                do = up * (sigma * (1.0 + o * (1.0 - sigma)))
                do_r[rows, lanes] = do
                dl_r[at, lanes] = map_sums(z, do * v)

        io.out(
            half_of(out_r, 4, core, span), final_r.at[:, :, pl.ds(core * z.held, z.held)]
        )
        io.out(half_of(out_r, 4, 1 - core, span), away_r)
        io.send(do_r)
        dl, dz, du = gate_back(dl_r[...], gate_r[...], inner, sq_r, ex_r, pix_r[:, 0:1])
        dl_r[...] = dl
        dz_r[...] = dz
        du_r[...] = du
        io.send(dl_r, dz_r)
        bias_sums(z, dl, dz, s_r, 2 * z.micro)

        @pl.loop(0, z.out // LANES, unroll=8)
        def _(j):
            lanes = pl.ds(pl.multiple_of(j * LANES, LANES), LANES)
            for m in range(z.micro):
                rows = slice(m * z.map, (m + 1) * z.map)
                at = slice(m * z.held, (m + 1) * z.held)
                centre, inverse = norms_at(z, t_r, n_r, m, lanes)
                k = (e_r[rows, lanes].astype(F32) - centre) * inverse
                h = do_r[rows, lanes] * spread(z, gate_r[at, lanes]) + spread(z, du_r[at, lanes])
                h = h * mask_r[rows, 0:1]
                h_r[rows, lanes] = h
                a, b = fold_sums(h, h * k)
                s_r[2 * m : 2 * m + 1, lanes] = a
                s_r[2 * m + 1 : 2 * m + 2, lanes] = b

    maps = (z.micro, z.half, z.held, z.half)
    return run(
        body,
        [
            Raw(final, BF16),
            Raw(maps + (span,), BF16),
            ((z.coarse, z.out), F32),
            Near(((z.coarse, z.out), F32)),
            ((z.maps, z.out), F32),
            ((z.maps, z.hid), F32),
            ((z.maps, z.out), F32),
            ((z.maps, z.hid), F32),
            Near(((2 * z.micro + 2, z.out), F32)),
        ],
        (place, Near(sums), counted, vectors, pix, e2, middle, up, squeeze, sq_bias, excite, mask),
        room=ROOM,
        ahead=ahead,
        scratch=[
            pltpu.VMEM(maps + (z.out,), BF16),
            pltpu.VMEM((z.maps, z.out), F32),
            pltpu.VMEM((z.maps, z.out), F32),
        ],
        spare=2,
    )


def wide_back(z, n_r, m, lanes, total_r, back_r, first, gain, e, h):
    centre, inverse = norms_at(z, total_r, n_r, m, lanes, first)
    k = (e - centre) * inverse
    at = first + 2 * m
    mean = back_r[at : at + 1, lanes] / n_r[z.micro + m]
    slope = back_r[at + 1 : at + 2, lanes] / n_r[z.micro + m]
    return (h - (mean + k * slope)) * (gain * inverse)


def unexpand_kernel(z, place, back, total, counted, vectors, row, e, h, w, total_n, vec_n, conv, mask, ahead):
    span = z.out // 2
    groups = back.shape[0] // (2 * z.micro)

    def body(
        io, place_r, b_r, t_r, n_r, vec_r, e_r, h_r, w_r, tn_r, vn_r, c_r, mask_r,
        de_r, live_r, s_r, *small_r,
    ):
        lanes = pl.ds(pl.multiple_of(place_r[0] * span, span), span)
        own = b_r[:, lanes]
        for g in range(groups):
            gains_out(own[2 * z.micro * g :], z.micro, small_r[2 * g], small_r[2 * g + 1])
        flat_row(own[2 * z.micro * groups : 2 * z.micro * groups + 1], small_r[-2])
        small_r[-1][...] = b_r[2 * z.micro * groups + 1 : 2 * z.micro * groups + 2, : z.hid]
        io.send(*small_r)

        @pl.loop(0, z.out // LANES, unroll=8)
        def _(j):
            lanes = pl.ds(pl.multiple_of(j * LANES, LANES), LANES)
            for m in range(z.micro):
                rows = slice(m * z.map, (m + 1) * z.map)
                h = h_r[rows, lanes]
                e = e_r[rows, lanes].astype(F32)
                d = wide_back(z, n_r, m, lanes, t_r, b_r, 0, vec_r[row : row + 1, lanes], e, h)
                de_r[rows, lanes] = (d * mask_r[rows, 0:1]).astype(BF16)

        io.send(de_r)
        io.need(w_r)
        da = dot_nt(de_r[...], w_r[...])
        norms = norm_rows(tn_r[...], counts_of(z, n_r, 1), z.micro)
        sums = []
        for m in range(z.micro):
            rows = slice(m * z.map, (m + 1) * z.map)
            centre, inverse = norms[m]
            k = (c_r[rows, :] - centre) * inverse
            v = (k * vn_r[0:1] + vn_r[1:2]) * mask_r[rows, 0:1]
            h = da[rows] * slope_of(v) * mask_r[rows, 0:1]
            live_r[rows, :] = h
            sums += fold_sums(h, h * k)
        to_all(z, sums, s_r)

    return run(
        body,
        [
            ((z.coarse, z.out), BF16),
            Near(((z.coarse, z.mid), F32)),
            Near(((2 * z.micro, z.mid), F32)),
            *([flat_of(span)] * (2 * groups + 1)),
            ((1, z.hid), F32),
        ],
        (place, Near(back), total, counted, vectors, e, h, w, total_n, vec_n, conv, mask),
        ahead=ahead,
        flops=2 * z.coarse * z.out * z.mid,
    )


def narrow_back(m, norms, back, counted, gain, conv, live, mask):
    centre, inverse = norms[m]
    k = (conv - centre) * inverse
    mean = back[2 * m : 2 * m + 1] / counted[m]
    slope = back[2 * m + 1 : 2 * m + 2] / counted[m]
    return (live - (mean + k * slope)) * (gain * inverse) * mask


def untap_kernel(z, place, back, total, counted, vec, conv, live, w, total_n, vec_n, conv_n, mask, strided, ahead):
    planes = 4 if strided else 1

    def body(io, place_r, b_r, t_r, n_r, vec_r, c_r, h_r, w_r, tn_r, vn_r, cn_r, mask_r, dc_r, live_r, gain_r, bias_r, s_r, tap_r):
        counted = counts_of(z, n_r, 1)
        back = b_r[...]
        gains_out(back, z.micro, gain_r, bias_r)
        io.send(gain_r, bias_r)
        norms = norm_rows(t_r[...], counted, z.micro)
        taps = ((0, 0), (1, 1)) if strided else ((0, 1), (1, 0), (2, -1))
        for m in range(z.micro):
            rows = slice(m * z.map, (m + 1) * z.map)
            d = narrow_back(
                m, norms, back, counted, vec_r[0:1], c_r[rows, :], h_r[rows, :], mask_r[rows, 0:1]
            )
            dc_r[rows, :] = d.astype(BF16)
            for lane in range(0, z.mid, LANES):
                place_patches(
                    d[:, lane : lane + LANES], taps, taps, tap_r, m * z.map, lane, z.mid, z.group
                )
        io.send(dc_r)
        norms = norm_rows(tn_r[...], counts_of(z, n_r, 0 if strided else 1), z.micro)
        acc = [[None, None] for _ in range(z.micro)]
        io.need(w_r, cn_r)
        for p in range(planes):
            da = None
            if strided:
                terms = [
                    (3 * i + j, 3 * rs + cs)
                    for i, rs in PLANE_TAPS[p // 2]
                    for j, cs in PLANE_TAPS[p % 2]
                ]
            else:
                terms = [(t, t) for t in range(9)]
            for t, slot in terms:
                part = dot_nt(
                    tap_r[:, slot * z.mid : (slot + 1) * z.mid], w_r[t * z.mid : (t + 1) * z.mid, :]
                )
                da = part if da is None else da + part
            for m in range(z.micro):
                rows = slice(m * z.map, (m + 1) * z.map)
                at = (p * z.micro + m) * z.map
                centre, inverse = norms[m]
                k = (cn_r[at : at + z.map, :] - centre) * inverse
                v = (k * vn_r[0:1] + vn_r[1:2]) * mask_r[rows, 0:1]
                h = da[rows] * slope_of(v) * mask_r[rows, 0:1]
                live_r[at : at + z.map, :] = h
                a, b = fold_sums(h, h * k)
                acc[m] = [a, b] if p == 0 else [acc[m][0] + a, acc[m][1] + b]
        to_all(z, [row for pair in acc for row in pair], s_r)

    return run(
        body,
        [
            ((z.coarse, z.mid), BF16),
            Near(((planes * z.coarse, z.mid), F32)),
            flat_of(z.mid),
            flat_of(z.mid),
            Near(((2 * z.micro, z.mid), F32)),
        ],
        (place, Near(back), total, counted, vec, conv, live, w, total_n, vec_n, conv_n, mask),
        ahead=ahead,
        scratch=[pltpu.VMEM((z.coarse, 9 * z.mid), BF16)],
        flops=2 * z.coarse * 9 * z.mid * z.mid,
    )


def unreduce_kernel(
    z, place, back, total, counted, vec, conv, live, w, do2, total_w, vectors, gate, inner, e1, p1, squeeze, excite, pix, mask, ahead
):
    side = 2 * z.micro

    def body(
        io, place_r, b_r, t_r, n_r, vec_r, c_r, h_r, w_r, do2_r, tw_r, vw_r, gate_r, in_r, e_r, p_r, sq_r, ex_r, pix_r, mask_r,
        dc_r, do_r, wide_r, gain_r, bias_r, dl_r, dz_r, s_r, du_r,
    ):
        counted = counts_of(z, n_r, 1)
        back = b_r[...]
        gains_out(back, z.micro, gain_r, bias_r)
        norms = norm_rows(t_r[...], counted, z.micro)
        for m in range(z.micro):
            rows = slice(m * z.map, (m + 1) * z.map)
            d = narrow_back(
                m, norms, back, counted, vec_r[0:1], c_r[rows, :], h_r[rows, :], mask_r[rows, 0:1]
            )
            dc_r[rows, :] = d.astype(BF16)
        io.send(gain_r, bias_r, dc_r)
        io.need(w_r, do2_r, e_r, p_r)

        @pl.loop(0, z.out // 256, unroll=2)
        def _(j):
            wide_lanes = pl.ds(pl.multiple_of(j * 256, 256), 256)
            dm = dot_nt(dc_r[...], w_r[wide_lanes, :])
            for i in range(2):
                lanes = pl.ds(pl.multiple_of(j * 256 + i * LANES, LANES), LANES)
                for m in range(z.micro):
                    rows = slice(m * z.map, (m + 1) * z.map)
                    at = slice(m * z.held, (m + 1) * z.held)
                    live = mask_r[rows, 0:1]
                    centre, inverse = norms_at(z, tw_r, n_r, m, lanes)
                    k = (e_r[rows, lanes].astype(F32) - centre) * inverse
                    q = (k * vw_r[0:1, lanes] + vw_r[1:2, lanes]) * live
                    centre, inverse = norms_at(z, tw_r, n_r, m, lanes, side)
                    kp = (p_r[rows, lanes].astype(F32) - centre) * inverse
                    t = (kp * vw_r[2:3, lanes] + vw_r[3:4, lanes]) * live
                    o = q * spread(z, gate_r[at, lanes]) + t
                    d = (dm[rows, i * LANES : (i + 1) * LANES] + do2_r[rows, lanes]) * slope_of(o)
                    do_r[rows, lanes] = d
                    dl_r[at, lanes] = map_sums(z, d * q)
                    d = d * live
                    a, b = fold_sums(d, d * kp)
                    s_r[side + 2 * m : side + 2 * m + 1, lanes] = a
                    s_r[side + 2 * m + 1 : side + 2 * m + 2, lanes] = b

        io.send(do_r)
        io.need(sq_r, ex_r)
        dl, dz, du = gate_back(dl_r[...], gate_r[...], in_r[...], sq_r, ex_r, pix_r[:, 0:1])
        dl_r[...] = dl
        dz_r[...] = dz
        du_r[...] = du
        io.send(dl_r, dz_r)
        bias_sums(z, dl, dz, s_r, 2 * side)

        @pl.loop(0, z.out // LANES, unroll=8)
        def _(j):
            lanes = pl.ds(pl.multiple_of(j * LANES, LANES), LANES)
            for m in range(z.micro):
                rows = slice(m * z.map, (m + 1) * z.map)
                at = slice(m * z.held, (m + 1) * z.held)
                centre, inverse = norms_at(z, tw_r, n_r, m, lanes)
                k = (e_r[rows, lanes].astype(F32) - centre) * inverse
                h = do_r[rows, lanes] * spread(z, gate_r[at, lanes]) + spread(z, du_r[at, lanes])
                h = h * mask_r[rows, 0:1]
                wide_r[rows, lanes] = h
                a, b = fold_sums(h, h * k)
                s_r[2 * m : 2 * m + 1, lanes] = a
                s_r[2 * m + 1 : 2 * m + 2, lanes] = b

    return run(
        body,
        [
            ((z.coarse, z.mid), BF16),
            ((z.coarse, z.out), F32),
            Near(((z.coarse, z.out), F32)),
            flat_of(z.mid),
            flat_of(z.mid),
            ((z.maps, z.out), F32),
            ((z.maps, z.hid), F32),
            Near(((2 * side + 2, z.out), F32)),
        ],
        (
            place, Near(back), total, counted, vec, conv, live, w, do2, total_w, vectors, gate, inner,
            e1, p1, squeeze, excite, pix, mask,
        ),
        scratch=[pltpu.VMEM((z.maps, z.out), F32)],
        ahead=ahead,
        flops=2 * z.coarse * z.out * z.mid,
    )


def side_kernel(z, place, back, total, counted, vectors, p1, do, mask):
    def body(io, place_r, b_r, t_r, n_r, vec_r, p_r, do_r, mask_r, dp_r):
        @pl.loop(0, z.out // LANES, unroll=8)
        def _(j):
            lanes = pl.ds(pl.multiple_of(j * LANES, LANES), LANES)
            for m in range(z.micro):
                rows = slice(m * z.map, (m + 1) * z.map)
                p = p_r[rows, lanes].astype(F32)
                h = do_r[rows, lanes]
                d = wide_back(z, n_r, m, lanes, t_r, b_r, 2 * z.micro, vec_r[2:3, lanes], p, h)
                dp_r[rows, lanes] = (d * mask_r[rows, 0:1]).astype(BF16)

    return run(
        body,
        [((z.coarse, z.out), BF16)],
        (place, back, total, counted, vectors, p1, do, mask),
    )[0]


def leave_kernel(z, place, back, total, counted, vec, conv, live, w_one, dp, w_side, perm, mask, final):
    block = 2 * z.map
    maps = (z.half, z.held, z.side)

    def body(
        io, place_r, b_r, t_r, n_r, vec_r, c_r, h_r, w_r, dp_r, ws_r, perm_r, mask_r,
        dc_r, final_r, away_r, gain_r, bias_r, keep_r, grad_r,
    ):
        core = place_r[0]
        counted = counts_of(z, n_r, 0)
        back = b_r[...]
        gains_out(back, z.micro, gain_r, bias_r)
        norms = norm_rows(t_r[...], counted, z.micro)
        for m in range(z.micro):
            for p in range(4):
                at = (p * z.micro + m) * z.map
                rows = slice(at, at + z.map)
                d = narrow_back(
                    m, norms, back, counted, vec_r[0:1], c_r[rows, :], h_r[rows, :],
                    mask_r[m * z.map : (m + 1) * z.map, 0:1],
                )
                dc_r[rows, :] = d.astype(BF16)
        io.send(dc_r)
        io.need(w_r, dp_r, ws_r)
        rows = z.map // 2
        sides = dot_nt(dp_r[...], ws_r[...])
        for m in range(z.micro):
            side = sides[m * z.map : (m + 1) * z.map]
            for half in range(2):
                stacked = jnp.concatenate(
                    [
                        dc_r[(p * z.micro + m) * z.map + half * rows : (p * z.micro + m) * z.map + (half + 1) * rows, :]
                        for p in range(4)
                    ],
                    axis=0,
                )
                ordered = dot_tn(perm_r[...], stacked).astype(BF16)
                grad = dot_nt(ordered, w_r[...])
                for n in range(z.cin // LANES):
                    lanes = slice(n * LANES, (n + 1) * LANES)
                    grad_r[n] = grad[:, lanes]
                    for o in range(z.half // 2):
                        for b in range(z.held):
                            at = 2 * o * z.held * z.side + b * z.side
                            src = half * rows + (o * z.held + b) * z.half
                            spots = pl.ds(at, z.half, stride=2)
                            grad_r[n, spots, :] = grad_r[n, spots, :] + side[src : src + z.half, lanes]

                @pl.when(core == half)
                def _():
                    for n in range(z.cin // LANES):
                        keep_r[m, :, :, :, n * LANES : (n + 1) * LANES] = grad_r[n].reshape(maps + (LANES,))

                @pl.when(core != half)
                def _():
                    for n in range(z.cin // LANES):
                        away_r[m, :, n * LANES : (n + 1) * LANES] = grad_r[n].astype(BF16)

            io.out(keep_r.at[m], final_r.at[m, :, pl.ds(core * z.held, z.held)])

    return run(
        body,
        [
            ((z.fine, z.mid), BF16),
            Raw(final, F32),
            ((z.micro, block, z.cin), BF16),
            flat_of(z.mid),
            flat_of(z.mid),
        ],
        (place, Near(back), total, counted, vec, conv, live, w_one, dp, w_side, perm, mask),
        scratch=[
            pltpu.VMEM((z.micro,) + maps + (z.cin,), F32),
            pltpu.VMEM((z.cin // LANES, block, LANES), F32),
        ],
        spare=z.micro,
        flops=2 * z.fine * z.cin * z.mid,
    )


def finish_images(z, place, got, final):
    maps = (z.half, z.held, z.side)

    def body(place_r, got_r, _, final_r, in_r, out_r, sems):
        other = 1 - place_r[0]
        loads = [pltpu.make_async_copy(got_r.at[m], in_r.at[m], sems.at[m]) for m in range(z.micro)]
        stores = [
            pltpu.make_async_copy(
                out_r.at[m], final_r.at[m, :, pl.ds(other * z.held, z.held)], sems.at[z.micro + m]
            )
            for m in range(z.micro)
        ]
        for copy in loads:
            copy.start()
        for m in range(z.micro):
            loads[m].wait()
            out_r[m] = in_r[m].astype(F32).reshape(maps + (z.cin,))
            stores[m].start()
        for copy in stores:
            copy.wait()

    any_spec = pl.BlockSpec(memory_space=pl.ANY)
    return pl.pallas_call(
        body,
        out_shape=jax.ShapeDtypeStruct(final.shape, final.dtype),
        in_specs=[pl.BlockSpec(memory_space=pltpu.SMEM), any_spec, any_spec],
        out_specs=any_spec,
        input_output_aliases={2: 0},
        scratch_shapes=[
            pltpu.VMEM(got.shape, got.dtype),
            pltpu.VMEM((z.micro,) + maps + (z.cin,), F32),
            pltpu.SemaphoreType.DMA((2 * z.micro,)),
        ],
        compiler_params=pltpu.CompilerParams(vmem_limit_bytes=5 << 20),
    )(place, got, final)


def finish_output(z, place, got, final):
    def body(place_r, got_r, _, final_r, buf_r, sems):
        other = 1 - place_r[0]
        copy = pltpu.make_async_copy(got_r, buf_r, sems.at[0])
        copy.start()
        copy.wait()
        copy = pltpu.make_async_copy(buf_r, final_r.at[:, :, pl.ds(other * z.held, z.held)], sems.at[1])
        copy.start()
        copy.wait()

    any_spec = pl.BlockSpec(memory_space=pl.ANY)
    return pl.pallas_call(
        body,
        out_shape=jax.ShapeDtypeStruct(final.shape, final.dtype),
        in_specs=[pl.BlockSpec(memory_space=pltpu.SMEM), any_spec, any_spec],
        out_specs=any_spec,
        input_output_aliases={2: 0},
        scratch_shapes=[pltpu.VMEM(got.shape, got.dtype), pltpu.SemaphoreType.DMA((2,))],
        compiler_params=pltpu.CompilerParams(vmem_limit_bytes=2 << 20),
    )(place, got, final)


def gradient_kernel(z, place, size, jobs, args):
    starts, at = [], 0
    for kind, i, j in jobs:
        starts.append(at)
        at += args[i].shape[1] * args[j].shape[1] // (2 * size * 512)
    height = at

    def body(io, place_r, *refs):
        out_r = refs[-1]
        refs = refs[:-1]
        core, me = place_r[0], place_r[1]

        def put(c, b, first, length, values):
            p = b ^ me
            p = p // 4 * 4 + p % 2 * 2 + p // 2 % 2 if c else p
            out_r[c ^ core, p, first : first + length, :] = values

        for (kind, i, j), start in zip(jobs, starts):
            lhs, rhs = refs[i], refs[j]
            io.need(lhs, rhs)
            k, n = lhs.shape[1], rhs.shape[1]
            if kind == "flat":
                per = k // (2 * size)
                for r in range(0, k, 512):
                    for c in range(0, n, 512):
                        d = dot_tn(lhs[: rhs.shape[0], r : r + 512], rhs[:, c : c + 512]).astype(BF16)
                        at = r
                        while at < r + 512:
                            chunk, inside = divmod(at, per)
                            length = min(per - inside, r + 512 - at)
                            first = start + (c // 512) * per + inside
                            put(chunk % 2, chunk // 2, first, length, d[at - r : at - r + length])
                            at += length
            elif kind == "rows" and n == 512:
                per = k // (2 * size)
                for r in range(0, k, 512):
                    d = dot_tn(lhs[:, r : r + 512], rhs[...]).astype(BF16)
                    for at in range(r, r + 512, per):
                        c, b = divmod(at // per, size)
                        put(c, b, start, per, d[at - r : at - r + per])
            elif kind == "rows":
                per = k // (2 * size)
                d = dot_tn(lhs[...].astype(BF16), rhs[...].astype(BF16)).astype(BF16)
                parts = 512 // n
                unit = per // parts
                for at in range(0, k, per):
                    c, b = divmod(at // per, size)
                    rows = [d[at + q * unit : at + (q + 1) * unit] for q in range(parts)]
                    put(c, b, start, unit, jnp.concatenate(rows, axis=1))
            else:
                d = dot_tn(lhs[...].astype(BF16), rhs[...].astype(BF16)).astype(BF16)
                across = n // 1024
                per = k * across // size
                for c in range(2):
                    for b in range(size):
                        r, lane = divmod(b, across)
                        first = c * (n // 2) + lane * 512
                        put(c, b, start, per, d[r * per : (r + 1) * per, first : first + 512])
    return body, height, starts


def gradients(z, place, size, jobs, args):
    body, height, starts = gradient_kernel(z, place, size, jobs, args)

    def outer(io, place_r, *refs):
        ins, (keep_r, send_r, both_r) = refs[:-3], refs[-3:]
        body(io, place_r, *ins, both_r)
        io.out(both_r.at[1], send_r)
        io.out(both_r.at[0], keep_r)

    shape = (size, height, 512)
    keep, send = run(
        outer,
        [Near((shape, BF16))] * 2,
        (place, *(Late(a) for a in args)),
        scratch=[pltpu.VMEM((2,) + shape, BF16)],
        spare=2,
    )
    return keep, send, starts


def part_kernel(sources, spans):
    count = sources[0][0].shape[0]
    outs = []
    for _, length, bit in spans:
        if bit:
            outs += [Near(((count // 2, length, 512), BF16))] * 2
        else:
            outs += [Near(((length, 512), BF16))] * count

    def body(io, *refs):
        ins, results = refs[: 2 * len(sources)], list(refs[2 * len(sources) :])
        pairs, at = [], 0
        for k in range(len(sources)):
            kept, come = ins[2 * k], ins[2 * k + 1]
            io.need(kept, come)
            pairs.append((at, at + kept.shape[1], kept, come))
            at += kept.shape[1]

        def pieces(first, length):
            for low, high, kept, come in pairs:
                start, stop = max(first, low), min(first + length, high)
                if start < stop:
                    yield start - first, slice(start - low, stop - low), kept, come

        for first, length, bit in spans:
            if not bit:
                for p in range(count):
                    ref = results.pop(0)
                    for to, rows, kept, come in pieces(first, length):
                        total = kept[p, rows].astype(F32) + come[p, rows].astype(F32)
                        ref[to : to + rows.stop - rows.start, :] = total.astype(BF16)
                continue
            kept_r, sent_r = results.pop(0), results.pop(0)
            for which, ref in ((1, sent_r), (0, kept_r)):
                for p in range(count):
                    if (p // bit) % 2 == which:
                        at = p // (2 * bit) * bit + p % bit
                        for to, rows, kept, come in pieces(first, length):
                            size = rows.stop - rows.start
                            total = kept[p, rows].astype(F32) + come[p, rows].astype(F32)
                            ref[at, to : to + size, :] = total.astype(BF16)

    return run(body, outs, [Near(a) for pair in sources for a in pair])


def second_step(kept, come, narrow):
    count, height = kept.shape[0] // 2, kept.shape[1]
    rows = narrow[0].shape[0]

    def body(io, a, b, *refs):
        *blocks, kept_r, sent_r = refs
        for p in range(count):
            total = a[2 * p + 1].astype(F32) + b[2 * p + 1].astype(F32)
            sent_r[p, :height, :] = total.astype(BF16)
            sent_r[p, height:, :] = blocks[p][...]
        for p in range(count):
            kept_r[p] = (a[2 * p].astype(F32) + b[2 * p].astype(F32)).astype(BF16)

    outs = [Near(((count, height, 512), BF16)), Near(((count, height + rows, 512), BF16))]
    return run(body, outs, [Near(a) for a in (kept, come, *narrow)])


def third_step(kept, come, narrow):
    count, height = kept.shape[0], kept.shape[1]
    rows = narrow[0].shape[0]

    def body(io, a, b, *refs):
        blocks, outs, part_r = refs[:count], refs[count : 2 * count], refs[2 * count]
        for p in reversed(range(count)):
            total = a[p].astype(F32) + b[p, :height].astype(F32)
            outs[p][...] = total.astype(BF16)
        for p in range(count):
            part_r[p] = blocks[p][...]
            part_r[count + p] = b[p, height:]

    outs = [Near(((height, 512), BF16))] * count + [Near(((2 * count, rows, 512), BF16))]
    return run(body, outs, [Near(a) for a in (kept, come, *narrow)])


def total_kernel(blocks, grads=None):
    shape = blocks[0].shape

    def body(io, *refs):
        ins, outs = refs[: len(blocks)], refs[len(blocks) :]
        if grads is None:
            outs[0][...] = tree_sum([ref[...].astype(F32) for ref in ins])
            return
        first = 0
        for out_r, (rows, width) in zip(outs, grads):
            height = rows * 512 // width
            for part in range(width // 512):
                at = first + part * height
                total = tree_sum([ref[at : at + height, :].astype(F32) for ref in ins])
                for k in range(512 // LANES):
                    spots = pl.ds(part * (512 // LANES) + k, height, stride=width // LANES)
                    out_r[spots, :] = total[:, k * LANES : (k + 1) * LANES]
            first += rows

    if grads is None:
        return run(body, [(shape, F32)], [Near(b) for b in blocks])[0]
    outs = [((rows * 512 // LANES, LANES), F32) for rows, _ in grads]
    return [flat.reshape(-1) for flat in run(body, outs, [Near(b) for b in blocks])]


def crossed(block, first, second):
    count = 2 * lax.axis_size("batch")
    route = [(i, (i // 2 ^ (second if i % 2 else first)) * 2 + i % 2) for i in range(count)]
    return lax.ppermute(block, ("batch", "rows"), route)


class Halving:
    def __init__(self, blocks):
        self.height = sum(keep.shape[1] for keep, _ in blocks)
        self.sources = blocks
        self.step = 0

    def prepare(self, *after):
        (kept, came), *others = self.sources
        bit = 1 if self.step < 2 else 0
        self.kept, *self.sent = part_kernel(
            [(tied(kept, *after), came), *others], ((0, self.height, bit),)
        )
        return self.sent[0]

    def send(self, *after):
        sent = [tied(s, *after) for s in self.sent]
        if self.step == 2:
            came = [swapped(s, "batch", 4 * (k + 1)) for k, s in enumerate(sent)]
            self.blocks = [self.kept] + came
        else:
            came = [crossed(sent[0], self.step + 1, 2 - self.step)]
            self.sources = [(self.kept, came[0])]
        self.step += 1
        return came

    def finish(self, grads):
        return total_kernel(self.blocks, grads)


def N(array):
    return Near(array)


def tied(value, *others):
    return lax.optimization_barrier((value, *others))[0] if others else value


def gathered_kernel(z, place, size, blocks, starts):
    across = z.out // 1024
    unit = z.out // 2 // size
    parts = 512 // z.hid
    tall = unit // parts
    wide = z.hid * across // size
    height = blocks[0].shape[1]

    def body(io, place_r, near_r, far_r, red_r, sqb_r, exb_r, sqa_r, exa_r, all_r):
        core, me = place_r[0], place_r[1]
        for high, ref in ((0, near_r), (1, far_r)):
            for low in range(2):
                for k in range(size // 4):
                    p = 4 * k + 2 * low + high + core * (high - low)
                    all_r[p] = ref[low * (size // 4) + k]

        def rows(p, first, length):
            return all_r[p, first : first + length].astype(F32)

        for b in range(size):
            p = b ^ me
            red_r[b * unit : (b + 1) * unit, :] = rows(p, starts[0], unit)
            for at, ref in ((starts[1], sqb_r), (starts[3], sqa_r)):
                block = rows(p, at, tall)
                for q in range(parts):
                    ref[b * unit + q * tall : b * unit + (q + 1) * tall, :] = block[:, q * z.hid : (q + 1) * z.hid]
            r, lane = divmod(b, across)
            for at, ref in ((starts[2], exb_r), (starts[4], exa_r)):
                ref[r * wide : (r + 1) * wide, lane * 512 : (lane + 1) * 512] = rows(p, at, wide)

    half = z.out // 2
    return run(
        body,
        [
            ((half, z.mid), F32),
            ((half, z.hid), F32),
            ((z.hid, half), F32),
            ((half, z.hid), F32),
            ((z.hid, half), F32),
        ],
        (place, *(Near(b) for b in blocks)),
        scratch=[pltpu.VMEM((size, height, 512), BF16)],
    )


def weight_dot(inputs, grads):
    return lax.dot_general(inputs, grads, (((0,), (0,)), ((), ())), preferred_element_type=F32)


def folded(grad):
    size = lax.axis_size("batch")
    rows, width = grad.shape
    grad = grad.astype(BF16).reshape(size, 2, rows // (2 * size), width // 512, 512)
    return jnp.swapaxes(grad, 2, 3).reshape(size, 2, -1, 512)


def unfolded(block, width):
    count = width // 512
    rows = block.shape[0] // count
    return jnp.swapaxes(block.reshape(count, rows, 512), 0, 1).reshape(-1)


def tree_sum(terms):
    while len(terms) > 1:
        terms = [a + b for a, b in zip(terms[::2], terms[1::2])] + terms[len(terms) // 2 * 2 :]
    return terms[0]


def wide_sum(parts, first=(), second=(), kind=F32):
    parts = parts.astype(kind)
    parts = parts.astype(F32) + swapped(parts, "rows", 1).astype(F32)
    bits = bits_of(lax.axis_size("batch"))
    partial = parts
    for at in range(0, len(bits), 2):
        parts = tied(parts, *(first if at == 0 else second if at == 2 else ()))
        pair = bits[at : at + 2]
        masks = [pair[0], pair[1], pair[0] + pair[1]] if len(pair) == 2 else pair
        parts = parts.astype(kind)
        terms = [parts] + [swapped(parts, "batch", mask) for mask in masks]
        parts = tree_sum([term.astype(F32) for term in terms])
        partial = parts if at == 0 else partial
    return parts, partial


def plain_gradients(jobs, size):
    blocks, starts, at = [], [], 0
    for kind, lhs, rhs in jobs:
        grad = weight_dot(lhs[: rhs.shape[0]].astype(BF16), rhs.astype(BF16))
        k, n = grad.shape
        if kind == "flat":
            block = core_sum(folded(grad), 1)
        elif kind == "rows" and n == 512:
            block = core_sum(grad.astype(BF16).reshape(2, size, -1, 512), 0)
        elif kind == "rows":
            parts = 512 // n
            block = grad.astype(BF16).reshape(2, size, parts, -1, n)
            block = core_sum(jnp.swapaxes(block, 2, 3).reshape(2, size, -1, 512), 0)
        else:
            across = n // 1024
            block = grad.astype(BF16).reshape(size // across, -1, 2, across, 512)
            block = core_sum(block.transpose(2, 0, 3, 1, 4).reshape(2, size, -1, 512), 0)
        starts.append(at)
        at += block.shape[1]
        blocks.append(block)
    return halved(jnp.concatenate(blocks, axis=1), two_orders), starts


def per_device(
    images,
    crop_sizes,
    reduce_a,
    reduce_gain_a,
    reduce_bias_a,
    spatial_a,
    spatial_gain_a,
    spatial_bias_a,
    expand_a,
    expand_gain_a,
    expand_bias_a,
    project_a,
    project_gain_a,
    project_bias_a,
    squeeze_a,
    squeeze_bias_a,
    excite_a,
    excite_bias_a,
    reduce_b,
    reduce_gain_b,
    reduce_bias_b,
    spatial_b,
    spatial_gain_b,
    spatial_bias_b,
    expand_b,
    expand_gain_b,
    expand_bias_b,
    squeeze_b,
    squeeze_bias_b,
    excite_b,
    excite_bias_b,
    cotangent,
):
    mid = reduce_a.shape[1]
    out = expand_a.shape[1]
    hid = squeeze_a.shape[1]
    size = lax.axis_size("batch")
    z = Sizes(images, mid, out, hid, size * lax.axis_size("rows"))
    micro, held, side, half = z.micro, z.held, z.side, z.half
    core = lax.axis_index("rows")
    me = lax.axis_index("batch")
    place = jnp.stack([core, me]).astype(jnp.int32)

    away = lax.dynamic_slice_in_dim(images, (1 - core) * held, held, axis=2)
    other = swapped(away, "rows", 1)
    vectors = jnp.stack(
        [
            expand_gain_a,
            expand_bias_a,
            project_gain_a,
            project_bias_a,
            expand_gain_b,
            expand_bias_b,
            excite_bias_a,
            excite_bias_b,
        ]
    )

    def pair(own, axis):
        return Pair(own, swapped(own, "rows", 1), axis)

    vectors = pair(vectors, 1)
    pair_sq_a, pair_sq_b = pair(squeeze_a, 0), pair(squeeze_b, 0)
    pair_ex_a, pair_ex_b = pair(excite_a, 1), pair(excite_b, 1)
    pair_red = pair(reduce_b, 0)
    sq_biases = jnp.stack([squeeze_bias_a, squeeze_bias_b])
    vec_one = jnp.stack([reduce_gain_a, reduce_bias_a])
    vec_two = jnp.stack([spatial_gain_a, spatial_bias_a])
    vec_four = jnp.stack([reduce_gain_b, reduce_bias_b])
    vec_five = jnp.stack([spatial_gain_b, spatial_bias_b])

    half_all = crop_sizes // 2
    counted = jnp.stack(
        [jnp.sum(crop_sizes * crop_sizes, axis=1), jnp.sum(half_all * half_all, axis=1)]
    ).astype(F32).reshape(-1)
    halves = lax.dynamic_slice_in_dim(half_all, (me * 2 + core) * held, held, axis=1)
    pix = jnp.broadcast_to((halves * halves).astype(F32).reshape(-1, 1), (z.maps, LANES))
    spots = jnp.arange(half, dtype=jnp.int32)
    limits = halves[:, None, :, None]
    inside = (spots[None, :, None, None] < limits) & (spots[None, None, None, :] < limits)
    mask = jnp.broadcast_to(inside.astype(F32).reshape(z.coarse, 1), (z.coarse, LANES))

    block = 2 * z.map
    spot = jnp.arange(block, dtype=jnp.int32)
    row_pair, rest = spot // (2 * z.group), spot % (2 * z.group)
    row_odd, spot_b, column = spot // (held * side) % 2, spot % (held * side) // side, spot % side
    row_pair = spot // (2 * held * side)
    target = ((row_odd * 2 + column % 2) * (half // 2) + row_pair) * z.group
    target = target + spot_b * half + column // 2
    perm = (target[None, :] == jnp.arange(block, dtype=jnp.int32)[:, None]).astype(BF16)

    other, perm, mask, pix, counted, sq_biases, vec_one, vec_two, vec_four, vec_five, vectors.own = (
        lax.optimization_barrier(
            (other, perm, mask, pix, counted, sq_biases, vec_one, vec_two, vec_four, vec_five, vectors.own)
        )
    )
    vectors.other = swapped(vectors.own, "rows", 1)

    first_one, first_perm, first_mask, first_images = run(
        lambda io, place_r: None, [], (place,), ahead=(reduce_a, perm, mask, Part(images, 2)), room=ROOM
    )
    planes, c1_near, c1, s1, *got = enter_kernel(
        z, place, N(first_images), N(other), N(first_perm), N(first_one), N(first_mask),
        (vec_one, spatial_a, mask),
    )
    vec_near, w_near, mask_near = map(N, got)
    patches_one, c2_near, c2, t1, s2, *got = taps_kernel(
        z, place, wide_sum(s1)[0], counted, vec_near, N(c1_near), w_near, mask_near, True,
        (vec_two, expand_a, mask, Top(planes, z.coarse), project_a, Away(cotangent, 2)),
    )
    vec_near, w_near, mask_near, *side_near = map(N, got[:5])
    up = Join(cotangent, 2, swapped(got[5], "rows", 1), 4)
    active_two, e1_near, e1, t2, p1_near, p1, s3, *got = expand_kernel(
        z, place, wide_sum(s2)[0], counted, vec_near, N(c2_near), w_near, mask_near, side_near,
        (vectors, pix, pair_sq_a, sq_biases, pair_ex_a, pair_red, mask),
    )
    vectors_near, pix_near, sq_near, sqb_near, ex_near, w_near, mask_near = map(N, got)
    sums_three, _ = wide_sum(s3)
    middle, c4_near, c4, gate_one, pool_one, inner_one, hidden_one, total_three, s4, *got = middle_kernel(
        z, place, sums_three, counted, vectors_near, pix_near, N(e1_near), N(p1_near), sq_near, sqb_near, ex_near,
        w_near, mask_near, (vec_four, spatial_b, mask),
    )
    vec_near, w_near, mask_near = map(N, got)
    patches_four, c5_near, c5, t4, s5, *got = taps_kernel(
        z, place, wide_sum(s4)[0], counted, vec_near, N(c4_near), w_near, mask_near, False,
        (vec_five, expand_b, mask),
    )
    vec_near, w_near, mask_near = map(N, got)
    active_five, e2_near, e2, t5, s6, *got = expand_kernel(
        z, place, wide_sum(s5)[0], counted, vec_near, N(c5_near), w_near, mask_near, None,
        (vectors, pix, middle, up, pair_sq_b, sq_biases, pair_ex_b, mask),
    )
    vectors_near, pix_near, mid_near, up_near, sq_near, sqb_near, ex_near, mask_near = map(N, got)
    sums_six, _ = wide_sum(s6)
    final = (micro, half, 2 * held, half, out // 2)
    block_out, block_away, do2, h_near, pool_two, hidden_two, dl_two, dz_two, b6, *got = output_kernel(
        z, place, sums_six, counted, vectors_near, pix_near, N(e2_near), mid_near, up_near,
        sq_near, sqb_near, ex_near, mask_near, final,
        (N(sums_six), vectors, e2, expand_b, t5, vec_five, c5, mask),
    )
    total_near, vectors_near, e_near, w_near, tn_near, vn_near, cn_near, mask_near = map(N, got)

    whole_tiles = mid * 9 // (2 * size) % 16 == 0

    def made(jobs):
        if not whole_tiles:
            return None
        args, spec = [], []
        for kind, lhs, rhs in jobs:
            spec.append((kind, len(args), len(args) + 1))
            args += [lhs, rhs]
        keep, send, _ = gradients(z, place, size, spec, args)
        return keep, send

    def steps(make):
        return list(make()) if whole_tiles else []

    def exchanged(blocks, *after):
        keep, send = blocks
        return keep, swapped(tied(send, *after), "rows", 1)

    back_six, _ = wide_sum(b6, kind=BF16)
    de2, live_near, b5, gain_six, bias_six, ex_bias_two, sq_bias_two, *got = unexpand_kernel(
        z, place, back_six, total_near, counted, vectors_near, 4, e_near, N(h_near), w_near,
        tn_near, vn_near, cn_near, mask_near, (t5, vec_five, c5, spatial_b, t4, vec_four, c4, mask),
    )
    t_near, v_near, c_near, w_near, tn_near, vn_near, cn_near, mask_near = map(N, got)
    jobs_e = (("flat", active_five, de2),)
    made_e = made(jobs_e)
    block_out = finish_output(z, place, swapped(block_away, "rows", 1), block_out)
    back_five, _ = wide_sum(b5, (), [block_out, *steps(lambda: [made_e[0]])])
    dc5, live_near, g5, h5, b4, *got = untap_kernel(
        z, place, back_five, t_near, counted, v_near, c_near, N(live_near), w_near,
        tn_near, vn_near, cn_near, mask_near, False,
        (t4, vec_four, c4, pair_red, do2, total_three, vectors, gate_one, inner_one, e1, p1, pair_sq_a, pair_ex_a, pix, mask),
    )
    t_near, v_near, c_near, w_near, *rest_near = map(N, got)
    jobs_s = (("flat", patches_four, dc5),)
    made_s = made(jobs_s)
    if whole_tiles:
        sum_e = Halving([exchanged(made_e, back_five)])
        b4 = tied(b4, sum_e.sources[0][1])
    back_four, _ = wide_sum(b4, (), steps(lambda: [made_s[0], sum_e.prepare()]))
    came = steps(lambda: sum_e.send(back_four))
    dc4, do1, h_near, g4, h4, dl_one, dz_one, b3, *got = unreduce_kernel(
        z, place, back_four, t_near, counted, v_near, c_near, N(live_near), w_near, *rest_near,
        (total_three, vectors, e1, expand_a, t2, vec_two, c2, mask),
    )
    total_near, vectors_near, e_near, w_near, tn_near, vn_near, cn_near, mask_near = map(N, got)
    jobs_n = (
        ("rows", middle, dc4),
        ("rows", pool_two, dz_two),
        ("lanes", hidden_two, dl_two),
        ("rows", pool_one, dz_one),
        ("lanes", hidden_one, dl_one),
    )
    made_n = made(jobs_n)
    if whole_tiles:
        sum_s = Halving([exchanged(made_s, back_four)])
        came += [sum_s.sources[0][1]]
    back_three, _ = wide_sum(
        tied(b3, *came), (), steps(lambda: [made_n[0], sum_s.prepare(), sum_e.prepare()]), BF16
    )
    came = steps(lambda: sum_s.send(back_three) + sum_e.send(back_three))
    (
        de1, live_near, b2, gain_three, bias_three, gain_side, bias_side, ex_bias_one, sq_bias_one, *got
    ) = unexpand_kernel(
        z, place, back_three, total_near, counted, vectors_near, 0, e_near, N(h_near), w_near,
        tn_near, vn_near, cn_near, mask_near, (t2, vec_two, c2, spatial_a, t1, vec_one, c1, mask),
    )
    t_near, v_near, c_near, w_near, tn_near, vn_near, cn_near, mask_near = map(N, got)
    dp1 = side_kernel(z, place, N(back_three), total_three, counted, vectors, p1, do1, mask)
    jobs_w = (("flat", active_two, de1), ("flat", planes, dp1))
    made_w = made(jobs_w)
    if whole_tiles:
        sum_n = Halving([exchanged(made_n, back_three)])
        came += [made_w[0], sum_n.sources[0][1]]
    back_two, _ = wide_sum(
        tied(b2, dp1, *came), (), steps(lambda: [sum_n.prepare(), sum_s.prepare(), sum_e.prepare()])
    )
    came = steps(lambda: sum_n.send(back_two) + sum_e.send(back_two))
    dc2, live_near, g2, h2, b1, *got = untap_kernel(
        z, place, back_two, t_near, counted, v_near, c_near, N(live_near), w_near,
        tn_near, vn_near, cn_near, mask_near, True,
        (t1, vec_one, c1, reduce_a, dp1, project_a, perm, mask),
    )
    t_near, v_near, c_near, *rest_near = map(N, got)
    jobs_t = (("flat", patches_one, dc2),)
    made_t = made(jobs_t)
    if whole_tiles:
        sum_w = Halving([exchanged(made_w, back_two)])
        came += [made_t[0], sum_w.sources[0][1]]
    back_one, _ = wide_sum(tied(b1, *came), (), steps(lambda: [sum_n.prepare(), sum_w.prepare()]))
    came_t = exchanged(made_t, back_one) if whole_tiles else None
    came = steps(lambda: sum_n.send(back_one) + sum_s.send(back_one))
    dc1, images_grad, grad_away, g1, h1 = leave_kernel(
        z, place, back_one, t_near, counted, v_near, c_near, N(live_near), *rest_near,
        (micro, side // 2, 2 * held, side, z.cin),
    )
    jobs_r = (("flat", planes, dc1),)
    made_r = made(jobs_r)

    images_grad = finish_images(z, place, swapped(grad_away, "rows", 1), images_grad)

    if whole_tiles:
        heights = [a.shape[1] * b.shape[1] // (2 * size * 512) for _, a, b in jobs_n]
        at_second = [sum(heights[:k]) for k in range(len(heights) + 1)]
        def rows_of(grad):
            return grad.size // (2 * size * 512), grad.shape[1]

        here = [made_r[0], *came, came_t[1]]
        came = sum_w.send(*here)
        came_r = exchanged(made_r, *here)
        sum_n.prepare(*here)
        came += sum_n.send()
        sum_t = Halving([came_t, came_r])
        here = [images_grad, *came, sum_t.prepare()]
        came = sum_t.send(*here)
        second = total_kernel([tied(sum_n.blocks[0], *here), *sum_n.blocks[1:]])
        narrows = second.astype(BF16)
        around = [swapped(narrows, "batch", 4 * k) for k in range(1, size // 4)]
        sum_w.prepare(*here)
        came += sum_w.send()
        sum_s.prepare(sum_w.sent[0])
        here = [*came, *around, *sum_s.send()]
        narrow = [narrows, *around]
        sum_e.blocks[0] = tied(sum_e.blocks[0], around[0])
        (out_expand_b,) = sum_e.finish([rows_of(expand_b)])
        sum_w.prepare(out_expand_b, *here)
        came = sum_w.send()
        (kept, come), = sum_t.sources
        kept, sent = second_step(tied(kept, sum_w.sent[0]), come, narrow)
        come = crossed(sent, 2, 1)
        sum_s.blocks[0] = tied(sum_s.blocks[0], sent)
        (out_spatial_b,) = sum_s.finish([rows_of(spatial_b)])
        *blocks, part = third_step(tied(kept, out_spatial_b, *came), come, narrow)
        sum_t.blocks = blocks[:1] + [
            swapped(block, "batch", 4 * (k + 1)) for k, block in enumerate(blocks[1:])
        ]
        every = part, crossed(part, 1, 2)
        narrow_outs = gathered_kernel(z, place, size, every, at_second)
        sum_t.blocks[0] = tied(sum_t.blocks[0], narrow_outs[0])
        sum_w.blocks[0] = tied(sum_w.blocks[0], every[1])
        out_expand_a, out_project_a = sum_w.finish([rows_of(expand_a), rows_of(project_a)])
        out_spatial_a, out_reduce_a = sum_t.finish([rows_of(spatial_a), rows_of(reduce_a)])
    else:
        second, at_second = plain_gradients(jobs_n, size)
        at_second = at_second + [second.shape[0]]
        edge_first = expand_b.size // (2 * size * 512)
        edge_rest = expand_a.size // (2 * size * 512)
        edge_third = spatial_a.size // (2 * size * 512)
        first = plain_gradients(jobs_e + jobs_s, size)[0]
        rest = plain_gradients(jobs_w, size)[0]
        third = plain_gradients(jobs_t + jobs_r, size)[0]
        out_expand_b, out_spatial_b = unfolded(first[:edge_first], out), unfolded(first[edge_first:], mid)
        out_expand_a, out_project_a = unfolded(rest[:edge_rest], out), unfolded(rest[edge_rest:], out)
        out_spatial_a, out_reduce_a = unfolded(third[:edge_third], mid), unfolded(third[edge_third:], mid)
    if whole_tiles:
        out_reduce, out_sq_b, out_ex_b, out_sq_a, out_ex_a = narrow_outs
    else:
        every = collected(second.astype(BF16)).astype(F32)

        def tall_of(k):
            block = every[:, at_second[k] : at_second[k + 1]]
            block = block.reshape(size, block.shape[1], 512 // hid, hid)
            return jnp.swapaxes(block, 1, 2).reshape(-1, hid)

        def flat_of(k):
            block = every[:, at_second[k] : at_second[k + 1]]
            across = (out // 2) // 512
            block = block.reshape(size // across, across, -1, 512)
            return jnp.swapaxes(block, 1, 2).reshape(hid, out // 2)

        out_reduce = every[:, : at_second[1]].reshape(-1, mid)
        out_sq_b, out_ex_b, out_sq_a, out_ex_a = tall_of(1), flat_of(2), tall_of(3), flat_of(4)
    span = out // 2

    return (
        block_out,
        images_grad,
        out_reduce_a,
        g1.reshape(-1),
        h1.reshape(-1),
        out_spatial_a,
        g2.reshape(-1),
        h2.reshape(-1),
        out_expand_a,
        gain_three.reshape(-1),
        bias_three.reshape(-1),
        out_project_a,
        gain_side.reshape(-1),
        bias_side.reshape(-1),
        out_sq_a,
        sq_bias_one.reshape(-1),
        out_ex_a,
        ex_bias_one.reshape(-1),
        out_reduce,
        g4.reshape(-1),
        h4.reshape(-1),
        out_spatial_b,
        g5.reshape(-1),
        h5.reshape(-1),
        out_expand_b,
        gain_six.reshape(-1),
        bias_six.reshape(-1),
        out_sq_b,
        sq_bias_two.reshape(-1),
        out_ex_b,
        ex_bias_two.reshape(-1),
    )


def solution(mesh):
    in_specs = (
        P(None, "rows", "batch", None, None),
        P(),
        P(),
        P(),
        P(),
        P(),
        P(),
        P(),
        P(),
        P("rows"),
        P("rows"),
        P(),
        P("rows"),
        P("rows"),
        P("rows", None),
        P(),
        P(None, "rows"),
        P("rows"),
        P("rows", None),
        P(),
        P(),
        P(),
        P(),
        P(),
        P(),
        P("rows"),
        P("rows"),
        P("rows", None),
        P(),
        P(None, "rows"),
        P("rows"),
        P(None, None, "batch", None, "rows"),
    )
    out_specs = (
        P(None, None, "batch", None, "rows"),
        P(None, "rows", "batch", None, None),
        P(("batch", "rows")),
        P(),
        P(),
        P(("batch", "rows")),
        P(),
        P(),
        P(("batch", "rows")),
        P("rows"),
        P("rows"),
        P(("batch", "rows")),
        P("rows"),
        P("rows"),
        P("rows", None),
        P(),
        P(None, "rows"),
        P("rows"),
        P("rows", None),
        P(),
        P(),
        P(("batch", "rows")),
        P(),
        P(),
        P(("batch", "rows")),
        P("rows"),
        P("rows"),
        P("rows", None),
        P(),
        P(None, "rows"),
        P("rows"),
    )
    return jax.shard_map(
        per_device, mesh=mesh, in_specs=in_specs, out_specs=out_specs, check_vma=False
    )
```

```python
import jax
import jax.numpy as jnp
from jax import lax
from jax.experimental import pallas as pl
from jax.experimental.pallas import tpu as pltpu
from jax.sharding import PartitionSpec as P

epsilon = 1e-05
HIGHEST = lax.Precision.HIGHEST
BF16 = jnp.bfloat16
F32 = jnp.float32

PLANE_TAPS = (((1, 0),), ((2, 0), (0, 1)))


def swapped(block, axis, mask):
    route = [(i, i ^ mask) for i in range(lax.axis_size(axis))]
    return lax.ppermute(block, axis, route)


def bits_of(size):
    return [1 << k for k in range(size.bit_length() - 1)]


def all_sum(parts):
    parts = parts + swapped(parts, "rows", 1)
    size = lax.axis_size("batch")
    spread = jnp.broadcast_to(parts[None], (size,) + parts.shape)
    return jnp.sum(lax.all_to_all(spread, "batch", 0, 0, tiled=True), axis=0)


def halved(block, orders):
    size = lax.axis_size("batch")
    place = lax.axis_index("batch")
    bits = bits_of(size)
    count = block.shape[1]
    cut = count // 2 // 16 * 16
    parts = []
    for part, order in zip((block[:, :cut], block[:, cut:]), orders(bits)):
        shape = part.shape[1:]
        left = list(reversed(bits))
        part = part.reshape((2,) * len(bits) + shape)
        for bit in order:
            axis = left.index(bit)
            mine = (place // bit) % 2
            gone = lax.dynamic_index_in_dim(part, 1 - mine, axis, keepdims=False)
            kept = lax.dynamic_index_in_dim(part, mine, axis, keepdims=False)
            total = kept.astype(F32) + swapped(gone, "batch", bit).astype(F32)
            left.pop(axis)
            part = total.astype(BF16) if left else total
        parts.append(part)
    return jnp.concatenate(parts, axis=0)


def two_orders(bits):
    return (bits, bits[1::-1] + bits[2:])


def collected(block):
    place = lax.axis_index("batch")
    block = block[None]
    for bit in bits_of(lax.axis_size("batch")):
        other = swapped(block, "batch", bit)
        upper = (place // bit) % 2 == 1
        block = jnp.concatenate([jnp.where(upper, other, block), jnp.where(upper, block, other)], axis=0)
    return block


def core_sum(block, axis):
    core = lax.axis_index("rows")
    gone = lax.dynamic_index_in_dim(block, 1 - core, axis, keepdims=False)
    kept = lax.dynamic_index_in_dim(block, core, axis, keepdims=False)
    return (kept.astype(F32) + swapped(gone, "rows", 1).astype(F32)).astype(BF16)


def both_cores(block, axis):
    core = lax.axis_index("rows")
    other = swapped(block, "rows", 1)
    first = jnp.where(core == 0, block, other)
    second = jnp.where(core == 0, other, block)
    return jnp.concatenate([first, second], axis=axis)


LANES = 128
VMEM_MIB = 64
ROOM = None
MARGIN_MIB = 3
READS = (((1, 0),), ((2, 0), (0, -1)))
ALL_TAPS = ((0, -1), (1, 0), (2, 1))


class Near:
    def __init__(self, array):
        self.array = array
        self.shape = array[0] if isinstance(array, tuple) else array.shape


class Both:
    def __init__(self, array):
        self.array = array


class Late:
    def __init__(self, array):
        self.array = array
        self.shape = array.shape


class Pair:
    def __init__(self, own, other, axis):
        self.own, self.other, self.axis = own, other, axis
        shape = list(own.shape)
        shape[axis] *= 2
        self.shape, self.dtype = tuple(shape), own.dtype


class Part:
    def __init__(self, array, axis):
        self.array, self.axis = array, axis
        shape = list(array.shape)
        shape[axis] //= 2
        self.shape, self.dtype = tuple(shape), array.dtype


class Top:
    def __init__(self, array, rows):
        self.array, self.rows = array, rows
        self.shape, self.dtype = (rows,) + tuple(array.shape[1:]), array.dtype


class Away:
    def __init__(self, array, axis):
        self.array, self.axis = array, axis
        shape = list(array.shape)
        shape[axis] //= 2
        self.shape, self.dtype = tuple(shape), array.dtype


class Join:
    def __init__(self, array, cut, other, axis):
        self.array, self.cut, self.other, self.axis = array, cut, other, axis
        shape = list(other.shape)
        shape[axis] *= 2
        self.shape, self.dtype = tuple(shape), array.dtype


class Raw:
    def __init__(self, shape, dtype):
        self.shape, self.dtype = shape, dtype


def half_of(ref, axis, which, length):
    start = which * length
    if axis >= len(ref.shape) - 2:
        start = pl.multiple_of(start, length)
    return ref.at[(slice(None),) * axis + (pl.ds(start, length),)]


class Copies:
    def __init__(self, sems):
        self.sems, self.used = sems, 0
        self.waiting, self.open = {}, []

    def start(self, source, target):
        copy = pltpu.make_async_copy(source, target, self.sems.at[self.used])
        self.used += 1
        copy.start()
        return copy

    def need(self, *refs):
        for ref in refs:
            for copy in self.waiting.pop(id(ref), ()):
                copy.wait()

    def out(self, source, target):
        self.open.append(self.start(source, target))


def run(body, outs, args, scratch=(), flops=0, spare=0, ahead=(), room=None):
    operands, specs, plans, buffers = [], [], [], []
    far = pl.BlockSpec(memory_space=pltpu.HBM)
    vmem = pl.BlockSpec(memory_space=pltpu.VMEM)
    count, next_up = 0, []

    def plan(arg, late, keep):
        nonlocal count
        if isinstance(arg, Near) and keep is next_up:
            plans.append(("copy", len(operands), (len(keep), 0), late))
            operands.append(arg.array)
            specs.append(vmem)
            keep.append((tuple(arg.shape), arg.array.dtype))
            count += 1
            return
        if isinstance(arg, Near):
            plans.append(("near", len(operands), None, late))
            operands.append(arg.array)
            specs.append(vmem)
            return
        if isinstance(arg, Pair):
            kind, axis, parts = "pair", arg.axis, [arg.own, arg.other]
        elif isinstance(arg, Part):
            kind, axis, parts = "part", arg.axis, [arg.array]
        elif isinstance(arg, Away):
            kind, axis, parts = "away", arg.axis, [arg.array]
        elif isinstance(arg, Top):
            kind, axis, parts = "top", 0, [arg.array]
        elif isinstance(arg, Join):
            kind, axis, parts = "join", (arg.cut, arg.axis), [arg.array, arg.other]
        elif arg.ndim == 1:
            plans.append(("near", len(operands), None, late))
            operands.append(arg)
            specs.append(pl.BlockSpec(memory_space=pltpu.SMEM))
            return
        else:
            kind, axis, parts = "copy", 0, [arg]
        plans.append((kind, len(operands), (len(keep), axis), late))
        operands.extend(parts)
        specs.extend([far] * len(parts))
        keep.append((tuple(arg.shape), arg.dtype))
        count += len(parts)

    for arg in args:
        late = isinstance(arg, Late)
        plan(arg.array if late else arg, late, buffers)
    first_ahead = len(plans)
    for arg in ahead:
        plan(arg, True, next_up)
    shapes, out_specs, ways = [], [], []
    for item in outs:
        if isinstance(item, Raw):
            ways.append(("raw", len(shapes), None))
            shapes.append(jax.ShapeDtypeStruct(item.shape, item.dtype))
            out_specs.append(far)
        elif isinstance(item, Near):
            ways.append(("near", len(shapes), None))
            shapes.append(jax.ShapeDtypeStruct(*item.array))
            out_specs.append(vmem)
        elif isinstance(item, Both):
            ways.append(("both", len(shapes), None))
            shapes += [jax.ShapeDtypeStruct(*item.array)] * 2
            out_specs += [vmem, far]
            count += 1
        else:
            ways.append(("copy", len(shapes), len(buffers)))
            shapes.append(jax.ShapeDtypeStruct(*item))
            out_specs.append(far)
            buffers.append(item)
            count += 1
    first_next = len(shapes)
    for item in next_up:
        shapes.append(jax.ShapeDtypeStruct(*item))
        out_specs.append(vmem)
    sems = pltpu.SemaphoreType.DMA((max(count + spare, 1),))

    def kernel(*refs):
        ins = refs[: len(operands)]
        results = refs[len(operands) : len(operands) + len(shapes)]
        rest = refs[len(operands) + len(shapes) :]
        bufs, own = rest[: len(buffers)], rest[len(buffers) : -1]
        io = Copies(rest[-1])
        views, early = [], []
        for k, (kind, at, spot, late) in enumerate(plans):
            if kind == "near":
                views.append(ins[at])
                continue
            index, axis = spot
            buf = results[first_next + index] if k >= first_ahead else bufs[index]
            if kind == "copy":
                copies = [io.start(ins[at], buf)]
            elif kind == "pair":
                core = ins[0][0]
                length = ins[at].shape[axis]
                copies = [
                    io.start(ins[at], half_of(buf, axis, core, length)),
                    io.start(ins[at + 1], half_of(buf, axis, 1 - core, length)),
                ]
            elif kind == "top":
                copies = [io.start(ins[at].at[pl.ds(0, buf.shape[0])], buf)]
            elif kind == "join":
                core, (cut, axis) = ins[0][0], axis
                mine = half_of(ins[at], cut, core, ins[at + 1].shape[cut])
                length = ins[at + 1].shape[axis]
                copies = [
                    io.start(mine, half_of(buf, axis, core, length)),
                    io.start(ins[at + 1], half_of(buf, axis, 1 - core, length)),
                ]
            else:
                core = ins[0][0] if kind == "part" else 1 - ins[0][0]
                copies = [io.start(half_of(ins[at], axis, core, buf.shape[axis]), buf)]
            io.waiting[id(buf)] = copies
            if k < first_ahead:
                views.append(buf)
                if not late:
                    early.append(buf)
        io.need(*early)
        targets = {}
        for kind, at, index in ways:
            if kind == "copy":
                views.append(bufs[index])
                targets[id(bufs[index])] = (bufs[index], results[at])
            else:
                views.append(results[at])
                if kind == "both":
                    targets[id(results[at])] = (results[at], results[at + 1])

        def send(*sent):
            for ref in sent:
                io.out(*targets.pop(id(ref)))

        io.send = send
        body(io, *views, *own)
        for buf, ref in targets.values():
            io.out(buf, ref)
        for copies in io.waiting.values():
            for copy in copies:
                copy.wait()
        for copy in io.open:
            copy.wait()

    def bytes_of(shape, dtype):
        size = 1
        for n in shape:
            size *= n
        return size * jnp.dtype(dtype).itemsize

    moved = sum(a.size * a.dtype.itemsize for a in operands) + sum(
        bytes_of(s.shape, s.dtype) for s in shapes
    )
    held = sum(bytes_of(*item) for item in buffers) + sum(bytes_of(s.shape, s.dtype) for s in scratch)
    limit = held + (MARGIN_MIB << 20)
    if room is not None:
        near = sum(a.size * a.dtype.itemsize for a, spec in zip(operands, specs) if spec is vmem)
        near += sum(bytes_of(s.shape, s.dtype) for s, spec in zip(shapes, out_specs) if spec is vmem)
        limit = max(limit, ((VMEM_MIB - room) << 20) - near)
    return pl.pallas_call(
        kernel,
        out_shape=shapes,
        in_specs=specs,
        out_specs=out_specs,
        scratch_shapes=[*(pltpu.VMEM(*item) for item in buffers), *scratch, sems],
        compiler_params=pltpu.CompilerParams(vmem_limit_bytes=limit),
        cost_estimate=pl.CostEstimate(flops=flops, bytes_accessed=0, transcendentals=0),
    )(*operands)


def dot(a, b):
    return lax.dot_general(a, b, (((1,), (0,)), ((), ())), preferred_element_type=F32)


def dot_nt(a, b):
    return lax.dot_general(a, b, (((1,), (1,)), ((), ())), preferred_element_type=F32)


def dot_tn(a, b):
    return lax.dot_general(a, b, (((0,), (0,)), ((), ())), preferred_element_type=F32)


def exact_dot(a, b, product):
    high = a.astype(BF16)
    low = (a - high.astype(F32)).astype(BF16)
    return product(high, b) + product(low, b)


def sigmoid(v):
    return 0.5 + 0.5 * jnp.tanh(0.5 * v)


def slope_of(v):
    sigma = sigmoid(v)
    return sigma * (1.0 + v * (1.0 - sigma))


def counts_of(z, n_r, which):
    return [n_r[which * z.micro + m] for m in range(z.micro)]


def norm_rows(total, counted, micro):
    rows = []
    for m in range(micro):
        centre = total[2 * m : 2 * m + 1] / counted[m]
        square = total[2 * m + 1 : 2 * m + 2] / counted[m]
        rows.append((centre, lax.rsqrt(square - centre * centre + epsilon)))
    return rows


def fold_sums(first, second):
    return jnp.sum(first, axis=0, keepdims=True), jnp.sum(second, axis=0, keepdims=True)


def flat_row(row, out_ref):
    for k in range(row.shape[1] // LANES):
        out_ref[k : k + 1, :] = row[:, k * LANES : (k + 1) * LANES]


def flat_of(n):
    return ((n // LANES, LANES), F32)


def gains_out(total, micro, gain_r, bias_r):
    flat_row(sum(total[2 * m + 1 : 2 * m + 2] for m in range(micro)), gain_r)
    flat_row(sum(total[2 * m : 2 * m + 1] for m in range(micro)), bias_r)


def to_all(z, rows, s_r):
    for k, row in enumerate(rows):
        s_r[k : k + 1, :] = row


def place_patches(values, row_taps, col_taps, out_ref, base, lane, ch, group):
    size = values.shape[0]
    q = lax.broadcasted_iota(jnp.int32, values.shape, 0) % 8
    for col, cs in col_taps:
        if cs == -1:
            turned = jnp.where(q == 0, 0.0, pltpu.roll(values, 1, 0))
        elif cs == 1:
            turned = jnp.where(q == 7, 0.0, pltpu.roll(values, size - 1, 0))
        else:
            turned = values
        turned = turned.astype(BF16)
        gap = jnp.zeros((group, values.shape[1]), BF16)
        for row, rs in row_taps:
            at = (3 * row + col) * ch + lane
            lanes = slice(at, at + values.shape[1])
            if rs == 0:
                out_ref[base : base + size, lanes] = turned
            elif rs == -1:
                out_ref[base : base + group, lanes] = gap
                out_ref[base + group : base + size, lanes] = turned[: size - group]
            else:
                out_ref[base : base + size - group, lanes] = turned[group:]
                out_ref[base + size - group : base + size, lanes] = gap


class Sizes:
    def __init__(self, images, mid, out, hid, devices):
        self.micro = images.shape[0]
        self.held = images.shape[2] // 2
        self.side = images.shape[3]
        self.half = self.side // 2
        self.cin = images.shape[4]
        self.mid, self.out, self.hid, self.devices = mid, out, hid, devices
        self.group = self.held * self.half
        self.map = self.half * self.group
        self.coarse = self.micro * self.map
        self.fine = 4 * self.coarse
        self.maps = self.micro * self.held


def enter_kernel(z, place, images, other, perm, w_one, mask, ahead):
    def body(io, place_r, mine_r, other_r, perm_r, w1_r, mask_r, planes_r, c1_r, s1_r):
        core = place_r[0]
        rows = z.map // 2
        for k, ref in ((0, mine_r), (1, other_r)):
            half = core if k == 0 else 1 - core
            io.need(ref)
            for m in range(z.micro):
                turned = dot(perm_r[...], ref[m].reshape(2 * z.map, z.cin)).astype(BF16)
                for p in range(4):
                    at = pl.multiple_of((p * z.micro + m) * z.map + half * rows, rows)
                    planes_r[pl.ds(at, rows), :] = turned[p * rows : (p + 1) * rows]
        io.send(planes_r)
        io.need(w1_r)
        c1_r[...] = dot(planes_r[...], w1_r[...])
        for m in range(z.micro):
            one = [None, None]
            for p in range(4):
                at = (p * z.micro + m) * z.map
                c = c1_r[at : at + z.map, :]
                live = c * mask_r[m * z.map : (m + 1) * z.map, 0:1]
                a, b = fold_sums(live, live * c)
                one = [a, b] if p == 0 else [one[0] + a, one[1] + b]
            s1_r[2 * m : 2 * m + 1, :] = one[0]
            s1_r[2 * m + 1 : 2 * m + 2, :] = one[1]
        io.send(c1_r)

    return run(
        body,
        [
            ((z.fine, z.cin), BF16),
            Both(((z.fine, z.mid), F32)),
            Near(((2 * z.micro, z.mid), F32)),
        ],
        (place, images, other, perm, w_one, mask),
        room=ROOM,
        ahead=ahead,
        flops=2 * z.fine * z.cin * z.mid,
    )


def taps_kernel(z, place, sums, counted, vec, conv, weight, mask, strided, ahead):
    planes = 4 if strided else 1
    nt = weight.shape[0]

    def body(io, place_r, sums_r, n_r, vec_r, c_r, w_r, mask_r, patch_r, out_r, t_r, s_r):
        total = sums_r[...]
        t_r[...] = total
        io.send(t_r)
        norms = norm_rows(total, counts_of(z, n_r, 0 if strided else 1), z.micro)
        for m in range(z.micro):
            centre, inverse = norms[m]
            scale = inverse * vec_r[0:1]
            offset = vec_r[1:2] - centre * scale
            live = mask_r[m * z.map : (m + 1) * z.map, 0:1]
            for p in range(planes):
                at = (p * z.micro + m) * z.map
                for lane in range(0, z.mid, LANES):
                    lanes = slice(lane, lane + LANES)
                    v = (c_r[at : at + z.map, lanes] * scale[:, lanes] + offset[:, lanes]) * live
                    v = v * sigmoid(v)
                    rows = READS[p // 2] if strided else ALL_TAPS
                    cols = READS[p % 2] if strided else ALL_TAPS
                    place_patches(v, rows, cols, patch_r, m * z.map, lane, z.mid, z.group)
        io.send(patch_r)
        io.need(w_r)
        c = dot(patch_r[...], w_r[...])
        out_r[...] = c
        io.send(out_r)
        for m in range(z.micro):
            part = c[m * z.map : (m + 1) * z.map]
            live = part * mask_r[m * z.map : (m + 1) * z.map, 0:1]
            a, b = fold_sums(live, live * part)
            s_r[2 * m : 2 * m + 1, :] = a
            s_r[2 * m + 1 : 2 * m + 2, :] = b

    return run(
        body,
        [
            ((z.coarse, nt), BF16),
            Both(((z.coarse, z.mid), F32)),
            ((2 * z.micro, z.mid), F32),
            Near(((2 * z.micro, z.mid), F32)),
        ],
        (place, Near(sums), counted, vec, conv, weight, mask),
        room=ROOM,
        ahead=ahead,
        flops=2 * z.coarse * nt * z.mid,
    )


def expand_kernel(z, place, sums, counted, vec, conv, weight, mask, side, ahead):
    height = 2 * z.micro

    def body(io, place_r, sums_r, n_r, vec_r, c_r, w_r, mask_r, *refs):
        if side is not None:
            plane_r, ws_r, act_r, out_r, t_r, p1_r, s_r = refs
        else:
            act_r, out_r, t_r, s_r = refs
        total = sums_r[...]
        t_r[...] = total
        io.send(t_r)
        norms = norm_rows(total, counts_of(z, n_r, 1), z.micro)
        for m in range(z.micro):
            rows = slice(m * z.map, (m + 1) * z.map)
            centre, inverse = norms[m]
            scale = inverse * vec_r[0:1]
            offset = vec_r[1:2] - centre * scale
            v = (c_r[rows, :] * scale + offset) * mask_r[rows, 0:1]
            act_r[rows, :] = (v * sigmoid(v)).astype(BF16)
        io.send(act_r)
        io.need(w_r)

        @pl.loop(0, z.out // 512, unroll=4)
        def _(j):
            lanes = pl.ds(pl.multiple_of(j * 512, 512), 512)
            products = [(dot(act_r[...], w_r[:, lanes]), out_r, 0)]
            if side is not None:
                products.append((dot(plane_r[...], ws_r[:, lanes]), p1_r, height))
            for p, ref, first in products:
                p = p.astype(BF16)
                ref[:, lanes] = p
                p = p.astype(F32)
                for m in range(z.micro):
                    part = p[m * z.map : (m + 1) * z.map]
                    live = part * mask_r[m * z.map : (m + 1) * z.map, 0:1]
                    a, b = fold_sums(live, live * part)
                    at = first + 2 * m
                    s_r[at : at + 1, lanes] = a
                    s_r[at + 1 : at + 2, lanes] = b

    extra = () if side is None else side
    wide = [] if side is None else [Both(((z.coarse, z.out), BF16))]
    return run(
        body,
        [
            ((z.coarse, z.mid), BF16),
            Both(((z.coarse, z.out), BF16)),
            ((2 * z.micro, z.mid), F32),
            *wide,
            Near(((height * (1 if side is None else 2), z.out), F32)),
        ],
        (place, Near(sums), counted, vec, conv, weight, mask, *extra),
        room=ROOM,
        ahead=ahead,
        flops=2 * z.coarse * z.out * z.mid,
    )


def by_map(z, v):
    return v.reshape(z.half, z.held, z.half, v.shape[-1])


def map_sums(z, v):
    return jnp.sum(jnp.sum(by_map(z, v), axis=0), axis=1)


def spread(z, rows):
    return jnp.broadcast_to(
        rows[None, :, None, :], (z.half, z.held, z.half, rows.shape[-1])
    ).reshape(z.map, rows.shape[-1])


def norms_at(z, total_r, n_r, m, lanes, first=0):
    counted = n_r[z.micro + m]
    at = first + 2 * m
    centre = total_r[at : at + 1, lanes] / counted
    square = total_r[at + 1 : at + 2, lanes] / counted
    return centre, lax.rsqrt(square - centre * centre + epsilon)


def gate_rows(pooled, squeeze_r, sq_bias, excite_r, ex_bias):
    inner = exact_dot(pooled, squeeze_r[...], dot) + sq_bias
    hidden = inner * sigmoid(inner)
    gate = sigmoid(exact_dot(hidden, excite_r[...], dot) + ex_bias)
    return inner, hidden, gate


def gate_back(dgate, gate, inner, squeeze_r, excite_r, pix):
    dl = dgate * gate * (1.0 - gate)
    dz = exact_dot(dl, excite_r[...], dot_nt) * slope_of(inner)
    du = exact_dot(dz, squeeze_r[...], dot_nt) / pix
    return dl, dz, du


def bias_sums(z, dl, dz, s_r, first):
    s_r[first : first + 1, :] = jnp.sum(dl, axis=0, keepdims=True)
    s_r[first + 1 : first + 2, :] = jnp.zeros((1, z.out), F32)
    s_r[first + 1 : first + 2, : z.hid] = jnp.sum(dz, axis=0, keepdims=True)


def middle_kernel(z, place, sums, counted, vectors, pix, e1, p1, squeeze, sq_bias, excite, w, mask, ahead):
    side = 2 * z.micro

    def body(
        io, place_r, t_r, n_r, vec_r, pix_r, e_r, p_r, sq_r, sqb_r, ex_r, w_r, mask_r,
        mid_r, c_r, gate_r, pool_r, inner_r, hid_r, total_r, s_r,
    ):
        io.out(t_r, total_r)

        @pl.loop(0, z.out // LANES, unroll=8)
        def _(j):
            lanes = pl.ds(pl.multiple_of(j * LANES, LANES), LANES)
            for m in range(z.micro):
                rows = slice(m * z.map, (m + 1) * z.map)
                centre, inverse = norms_at(z, t_r, n_r, m, lanes)
                scale = inverse * vec_r[0:1, lanes]
                offset = vec_r[1:2, lanes] - centre * scale
                v = (e_r[rows, lanes].astype(F32) * scale + offset) * mask_r[rows, 0:1]
                at = slice(m * z.held, (m + 1) * z.held)
                pool_r[at, lanes] = map_sums(z, v) / pix_r[at, 0:1]

        io.need(sq_r, ex_r)
        inner, hidden, gate = gate_rows(pool_r[...], sq_r, sqb_r[0:1], ex_r, vec_r[6:7])
        gate_r[...] = gate
        inner_r[...] = inner
        hid_r[...] = hidden
        io.send(gate_r, inner_r, hid_r, pool_r)
        io.need(p_r)

        @pl.loop(0, z.out // LANES, unroll=8)
        def _(j):
            lanes = pl.ds(pl.multiple_of(j * LANES, LANES), LANES)
            for m in range(z.micro):
                rows = slice(m * z.map, (m + 1) * z.map)
                centre, inverse = norms_at(z, t_r, n_r, m, lanes)
                scale = inverse * vec_r[0:1, lanes]
                offset = vec_r[1:2, lanes] - centre * scale
                v = e_r[rows, lanes].astype(F32) * scale + offset
                centre, inverse = norms_at(z, t_r, n_r, m, lanes, side)
                scale = inverse * vec_r[2:3, lanes]
                offset = vec_r[3:4, lanes] - centre * scale
                o = v * spread(z, gate_r[m * z.held : (m + 1) * z.held, lanes])
                o = (o + (p_r[rows, lanes].astype(F32) * scale + offset)) * mask_r[rows, 0:1]
                mid_r[rows, lanes] = (o * sigmoid(o)).astype(BF16)

        io.send(mid_r)
        io.need(w_r)
        c = dot(mid_r[...], w_r[...])
        c_r[...] = c
        io.send(c_r)
        for m in range(z.micro):
            part = c[m * z.map : (m + 1) * z.map]
            live = part * mask_r[m * z.map : (m + 1) * z.map, 0:1]
            a, b = fold_sums(live, live * part)
            s_r[2 * m : 2 * m + 1, :] = a
            s_r[2 * m + 1 : 2 * m + 2, :] = b

    return run(
        body,
        [
            ((z.coarse, z.out), BF16),
            Both(((z.coarse, z.mid), F32)),
            ((z.maps, z.out), F32),
            ((z.maps, z.out), F32),
            ((z.maps, z.hid), F32),
            ((z.maps, z.hid), F32),
            Raw((2 * side, z.out), F32),
            Near(((2 * z.micro, z.mid), F32)),
        ],
        (place, Near(sums), counted, vectors, pix, e1, p1, squeeze, sq_bias, excite, w, mask),
        room=ROOM,
        ahead=ahead,
        spare=1,
        flops=2 * z.coarse * z.out * z.mid,
    )


def output_kernel(z, place, sums, counted, vectors, pix, e2, middle, up, squeeze, sq_bias, excite, mask, final, ahead):
    span = z.out // 2

    def body(
        io, place_r, t_r, n_r, vec_r, pix_r, e_r, mid_r, up_r, sq_r, sqb_r, ex_r, mask_r,
        final_r, away_r, do_r, h_r, pool_r, hid_r, dl_r, dz_r, s_r, out_r, gate_r, du_r,
    ):
        core = place_r[0]

        @pl.loop(0, z.out // LANES, unroll=8)
        def _(j):
            lanes = pl.ds(pl.multiple_of(j * LANES, LANES), LANES)
            for m in range(z.micro):
                rows = slice(m * z.map, (m + 1) * z.map)
                centre, inverse = norms_at(z, t_r, n_r, m, lanes)
                scale = inverse * vec_r[4:5, lanes]
                offset = vec_r[5:6, lanes] - centre * scale
                v = (e_r[rows, lanes].astype(F32) * scale + offset) * mask_r[rows, 0:1]
                at = slice(m * z.held, (m + 1) * z.held)
                pool_r[at, lanes] = map_sums(z, v) / pix_r[at, 0:1]

        io.need(sq_r, ex_r)
        inner, hidden, gate = gate_rows(pool_r[...], sq_r, sqb_r[1:2], ex_r, vec_r[7:8])
        gate_r[...] = gate
        hid_r[...] = hidden
        io.send(pool_r, hid_r)
        io.need(mid_r, up_r)

        @pl.loop(0, z.out // LANES, unroll=8)
        def _(j):
            lanes = pl.ds(pl.multiple_of(j * LANES, LANES), LANES)
            for m in range(z.micro):
                rows = slice(m * z.map, (m + 1) * z.map)
                at = slice(m * z.held, (m + 1) * z.held)
                centre, inverse = norms_at(z, t_r, n_r, m, lanes)
                scale = inverse * vec_r[4:5, lanes]
                offset = vec_r[5:6, lanes] - centre * scale
                v = (e_r[rows, lanes].astype(F32) * scale + offset) * mask_r[rows, 0:1]
                o = v * spread(z, gate_r[at, lanes]) + mid_r[rows, lanes].astype(F32)
                sigma = sigmoid(o)
                out_r[m, :, :, :, lanes] = by_map(z, o * sigma).astype(BF16)
                up = up_r[m, :, :, :, lanes].astype(F32).reshape(z.map, LANES)
                do = up * (sigma * (1.0 + o * (1.0 - sigma)))
                do_r[rows, lanes] = do
                dl_r[at, lanes] = map_sums(z, do * v)

        io.out(
            half_of(out_r, 4, core, span), final_r.at[:, :, pl.ds(core * z.held, z.held)]
        )
        io.out(half_of(out_r, 4, 1 - core, span), away_r)
        io.send(do_r)
        dl, dz, du = gate_back(dl_r[...], gate_r[...], inner, sq_r, ex_r, pix_r[:, 0:1])
        dl_r[...] = dl
        dz_r[...] = dz
        du_r[...] = du
        io.send(dl_r, dz_r)
        bias_sums(z, dl, dz, s_r, 2 * z.micro)

        @pl.loop(0, z.out // LANES, unroll=8)
        def _(j):
            lanes = pl.ds(pl.multiple_of(j * LANES, LANES), LANES)
            for m in range(z.micro):
                rows = slice(m * z.map, (m + 1) * z.map)
                at = slice(m * z.held, (m + 1) * z.held)
                centre, inverse = norms_at(z, t_r, n_r, m, lanes)
                k = (e_r[rows, lanes].astype(F32) - centre) * inverse
                h = do_r[rows, lanes] * spread(z, gate_r[at, lanes]) + spread(z, du_r[at, lanes])
                h = h * mask_r[rows, 0:1]
                h_r[rows, lanes] = h
                a, b = fold_sums(h, h * k)
                s_r[2 * m : 2 * m + 1, lanes] = a
                s_r[2 * m + 1 : 2 * m + 2, lanes] = b

    maps = (z.micro, z.half, z.held, z.half)
    return run(
        body,
        [
            Raw(final, BF16),
            Raw(maps + (span,), BF16),
            ((z.coarse, z.out), F32),
            Near(((z.coarse, z.out), F32)),
            ((z.maps, z.out), F32),
            ((z.maps, z.hid), F32),
            ((z.maps, z.out), F32),
            ((z.maps, z.hid), F32),
            Near(((2 * z.micro + 2, z.out), F32)),
        ],
        (place, Near(sums), counted, vectors, pix, e2, middle, up, squeeze, sq_bias, excite, mask),
        room=ROOM,
        ahead=ahead,
        scratch=[
            pltpu.VMEM(maps + (z.out,), BF16),
            pltpu.VMEM((z.maps, z.out), F32),
            pltpu.VMEM((z.maps, z.out), F32),
        ],
        spare=2,
    )


def wide_back(z, n_r, m, lanes, total_r, back_r, first, gain, e, h):
    centre, inverse = norms_at(z, total_r, n_r, m, lanes, first)
    k = (e - centre) * inverse
    at = first + 2 * m
    mean = back_r[at : at + 1, lanes] / n_r[z.micro + m]
    slope = back_r[at + 1 : at + 2, lanes] / n_r[z.micro + m]
    return (h - (mean + k * slope)) * (gain * inverse)


def unexpand_kernel(z, place, back, total, counted, vectors, row, e, h, w, total_n, vec_n, conv, mask, ahead):
    span = z.out // 2
    groups = back.shape[0] // (2 * z.micro)

    def body(
        io, place_r, b_r, t_r, n_r, vec_r, e_r, h_r, w_r, tn_r, vn_r, c_r, mask_r,
        de_r, live_r, s_r, *small_r,
    ):
        lanes = pl.ds(pl.multiple_of(place_r[0] * span, span), span)
        own = b_r[:, lanes]
        for g in range(groups):
            gains_out(own[2 * z.micro * g :], z.micro, small_r[2 * g], small_r[2 * g + 1])
        flat_row(own[2 * z.micro * groups : 2 * z.micro * groups + 1], small_r[-2])
        small_r[-1][...] = b_r[2 * z.micro * groups + 1 : 2 * z.micro * groups + 2, : z.hid]
        io.send(*small_r)

        @pl.loop(0, z.out // LANES, unroll=8)
        def _(j):
            lanes = pl.ds(pl.multiple_of(j * LANES, LANES), LANES)
            for m in range(z.micro):
                rows = slice(m * z.map, (m + 1) * z.map)
                h = h_r[rows, lanes]
                e = e_r[rows, lanes].astype(F32)
                d = wide_back(z, n_r, m, lanes, t_r, b_r, 0, vec_r[row : row + 1, lanes], e, h)
                de_r[rows, lanes] = (d * mask_r[rows, 0:1]).astype(BF16)

        io.send(de_r)
        io.need(w_r)
        da = dot_nt(de_r[...], w_r[...])
        norms = norm_rows(tn_r[...], counts_of(z, n_r, 1), z.micro)
        sums = []
        for m in range(z.micro):
            rows = slice(m * z.map, (m + 1) * z.map)
            centre, inverse = norms[m]
            k = (c_r[rows, :] - centre) * inverse
            v = (k * vn_r[0:1] + vn_r[1:2]) * mask_r[rows, 0:1]
            h = da[rows] * slope_of(v) * mask_r[rows, 0:1]
            live_r[rows, :] = h
            sums += fold_sums(h, h * k)
        to_all(z, sums, s_r)

    return run(
        body,
        [
            ((z.coarse, z.out), BF16),
            Near(((z.coarse, z.mid), F32)),
            Near(((2 * z.micro, z.mid), F32)),
            *([flat_of(span)] * (2 * groups + 1)),
            ((1, z.hid), F32),
        ],
        (place, Near(back), total, counted, vectors, e, h, w, total_n, vec_n, conv, mask),
        ahead=ahead,
        flops=2 * z.coarse * z.out * z.mid,
    )


def narrow_back(m, norms, back, counted, gain, conv, live, mask):
    centre, inverse = norms[m]
    k = (conv - centre) * inverse
    mean = back[2 * m : 2 * m + 1] / counted[m]
    slope = back[2 * m + 1 : 2 * m + 2] / counted[m]
    return (live - (mean + k * slope)) * (gain * inverse) * mask


def untap_kernel(z, place, back, total, counted, vec, conv, live, w, total_n, vec_n, conv_n, mask, strided, ahead):
    planes = 4 if strided else 1

    def body(io, place_r, b_r, t_r, n_r, vec_r, c_r, h_r, w_r, tn_r, vn_r, cn_r, mask_r, dc_r, live_r, gain_r, bias_r, s_r, tap_r):
        counted = counts_of(z, n_r, 1)
        back = b_r[...]
        gains_out(back, z.micro, gain_r, bias_r)
        io.send(gain_r, bias_r)
        norms = norm_rows(t_r[...], counted, z.micro)
        taps = ((0, 0), (1, 1)) if strided else ((0, 1), (1, 0), (2, -1))
        for m in range(z.micro):
            rows = slice(m * z.map, (m + 1) * z.map)
            d = narrow_back(
                m, norms, back, counted, vec_r[0:1], c_r[rows, :], h_r[rows, :], mask_r[rows, 0:1]
            )
            dc_r[rows, :] = d.astype(BF16)
            for lane in range(0, z.mid, LANES):
                place_patches(
                    d[:, lane : lane + LANES], taps, taps, tap_r, m * z.map, lane, z.mid, z.group
                )
        io.send(dc_r)
        norms = norm_rows(tn_r[...], counts_of(z, n_r, 0 if strided else 1), z.micro)
        acc = [[None, None] for _ in range(z.micro)]
        io.need(w_r, cn_r)
        for p in range(planes):
            da = None
            if strided:
                terms = [
                    (3 * i + j, 3 * rs + cs)
                    for i, rs in PLANE_TAPS[p // 2]
                    for j, cs in PLANE_TAPS[p % 2]
                ]
            else:
                terms = [(t, t) for t in range(9)]
            for t, slot in terms:
                part = dot_nt(
                    tap_r[:, slot * z.mid : (slot + 1) * z.mid], w_r[t * z.mid : (t + 1) * z.mid, :]
                )
                da = part if da is None else da + part
            for m in range(z.micro):
                rows = slice(m * z.map, (m + 1) * z.map)
                at = (p * z.micro + m) * z.map
                centre, inverse = norms[m]
                k = (cn_r[at : at + z.map, :] - centre) * inverse
                v = (k * vn_r[0:1] + vn_r[1:2]) * mask_r[rows, 0:1]
                h = da[rows] * slope_of(v) * mask_r[rows, 0:1]
                live_r[at : at + z.map, :] = h
                a, b = fold_sums(h, h * k)
                acc[m] = [a, b] if p == 0 else [acc[m][0] + a, acc[m][1] + b]
        to_all(z, [row for pair in acc for row in pair], s_r)

    return run(
        body,
        [
            ((z.coarse, z.mid), BF16),
            Near(((planes * z.coarse, z.mid), F32)),
            flat_of(z.mid),
            flat_of(z.mid),
            Near(((2 * z.micro, z.mid), F32)),
        ],
        (place, Near(back), total, counted, vec, conv, live, w, total_n, vec_n, conv_n, mask),
        ahead=ahead,
        scratch=[pltpu.VMEM((z.coarse, 9 * z.mid), BF16)],
        flops=2 * z.coarse * 9 * z.mid * z.mid,
    )


def unreduce_kernel(
    z, place, back, total, counted, vec, conv, live, w, do2, total_w, vectors, gate, inner, e1, p1, squeeze, excite, pix, mask, ahead
):
    side = 2 * z.micro

    def body(
        io, place_r, b_r, t_r, n_r, vec_r, c_r, h_r, w_r, do2_r, tw_r, vw_r, gate_r, in_r, e_r, p_r, sq_r, ex_r, pix_r, mask_r,
        dc_r, do_r, wide_r, gain_r, bias_r, dl_r, dz_r, s_r, du_r,
    ):
        counted = counts_of(z, n_r, 1)
        back = b_r[...]
        gains_out(back, z.micro, gain_r, bias_r)
        norms = norm_rows(t_r[...], counted, z.micro)
        for m in range(z.micro):
            rows = slice(m * z.map, (m + 1) * z.map)
            d = narrow_back(
                m, norms, back, counted, vec_r[0:1], c_r[rows, :], h_r[rows, :], mask_r[rows, 0:1]
            )
            dc_r[rows, :] = d.astype(BF16)
        io.send(gain_r, bias_r, dc_r)
        io.need(w_r, do2_r, e_r, p_r)

        @pl.loop(0, z.out // 256, unroll=2)
        def _(j):
            wide_lanes = pl.ds(pl.multiple_of(j * 256, 256), 256)
            dm = dot_nt(dc_r[...], w_r[wide_lanes, :])
            for i in range(2):
                lanes = pl.ds(pl.multiple_of(j * 256 + i * LANES, LANES), LANES)
                for m in range(z.micro):
                    rows = slice(m * z.map, (m + 1) * z.map)
                    at = slice(m * z.held, (m + 1) * z.held)
                    live = mask_r[rows, 0:1]
                    centre, inverse = norms_at(z, tw_r, n_r, m, lanes)
                    k = (e_r[rows, lanes].astype(F32) - centre) * inverse
                    q = (k * vw_r[0:1, lanes] + vw_r[1:2, lanes]) * live
                    centre, inverse = norms_at(z, tw_r, n_r, m, lanes, side)
                    kp = (p_r[rows, lanes].astype(F32) - centre) * inverse
                    t = (kp * vw_r[2:3, lanes] + vw_r[3:4, lanes]) * live
                    o = q * spread(z, gate_r[at, lanes]) + t
                    d = (dm[rows, i * LANES : (i + 1) * LANES] + do2_r[rows, lanes]) * slope_of(o)
                    do_r[rows, lanes] = d
                    dl_r[at, lanes] = map_sums(z, d * q)
                    d = d * live
                    a, b = fold_sums(d, d * kp)
                    s_r[side + 2 * m : side + 2 * m + 1, lanes] = a
                    s_r[side + 2 * m + 1 : side + 2 * m + 2, lanes] = b

        io.send(do_r)
        io.need(sq_r, ex_r)
        dl, dz, du = gate_back(dl_r[...], gate_r[...], in_r[...], sq_r, ex_r, pix_r[:, 0:1])
        dl_r[...] = dl
        dz_r[...] = dz
        du_r[...] = du
        io.send(dl_r, dz_r)
        bias_sums(z, dl, dz, s_r, 2 * side)

        @pl.loop(0, z.out // LANES, unroll=8)
        def _(j):
            lanes = pl.ds(pl.multiple_of(j * LANES, LANES), LANES)
            for m in range(z.micro):
                rows = slice(m * z.map, (m + 1) * z.map)
                at = slice(m * z.held, (m + 1) * z.held)
                centre, inverse = norms_at(z, tw_r, n_r, m, lanes)
                k = (e_r[rows, lanes].astype(F32) - centre) * inverse
                h = do_r[rows, lanes] * spread(z, gate_r[at, lanes]) + spread(z, du_r[at, lanes])
                h = h * mask_r[rows, 0:1]
                wide_r[rows, lanes] = h
                a, b = fold_sums(h, h * k)
                s_r[2 * m : 2 * m + 1, lanes] = a
                s_r[2 * m + 1 : 2 * m + 2, lanes] = b

    return run(
        body,
        [
            ((z.coarse, z.mid), BF16),
            ((z.coarse, z.out), F32),
            Near(((z.coarse, z.out), F32)),
            flat_of(z.mid),
            flat_of(z.mid),
            ((z.maps, z.out), F32),
            ((z.maps, z.hid), F32),
            Near(((2 * side + 2, z.out), F32)),
        ],
        (
            place, Near(back), total, counted, vec, conv, live, w, do2, total_w, vectors, gate, inner,
            e1, p1, squeeze, excite, pix, mask,
        ),
        scratch=[pltpu.VMEM((z.maps, z.out), F32)],
        ahead=ahead,
        flops=2 * z.coarse * z.out * z.mid,
    )


def side_kernel(z, place, back, total, counted, vectors, p1, do, mask):
    def body(io, place_r, b_r, t_r, n_r, vec_r, p_r, do_r, mask_r, dp_r):
        @pl.loop(0, z.out // LANES, unroll=8)
        def _(j):
            lanes = pl.ds(pl.multiple_of(j * LANES, LANES), LANES)
            for m in range(z.micro):
                rows = slice(m * z.map, (m + 1) * z.map)
                p = p_r[rows, lanes].astype(F32)
                h = do_r[rows, lanes]
                d = wide_back(z, n_r, m, lanes, t_r, b_r, 2 * z.micro, vec_r[2:3, lanes], p, h)
                dp_r[rows, lanes] = (d * mask_r[rows, 0:1]).astype(BF16)

    return run(
        body,
        [((z.coarse, z.out), BF16)],
        (place, back, total, counted, vectors, p1, do, mask),
    )[0]


def leave_kernel(z, place, back, total, counted, vec, conv, live, w_one, dp, w_side, perm, mask, final):
    block = 2 * z.map
    maps = (z.half, z.held, z.side)

    def body(
        io, place_r, b_r, t_r, n_r, vec_r, c_r, h_r, w_r, dp_r, ws_r, perm_r, mask_r,
        dc_r, final_r, away_r, gain_r, bias_r, keep_r, grad_r,
    ):
        core = place_r[0]
        counted = counts_of(z, n_r, 0)
        back = b_r[...]
        gains_out(back, z.micro, gain_r, bias_r)
        norms = norm_rows(t_r[...], counted, z.micro)
        for m in range(z.micro):
            for p in range(4):
                at = (p * z.micro + m) * z.map
                rows = slice(at, at + z.map)
                d = narrow_back(
                    m, norms, back, counted, vec_r[0:1], c_r[rows, :], h_r[rows, :],
                    mask_r[m * z.map : (m + 1) * z.map, 0:1],
                )
                dc_r[rows, :] = d.astype(BF16)
        io.send(dc_r)
        io.need(w_r, dp_r, ws_r)
        rows = z.map // 2
        sides = dot_nt(dp_r[...], ws_r[...])
        for m in range(z.micro):
            side = sides[m * z.map : (m + 1) * z.map]
            for half in range(2):
                stacked = jnp.concatenate(
                    [
                        dc_r[(p * z.micro + m) * z.map + half * rows : (p * z.micro + m) * z.map + (half + 1) * rows, :]
                        for p in range(4)
                    ],
                    axis=0,
                )
                ordered = dot_tn(perm_r[...], stacked).astype(BF16)
                grad = dot_nt(ordered, w_r[...])
                for n in range(z.cin // LANES):
                    lanes = slice(n * LANES, (n + 1) * LANES)
                    grad_r[n] = grad[:, lanes]
                    for o in range(z.half // 2):
                        for b in range(z.held):
                            at = 2 * o * z.held * z.side + b * z.side
                            src = half * rows + (o * z.held + b) * z.half
                            spots = pl.ds(at, z.half, stride=2)
                            grad_r[n, spots, :] = grad_r[n, spots, :] + side[src : src + z.half, lanes]

                @pl.when(core == half)
                def _():
                    for n in range(z.cin // LANES):
                        keep_r[m, :, :, :, n * LANES : (n + 1) * LANES] = grad_r[n].reshape(maps + (LANES,))

                @pl.when(core != half)
                def _():
                    for n in range(z.cin // LANES):
                        away_r[m, :, n * LANES : (n + 1) * LANES] = grad_r[n].astype(BF16)

            io.out(keep_r.at[m], final_r.at[m, :, pl.ds(core * z.held, z.held)])

    return run(
        body,
        [
            ((z.fine, z.mid), BF16),
            Raw(final, F32),
            ((z.micro, block, z.cin), BF16),
            flat_of(z.mid),
            flat_of(z.mid),
        ],
        (place, Near(back), total, counted, vec, conv, live, w_one, dp, w_side, perm, mask),
        scratch=[
            pltpu.VMEM((z.micro,) + maps + (z.cin,), F32),
            pltpu.VMEM((z.cin // LANES, block, LANES), F32),
        ],
        spare=z.micro,
        flops=2 * z.fine * z.cin * z.mid,
    )


def finish_images(z, place, got, final):
    maps = (z.half, z.held, z.side)

    def body(place_r, got_r, _, final_r, in_r, out_r, sems):
        other = 1 - place_r[0]
        loads = [pltpu.make_async_copy(got_r.at[m], in_r.at[m], sems.at[m]) for m in range(z.micro)]
        stores = [
            pltpu.make_async_copy(
                out_r.at[m], final_r.at[m, :, pl.ds(other * z.held, z.held)], sems.at[z.micro + m]
            )
            for m in range(z.micro)
        ]
        for copy in loads:
            copy.start()
        for m in range(z.micro):
            loads[m].wait()
            out_r[m] = in_r[m].astype(F32).reshape(maps + (z.cin,))
            stores[m].start()
        for copy in stores:
            copy.wait()

    any_spec = pl.BlockSpec(memory_space=pl.ANY)
    return pl.pallas_call(
        body,
        out_shape=jax.ShapeDtypeStruct(final.shape, final.dtype),
        in_specs=[pl.BlockSpec(memory_space=pltpu.SMEM), any_spec, any_spec],
        out_specs=any_spec,
        input_output_aliases={2: 0},
        scratch_shapes=[
            pltpu.VMEM(got.shape, got.dtype),
            pltpu.VMEM((z.micro,) + maps + (z.cin,), F32),
            pltpu.SemaphoreType.DMA((2 * z.micro,)),
        ],
        compiler_params=pltpu.CompilerParams(vmem_limit_bytes=5 << 20),
    )(place, got, final)


def finish_output(z, place, got, final):
    def body(place_r, got_r, _, final_r, buf_r, sems):
        other = 1 - place_r[0]
        copy = pltpu.make_async_copy(got_r, buf_r, sems.at[0])
        copy.start()
        copy.wait()
        copy = pltpu.make_async_copy(buf_r, final_r.at[:, :, pl.ds(other * z.held, z.held)], sems.at[1])
        copy.start()
        copy.wait()

    any_spec = pl.BlockSpec(memory_space=pl.ANY)
    return pl.pallas_call(
        body,
        out_shape=jax.ShapeDtypeStruct(final.shape, final.dtype),
        in_specs=[pl.BlockSpec(memory_space=pltpu.SMEM), any_spec, any_spec],
        out_specs=any_spec,
        input_output_aliases={2: 0},
        scratch_shapes=[pltpu.VMEM(got.shape, got.dtype), pltpu.SemaphoreType.DMA((2,))],
        compiler_params=pltpu.CompilerParams(vmem_limit_bytes=2 << 20),
    )(place, got, final)


def gradient_kernel(z, place, size, jobs, args):
    starts, at = [], 0
    for kind, i, j in jobs:
        starts.append(at)
        at += args[i].shape[1] * args[j].shape[1] // (2 * size * 512)
    height = at

    def body(io, place_r, *refs):
        out_r = refs[-1]
        refs = refs[:-1]
        core, me = place_r[0], place_r[1]

        def put(c, b, first, length, values):
            p = b ^ me
            p = p // 4 * 4 + p % 2 * 2 + p // 2 % 2 if c else p
            out_r[c ^ core, p, first : first + length, :] = values

        for (kind, i, j), start in zip(jobs, starts):
            lhs, rhs = refs[i], refs[j]
            io.need(lhs, rhs)
            k, n = lhs.shape[1], rhs.shape[1]
            if kind == "flat":
                per = k // (2 * size)
                for r in range(0, k, 512):
                    for c in range(0, n, 512):
                        d = dot_tn(lhs[: rhs.shape[0], r : r + 512], rhs[:, c : c + 512]).astype(BF16)
                        at = r
                        while at < r + 512:
                            chunk, inside = divmod(at, per)
                            length = min(per - inside, r + 512 - at)
                            first = start + (c // 512) * per + inside
                            put(chunk % 2, chunk // 2, first, length, d[at - r : at - r + length])
                            at += length
            elif kind == "rows" and n == 512:
                per = k // (2 * size)
                for r in range(0, k, 512):
                    d = dot_tn(lhs[:, r : r + 512], rhs[...]).astype(BF16)
                    for at in range(r, r + 512, per):
                        c, b = divmod(at // per, size)
                        put(c, b, start, per, d[at - r : at - r + per])
            elif kind == "rows":
                per = k // (2 * size)
                d = dot_tn(lhs[...].astype(BF16), rhs[...].astype(BF16)).astype(BF16)
                parts = 512 // n
                unit = per // parts
                for at in range(0, k, per):
                    c, b = divmod(at // per, size)
                    rows = [d[at + q * unit : at + (q + 1) * unit] for q in range(parts)]
                    put(c, b, start, unit, jnp.concatenate(rows, axis=1))
            else:
                d = dot_tn(lhs[...].astype(BF16), rhs[...].astype(BF16)).astype(BF16)
                across = n // 1024
                per = k * across // size
                for c in range(2):
                    for b in range(size):
                        r, lane = divmod(b, across)
                        first = c * (n // 2) + lane * 512
                        put(c, b, start, per, d[r * per : (r + 1) * per, first : first + 512])
    return body, height, starts


def gradients(z, place, size, jobs, args):
    body, height, starts = gradient_kernel(z, place, size, jobs, args)

    def outer(io, place_r, *refs):
        ins, (keep_r, send_r, both_r) = refs[:-3], refs[-3:]
        body(io, place_r, *ins, both_r)
        io.out(both_r.at[1], send_r)
        io.out(both_r.at[0], keep_r)

    shape = (size, height, 512)
    keep, send = run(
        outer,
        [Near((shape, BF16))] * 2,
        (place, *(Late(a) for a in args)),
        scratch=[pltpu.VMEM((2,) + shape, BF16)],
        spare=2,
    )
    return keep, send, starts


def part_kernel(sources, spans):
    count = sources[0][0].shape[0]
    outs = []
    for _, length, bit in spans:
        if bit:
            outs += [Near(((count // 2, length, 512), BF16))] * 2
        else:
            outs += [Near(((length, 512), BF16))] * count

    def body(io, *refs):
        ins, results = refs[: 2 * len(sources)], list(refs[2 * len(sources) :])
        pairs, at = [], 0
        for k in range(len(sources)):
            kept, come = ins[2 * k], ins[2 * k + 1]
            io.need(kept, come)
            pairs.append((at, at + kept.shape[1], kept, come))
            at += kept.shape[1]

        def pieces(first, length):
            for low, high, kept, come in pairs:
                start, stop = max(first, low), min(first + length, high)
                if start < stop:
                    yield start - first, slice(start - low, stop - low), kept, come

        for first, length, bit in spans:
            if not bit:
                for p in range(count):
                    ref = results.pop(0)
                    for to, rows, kept, come in pieces(first, length):
                        total = kept[p, rows].astype(F32) + come[p, rows].astype(F32)
                        ref[to : to + rows.stop - rows.start, :] = total.astype(BF16)
                continue
            kept_r, sent_r = results.pop(0), results.pop(0)
            for which, ref in ((1, sent_r), (0, kept_r)):
                for p in range(count):
                    if (p // bit) % 2 == which:
                        at = p // (2 * bit) * bit + p % bit
                        for to, rows, kept, come in pieces(first, length):
                            size = rows.stop - rows.start
                            total = kept[p, rows].astype(F32) + come[p, rows].astype(F32)
                            ref[at, to : to + size, :] = total.astype(BF16)

    return run(body, outs, [Near(a) for pair in sources for a in pair])


def second_step(kept, come, narrow):
    count, height = kept.shape[0] // 2, kept.shape[1]
    rows = narrow[0].shape[0]

    def body(io, a, b, *refs):
        *blocks, kept_r, sent_r = refs
        for p in range(count):
            total = a[2 * p + 1].astype(F32) + b[2 * p + 1].astype(F32)
            sent_r[p, :height, :] = total.astype(BF16)
            sent_r[p, height:, :] = blocks[p][...]
        for p in range(count):
            kept_r[p] = (a[2 * p].astype(F32) + b[2 * p].astype(F32)).astype(BF16)

    outs = [Near(((count, height, 512), BF16)), Near(((count, height + rows, 512), BF16))]
    return run(body, outs, [Near(a) for a in (kept, come, *narrow)])


def third_step(kept, come, narrow):
    count, height = kept.shape[0], kept.shape[1]
    rows = narrow[0].shape[0]

    def body(io, a, b, *refs):
        blocks, outs, part_r = refs[:count], refs[count : 2 * count], refs[2 * count]
        for p in reversed(range(count)):
            total = a[p].astype(F32) + b[p, :height].astype(F32)
            outs[p][...] = total.astype(BF16)
        for p in range(count):
            part_r[p] = blocks[p][...]
            part_r[count + p] = b[p, height:]

    outs = [Near(((height, 512), BF16))] * count + [Near(((2 * count, rows, 512), BF16))]
    return run(body, outs, [Near(a) for a in (kept, come, *narrow)])


def total_kernel(blocks, grads=None):
    shape = blocks[0].shape

    def body(io, *refs):
        ins, outs = refs[: len(blocks)], refs[len(blocks) :]
        if grads is None:
            outs[0][...] = tree_sum([ref[...].astype(F32) for ref in ins])
            return
        first = 0
        for out_r, (rows, width) in zip(outs, grads):
            height = rows * 512 // width
            for part in range(width // 512):
                at = first + part * height
                total = tree_sum([ref[at : at + height, :].astype(F32) for ref in ins])
                for k in range(512 // LANES):
                    spots = pl.ds(part * (512 // LANES) + k, height, stride=width // LANES)
                    out_r[spots, :] = total[:, k * LANES : (k + 1) * LANES]
            first += rows

    if grads is None:
        return run(body, [(shape, F32)], [Near(b) for b in blocks])[0]
    outs = [((rows * 512 // LANES, LANES), F32) for rows, _ in grads]
    return [flat.reshape(-1) for flat in run(body, outs, [Near(b) for b in blocks])]


def crossed(block, first, second):
    count = 2 * lax.axis_size("batch")
    route = [(i, (i // 2 ^ (second if i % 2 else first)) * 2 + i % 2) for i in range(count)]
    return lax.ppermute(block, ("batch", "rows"), route)


class Halving:
    def __init__(self, blocks):
        self.height = sum(keep.shape[1] for keep, _ in blocks)
        self.sources = blocks
        self.step = 0

    def prepare(self, *after):
        (kept, came), *others = self.sources
        bit = 1 if self.step < 2 else 0
        self.kept, *self.sent = part_kernel(
            [(tied(kept, *after), came), *others], ((0, self.height, bit),)
        )
        return self.sent[0]

    def send(self, *after):
        sent = [tied(s, *after) for s in self.sent]
        if self.step == 2:
            came = [swapped(s, "batch", 4 * (k + 1)) for k, s in enumerate(sent)]
            self.blocks = [self.kept] + came
        else:
            came = [crossed(sent[0], self.step + 1, 2 - self.step)]
            self.sources = [(self.kept, came[0])]
        self.step += 1
        return came

    def finish(self, grads):
        return total_kernel(self.blocks, grads)


def N(array):
    return Near(array)


def tied(value, *others):
    return lax.optimization_barrier((value, *others))[0] if others else value


def gathered_kernel(z, place, size, blocks, starts):
    across = z.out // 1024
    unit = z.out // 2 // size
    parts = 512 // z.hid
    tall = unit // parts
    wide = z.hid * across // size
    height = blocks[0].shape[1]

    def body(io, place_r, near_r, far_r, red_r, sqb_r, exb_r, sqa_r, exa_r, all_r):
        core, me = place_r[0], place_r[1]
        for high, ref in ((0, near_r), (1, far_r)):
            for low in range(2):
                for k in range(size // 4):
                    p = 4 * k + 2 * low + high + core * (high - low)
                    all_r[p] = ref[low * (size // 4) + k]

        def rows(p, first, length):
            return all_r[p, first : first + length].astype(F32)

        for b in range(size):
            p = b ^ me
            red_r[b * unit : (b + 1) * unit, :] = rows(p, starts[0], unit)
            for at, ref in ((starts[1], sqb_r), (starts[3], sqa_r)):
                block = rows(p, at, tall)
                for q in range(parts):
                    ref[b * unit + q * tall : b * unit + (q + 1) * tall, :] = block[:, q * z.hid : (q + 1) * z.hid]
            r, lane = divmod(b, across)
            for at, ref in ((starts[2], exb_r), (starts[4], exa_r)):
                ref[r * wide : (r + 1) * wide, lane * 512 : (lane + 1) * 512] = rows(p, at, wide)

    half = z.out // 2
    return run(
        body,
        [
            ((half, z.mid), F32),
            ((half, z.hid), F32),
            ((z.hid, half), F32),
            ((half, z.hid), F32),
            ((z.hid, half), F32),
        ],
        (place, *(Near(b) for b in blocks)),
        scratch=[pltpu.VMEM((size, height, 512), BF16)],
    )


def weight_dot(inputs, grads):
    return lax.dot_general(inputs, grads, (((0,), (0,)), ((), ())), preferred_element_type=F32)


def folded(grad):
    size = lax.axis_size("batch")
    rows, width = grad.shape
    grad = grad.astype(BF16).reshape(size, 2, rows // (2 * size), width // 512, 512)
    return jnp.swapaxes(grad, 2, 3).reshape(size, 2, -1, 512)


def unfolded(block, width):
    count = width // 512
    rows = block.shape[0] // count
    return jnp.swapaxes(block.reshape(count, rows, 512), 0, 1).reshape(-1)


def tree_sum(terms):
    while len(terms) > 1:
        terms = [a + b for a, b in zip(terms[::2], terms[1::2])] + terms[len(terms) // 2 * 2 :]
    return terms[0]


def wide_sum(parts, first=(), second=(), kind=F32):
    parts = parts.astype(kind)
    parts = parts.astype(F32) + swapped(parts, "rows", 1).astype(F32)
    bits = bits_of(lax.axis_size("batch"))
    partial = parts
    for at in range(0, len(bits), 2):
        parts = tied(parts, *(first if at == 0 else second if at == 2 else ()))
        pair = bits[at : at + 2]
        masks = [pair[0], pair[1], pair[0] + pair[1]] if len(pair) == 2 else pair
        parts = parts.astype(kind)
        terms = [parts] + [swapped(parts, "batch", mask) for mask in masks]
        parts = tree_sum([term.astype(F32) for term in terms])
        partial = parts if at == 0 else partial
    return parts, partial


def plain_gradients(jobs, size):
    blocks, starts, at = [], [], 0
    for kind, lhs, rhs in jobs:
        grad = weight_dot(lhs[: rhs.shape[0]].astype(BF16), rhs.astype(BF16))
        k, n = grad.shape
        if kind == "flat":
            block = core_sum(folded(grad), 1)
        elif kind == "rows" and n == 512:
            block = core_sum(grad.astype(BF16).reshape(2, size, -1, 512), 0)
        elif kind == "rows":
            parts = 512 // n
            block = grad.astype(BF16).reshape(2, size, parts, -1, n)
            block = core_sum(jnp.swapaxes(block, 2, 3).reshape(2, size, -1, 512), 0)
        else:
            across = n // 1024
            block = grad.astype(BF16).reshape(size // across, -1, 2, across, 512)
            block = core_sum(block.transpose(2, 0, 3, 1, 4).reshape(2, size, -1, 512), 0)
        starts.append(at)
        at += block.shape[1]
        blocks.append(block)
    return halved(jnp.concatenate(blocks, axis=1), two_orders), starts


def per_device(
    images,
    crop_sizes,
    reduce_a,
    reduce_gain_a,
    reduce_bias_a,
    spatial_a,
    spatial_gain_a,
    spatial_bias_a,
    expand_a,
    expand_gain_a,
    expand_bias_a,
    project_a,
    project_gain_a,
    project_bias_a,
    squeeze_a,
    squeeze_bias_a,
    excite_a,
    excite_bias_a,
    reduce_b,
    reduce_gain_b,
    reduce_bias_b,
    spatial_b,
    spatial_gain_b,
    spatial_bias_b,
    expand_b,
    expand_gain_b,
    expand_bias_b,
    squeeze_b,
    squeeze_bias_b,
    excite_b,
    excite_bias_b,
    cotangent,
):
    mid = reduce_a.shape[1]
    out = expand_a.shape[1]
    hid = squeeze_a.shape[1]
    size = lax.axis_size("batch")
    z = Sizes(images, mid, out, hid, size * lax.axis_size("rows"))
    micro, held, side, half = z.micro, z.held, z.side, z.half
    core = lax.axis_index("rows")
    me = lax.axis_index("batch")
    place = jnp.stack([core, me]).astype(jnp.int32)

    away = lax.dynamic_slice_in_dim(images, (1 - core) * held, held, axis=2)
    other = swapped(away, "rows", 1)
    vectors = jnp.stack(
        [
            expand_gain_a,
            expand_bias_a,
            project_gain_a,
            project_bias_a,
            expand_gain_b,
            expand_bias_b,
            excite_bias_a,
            excite_bias_b,
        ]
    )

    def pair(own, axis):
        return Pair(own, swapped(own, "rows", 1), axis)

    vectors = pair(vectors, 1)
    pair_sq_a, pair_sq_b = pair(squeeze_a, 0), pair(squeeze_b, 0)
    pair_ex_a, pair_ex_b = pair(excite_a, 1), pair(excite_b, 1)
    pair_red = pair(reduce_b, 0)
    sq_biases = jnp.stack([squeeze_bias_a, squeeze_bias_b])
    vec_one = jnp.stack([reduce_gain_a, reduce_bias_a])
    vec_two = jnp.stack([spatial_gain_a, spatial_bias_a])
    vec_four = jnp.stack([reduce_gain_b, reduce_bias_b])
    vec_five = jnp.stack([spatial_gain_b, spatial_bias_b])

    half_all = crop_sizes // 2
    counted = jnp.stack(
        [jnp.sum(crop_sizes * crop_sizes, axis=1), jnp.sum(half_all * half_all, axis=1)]
    ).astype(F32).reshape(-1)
    halves = lax.dynamic_slice_in_dim(half_all, (me * 2 + core) * held, held, axis=1)
    pix = jnp.broadcast_to((halves * halves).astype(F32).reshape(-1, 1), (z.maps, LANES))
    spots = jnp.arange(half, dtype=jnp.int32)
    limits = halves[:, None, :, None]
    inside = (spots[None, :, None, None] < limits) & (spots[None, None, None, :] < limits)
    mask = jnp.broadcast_to(inside.astype(F32).reshape(z.coarse, 1), (z.coarse, LANES))

    block = 2 * z.map
    spot = jnp.arange(block, dtype=jnp.int32)
    row_pair, rest = spot // (2 * z.group), spot % (2 * z.group)
    row_odd, spot_b, column = spot // (held * side) % 2, spot % (held * side) // side, spot % side
    row_pair = spot // (2 * held * side)
    target = ((row_odd * 2 + column % 2) * (half // 2) + row_pair) * z.group
    target = target + spot_b * half + column // 2
    perm = (target[None, :] == jnp.arange(block, dtype=jnp.int32)[:, None]).astype(BF16)

    other, perm, mask, pix, counted, sq_biases, vec_one, vec_two, vec_four, vec_five, vectors.own = (
        lax.optimization_barrier(
            (other, perm, mask, pix, counted, sq_biases, vec_one, vec_two, vec_four, vec_five, vectors.own)
        )
    )
    vectors.other = swapped(vectors.own, "rows", 1)

    first_one, first_perm, first_mask, first_images = run(
        lambda io, place_r: None, [], (place,), ahead=(reduce_a, perm, mask, Part(images, 2)), room=ROOM
    )
    planes, c1_near, c1, s1, *got = enter_kernel(
        z, place, N(first_images), N(other), N(first_perm), N(first_one), N(first_mask),
        (vec_one, spatial_a, mask),
    )
    vec_near, w_near, mask_near = map(N, got)
    patches_one, c2_near, c2, t1, s2, *got = taps_kernel(
        z, place, wide_sum(s1)[0], counted, vec_near, N(c1_near), w_near, mask_near, True,
        (vec_two, expand_a, mask, Top(planes, z.coarse), project_a, Away(cotangent, 2)),
    )
    vec_near, w_near, mask_near, *side_near = map(N, got[:5])
    up = Join(cotangent, 2, swapped(got[5], "rows", 1), 4)
    active_two, e1_near, e1, t2, p1_near, p1, s3, *got = expand_kernel(
        z, place, wide_sum(s2)[0], counted, vec_near, N(c2_near), w_near, mask_near, side_near,
        (vectors, pix, pair_sq_a, sq_biases, pair_ex_a, pair_red, mask),
    )
    vectors_near, pix_near, sq_near, sqb_near, ex_near, w_near, mask_near = map(N, got)
    sums_three, _ = wide_sum(s3)
    middle, c4_near, c4, gate_one, pool_one, inner_one, hidden_one, total_three, s4, *got = middle_kernel(
        z, place, sums_three, counted, vectors_near, pix_near, N(e1_near), N(p1_near), sq_near, sqb_near, ex_near,
        w_near, mask_near, (vec_four, spatial_b, mask),
    )
    vec_near, w_near, mask_near = map(N, got)
    patches_four, c5_near, c5, t4, s5, *got = taps_kernel(
        z, place, wide_sum(s4)[0], counted, vec_near, N(c4_near), w_near, mask_near, False,
        (vec_five, expand_b, mask),
    )
    vec_near, w_near, mask_near = map(N, got)
    active_five, e2_near, e2, t5, s6, *got = expand_kernel(
        z, place, wide_sum(s5)[0], counted, vec_near, N(c5_near), w_near, mask_near, None,
        (vectors, pix, middle, up, pair_sq_b, sq_biases, pair_ex_b, mask),
    )
    vectors_near, pix_near, mid_near, up_near, sq_near, sqb_near, ex_near, mask_near = map(N, got)
    sums_six, _ = wide_sum(s6)
    final = (micro, half, 2 * held, half, out // 2)
    block_out, block_away, do2, h_near, pool_two, hidden_two, dl_two, dz_two, b6, *got = output_kernel(
        z, place, sums_six, counted, vectors_near, pix_near, N(e2_near), mid_near, up_near,
        sq_near, sqb_near, ex_near, mask_near, final,
        (N(sums_six), vectors, e2, expand_b, t5, vec_five, c5, mask),
    )
    total_near, vectors_near, e_near, w_near, tn_near, vn_near, cn_near, mask_near = map(N, got)

    whole_tiles = mid * 9 // (2 * size) % 16 == 0

    def made(jobs):
        if not whole_tiles:
            return None
        args, spec = [], []
        for kind, lhs, rhs in jobs:
            spec.append((kind, len(args), len(args) + 1))
            args += [lhs, rhs]
        keep, send, _ = gradients(z, place, size, spec, args)
        return keep, send

    def steps(make):
        return list(make()) if whole_tiles else []

    def exchanged(blocks, *after):
        keep, send = blocks
        return keep, swapped(tied(send, *after), "rows", 1)

    back_six, _ = wide_sum(b6, kind=BF16)
    de2, live_near, b5, gain_six, bias_six, ex_bias_two, sq_bias_two, *got = unexpand_kernel(
        z, place, back_six, total_near, counted, vectors_near, 4, e_near, N(h_near), w_near,
        tn_near, vn_near, cn_near, mask_near, (t5, vec_five, c5, spatial_b, t4, vec_four, c4, mask),
    )
    t_near, v_near, c_near, w_near, tn_near, vn_near, cn_near, mask_near = map(N, got)
    jobs_e = (("flat", active_five, de2),)
    made_e = made(jobs_e)
    block_out = finish_output(z, place, swapped(block_away, "rows", 1), block_out)
    back_five, _ = wide_sum(b5, (), [block_out, *steps(lambda: [made_e[0]])], BF16)
    dc5, live_near, g5, h5, b4, *got = untap_kernel(
        z, place, back_five, t_near, counted, v_near, c_near, N(live_near), w_near,
        tn_near, vn_near, cn_near, mask_near, False,
        (t4, vec_four, c4, pair_red, do2, total_three, vectors, gate_one, inner_one, e1, p1, pair_sq_a, pair_ex_a, pix, mask),
    )
    t_near, v_near, c_near, w_near, *rest_near = map(N, got)
    jobs_s = (("flat", patches_four, dc5),)
    made_s = made(jobs_s)
    if whole_tiles:
        sum_e = Halving([exchanged(made_e, back_five)])
        b4 = tied(b4, sum_e.sources[0][1])
    back_four, _ = wide_sum(b4, (), steps(lambda: [made_s[0], sum_e.prepare()]), BF16)
    came = steps(lambda: sum_e.send(back_four))
    dc4, do1, h_near, g4, h4, dl_one, dz_one, b3, *got = unreduce_kernel(
        z, place, back_four, t_near, counted, v_near, c_near, N(live_near), w_near, *rest_near,
        (total_three, vectors, e1, expand_a, t2, vec_two, c2, mask),
    )
    total_near, vectors_near, e_near, w_near, tn_near, vn_near, cn_near, mask_near = map(N, got)
    jobs_n = (
        ("rows", middle, dc4),
        ("rows", pool_two, dz_two),
        ("lanes", hidden_two, dl_two),
        ("rows", pool_one, dz_one),
        ("lanes", hidden_one, dl_one),
    )
    made_n = made(jobs_n)
    if whole_tiles:
        sum_s = Halving([exchanged(made_s, back_four)])
        came += [sum_s.sources[0][1]]
    back_three, _ = wide_sum(
        tied(b3, *came), (), steps(lambda: [made_n[0], sum_s.prepare(), sum_e.prepare()]), BF16
    )
    came = steps(lambda: sum_s.send(back_three) + sum_e.send(back_three))
    (
        de1, live_near, b2, gain_three, bias_three, gain_side, bias_side, ex_bias_one, sq_bias_one, *got
    ) = unexpand_kernel(
        z, place, back_three, total_near, counted, vectors_near, 0, e_near, N(h_near), w_near,
        tn_near, vn_near, cn_near, mask_near, (t2, vec_two, c2, spatial_a, t1, vec_one, c1, mask),
    )
    t_near, v_near, c_near, w_near, tn_near, vn_near, cn_near, mask_near = map(N, got)
    dp1 = side_kernel(z, place, N(back_three), total_three, counted, vectors, p1, do1, mask)
    jobs_w = (("flat", active_two, de1), ("flat", planes, dp1))
    made_w = made(jobs_w)
    if whole_tiles:
        sum_n = Halving([exchanged(made_n, back_three)])
        came += [made_w[0], sum_n.sources[0][1]]
    back_two, _ = wide_sum(
        tied(b2, dp1, *came), (), steps(lambda: [sum_n.prepare(), sum_s.prepare(), sum_e.prepare()]), BF16
    )
    came = steps(lambda: sum_n.send(back_two) + sum_e.send(back_two))
    dc2, live_near, g2, h2, b1, *got = untap_kernel(
        z, place, back_two, t_near, counted, v_near, c_near, N(live_near), w_near,
        tn_near, vn_near, cn_near, mask_near, True,
        (t1, vec_one, c1, reduce_a, dp1, project_a, perm, mask),
    )
    t_near, v_near, c_near, *rest_near = map(N, got)
    jobs_t = (("flat", patches_one, dc2),)
    made_t = made(jobs_t)
    if whole_tiles:
        sum_w = Halving([exchanged(made_w, back_two)])
        came += [made_t[0], sum_w.sources[0][1]]
    back_one, _ = wide_sum(tied(b1, *came), (), steps(lambda: [sum_n.prepare(), sum_w.prepare()]), BF16)
    came_t = exchanged(made_t, back_one) if whole_tiles else None
    came = steps(lambda: sum_n.send(back_one) + sum_s.send(back_one))
    dc1, images_grad, grad_away, g1, h1 = leave_kernel(
        z, place, back_one, t_near, counted, v_near, c_near, N(live_near), *rest_near,
        (micro, side // 2, 2 * held, side, z.cin),
    )
    jobs_r = (("flat", planes, dc1),)
    made_r = made(jobs_r)

    images_grad = finish_images(z, place, swapped(grad_away, "rows", 1), images_grad)

    if whole_tiles:
        heights = [a.shape[1] * b.shape[1] // (2 * size * 512) for _, a, b in jobs_n]
        at_second = [sum(heights[:k]) for k in range(len(heights) + 1)]
        def rows_of(grad):
            return grad.size // (2 * size * 512), grad.shape[1]

        here = [made_r[0], *came, came_t[1]]
        came = sum_w.send(*here)
        came_r = exchanged(made_r, *here)
        sum_n.prepare(*here)
        came += sum_n.send()
        sum_t = Halving([came_t, came_r])
        here = [images_grad, *came, sum_t.prepare()]
        came = sum_t.send(*here)
        second = total_kernel([tied(sum_n.blocks[0], *here), *sum_n.blocks[1:]])
        narrows = second.astype(BF16)
        around = [swapped(narrows, "batch", 4 * k) for k in range(1, size // 4)]
        sum_w.prepare(*here)
        came += sum_w.send()
        sum_s.prepare(sum_w.sent[0])
        here = [*came, *around, *sum_s.send()]
        narrow = [narrows, *around]
        sum_e.blocks[0] = tied(sum_e.blocks[0], around[0])
        (out_expand_b,) = sum_e.finish([rows_of(expand_b)])
        sum_w.prepare(out_expand_b, *here)
        came = sum_w.send()
        (kept, come), = sum_t.sources
        kept, sent = second_step(tied(kept, sum_w.sent[0]), come, narrow)
        come = crossed(sent, 2, 1)
        sum_s.blocks[0] = tied(sum_s.blocks[0], sent)
        (out_spatial_b,) = sum_s.finish([rows_of(spatial_b)])
        *blocks, part = third_step(tied(kept, out_spatial_b, *came), come, narrow)
        sum_t.blocks = blocks[:1] + [
            swapped(block, "batch", 4 * (k + 1)) for k, block in enumerate(blocks[1:])
        ]
        every = part, crossed(part, 1, 2)
        narrow_outs = gathered_kernel(z, place, size, every, at_second)
        sum_t.blocks[0] = tied(sum_t.blocks[0], narrow_outs[0])
        sum_w.blocks[0] = tied(sum_w.blocks[0], every[1])
        out_expand_a, out_project_a = sum_w.finish([rows_of(expand_a), rows_of(project_a)])
        out_spatial_a, out_reduce_a = sum_t.finish([rows_of(spatial_a), rows_of(reduce_a)])
    else:
        second, at_second = plain_gradients(jobs_n, size)
        at_second = at_second + [second.shape[0]]
        edge_first = expand_b.size // (2 * size * 512)
        edge_rest = expand_a.size // (2 * size * 512)
        edge_third = spatial_a.size // (2 * size * 512)
        first = plain_gradients(jobs_e + jobs_s, size)[0]
        rest = plain_gradients(jobs_w, size)[0]
        third = plain_gradients(jobs_t + jobs_r, size)[0]
        out_expand_b, out_spatial_b = unfolded(first[:edge_first], out), unfolded(first[edge_first:], mid)
        out_expand_a, out_project_a = unfolded(rest[:edge_rest], out), unfolded(rest[edge_rest:], out)
        out_spatial_a, out_reduce_a = unfolded(third[:edge_third], mid), unfolded(third[edge_third:], mid)
    if whole_tiles:
        out_reduce, out_sq_b, out_ex_b, out_sq_a, out_ex_a = narrow_outs
    else:
        every = collected(second.astype(BF16)).astype(F32)

        def tall_of(k):
            block = every[:, at_second[k] : at_second[k + 1]]
            block = block.reshape(size, block.shape[1], 512 // hid, hid)
            return jnp.swapaxes(block, 1, 2).reshape(-1, hid)

        def flat_of(k):
            block = every[:, at_second[k] : at_second[k + 1]]
            across = (out // 2) // 512
            block = block.reshape(size // across, across, -1, 512)
            return jnp.swapaxes(block, 1, 2).reshape(hid, out // 2)

        out_reduce = every[:, : at_second[1]].reshape(-1, mid)
        out_sq_b, out_ex_b, out_sq_a, out_ex_a = tall_of(1), flat_of(2), tall_of(3), flat_of(4)
    span = out // 2

    return (
        block_out,
        images_grad,
        out_reduce_a,
        g1.reshape(-1),
        h1.reshape(-1),
        out_spatial_a,
        g2.reshape(-1),
        h2.reshape(-1),
        out_expand_a,
        gain_three.reshape(-1),
        bias_three.reshape(-1),
        out_project_a,
        gain_side.reshape(-1),
        bias_side.reshape(-1),
        out_sq_a,
        sq_bias_one.reshape(-1),
        out_ex_a,
        ex_bias_one.reshape(-1),
        out_reduce,
        g4.reshape(-1),
        h4.reshape(-1),
        out_spatial_b,
        g5.reshape(-1),
        h5.reshape(-1),
        out_expand_b,
        gain_six.reshape(-1),
        bias_six.reshape(-1),
        out_sq_b,
        sq_bias_two.reshape(-1),
        out_ex_b,
        ex_bias_two.reshape(-1),
    )


def solution(mesh):
    in_specs = (
        P(None, "rows", "batch", None, None),
        P(),
        P(),
        P(),
        P(),
        P(),
        P(),
        P(),
        P(),
        P("rows"),
        P("rows"),
        P(),
        P("rows"),
        P("rows"),
        P("rows", None),
        P(),
        P(None, "rows"),
        P("rows"),
        P("rows", None),
        P(),
        P(),
        P(),
        P(),
        P(),
        P(),
        P("rows"),
        P("rows"),
        P("rows", None),
        P(),
        P(None, "rows"),
        P("rows"),
        P(None, None, "batch", None, "rows"),
    )
    out_specs = (
        P(None, None, "batch", None, "rows"),
        P(None, "rows", "batch", None, None),
        P(("batch", "rows")),
        P(),
        P(),
        P(("batch", "rows")),
        P(),
        P(),
        P(("batch", "rows")),
        P("rows"),
        P("rows"),
        P(("batch", "rows")),
        P("rows"),
        P("rows"),
        P("rows", None),
        P(),
        P(None, "rows"),
        P("rows"),
        P("rows", None),
        P(),
        P(),
        P(("batch", "rows")),
        P(),
        P(),
        P(("batch", "rows")),
        P("rows"),
        P("rows"),
        P("rows", None),
        P(),
        P(None, "rows"),
        P("rows"),
    )
    return jax.shard_map(
        per_device, mesh=mesh, in_specs=in_specs, out_specs=out_specs, check_vma=False
    )
```
